32 devices in a mesh: gx: 4 (over y, x), gy: 8 (over z, core).
Axes of the slice: x: 2, y: 2, z: 4, core: 2. Of those that a mesh axis runs over, the one named last changes fastest.
Arguments:
- ice_displacement: float32 [2, 32, 64, 128], P(None, 'gx', 'gy'), may hold values from -1.8 to 1.8
- ice_velocity: float32 [2, 32, 64, 128], P(None, 'gx', 'gy'), may hold values from -6 to 6
- jitter: float32 [2, 32, 64, 128], P(None, 'gx', 'gy'), may hold values from -0.2 to 0.2
- bond_mask: int32 [32, 64, 9], P('gx', 'gy'), may hold values from -2147483648 to 2147483647, as said below
- contact_node: int32 [64, 128], P('gy'), may hold values from 0 to 2097151, as said below
- intersection: float32 [64, 128], P('gy'), may hold values from -0.5 to 1
- shell_deflection: float32 [512, 4096], P('gx', 'gy'), may hold values from -1.8 to 1.8
- shell_velocity: float32 [512, 4096], P('gx', 'gy'), may hold values from -6 to 6
Outputs:
- ice_moved: float32 [2, 32, 64, 128], P(None, 'gx', 'gy')
- ice_speed: float32 [2, 32, 64, 128], P(None, 'gx', 'gy')
- shell_moved: float32 [512, 4096], P('gx', 'gy')
- shell_speed: float32 [512, 4096], P('gx', 'gy')
The draws below stay inside these ranges and needn't reach their ends.
Inputs may be any that keep to these rules, and one draw needn't show every extreme that they name: Bit 4 * i + k of bond_mask[a, b, s] (bit 31 being the sign bit) is 1 where the bonds from the points of lengthwise row i of tile (a, b) to the points q with 4 q // 128 == k of neighbouring tile s are intact. contact_node = r * 4096 + c for shell row r and column c; for point q of tile column t, c // 4 == t * 16 + q % 16 and r // 64 == q // 16.
All inputs are finite; a program needn't handle non-finite values.
Results may differ from the reference program's by a relative error of at most 0.0001.
Values sent between devices are 32-bit elements; how exact they have to be, the bound alone decides.
No kernel may reach another device: no remote copies, remote signals or barrier semaphores. Data moves between devices by JAX's collectives and lax.ppermute only.
A program may use at most 64 MiB of HBM per device.

```python
import jax
import jax.numpy as jnp
from jax import lax

TILE_X = 8
TILE_Y = 16
PTS = 128
STEPS = 2
GX_T = 32
GY_T = 64
SH_H = 512
SH_C = 4096
SHELL_NODES = 2097152


def draw_bond_mask(key, part):
    pieces = jax.random.randint(jax.random.fold_in(key, 3), (32, GX_T, GY_T, 9), 0, 5)
    intact = (pieces > 0).astype(jnp.int32)
    packed = jnp.zeros((GX_T, GY_T, 9), jnp.int32)
    for bit_place in range(31):
        packed = packed + intact[bit_place] * 2 ** bit_place
    return packed + intact[31] * jnp.int32(-2147483648)


def draw_contact_node(key, part):
    key_rows, key_cols = jax.random.split(jax.random.fold_in(key, 7), 2)
    band_rows = SH_H // TILE_X
    point_ids = jnp.arange(PTS, dtype=jnp.int32)
    tile_ids = jnp.arange(GY_T, dtype=jnp.int32)
    depth_row = (point_ids // TILE_Y)[None, :]
    lateral = tile_ids[:, None] * TILE_Y + (point_ids % TILE_Y)[None, :]
    row_ids = depth_row * band_rows + jax.random.randint(key_rows, (GY_T, PTS), 0, band_rows)
    col_ids = 4 * lateral + jax.random.randint(key_cols, (GY_T, PTS), 0, 4)
    return (row_ids * SH_C + col_ids).astype(jnp.int32)


def level_of(rng, extent, shards, low, top_value):
    def one(position, shards_of):
        steps = jax.random.uniform(jax.random.fold_in(jax.random.fold_in(rng, 6), position), (shards_of,), jnp.float32, low / len(shards), top_value / len(shards))
        return jnp.repeat(jnp.exp(steps), extent[position] // shards_of).reshape((-1,) + (1,) * (len(extent) - position - 1))

    factor_of = one(*shards[0])
    for cut in shards[1:]:
        factor_of = factor_of * one(*cut)
    return factor_of


def noise(rng, shape, width, limit, shards=(), held_as=jnp.bfloat16):
    factor_of = level_of(rng, shape, shards, -0.22, 0.18) if shards else 1.0
    result = jax.random.normal(rng, shape, jnp.float32) * width * factor_of
    return jnp.minimum(jnp.maximum(result, -limit), limit).astype(held_as)


def setup_inputs(seed: int = 0) -> dict:
    key_of = jax.random.split(jax.random.key(seed), 9)
    ice_displacement = noise(key_of[0], (2, GX_T, GY_T, PTS), 0.3, 1.8, ((1, 4), (2, 8)), jnp.float32)
    ice_velocity = noise(key_of[1], (2, GX_T, GY_T, PTS), 1.0, 6.0, ((1, 4), (2, 8)), jnp.float32)
    jitter = jnp.clip(jax.random.uniform(key_of[2], (2, GX_T, GY_T, PTS), jnp.float32, -0.2, 0.2) * level_of(key_of[2], (2, GX_T, GY_T, PTS), ((1, 4), (2, 8)), -0.4, 0.0), -0.2, 0.2)
    bond_mask = draw_bond_mask(jax.random.fold_in(key_of[8], 71), 0)
    contact_node = draw_contact_node(jax.random.fold_in(key_of[8], 71), 0)
    intersection = jnp.clip(-0.5 + 1.5 * jax.random.uniform(key_of[5], (GY_T, PTS), jnp.float32) ** level_of(key_of[5], (GY_T, PTS), ((0, 8),), -0.2, 0.2), -0.5, 1.0)
    shell_deflection = noise(key_of[6], (SH_H, SH_C), 0.3, 1.8, ((0, 4), (1, 8)), jnp.float32)
    shell_velocity = noise(key_of[7], (SH_H, SH_C), 1.0, 6.0, ((0, 4), (1, 8)), jnp.float32)
    return {"ice_displacement": ice_displacement, "ice_velocity": ice_velocity, "jitter": jitter, "bond_mask": bond_mask, "contact_node": contact_node, "intersection": intersection, "shell_deflection": shell_deflection, "shell_velocity": shell_velocity}


BOND_C = 1.0
HORIZON = 3.5
DELTA_SQ = 0.25
PENALTY = 4.0
BEND = 0.5
STEP_DT = 0.2

def pair_force(center, nearby, words, shift_x, shift_y):
    points = jnp.arange(TILE_X * TILE_Y, dtype=jnp.int32)
    bit_index = 4 * (points // TILE_Y)[:, None] + (4 * points // PTS)[None, :]
    intact = jnp.right_shift(words[..., None, None], bit_index) & 1
    lengthwise = (points // TILE_Y).astype(jnp.float32)
    sideways = (points % TILE_Y).astype(jnp.float32)
    base_x = shift_x * TILE_X + lengthwise[None, :] - lengthwise[:, None]
    base_y = shift_y * TILE_Y + sideways[None, :] - sideways[:, None]
    rest_x = base_x + (nearby[2][..., None, :] - center[2][..., :, None])
    rest_y = base_y + (nearby[3][..., None, :] - center[3][..., :, None])
    now_x = rest_x + (nearby[0][..., None, :] - center[0][..., :, None])
    now_y = rest_y + (nearby[1][..., None, :] - center[1][..., :, None])
    radius = jnp.sqrt(rest_x * rest_x + rest_y * rest_y + DELTA_SQ)
    stretched = jnp.sqrt(now_x * now_x + now_y * now_y + DELTA_SQ)
    reach = jnp.maximum(1.0 - radius / HORIZON, 0.0)
    factor = BOND_C * intact.astype(jnp.float32) * reach * reach * (stretched - radius) / (radius * stretched)
    return jnp.stack([lax.optimization_barrier(jnp.sum(factor * now_x, axis=-1)), lax.optimization_barrier(jnp.sum(factor * now_y, axis=-1))])

def ice_forces(displacement, jitter, bond_mask):
    rows = displacement.shape[1]
    columns = displacement.shape[2]
    fields = jnp.concatenate([displacement, jitter], axis=0)
    padded = jnp.pad(fields, ((0, 0), (1, 1), (1, 1), (0, 0)))
    inside = jnp.pad(jnp.ones((rows, columns), jnp.float32), 1)

    def one_row(index):
        window = lax.dynamic_slice_in_dim(padded, index, 3, axis=1)
        present = lax.dynamic_slice_in_dim(inside, index, 3, axis=0)
        masks = lax.dynamic_index_in_dim(bond_mask, index, axis=0, keepdims=False)
        center = window[:, 1, 1:1 + columns]
        totals = jnp.zeros((2, columns, TILE_X * TILE_Y), jnp.float32)
        for offset in range(9):
            shift_x = offset // 3 - 1
            shift_y = offset % 3 - 1
            nearby = window[:, 1 + shift_x, 1 + shift_y:1 + shift_y + columns]
            weight = present[1 + shift_x, 1 + shift_y:1 + shift_y + columns]
            totals = totals + pair_force(center, nearby, masks[:, offset], shift_x, shift_y) * weight[None, :, None]
        return totals
    forces = lax.map(one_row, jnp.arange(rows, dtype=jnp.int32))
    return jnp.transpose(forces, (1, 0, 2, 3))

def laplace(field):
    return field[2:, 1:-1] + field[:-2, 1:-1] + field[1:-1, 2:] + field[1:-1, :-2] - 4.0 * field[1:-1, 1:-1]

def reference(ice_displacement, ice_velocity, jitter, bond_mask, contact_node, intersection, shell_deflection, shell_velocity):
    flat_nodes = contact_node.reshape(-1)
    for iteration in range(STEPS):
        forces = ice_forces(ice_displacement, jitter, bond_mask)
        front_gap = ice_displacement[0, GX_T - 1] + intersection
        reached = shell_deflection.reshape(-1)[flat_nodes].reshape(front_gap.shape)
        pushes = PENALTY * jnp.maximum(front_gap - reached, 0.0)
        forces = forces.at[0, GX_T - 1].add(-pushes)
        loading = jax.ops.segment_sum(pushes.reshape(-1), flat_nodes, num_segments=SHELL_NODES).reshape(SH_H, SH_C)
        bending = laplace(laplace(jnp.pad(shell_deflection, 2)))
        ice_velocity = ice_velocity + STEP_DT * forces
        ice_displacement = ice_displacement + STEP_DT * ice_velocity
        shell_velocity = shell_velocity + STEP_DT * (loading - BEND * bending)
        shell_deflection = shell_deflection + STEP_DT * shell_velocity
    return (ice_displacement, ice_velocity, shell_deflection, shell_velocity)
```

```python
import functools

import jax
import jax.numpy as jnp
from jax import lax
from jax.experimental import pallas as pl
from jax.experimental.pallas import tpu as pltpu
from jax.sharding import PartitionSpec as P

TILE_X = 8
TILE_Y = 16
PTS = 128
SPLIT = 4

HORIZON = 3.5
DELTA_SQ = 0.25
PENALTY = 4.0
BEND = 0.5
STEP_DT = 0.2

F32 = jnp.float32
I32 = jnp.int32

STRIDE = 24
WIDE = 640
PAD = 16


def bond_offsets():
    limit = HORIZON * HORIZON - DELTA_SQ
    found = []
    for oy in range(-4, 5):
        for ox in range(-4, 5):
            near = max(abs(ox) - 0.4, 0.0) ** 2 + max(abs(oy) - 0.4, 0.0) ** 2
            if near < limit and (ox or oy):
                found.append((ox, oy))
    return found


OFFSETS = bond_offsets()
SIDEWAYS = sorted({oy for _, oy in OFFSETS})


def sign(value):
    return (value > 0) - (value < 0)


def lanes():
    return lax.broadcasted_iota(I32, (8, PTS), 1)


def subs():
    return lax.broadcasted_iota(I32, (8, PTS), 0)


def turn(values, shift):
    size = values.shape[1]
    return pltpu.roll(values, shift % size, 1) if shift % size else values


def slot(dx, dy):
    return 3 * (dx + 1) + dy + 1


def lane_masks():
    lane = lanes()
    row, col = lane // TILE_Y, lane % TILE_Y
    masks = {}
    for o in (1, 2, 3):
        masks["col_at", o] = col < o
        masks["col_at", -o] = col >= TILE_Y - o
        masks["col_from", o] = col >= TILE_Y - o
        masks["col_from", -o] = col < o
        masks["row_at", o] = row < o
        masks["row_at", -o] = row >= TILE_X - o
        masks["row_from", o] = row >= TILE_X - o
        masks["row_from", -o] = row < o
    bits = {}
    for ox in range(-3, 4):
        bits[ox] = jnp.left_shift(jnp.int32(1), 4 * row + ((row + ox) & 7) // 2)
    return masks, bits


def moved(get, oy, masks):
    out = {}
    for dx in (-1, 0, 1):
        held = get(dx, 0)
        if oy:
            held = turn(jnp.where(masks["col_at", oy], get(dx, sign(oy)), held), -oy)
        out[dx] = held
    return out


def across(cells, ox, masks):
    if not ox:
        return cells[0]
    return turn(jnp.where(masks["row_at", ox], cells[sign(ox)], cells[0]), -TILE_Y * ox)


def first_forces(get_jx, get_jy, get_dx, get_dy, get_words, keep=None, both=True):
    masks, bits = lane_masks()
    jx0, jy0, dx0, dy0 = get_jx(0, 0), get_jy(0, 0), get_dx(0, 0), get_dy(0, 0)
    fx = jnp.zeros((8, PTS), F32)
    fy = jnp.zeros((8, PTS), F32)
    for oy in SIDEWAYS:
        jxs, jys = moved(get_jx, oy, masks), moved(get_jy, oy, masks)
        dxs, dys = moved(get_dx, oy, masks), moved(get_dy, oy, masks)
        words = {}
        for dx in (-1, 0, 1):
            words[dx] = get_words(dx, 0)
            if oy:
                words[dx] = jnp.where(masks["col_from", oy], get_words(dx, sign(oy)), words[dx])
        for number, (ox, other) in enumerate(OFFSETS):
            if other != oy:
                continue
            word = words[0]
            if ox:
                word = jnp.where(masks["row_from", ox], words[sign(ox)], word)
            intact = (word & bits[ox]) != 0
            rest_x = across(jxs, ox, masks) - (jx0 - float(ox))
            rest_y = across(jys, ox, masks) - (jy0 - float(oy))
            now_x = across(dxs, ox, masks) - (dx0 - float(ox))
            now_y = across(dys, ox, masks) - (dy0 - float(oy))
            rest_sq = rest_x * rest_x + rest_y * rest_y + DELTA_SQ
            now_sq = now_x * now_x + now_y * now_y + DELTA_SQ
            rest_inv = lax.rsqrt(rest_sq)
            reach = jnp.maximum(1.0 - rest_sq * rest_inv * (1.0 / HORIZON), 0.0)
            weight = jnp.where(intact, reach * reach, 0.0)
            level = weight * rest_inv
            if keep is not None:
                keep(number, weight, level)
            factor = level - weight * lax.rsqrt(now_sq)
            fx = fx + factor * now_x
            if both:
                fy = fy + factor * now_y
    return fx, fy


def second_forces(get_dx, get_dy, kept):
    masks, _ = lane_masks()
    dx0, dy0 = get_dx(0, 0), get_dy(0, 0)
    fx = jnp.zeros((8, PTS), F32)
    fy = jnp.zeros((8, PTS), F32)
    for oy in SIDEWAYS:
        dxs, dys = moved(get_dx, oy, masks), moved(get_dy, oy, masks)
        for number, (ox, other) in enumerate(OFFSETS):
            if other != oy:
                continue
            now_x = across(dxs, ox, masks) - (dx0 - float(ox))
            now_y = across(dys, ox, masks) - (dy0 - float(oy))
            now_sq = now_x * now_x + now_y * now_y + DELTA_SQ
            weight, level = kept(number)
            factor = level - weight * lax.rsqrt(now_sq)
            fx = fx + factor * now_x
            fy = fy + factor * now_y
    return fx, fy


def widen(row_of, count):
    lane, sub = lanes(), subs()
    index = sub * TILE_Y + (lane % 64) // SPLIT
    out = []
    for j in range(count):
        left, right = (
            jnp.take_along_axis(jnp.broadcast_to(row_of(b), (8, PTS)), index, axis=1) for b in (2 * j, 2 * j + 1)
        )
        out.append(jnp.where(lane < 64, left, right))
    return out


def narrow(block_of, tiles):
    lane, sub = lanes(), subs()
    out = []
    for b in tiles:
        held = block_of(b // 2)
        held = held + turn(held, -1)
        held = held + turn(held, -2)
        picked = jnp.take_along_axis(held, 64 * (b % 2) + SPLIT * (lane % TILE_Y), axis=1)
        out.append(jnp.sum(jnp.where(sub == lane // TILE_Y, picked, 0.0), axis=0, keepdims=True))
    return out


def lay_out(ref, at, j, block):
    for row in range(TILE_X):
        ref[at + (row, slice(None), slice(j * PTS, (j + 1) * PTS))] = jnp.broadcast_to(block[row : row + 1], (8, PTS))


class Place:
    def __init__(self, nx, ny, shell_rows, shell_cols):
        self.nx, self.ny = nx, ny
        self.gx, self.gy = lax.axis_index("gx"), lax.axis_index("gy")
        self.shell_rows, self.shell_cols = shell_rows, shell_cols
        self.width = shell_cols * ny
        self.band = shell_rows * nx // TILE_X
        self.bands = shell_rows // self.band
        self.front = self.gx == nx - 1

    def sides(self, first, second):
        even = self.gy % 2 == 0
        right = jnp.where(even, first, second)
        left = jnp.where(even, second, first)
        right = jnp.where(self.gy < self.ny - 1, right, 0.0)
        left = jnp.where(self.gy > 0, left, 0.0)
        return right, left

    def nodes(self, row, columns):
        shape = (8, columns)
        col = lax.broadcasted_iota(I32, shape, 1)
        if columns > self.shell_cols:
            col = jnp.where(col >= self.shell_cols + 64, col - columns, col)
        first = (self.gx * self.shell_rows + row) * self.width + self.gy * self.shell_cols
        return (first + lax.broadcasted_iota(I32, shape, 0) * self.width + col).astype(F32)

    def band_of(self, row):
        return jnp.clip((self.gx * self.shell_rows + row + self.band) // self.band - 1, 0, TILE_X - 1)


Y_ROWS = 88


def pack_sides(place_args, disp, vel, jit, words, node, inter, shell, speed, first, second, wide_ref):
    place = Place(*place_args)
    tiles = disp.shape[2]
    even = place.gy % 2 == 0
    blocks = place.shell_cols // PTS
    numbers = node[...].astype(F32)
    edge_blocks = (0, blocks - 1)
    for j in edge_blocks:
        lay_out(wide_ref, (), j, widen(lambda b: numbers[b : b + 1], blocks)[j])
    held = {}
    for j in edge_blocks:
        total = jnp.zeros((8, PTS), F32)
        for part in range(place.bands):
            summed = jnp.zeros((8, PTS), F32)
            for row in range(part * place.band, (part + 1) * place.band, 8):
                wanted = wide_ref[place.band_of(row), :, j * PTS : (j + 1) * PTS]
                ids = place.nodes(row, PTS) + float(j * PTS)
                summed = summed + jnp.where(wanted == ids, shell[row : row + 8, j * PTS : (j + 1) * PTS], 0.0)
            summed = jnp.sum(summed, axis=0, keepdims=True)
            total = total + jnp.where(subs() == place.band_of(part * place.band), summed, 0.0)
        held[j] = total
    met = narrow(lambda j: held[j], (0, tiles - 1))

    def send(ref, to_right):
        edge = jnp.where(to_right, tiles - 1, 0)
        for f, source in enumerate((disp, disp, vel, vel, jit, jit)):
            ref[8 * f : 8 * f + 8, :] = jnp.where(
                to_right, source[f % 2, :, tiles - 1, :], source[f % 2, :, 0, :]
            )
        ref[48:Y_ROWS, :] = jnp.zeros((Y_ROWS - 48, PTS), F32)
        edge_words = jnp.where(to_right, words[:, tiles - 1, :], words[:, 0, :])
        ref[48:56, 0:9] = (edge_words & 65535).astype(F32)
        ref[56:64, 0:9] = jnp.right_shift(edge_words, 16).astype(F32)
        ref[64:65, :] = jnp.where(to_right, numbers[tiles - 1 : tiles], numbers[0:1])
        ref[65:66, :] = jnp.where(to_right, inter[tiles - 1 : tiles, :], inter[0:1, :])
        ref[66:67, :] = jnp.where(to_right, met[1], met[0])
        for f, source in enumerate((shell, speed)):
            last = jnp.transpose(source[:, place.shell_cols - PTS :])[PTS - 8 :]
            head = jnp.transpose(source[:, 0:PTS])[:8]
            ref[72 + 8 * f : 80 + 8 * f, :] = jnp.where(to_right, last, head)

    send(first, even)
    send(second, jnp.logical_not(even))


HALO_ROWS = 120
CONTACT_ROWS = 24


def shell_strip(right, left, at):
    middle = jnp.zeros((PTS - 16, PTS), F32)
    return jnp.transpose(jnp.concatenate([right[at : at + 8], middle, left[at : at + 8]], axis=0))


def laplace_pass(source, target, blocks):
    for k in blocks:
        row = 8 * k
        here = source[row : row + 8, :]
        around = source[row - 1 : row + 7, :] + source[row + 1 : row + 9, :] + turn(here, 1) + turn(here, -1)
        target[row : row + 8, :] = around - 4.0 * here


def laplace_of(source, k):
    row = 8 * k
    here = source[row : row + 8, :]
    around = source[row - 1 : row + 7, :] + source[row + 1 : row + 9, :] + turn(here, 1) + turn(here, -1)
    return around - 4.0 * here


def pack_ends(
    place_args, shifts, disp, vel, jit, words, node, inter, shell, speed, first, second, *refs
):
    place = Place(*place_args)
    outs = refs[: len(shifts)]
    own, strip_d, strip_v, grid, tall, tall_v, bent, wide_ref = refs[len(shifts) :]
    rows_a, tiles = disp.shape[1], disp.shape[2]
    rows, cols = place.shell_rows, place.shell_cols
    right, left = place.sides(first[...], second[...])

    grid[...] = jnp.zeros_like(grid)
    for f, (source, at) in enumerate(((jit, 32), (jit, 40), (disp, 0), (disp, 8))):
        for level, a in enumerate((rows_a - 2, rows_a - 1)):
            base = (level + 1) * STRIDE
            values, from_right, from_left = source[f % 2, a], right[at + a : at + a + 1], left[at + a : at + a + 1]
            if f >= 2:
                far = 32 + 8 * (f % 2) + a
                values = values + jit[f % 2, a]
                from_right = from_right + right[far : far + 1]
                from_left = from_left + left[far : far + 1]
            grid[f, base + 8 : base + 16, :] = values
            grid[f, base + 16 : base + 17, :] = from_right
            grid[f, base + 7 : base + 8, :] = from_left

    def tile_getter(f):
        held = {}

        def get(dx, dy):
            if (dx, dy) not in held:
                base = (2 + dx) * STRIDE + 8 + dy
                held[dx, dy] = turn(grid[f, base : base + 8, :], TILE_Y * dy)
            return held[dx, dy]

        return get

    def words_getter():
        held = {}
        sub = subs()

        def get(dx, dy):
            if (dx, dy) not in held:
                s = slot(dx, dy)
                word = jnp.broadcast_to(words[rows_a - 1, :, s : s + 1], (8, PTS))
                if dx > 0:
                    word = jnp.zeros_like(word)
                if dy < 0:
                    word = jnp.where((sub == 0) & (place.gy == 0), 0, word)
                if dy > 0:
                    word = jnp.where((sub == tiles - 1) & (place.gy == place.ny - 1), 0, word)
                held[dx, dy] = word
            return held[dx, dy]

        return get

    force, _ = first_forces(
        tile_getter(0), tile_getter(1), tile_getter(2), tile_getter(3), words_getter(), both=False
    )
    gap = disp[0, rows_a - 1] + inter[...]
    last = rows_a - 1
    own[0:8, :] = gap + STEP_DT * (vel[0, last] + STEP_DT * force)
    own[8:16, :] = gap
    own[16:24, :] = jnp.zeros((8, PTS), F32)
    own[16:17, :] = right[last : last + 1] + right[65:66]
    own[17:18, :] = left[last : last + 1] + left[65:66]

    halo_d = shell_strip(right, left, 72)
    halo_v = shell_strip(right, left, 80)
    strip_d[...] = halo_d
    strip_v[...] = halo_v
    tall[...] = jnp.zeros_like(tall)
    tall_v[...] = jnp.zeros_like(tall_v)
    tall[PAD : PAD + rows, 0:cols] = shell[...]
    tall[PAD : PAD + rows, cols:WIDE] = halo_d
    tall_v[PAD : PAD + rows, 0:cols] = speed[...]
    bent[...] = jnp.zeros_like(bent)
    span = range(PAD // 8 - 1, (PAD + rows) // 8 + 1)
    laplace_pass(tall, bent, span)
    numbers = node[...].astype(F32)
    for j, block in enumerate(widen(lambda b: numbers[b : b + 1], cols // PTS)):
        lay_out(wide_ref, (), j, block)
    sub_wide = lax.broadcasted_iota(I32, (8, cols), 0)
    ahead = jnp.zeros((8, cols), F32)
    met = jnp.zeros((8, cols), F32)
    parts = [[-8]] + [list(range(p * place.band, (p + 1) * place.band, 8)) for p in range(place.bands)] + [[rows]]
    for part in parts:
        soon = jnp.zeros((8, cols), F32)
        now = jnp.zeros((8, cols), F32)
        band = place.band_of(part[0])
        for row in part:
            k = (PAD + row) // 8
            hit = wide_ref[band] == place.nodes(row, cols)
            bending = laplace_of(bent, k)[:, 0:cols]
            here = tall[PAD + row : PAD + row + 8, 0:cols]
            later = here + STEP_DT * (tall_v[PAD + row : PAD + row + 8, 0:cols] - (STEP_DT * BEND) * bending)
            soon = soon + jnp.where(hit, later, 0.0)
            if 0 <= row < rows:
                now = now + jnp.where(hit, here, 0.0)
        ahead = ahead + jnp.where(sub_wide == band, jnp.sum(soon, axis=0, keepdims=True), 0.0)
        if 0 <= part[0] < rows:
            met = met + jnp.where(sub_wide == band, jnp.sum(now, axis=0, keepdims=True), 0.0)
    base = CONTACT_ROWS
    own[base + 16 : base + 24, :] = jnp.zeros((8, PTS), F32)
    for b, row in enumerate(narrow(lambda j: ahead[:, j * PTS : (j + 1) * PTS], range(tiles))):
        own[base + b : base + b + 1, :] = row
    for b, row in enumerate(narrow(lambda j: met[:, j * PTS : (j + 1) * PTS], range(tiles))):
        own[base + 8 + b : base + 9 + b, :] = row
    own[base + 16 : base + 17, :] = right[66:67]
    own[base + 17 : base + 18, :] = left[66:67]

    mine = jnp.where(place.front, own[0:CONTACT_ROWS, :], own[base : base + CONTACT_ROWS, :])
    for shift, out in zip(shifts, outs):
        at = 0
        if shift & (shift + 1) == 0:
            at = HALO_ROWS
            down = (place.gx ^ shift) > place.gx
            edge = jnp.where(down, rows_a - 1, 0)
            for f, source in enumerate((disp, disp, vel, vel, jit, jit)):
                out[8 * f : 8 * f + 8, :] = source[f % 2, edge]
            out[48:80, :] = jnp.zeros((32, PTS), F32)
            edge_words = words[edge]
            out[48:56, 0:9] = (edge_words & 65535).astype(F32)
            out[56:64, 0:9] = jnp.right_shift(edge_words, 16).astype(F32)
            for f in range(8):
                for side, values in ((64, right), (72, left)):
                    low, high = values[8 * f : 8 * f + 1], values[8 * f + rows_a - 1 : 8 * f + rows_a]
                    out[side + f : side + f + 1, :] = jnp.where(down, high, low)
            for j in range(WIDE // PTS):
                cut = slice(j * PTS, (j + 1) * PTS)
                if j < cols // PTS:
                    d_low, d_high = shell[0:4, cut], shell[rows - 4 : rows, cut]
                    v_low, v_high = speed[0:2, cut], speed[rows - 2 : rows, cut]
                else:
                    d_low, d_high = halo_d[0:4], halo_d[rows - 4 : rows]
                    v_low, v_high = halo_v[0:2], halo_v[rows - 2 : rows]
                out[80 + 8 * j : 84 + 8 * j, :] = jnp.where(down, d_high, d_low)
                out[84 + 8 * j : 86 + 8 * j, :] = jnp.where(down, v_high, v_low)
                out[86 + 8 * j : 88 + 8 * j, :] = jnp.zeros((2, PTS), F32)
        out[at : at + CONTACT_ROWS, :] = mine


def both_steps(
    place_args, shifts, disp, vel, jit, words, node, inter, shell, speed, first, second, own, strip_d, strip_v, *refs
):
    place = Place(*place_args)
    ends = refs[: len(shifts)]
    out_disp, out_vel, out_shell, out_speed = refs[len(shifts) : len(shifts) + 4]
    grid, near, vels, kinds, weights, levels, tall, tall_v, bent, pushed, gaps, trial, halo = refs[len(shifts) + 4 :]
    rows_a, tiles = disp.shape[1], disp.shape[2]
    rows, cols = place.shell_rows, place.shell_cols
    right, left = place.sides(first[...], second[...])

    halo[...] = jnp.zeros_like(halo)
    contact = jnp.where(place.front, own[0:CONTACT_ROWS, :], 0.0)
    owners = own[CONTACT_ROWS:, :]
    for shift, ref in zip(shifts, ends):
        partner = place.gx ^ shift
        at = 0
        if shift & (shift + 1) == 0:
            at = HALO_ROWS

            @pl.when(partner == place.gx - 1)
            def _():
                halo[0] = ref[0:HALO_ROWS, :]

            @pl.when(partner == place.gx + 1)
            def _():
                halo[1] = ref[0:HALO_ROWS, :]

        got = ref[at : at + CONTACT_ROWS, :]
        contact = jnp.where(partner == place.nx - 1, got, contact)
        owners = owners + got

    tall[...] = jnp.zeros_like(tall)
    tall_v[...] = jnp.zeros_like(tall_v)
    tall[PAD : PAD + rows, 0:cols] = shell[...]
    tall[PAD : PAD + rows, cols:WIDE] = strip_d[...]
    tall_v[PAD : PAD + rows, 0:cols] = speed[...]
    tall_v[PAD : PAD + rows, cols:WIDE] = strip_v[...]
    for j in range(WIDE // PTS):
        cut = slice(j * PTS, (j + 1) * PTS)
        tall[PAD - 4 : PAD, cut] = halo[0, 80 + 8 * j : 84 + 8 * j, :]
        tall_v[PAD - 2 : PAD, cut] = halo[0, 84 + 8 * j : 86 + 8 * j, :]
        tall[PAD + rows : PAD + rows + 4, cut] = halo[1, 80 + 8 * j : 84 + 8 * j, :]
        tall_v[PAD + rows : PAD + rows + 2, cut] = halo[1, 84 + 8 * j : 86 + 8 * j, :]
    numbers = node[...].astype(F32)
    node_rows = [numbers[b : b + 1] for b in range(tiles)] + [right[64:65], left[64:65]]
    gap_rows = [contact[8 + b : 9 + b] for b in range(tiles)] + [contact[16:17], contact[17:18]]
    soon_rows = [contact[b : b + 1] for b in range(tiles)]
    for j, (nodes, gap) in enumerate(zip(widen(node_rows.__getitem__, 5), widen(gap_rows.__getitem__, 5))):
        lay_out(gaps, (0,), j, nodes)
        lay_out(gaps, (1,), j, gap)
    for j, soon in enumerate(widen(soon_rows.__getitem__, 4)):
        lay_out(gaps, (2,), j, soon)
    bent[...] = jnp.zeros_like(bent)
    span = range(PAD // 8 - 1, (PAD + rows) // 8 + 1)
    laplace_pass(tall, bent, span)
    col = lax.broadcasted_iota(I32, (8, WIDE), 1)
    inside = jnp.where(col < cols, 1.0, 0.0)
    inside = jnp.where((col >= cols) & (col < cols + 64) & (place.gy < place.ny - 1), 1.0, inside)
    inside = jnp.where((col >= cols + 64) & (place.gy > 0), 1.0, inside)
    for k in span:
        row = 8 * k - PAD
        cut = slice(8 * k, 8 * k + 8)
        here = tall[cut, :]
        band = place.band_of(row)
        hit = gaps[0, band] == place.nodes(row, WIDE)
        push = jnp.where(hit, PENALTY * jnp.maximum(gaps[1, band] - here, 0.0), 0.0)
        fast = tall_v[cut, :] + STEP_DT * (push - BEND * laplace_of(bent, k))
        there = here + STEP_DT * fast
        keep = inside
        if row < 0:
            keep = inside * jnp.where(place.gx > 0, 1.0, 0.0)
        elif row >= rows:
            keep = inside * jnp.where(place.gx < place.nx - 1, 1.0, 0.0)
        tall[cut, :] = there * keep
        if 0 <= row < rows:
            tall_v[cut, :] = fast
            pushed[cut, :] = push
    laplace_pass(tall, bent, span)
    for k in range(PAD // 8, (PAD + rows) // 8):
        row = 8 * k - PAD
        cut = slice(8 * k, 8 * k + 8)
        here = tall[cut, 0:cols]
        band = place.band_of(row)
        hit = gaps[0, band, :, 0:cols] == place.nodes(row, cols)
        gap = gaps[2, band, :, 0:cols] - (STEP_DT * STEP_DT) * pushed[cut, 0:cols]
        push = jnp.where(hit, PENALTY * jnp.maximum(gap - here, 0.0), 0.0)
        fast = tall_v[cut, 0:cols] + STEP_DT * (push - BEND * laplace_of(bent, k)[:, 0:cols])
        out_speed[row : row + 8, :] = fast
        out_shell[row : row + 8, :] = here + STEP_DT * fast

    grid[...] = jnp.zeros_like(grid)
    top, low = STRIDE, (rows_a + 2) * STRIDE
    for f in range(4):
        source, at = ((jit, 32 + 8 * f), (disp, 8 * (f - 2)))[f >= 2]
        extra = 32 + 8 * (f - 2)

        def with_rest(values, rest):
            return values + rest if f >= 2 else values

        for a in range(rows_a):
            base = (a + 2) * STRIDE + 8
            grid[f, base : base + tiles, :] = with_rest(source[f % 2, a], jit[f % 2, a])
        for side, offset in ((right, 16), (left, 7)):
            grid[f, pl.ds(2 * STRIDE + offset, rows_a, stride=STRIDE), :] = with_rest(
                side[at : at + 8], side[extra : extra + 8]
            )
        for end, base in ((0, top), (1, low)):
            grid[f, base + 8 : base + 16, :] = with_rest(halo[end, at : at + 8, :], halo[end, extra : extra + 8, :])
            for part, offset in ((64, 16), (72, 7)):
                grid[f, base + offset : base + offset + 1, :] = with_rest(
                    halo[end, part + at // 8 : part + at // 8 + 1, :],
                    halo[end, part + extra // 8 : part + extra // 8 + 1, :],
                )

    blocks = rows_a + 5
    corner = 8 * (rows_a + 4)

    def spread_grid(f, row_blocks, edges):
        for dx in (-1, 0, 1):
            for dy in (-1, 0, 1):
                s = slot(dx, dy)
                for t in row_blocks:
                    a = t if t < rows_a else (-1, rows_a)[t - rows_a]
                    base = (a + 2 + dx) * STRIDE + 8 + dy
                    near[f, s, 8 * t : 8 * t + 8, :] = turn(grid[f, base : base + 8, :], TILE_Y * dy)
                if edges:
                    for t, offset in ((rows_a + 2, 7), (rows_a + 3, 16)):
                        near[f, s, 8 * t : 8 * t + 8, :] = turn(
                            grid[f, pl.ds((2 + dx) * STRIDE + offset + dy, 8, stride=STRIDE), :], TILE_Y * dy
                        )
                    near[f, s, corner : corner + 8, :] = jnp.zeros((8, PTS), F32)
                    for n, offset in enumerate((7, 16)):
                        for m, base in enumerate((top, low)):
                            start = base + dx * STRIDE + offset + dy
                            at = corner + 2 * n + m
                            near[f, s, at : at + 1, :] = turn(grid[f, start : start + 1, :], TILE_Y * dy)

    for f in range(4):
        spread_grid(f, range(rows_a + 2), True)

    for f in range(2):
        at = 16 + 8 * f
        for a in range(rows_a):
            vels[f, 8 * a : 8 * a + 8, :] = vel[f, a]
        for end in (0, 1):
            t = rows_a + end
            vels[f, 8 * t : 8 * t + 8, :] = halo[end, at : at + 8, :]
        vels[f, corner - 16 : corner - 8, :] = left[at : at + 8]
        vels[f, corner - 8 : corner, :] = right[at : at + 8]
        vels[f, corner : corner + 8, :] = jnp.zeros((8, PTS), F32)
        for n, part in enumerate((72, 64)):
            for end in (0, 1):
                vels[f, corner + 2 * n + end : corner + 2 * n + end + 1, :] = halo[
                    end, part + 2 + f : part + 3 + f, :
                ]

    def joined(low_part, high_part):
        return jnp.left_shift(high_part.astype(I32), 16) | low_part.astype(I32)

    sub = subs()
    west, east = place.gy == 0, place.gy == place.ny - 1
    north, south = place.gx == 0, place.gx == place.nx - 1
    for t in range(blocks):
        if t < rows_a:
            packed = words[t]
        elif t < rows_a + 2:
            packed = joined(halo[t - rows_a, 48:56, :], halo[t - rows_a, 56:64, :])
        elif t < rows_a + 4:
            side = (left, right)[t - rows_a - 2]
            packed = joined(side[48:56], side[56:64])
        else:
            zero = jnp.zeros((4, PTS), F32)
            lows = [halo[end, part + 6 : part + 7, :] for part in (72, 64) for end in (0, 1)]
            highs = [halo[end, part + 7 : part + 8, :] for part in (72, 64) for end in (0, 1)]
            packed = joined(jnp.concatenate(lows + [zero], axis=0), jnp.concatenate(highs + [zero], axis=0))
        for dx in (-1, 0, 1):
            for dy in (-1, 0, 1):
                s = slot(dx, dy)
                word = jnp.broadcast_to(packed[:, s : s + 1], (8, PTS))
                if t < rows_a + 2:
                    if dy < 0:
                        word = jnp.where((sub == 0) & west, 0, word)
                    if dy > 0:
                        word = jnp.where((sub == tiles - 1) & east, 0, word)
                    if dx < 0 and t == 0:
                        word = jnp.where(north, 0, word)
                    if dx > 0 and t == rows_a - 1:
                        word = jnp.where(south, 0, word)
                elif t < rows_a + 4:
                    if dx < 0:
                        word = jnp.where((sub == 0) & north, 0, word)
                    if dx > 0:
                        word = jnp.where((sub == rows_a - 1) & south, 0, word)
                kinds[s, 8 * t : 8 * t + 8, :] = word

    def getter(ref, f, at):
        held = {}

        def get(dx, dy):
            if (dx, dy) not in held:
                cut = (slot(dx, dy), pl.ds(at, 8), slice(None))
                held[dx, dy] = ref[cut] if f is None else ref[(f,) + cut]
            return held[dx, dy]

        return get

    @pl.loop(0, blocks)
    def _(t):
        at = pl.multiple_of(8 * t, 8)

        def keep(number, weight, level):
            weights[number, pl.ds(at, 8), :] = weight
            levels[number, pl.ds(at, 8), :] = level

        fx, fy = first_forces(
            getter(near, 0, at),
            getter(near, 1, at),
            getter(near, 2, at),
            getter(near, 3, at),
            getter(kinds, None, at),
            keep,
        )
        trial[0, pl.ds(at, 8), :] = fx
        trial[1, pl.ds(at, 8), :] = fy

    here = jnp.where(place.front, 1.0, 0.0)
    push = PENALTY * here * jnp.maximum(contact[8:18] - owners[8:18], 0.0)
    last = rows_a - 1
    trial[0, 8 * last : 8 * last + 8, :] -= push[0:8]
    at = 8 * (rows_a + 2) + last
    trial[0, at : at + 1, :] -= push[9:10]
    trial[0, at + 8 : at + 9, :] -= push[8:9]
    for f in range(2):
        vels[f] = vels[f] + STEP_DT * trial[f]
        trial[f] = near[2 + f, slot(0, 0)] + STEP_DT * vels[f]
        for t in range(rows_a + 2):
            a = t if t < rows_a else (-1, rows_a)[t - rows_a]
            grid[2 + f, (a + 2) * STRIDE + 8 : (a + 2) * STRIDE + 16, :] = trial[f, 8 * t : 8 * t + 8, :]
        for t, offset in ((rows_a + 2, 7), (rows_a + 3, 16)):
            grid[2 + f, pl.ds(2 * STRIDE + offset, 8, stride=STRIDE), :] = trial[f, 8 * t : 8 * t + 8, :]
        for n, offset in enumerate((7, 16)):
            for m, base in enumerate((top, low)):
                at = corner + 2 * n + m
                grid[2 + f, base + offset : base + offset + 1, :] = trial[f, at : at + 1, :]
        spread_grid(2 + f, range(rows_a), False)

    @pl.loop(0, rows_a)
    def _(t):
        at = pl.multiple_of(8 * t, 8)

        def kept(number):
            return weights[number, pl.ds(at, 8), :], levels[number, pl.ds(at, 8), :]

        fx, fy = second_forces(getter(near, 2, at), getter(near, 3, at), kept)
        out_vel[0, t] = vels[0, pl.ds(at, 8), :] + STEP_DT * fx
        out_vel[1, t] = vels[1, pl.ds(at, 8), :] + STEP_DT * fy

    gap = trial[0, 8 * last : 8 * last + 8, :] - jit[0, last] + inter[...]
    reached = owners[0:8] + (STEP_DT * STEP_DT) * push[0:8]
    out_vel[0, last] = out_vel[0, last] - (STEP_DT * PENALTY) * here * jnp.maximum(gap - reached, 0.0)
    for f in range(2):
        for a in range(rows_a):
            out_disp[f, a] = (trial[f, 8 * a : 8 * a + 8, :] - jit[f, a]) + STEP_DT * out_vel[f, a]


def on_device(nx, ny, disp, vel, jit, words, node, inter, shell, speed):
    rows_a = disp.shape[1]
    rows, cols = shell.shape
    place_args = (nx, ny, rows, cols)
    shifts = tuple(range(1, nx))
    base = (disp, vel, jit, words, node, inter, shell, speed)

    def call(body, out, scratch, *args):
        return pl.pallas_call(
            body,
            out_shape=out,
            scratch_shapes=scratch,
            compiler_params=pltpu.CompilerParams(vmem_limit_bytes=40 * 1024 * 1024),
        )(*args)

    side = jax.ShapeDtypeStruct((Y_ROWS, PTS), F32)
    first, second = call(
        functools.partial(pack_sides, place_args), (side, side), [pltpu.VMEM((TILE_X, 8, cols), F32)], *base
    )
    first = lax.ppermute(first, "gy", [(i, i ^ 1) for i in range(ny)])
    second = lax.ppermute(second, "gy", [(i, ((i - 1) ^ 1) + 1 if 0 < i < ny - 1 else ny - 1 - i) for i in range(ny)])

    tall = pltpu.VMEM((rows + 2 * PAD, WIDE), F32)
    outs = [
        jax.ShapeDtypeStruct((CONTACT_ROWS + (HALO_ROWS if s & (s + 1) == 0 else 0), PTS), F32) for s in shifts
    ]
    outs += [jax.ShapeDtypeStruct((2 * CONTACT_ROWS, PTS), F32)]
    outs += [jax.ShapeDtypeStruct((rows, PTS), F32)] * 2
    *ends, own, strip_d, strip_v = call(
        functools.partial(pack_ends, place_args, shifts),
        outs,
        [pltpu.VMEM((4, 4 * STRIDE, PTS), F32), tall, tall, tall, pltpu.VMEM((TILE_X, 8, cols), F32)],
        *base,
        first,
        second,
    )
    ends = [lax.ppermute(e, "gx", [(i, i ^ s) for i in range(nx)]) for s, e in zip(shifts, ends)]

    held = 8 * (rows_a + 5)
    scratch = [
        pltpu.VMEM((4, (rows_a + 4) * STRIDE, PTS), F32),
        pltpu.VMEM((4, 9, held, PTS), F32),
        pltpu.VMEM((2, held, PTS), F32),
        pltpu.VMEM((9, held, PTS), I32),
        pltpu.VMEM((len(OFFSETS), held, PTS), F32),
        pltpu.VMEM((len(OFFSETS), held, PTS), F32),
        tall,
        tall,
        tall,
        tall,
        pltpu.VMEM((3, TILE_X, 8, WIDE), F32),
        pltpu.VMEM((2, held, PTS), F32),
        pltpu.VMEM((2, HALO_ROWS, PTS), F32),
    ]
    out = [jax.ShapeDtypeStruct(x.shape, F32) for x in (disp, vel, shell, speed)]
    return tuple(
        call(functools.partial(both_steps, place_args, shifts), out, scratch, *base, first, second, own, strip_d, strip_v, *ends)
    )


def solution(mesh):
    in_specs = (
        P(None, "gx", "gy", None),
        P(None, "gx", "gy", None),
        P(None, "gx", "gy", None),
        P("gx", "gy", None),
        P("gy", None),
        P("gy", None),
        P("gx", "gy"),
        P("gx", "gy"),
    )
    out_specs = (P(None, "gx", "gy", None), P(None, "gx", "gy", None), P("gx", "gy"), P("gx", "gy"))
    body = functools.partial(on_device, mesh.shape["gx"], mesh.shape["gy"])
    return jax.shard_map(body, mesh=mesh, in_specs=in_specs, out_specs=out_specs, check_vma=False)
```

```python
import functools

import jax
import jax.numpy as jnp
from jax import lax
from jax.experimental import pallas as pl
from jax.experimental.pallas import tpu as pltpu
from jax.sharding import PartitionSpec as P

TILE_X = 8
TILE_Y = 16
PTS = 128
SPLIT = 4

HORIZON = 3.5
DELTA_SQ = 0.25
PENALTY = 4.0
BEND = 0.5
STEP_DT = 0.2

F32 = jnp.float32
I32 = jnp.int32

STRIDE = 24
WIDE = 640
PAD = 16


def bond_offsets():
    limit = HORIZON * HORIZON - DELTA_SQ
    found = []
    for oy in range(-4, 5):
        for ox in range(-4, 5):
            near = max(abs(ox) - 0.4, 0.0) ** 2 + max(abs(oy) - 0.4, 0.0) ** 2
            if near < limit and (ox or oy):
                found.append((ox, oy))
    return found


OFFSETS = bond_offsets()
SIDEWAYS = sorted({oy for _, oy in OFFSETS})


def sign(value):
    return (value > 0) - (value < 0)


def lanes():
    return lax.broadcasted_iota(I32, (8, PTS), 1)


def subs():
    return lax.broadcasted_iota(I32, (8, PTS), 0)


def turn(values, shift):
    size = values.shape[1]
    return pltpu.roll(values, shift % size, 1) if shift % size else values


def slot(dx, dy):
    return 3 * (dx + 1) + dy + 1


def lane_masks():
    lane = lanes()
    row, col = lane // TILE_Y, lane % TILE_Y
    masks = {}
    for o in (1, 2, 3):
        masks["col_at", o] = col < o
        masks["col_at", -o] = col >= TILE_Y - o
        masks["col_from", o] = col >= TILE_Y - o
        masks["col_from", -o] = col < o
        masks["row_at", o] = row < o
        masks["row_at", -o] = row >= TILE_X - o
        masks["row_from", o] = row >= TILE_X - o
        masks["row_from", -o] = row < o
    bits = {}
    for ox in range(-3, 4):
        bits[ox] = jnp.left_shift(jnp.int32(1), 4 * row + ((row + ox) & 7) // 2)
    return masks, bits


def moved(get, oy, masks):
    out = {}
    for dx in (-1, 0, 1):
        held = get(dx, 0)
        if oy:
            held = turn(jnp.where(masks["col_at", oy], get(dx, sign(oy)), held), -oy)
        out[dx] = held
    return out


def across(cells, ox, masks):
    if not ox:
        return cells[0]
    return turn(jnp.where(masks["row_at", ox], cells[sign(ox)], cells[0]), -TILE_Y * ox)


def first_forces(get_jx, get_jy, get_dx, get_dy, get_words, keep=None, both=True):
    masks, bits = lane_masks()
    jx0, jy0, dx0, dy0 = get_jx(0, 0), get_jy(0, 0), get_dx(0, 0), get_dy(0, 0)
    fx = jnp.zeros((8, PTS), F32)
    fy = jnp.zeros((8, PTS), F32)
    for oy in SIDEWAYS:
        jxs, jys = moved(get_jx, oy, masks), moved(get_jy, oy, masks)
        dxs, dys = moved(get_dx, oy, masks), moved(get_dy, oy, masks)
        words = {}
        for dx in (-1, 0, 1):
            words[dx] = get_words(dx, 0)
            if oy:
                words[dx] = jnp.where(masks["col_from", oy], get_words(dx, sign(oy)), words[dx])
        for number, (ox, other) in enumerate(OFFSETS):
            if other != oy:
                continue
            word = words[0]
            if ox:
                word = jnp.where(masks["row_from", ox], words[sign(ox)], word)
            intact = (word & bits[ox]) != 0
            rest_x = across(jxs, ox, masks) - (jx0 - float(ox))
            rest_y = across(jys, ox, masks) - (jy0 - float(oy))
            now_x = across(dxs, ox, masks) - (dx0 - float(ox))
            now_y = across(dys, ox, masks) - (dy0 - float(oy))
            rest_sq = rest_x * rest_x + rest_y * rest_y + DELTA_SQ
            now_sq = now_x * now_x + now_y * now_y + DELTA_SQ
            rest_inv = lax.rsqrt(rest_sq)
            reach = jnp.maximum(1.0 - rest_sq * rest_inv * (1.0 / HORIZON), 0.0)
            weight = jnp.where(intact, reach * reach, 0.0)
            level = weight * rest_inv
            if keep is not None:
                keep(number, weight, level)
            factor = level - weight * lax.rsqrt(now_sq)
            fx = fx + factor * now_x
            if both:
                fy = fy + factor * now_y
    return fx, fy


def second_forces(get_dx, get_dy, kept):
    masks, _ = lane_masks()
    dx0, dy0 = get_dx(0, 0), get_dy(0, 0)
    fx = jnp.zeros((8, PTS), F32)
    fy = jnp.zeros((8, PTS), F32)
    for oy in SIDEWAYS:
        dxs, dys = moved(get_dx, oy, masks), moved(get_dy, oy, masks)
        for number, (ox, other) in enumerate(OFFSETS):
            if other != oy:
                continue
            now_x = across(dxs, ox, masks) - (dx0 - float(ox))
            now_y = across(dys, ox, masks) - (dy0 - float(oy))
            now_sq = now_x * now_x + now_y * now_y + DELTA_SQ
            weight, level = kept(number)
            factor = level - weight * lax.rsqrt(now_sq)
            fx = fx + factor * now_x
            fy = fy + factor * now_y
    return fx, fy


def widen(row_of, count):
    lane, sub = lanes(), subs()
    index = sub * TILE_Y + (lane % 64) // SPLIT
    out = []
    for j in range(count):
        left, right = (
            jnp.take_along_axis(jnp.broadcast_to(row_of(b), (8, PTS)), index, axis=1) for b in (2 * j, 2 * j + 1)
        )
        out.append(jnp.where(lane < 64, left, right))
    return out


def narrow(block_of, tiles):
    lane, sub = lanes(), subs()
    out = []
    for b in tiles:
        held = block_of(b // 2)
        held = held + turn(held, -1)
        held = held + turn(held, -2)
        picked = jnp.take_along_axis(held, 64 * (b % 2) + SPLIT * (lane % TILE_Y), axis=1)
        out.append(jnp.sum(jnp.where(sub == lane // TILE_Y, picked, 0.0), axis=0, keepdims=True))
    return out


def lay_out(ref, at, j, block):
    for row in range(TILE_X):
        ref[at + (row, slice(None), slice(j * PTS, (j + 1) * PTS))] = jnp.broadcast_to(block[row : row + 1], (8, PTS))


class Place:
    def __init__(self, nx, ny, shell_rows, shell_cols):
        self.nx, self.ny = nx, ny
        self.gx, self.gy = lax.axis_index("gx"), lax.axis_index("gy")
        self.shell_rows, self.shell_cols = shell_rows, shell_cols
        self.width = shell_cols * ny
        self.band = shell_rows * nx // TILE_X
        self.bands = shell_rows // self.band
        self.front = self.gx == nx - 1

    def sides(self, first, second):
        even = self.gy % 2 == 0
        right = jnp.where(even, first, second)
        left = jnp.where(even, second, first)
        right = jnp.where(self.gy < self.ny - 1, right, 0.0)
        left = jnp.where(self.gy > 0, left, 0.0)
        return right, left

    def nodes(self, row, columns):
        shape = (8, columns)
        col = lax.broadcasted_iota(I32, shape, 1)
        if columns > self.shell_cols:
            col = jnp.where(col >= self.shell_cols + 64, col - columns, col)
        first = (self.gx * self.shell_rows + row) * self.width + self.gy * self.shell_cols
        return (first + lax.broadcasted_iota(I32, shape, 0) * self.width + col).astype(F32)

    def band_of(self, row):
        return jnp.clip((self.gx * self.shell_rows + row + self.band) // self.band - 1, 0, TILE_X - 1)


Y_ROWS = 88


def fetch(pairs, sems):
    copies = [pltpu.make_async_copy(source, target, sems.at[n]) for n, (source, target) in enumerate(pairs)]
    for copy in copies:
        copy.start()
    for copy in copies:
        copy.wait()


def pack_sides(place_args, *refs):
    sources, (first, second), held, (wide_ref, sems) = refs[:8], refs[8:10], refs[10:18], refs[18:]
    place = Place(*place_args)
    fetch(list(zip(sources, held)), sems)
    disp, vel, jit, words, node, inter, shell, speed = held
    tiles = disp.shape[2]
    even = place.gy % 2 == 0
    blocks = place.shell_cols // PTS
    numbers = node[...].astype(F32)
    edge_blocks = (0, blocks - 1)
    for j in edge_blocks:
        lay_out(wide_ref, (), j, widen(lambda b: numbers[b : b + 1], blocks)[j])
    held = {}
    for j in edge_blocks:
        total = jnp.zeros((8, PTS), F32)
        for part in range(place.bands):
            summed = jnp.zeros((8, PTS), F32)
            for row in range(part * place.band, (part + 1) * place.band, 8):
                wanted = wide_ref[place.band_of(row), :, j * PTS : (j + 1) * PTS]
                ids = place.nodes(row, PTS) + float(j * PTS)
                summed = summed + jnp.where(wanted == ids, shell[row : row + 8, j * PTS : (j + 1) * PTS], 0.0)
            summed = jnp.sum(summed, axis=0, keepdims=True)
            total = total + jnp.where(subs() == place.band_of(part * place.band), summed, 0.0)
        held[j] = total
    met = narrow(lambda j: held[j], (0, tiles - 1))

    def send(ref, to_right):
        edge = jnp.where(to_right, tiles - 1, 0)
        for f, source in enumerate((disp, disp, vel, vel, jit, jit)):
            ref[8 * f : 8 * f + 8, :] = jnp.where(
                to_right, source[f % 2, :, tiles - 1, :], source[f % 2, :, 0, :]
            )
        ref[48:Y_ROWS, :] = jnp.zeros((Y_ROWS - 48, PTS), F32)
        edge_words = jnp.where(to_right, words[:, tiles - 1, :], words[:, 0, :])
        ref[48:56, 0:9] = (edge_words & 65535).astype(F32)
        ref[56:64, 0:9] = jnp.right_shift(edge_words, 16).astype(F32)
        ref[64:65, :] = jnp.where(to_right, numbers[tiles - 1 : tiles], numbers[0:1])
        ref[65:66, :] = jnp.where(to_right, inter[tiles - 1 : tiles, :], inter[0:1, :])
        ref[66:67, :] = jnp.where(to_right, met[1], met[0])
        for f, source in enumerate((shell, speed)):
            last = jnp.transpose(source[:, place.shell_cols - PTS :])[PTS - 8 :]
            head = jnp.transpose(source[:, 0:PTS])[:8]
            ref[72 + 8 * f : 80 + 8 * f, :] = jnp.where(to_right, last, head)

    send(first, even)
    send(second, jnp.logical_not(even))


HALO_ROWS = 120
CONTACT_ROWS = 24


def shell_strip(right, left, at):
    middle = jnp.zeros((PTS - 16, PTS), F32)
    return jnp.transpose(jnp.concatenate([right[at : at + 8], middle, left[at : at + 8]], axis=0))


def laplace_pass(source, target, blocks):
    for k in blocks:
        row = 8 * k
        here = source[row : row + 8, :]
        around = source[row - 1 : row + 7, :] + source[row + 1 : row + 9, :] + turn(here, 1) + turn(here, -1)
        target[row : row + 8, :] = around - 4.0 * here


def laplace_of(source, k):
    row = 8 * k
    here = source[row : row + 8, :]
    around = source[row - 1 : row + 7, :] + source[row + 1 : row + 9, :] + turn(here, 1) + turn(here, -1)
    return around - 4.0 * here


def pack_ends(
    place_args, shifts, disp, vel, jit, words, node, inter, shell, speed, first, second, *refs
):
    place = Place(*place_args)
    outs = refs[: len(shifts)]
    own, strip_d, strip_v, grid, tall, tall_v, bent, wide_ref = refs[len(shifts) :]
    rows_a, tiles = disp.shape[1], disp.shape[2]
    rows, cols = place.shell_rows, place.shell_cols
    right, left = place.sides(first[...], second[...])

    grid[...] = jnp.zeros_like(grid)
    for f, (source, at) in enumerate(((jit, 32), (jit, 40), (disp, 0), (disp, 8))):
        for level, a in enumerate((rows_a - 2, rows_a - 1)):
            base = (level + 1) * STRIDE
            values, from_right, from_left = source[f % 2, a], right[at + a : at + a + 1], left[at + a : at + a + 1]
            if f >= 2:
                far = 32 + 8 * (f % 2) + a
                values = values + jit[f % 2, a]
                from_right = from_right + right[far : far + 1]
                from_left = from_left + left[far : far + 1]
            grid[f, base + 8 : base + 16, :] = values
            grid[f, base + 16 : base + 17, :] = from_right
            grid[f, base + 7 : base + 8, :] = from_left

    def tile_getter(f):
        held = {}

        def get(dx, dy):
            if (dx, dy) not in held:
                base = (2 + dx) * STRIDE + 8 + dy
                held[dx, dy] = turn(grid[f, base : base + 8, :], TILE_Y * dy)
            return held[dx, dy]

        return get

    def words_getter():
        held = {}
        sub = subs()

        def get(dx, dy):
            if (dx, dy) not in held:
                s = slot(dx, dy)
                word = jnp.broadcast_to(words[rows_a - 1, :, s : s + 1], (8, PTS))
                if dx > 0:
                    word = jnp.zeros_like(word)
                if dy < 0:
                    word = jnp.where((sub == 0) & (place.gy == 0), 0, word)
                if dy > 0:
                    word = jnp.where((sub == tiles - 1) & (place.gy == place.ny - 1), 0, word)
                held[dx, dy] = word
            return held[dx, dy]

        return get

    force, _ = first_forces(
        tile_getter(0), tile_getter(1), tile_getter(2), tile_getter(3), words_getter(), both=False
    )
    gap = disp[0, rows_a - 1] + inter[...]
    last = rows_a - 1
    own[0:8, :] = gap + STEP_DT * (vel[0, last] + STEP_DT * force)
    own[8:16, :] = gap
    own[16:24, :] = jnp.zeros((8, PTS), F32)
    own[16:17, :] = right[last : last + 1] + right[65:66]
    own[17:18, :] = left[last : last + 1] + left[65:66]

    halo_d = shell_strip(right, left, 72)
    halo_v = shell_strip(right, left, 80)
    strip_d[...] = halo_d
    strip_v[...] = halo_v
    tall[...] = jnp.zeros_like(tall)
    tall_v[...] = jnp.zeros_like(tall_v)
    tall[PAD : PAD + rows, 0:cols] = shell[...]
    tall[PAD : PAD + rows, cols:WIDE] = halo_d
    tall_v[PAD : PAD + rows, 0:cols] = speed[...]
    bent[...] = jnp.zeros_like(bent)
    span = range(PAD // 8 - 1, (PAD + rows) // 8 + 1)
    laplace_pass(tall, bent, span)
    numbers = node[...].astype(F32)
    for j, block in enumerate(widen(lambda b: numbers[b : b + 1], cols // PTS)):
        lay_out(wide_ref, (), j, block)
    sub_wide = lax.broadcasted_iota(I32, (8, cols), 0)
    ahead = jnp.zeros((8, cols), F32)
    met = jnp.zeros((8, cols), F32)
    parts = [[-8]] + [list(range(p * place.band, (p + 1) * place.band, 8)) for p in range(place.bands)] + [[rows]]
    for part in parts:
        soon = jnp.zeros((8, cols), F32)
        now = jnp.zeros((8, cols), F32)
        band = place.band_of(part[0])
        for row in part:
            k = (PAD + row) // 8
            hit = wide_ref[band] == place.nodes(row, cols)
            bending = laplace_of(bent, k)[:, 0:cols]
            here = tall[PAD + row : PAD + row + 8, 0:cols]
            later = here + STEP_DT * (tall_v[PAD + row : PAD + row + 8, 0:cols] - (STEP_DT * BEND) * bending)
            soon = soon + jnp.where(hit, later, 0.0)
            if 0 <= row < rows:
                now = now + jnp.where(hit, here, 0.0)
        ahead = ahead + jnp.where(sub_wide == band, jnp.sum(soon, axis=0, keepdims=True), 0.0)
        if 0 <= part[0] < rows:
            met = met + jnp.where(sub_wide == band, jnp.sum(now, axis=0, keepdims=True), 0.0)
    base = CONTACT_ROWS
    own[base + 16 : base + 24, :] = jnp.zeros((8, PTS), F32)
    for b, row in enumerate(narrow(lambda j: ahead[:, j * PTS : (j + 1) * PTS], range(tiles))):
        own[base + b : base + b + 1, :] = row
    for b, row in enumerate(narrow(lambda j: met[:, j * PTS : (j + 1) * PTS], range(tiles))):
        own[base + 8 + b : base + 9 + b, :] = row
    own[base + 16 : base + 17, :] = right[66:67]
    own[base + 17 : base + 18, :] = left[66:67]

    mine = jnp.where(place.front, own[0:CONTACT_ROWS, :], own[base : base + CONTACT_ROWS, :])
    for shift, out in zip(shifts, outs):
        at = 0
        if shift & (shift + 1) == 0:
            at = HALO_ROWS
            down = (place.gx ^ shift) > place.gx
            edge = jnp.where(down, rows_a - 1, 0)
            for f, source in enumerate((disp, disp, vel, vel, jit, jit)):
                out[8 * f : 8 * f + 8, :] = source[f % 2, edge]
            out[48:80, :] = jnp.zeros((32, PTS), F32)
            edge_words = words[edge]
            out[48:56, 0:9] = (edge_words & 65535).astype(F32)
            out[56:64, 0:9] = jnp.right_shift(edge_words, 16).astype(F32)
            for f in range(8):
                for side, values in ((64, right), (72, left)):
                    low, high = values[8 * f : 8 * f + 1], values[8 * f + rows_a - 1 : 8 * f + rows_a]
                    out[side + f : side + f + 1, :] = jnp.where(down, high, low)
            for j in range(WIDE // PTS):
                cut = slice(j * PTS, (j + 1) * PTS)
                if j < cols // PTS:
                    d_low, d_high = shell[0:4, cut], shell[rows - 4 : rows, cut]
                    v_low, v_high = speed[0:2, cut], speed[rows - 2 : rows, cut]
                else:
                    d_low, d_high = halo_d[0:4], halo_d[rows - 4 : rows]
                    v_low, v_high = halo_v[0:2], halo_v[rows - 2 : rows]
                out[80 + 8 * j : 84 + 8 * j, :] = jnp.where(down, d_high, d_low)
                out[84 + 8 * j : 86 + 8 * j, :] = jnp.where(down, v_high, v_low)
                out[86 + 8 * j : 88 + 8 * j, :] = jnp.zeros((2, PTS), F32)
        out[at : at + CONTACT_ROWS, :] = mine


def both_steps(
    place_args, shifts, disp, vel, jit, words, node, inter, shell, speed, first, second, own, strip_d, strip_v, *refs
):
    place = Place(*place_args)
    ends = refs[: len(shifts)]
    out_disp, out_vel, out_shell, out_speed = refs[len(shifts) : len(shifts) + 4]
    grid, near, vels, kinds, weights, levels, tall, tall_v, bent, pushed, gaps, trial, halo = refs[len(shifts) + 4 :]
    rows_a, tiles = disp.shape[1], disp.shape[2]
    rows, cols = place.shell_rows, place.shell_cols
    right, left = place.sides(first[...], second[...])

    halo[...] = jnp.zeros_like(halo)
    contact = jnp.where(place.front, own[0:CONTACT_ROWS, :], 0.0)
    owners = own[CONTACT_ROWS:, :]
    for shift, ref in zip(shifts, ends):
        partner = place.gx ^ shift
        at = 0
        if shift & (shift + 1) == 0:
            at = HALO_ROWS

            @pl.when(partner == place.gx - 1)
            def _():
                halo[0] = ref[0:HALO_ROWS, :]

            @pl.when(partner == place.gx + 1)
            def _():
                halo[1] = ref[0:HALO_ROWS, :]

        got = ref[at : at + CONTACT_ROWS, :]
        contact = jnp.where(partner == place.nx - 1, got, contact)
        owners = owners + got

    tall[...] = jnp.zeros_like(tall)
    tall_v[...] = jnp.zeros_like(tall_v)
    tall[PAD : PAD + rows, 0:cols] = shell[...]
    tall[PAD : PAD + rows, cols:WIDE] = strip_d[...]
    tall_v[PAD : PAD + rows, 0:cols] = speed[...]
    tall_v[PAD : PAD + rows, cols:WIDE] = strip_v[...]
    for j in range(WIDE // PTS):
        cut = slice(j * PTS, (j + 1) * PTS)
        tall[PAD - 4 : PAD, cut] = halo[0, 80 + 8 * j : 84 + 8 * j, :]
        tall_v[PAD - 2 : PAD, cut] = halo[0, 84 + 8 * j : 86 + 8 * j, :]
        tall[PAD + rows : PAD + rows + 4, cut] = halo[1, 80 + 8 * j : 84 + 8 * j, :]
        tall_v[PAD + rows : PAD + rows + 2, cut] = halo[1, 84 + 8 * j : 86 + 8 * j, :]
    numbers = node[...].astype(F32)
    node_rows = [numbers[b : b + 1] for b in range(tiles)] + [right[64:65], left[64:65]]
    gap_rows = [contact[8 + b : 9 + b] for b in range(tiles)] + [contact[16:17], contact[17:18]]
    soon_rows = [contact[b : b + 1] for b in range(tiles)]
    for j, (nodes, gap) in enumerate(zip(widen(node_rows.__getitem__, 5), widen(gap_rows.__getitem__, 5))):
        lay_out(gaps, (0,), j, nodes)
        lay_out(gaps, (1,), j, gap)
    for j, soon in enumerate(widen(soon_rows.__getitem__, 4)):
        lay_out(gaps, (2,), j, soon)
    bent[...] = jnp.zeros_like(bent)
    span = range(PAD // 8 - 1, (PAD + rows) // 8 + 1)
    laplace_pass(tall, bent, span)
    col = lax.broadcasted_iota(I32, (8, WIDE), 1)
    inside = jnp.where(col < cols, 1.0, 0.0)
    inside = jnp.where((col >= cols) & (col < cols + 64) & (place.gy < place.ny - 1), 1.0, inside)
    inside = jnp.where((col >= cols + 64) & (place.gy > 0), 1.0, inside)
    for k in span:
        row = 8 * k - PAD
        cut = slice(8 * k, 8 * k + 8)
        here = tall[cut, :]
        band = place.band_of(row)
        hit = gaps[0, band] == place.nodes(row, WIDE)
        push = jnp.where(hit, PENALTY * jnp.maximum(gaps[1, band] - here, 0.0), 0.0)
        fast = tall_v[cut, :] + STEP_DT * (push - BEND * laplace_of(bent, k))
        there = here + STEP_DT * fast
        keep = inside
        if row < 0:
            keep = inside * jnp.where(place.gx > 0, 1.0, 0.0)
        elif row >= rows:
            keep = inside * jnp.where(place.gx < place.nx - 1, 1.0, 0.0)
        tall[cut, :] = there * keep
        if 0 <= row < rows:
            tall_v[cut, :] = fast
            pushed[cut, :] = push
    laplace_pass(tall, bent, span)
    for k in range(PAD // 8, (PAD + rows) // 8):
        row = 8 * k - PAD
        cut = slice(8 * k, 8 * k + 8)
        here = tall[cut, 0:cols]
        band = place.band_of(row)
        hit = gaps[0, band, :, 0:cols] == place.nodes(row, cols)
        gap = gaps[2, band, :, 0:cols] - (STEP_DT * STEP_DT) * pushed[cut, 0:cols]
        push = jnp.where(hit, PENALTY * jnp.maximum(gap - here, 0.0), 0.0)
        fast = tall_v[cut, 0:cols] + STEP_DT * (push - BEND * laplace_of(bent, k)[:, 0:cols])
        out_speed[row : row + 8, :] = fast
        out_shell[row : row + 8, :] = here + STEP_DT * fast

    grid[...] = jnp.zeros_like(grid)
    top, low = STRIDE, (rows_a + 2) * STRIDE
    for f in range(4):
        source, at = ((jit, 32 + 8 * f), (disp, 8 * (f - 2)))[f >= 2]
        extra = 32 + 8 * (f - 2)

        def with_rest(values, rest):
            return values + rest if f >= 2 else values

        for a in range(rows_a):
            base = (a + 2) * STRIDE + 8
            grid[f, base : base + tiles, :] = with_rest(source[f % 2, a], jit[f % 2, a])
        for side, offset in ((right, 16), (left, 7)):
            grid[f, pl.ds(2 * STRIDE + offset, rows_a, stride=STRIDE), :] = with_rest(
                side[at : at + 8], side[extra : extra + 8]
            )
        for end, base in ((0, top), (1, low)):
            grid[f, base + 8 : base + 16, :] = with_rest(halo[end, at : at + 8, :], halo[end, extra : extra + 8, :])
            for part, offset in ((64, 16), (72, 7)):
                grid[f, base + offset : base + offset + 1, :] = with_rest(
                    halo[end, part + at // 8 : part + at // 8 + 1, :],
                    halo[end, part + extra // 8 : part + extra // 8 + 1, :],
                )

    blocks = rows_a + 5
    corner = 8 * (rows_a + 4)

    def spread_grid(f, row_blocks, edges):
        for dx in (-1, 0, 1):
            for dy in (-1, 0, 1):
                s = slot(dx, dy)
                for t in row_blocks:
                    a = t if t < rows_a else (-1, rows_a)[t - rows_a]
                    base = (a + 2 + dx) * STRIDE + 8 + dy
                    near[f, s, 8 * t : 8 * t + 8, :] = turn(grid[f, base : base + 8, :], TILE_Y * dy)
                if edges:
                    for t, offset in ((rows_a + 2, 7), (rows_a + 3, 16)):
                        near[f, s, 8 * t : 8 * t + 8, :] = turn(
                            grid[f, pl.ds((2 + dx) * STRIDE + offset + dy, 8, stride=STRIDE), :], TILE_Y * dy
                        )
                    near[f, s, corner : corner + 8, :] = jnp.zeros((8, PTS), F32)
                    for n, offset in enumerate((7, 16)):
                        for m, base in enumerate((top, low)):
                            start = base + dx * STRIDE + offset + dy
                            at = corner + 2 * n + m
                            near[f, s, at : at + 1, :] = turn(grid[f, start : start + 1, :], TILE_Y * dy)

    for f in range(4):
        spread_grid(f, range(rows_a + 2), True)

    for f in range(2):
        at = 16 + 8 * f
        for a in range(rows_a):
            vels[f, 8 * a : 8 * a + 8, :] = vel[f, a]
        for end in (0, 1):
            t = rows_a + end
            vels[f, 8 * t : 8 * t + 8, :] = halo[end, at : at + 8, :]
        vels[f, corner - 16 : corner - 8, :] = left[at : at + 8]
        vels[f, corner - 8 : corner, :] = right[at : at + 8]
        vels[f, corner : corner + 8, :] = jnp.zeros((8, PTS), F32)
        for n, part in enumerate((72, 64)):
            for end in (0, 1):
                vels[f, corner + 2 * n + end : corner + 2 * n + end + 1, :] = halo[
                    end, part + 2 + f : part + 3 + f, :
                ]

    def joined(low_part, high_part):
        return jnp.left_shift(high_part.astype(I32), 16) | low_part.astype(I32)

    sub = subs()
    west, east = place.gy == 0, place.gy == place.ny - 1
    north, south = place.gx == 0, place.gx == place.nx - 1
    for t in range(blocks):
        if t < rows_a:
            packed = words[t]
        elif t < rows_a + 2:
            packed = joined(halo[t - rows_a, 48:56, :], halo[t - rows_a, 56:64, :])
        elif t < rows_a + 4:
            side = (left, right)[t - rows_a - 2]
            packed = joined(side[48:56], side[56:64])
        else:
            zero = jnp.zeros((4, PTS), F32)
            lows = [halo[end, part + 6 : part + 7, :] for part in (72, 64) for end in (0, 1)]
            highs = [halo[end, part + 7 : part + 8, :] for part in (72, 64) for end in (0, 1)]
            packed = joined(jnp.concatenate(lows + [zero], axis=0), jnp.concatenate(highs + [zero], axis=0))
        for dx in (-1, 0, 1):
            for dy in (-1, 0, 1):
                s = slot(dx, dy)
                word = jnp.broadcast_to(packed[:, s : s + 1], (8, PTS))
                if t < rows_a + 2:
                    if dy < 0:
                        word = jnp.where((sub == 0) & west, 0, word)
                    if dy > 0:
                        word = jnp.where((sub == tiles - 1) & east, 0, word)
                    if dx < 0 and t == 0:
                        word = jnp.where(north, 0, word)
                    if dx > 0 and t == rows_a - 1:
                        word = jnp.where(south, 0, word)
                elif t < rows_a + 4:
                    if dx < 0:
                        word = jnp.where((sub == 0) & north, 0, word)
                    if dx > 0:
                        word = jnp.where((sub == rows_a - 1) & south, 0, word)
                kinds[s, 8 * t : 8 * t + 8, :] = word

    def getter(ref, f, at):
        held = {}

        def get(dx, dy):
            if (dx, dy) not in held:
                cut = (slot(dx, dy), pl.ds(at, 8), slice(None))
                held[dx, dy] = ref[cut] if f is None else ref[(f,) + cut]
            return held[dx, dy]

        return get

    @pl.loop(0, blocks)
    def _(t):
        at = pl.multiple_of(8 * t, 8)

        def keep(number, weight, level):
            weights[number, pl.ds(at, 8), :] = weight
            levels[number, pl.ds(at, 8), :] = level

        fx, fy = first_forces(
            getter(near, 0, at),
            getter(near, 1, at),
            getter(near, 2, at),
            getter(near, 3, at),
            getter(kinds, None, at),
            keep,
        )
        trial[0, pl.ds(at, 8), :] = fx
        trial[1, pl.ds(at, 8), :] = fy

    here = jnp.where(place.front, 1.0, 0.0)
    push = PENALTY * here * jnp.maximum(contact[8:18] - owners[8:18], 0.0)
    last = rows_a - 1
    trial[0, 8 * last : 8 * last + 8, :] -= push[0:8]
    at = 8 * (rows_a + 2) + last
    trial[0, at : at + 1, :] -= push[9:10]
    trial[0, at + 8 : at + 9, :] -= push[8:9]
    for f in range(2):
        vels[f] = vels[f] + STEP_DT * trial[f]
        trial[f] = near[2 + f, slot(0, 0)] + STEP_DT * vels[f]
        for t in range(rows_a + 2):
            a = t if t < rows_a else (-1, rows_a)[t - rows_a]
            grid[2 + f, (a + 2) * STRIDE + 8 : (a + 2) * STRIDE + 16, :] = trial[f, 8 * t : 8 * t + 8, :]
        for t, offset in ((rows_a + 2, 7), (rows_a + 3, 16)):
            grid[2 + f, pl.ds(2 * STRIDE + offset, 8, stride=STRIDE), :] = trial[f, 8 * t : 8 * t + 8, :]
        for n, offset in enumerate((7, 16)):
            for m, base in enumerate((top, low)):
                at = corner + 2 * n + m
                grid[2 + f, base + offset : base + offset + 1, :] = trial[f, at : at + 1, :]
        spread_grid(2 + f, range(rows_a), False)

    @pl.loop(0, rows_a)
    def _(t):
        at = pl.multiple_of(8 * t, 8)

        def kept(number):
            return weights[number, pl.ds(at, 8), :], levels[number, pl.ds(at, 8), :]

        fx, fy = second_forces(getter(near, 2, at), getter(near, 3, at), kept)
        out_vel[0, t] = vels[0, pl.ds(at, 8), :] + STEP_DT * fx
        out_vel[1, t] = vels[1, pl.ds(at, 8), :] + STEP_DT * fy

    gap = trial[0, 8 * last : 8 * last + 8, :] - jit[0, last] + inter[...]
    reached = owners[0:8] + (STEP_DT * STEP_DT) * push[0:8]
    out_vel[0, last] = out_vel[0, last] - (STEP_DT * PENALTY) * here * jnp.maximum(gap - reached, 0.0)
    for f in range(2):
        for a in range(rows_a):
            out_disp[f, a] = (trial[f, 8 * a : 8 * a + 8, :] - jit[f, a]) + STEP_DT * out_vel[f, a]


def on_device(nx, ny, disp, vel, jit, words, node, inter, shell, speed):
    rows_a = disp.shape[1]
    rows, cols = shell.shape
    place_args = (nx, ny, rows, cols)
    shifts = tuple(range(1, nx))
    base = (disp, vel, jit, words, node, inter, shell, speed)

    def call(body, out, scratch, *args, far=0):
        args = [pltpu.with_memory_space_constraint(x, pltpu.MemorySpace.HBM) for x in args[:far]] + list(args[far:])
        specs = [pl.BlockSpec(memory_space=pltpu.MemorySpace.HBM)] * far
        specs += [pl.BlockSpec(memory_space=pltpu.VMEM)] * (len(args) - far)
        return pl.pallas_call(
            body,
            out_shape=out,
            in_specs=specs,
            scratch_shapes=scratch,
            compiler_params=pltpu.CompilerParams(vmem_limit_bytes=40 * 1024 * 1024),
        )(*args)

    side = jax.ShapeDtypeStruct((Y_ROWS, PTS), F32)
    first, second, *base = call(
        functools.partial(pack_sides, place_args),
        [side, side] + [jax.ShapeDtypeStruct(x.shape, x.dtype) for x in base],
        [pltpu.VMEM((TILE_X, 8, cols), F32), pltpu.SemaphoreType.DMA((len(base),))],
        *base,
        far=len(base),
    )
    first = lax.ppermute(first, "gy", [(i, i ^ 1) for i in range(ny)])
    second = lax.ppermute(second, "gy", [(i, ((i - 1) ^ 1) + 1 if 0 < i < ny - 1 else ny - 1 - i) for i in range(ny)])

    tall = pltpu.VMEM((rows + 2 * PAD, WIDE), F32)
    outs = [
        jax.ShapeDtypeStruct((CONTACT_ROWS + (HALO_ROWS if s & (s + 1) == 0 else 0), PTS), F32) for s in shifts
    ]
    outs += [jax.ShapeDtypeStruct((2 * CONTACT_ROWS, PTS), F32)]
    outs += [jax.ShapeDtypeStruct((rows, PTS), F32)] * 2
    *ends, own, strip_d, strip_v = call(
        functools.partial(pack_ends, place_args, shifts),
        outs,
        [pltpu.VMEM((4, 4 * STRIDE, PTS), F32), tall, tall, tall, pltpu.VMEM((TILE_X, 8, cols), F32)],
        *base,
        first,
        second,
    )
    ends = [lax.ppermute(e, "gx", [(i, i ^ s) for i in range(nx)]) for s, e in zip(shifts, ends)]

    held = 8 * (rows_a + 5)
    scratch = [
        pltpu.VMEM((4, (rows_a + 4) * STRIDE, PTS), F32),
        pltpu.VMEM((4, 9, held, PTS), F32),
        pltpu.VMEM((2, held, PTS), F32),
        pltpu.VMEM((9, held, PTS), I32),
        pltpu.VMEM((len(OFFSETS), held, PTS), F32),
        pltpu.VMEM((len(OFFSETS), held, PTS), F32),
        tall,
        tall,
        tall,
        tall,
        pltpu.VMEM((3, TILE_X, 8, WIDE), F32),
        pltpu.VMEM((2, held, PTS), F32),
        pltpu.VMEM((2, HALO_ROWS, PTS), F32),
    ]
    out = [jax.ShapeDtypeStruct(x.shape, F32) for x in (disp, vel, shell, speed)]
    return tuple(
        call(functools.partial(both_steps, place_args, shifts), out, scratch, *base, first, second, own, strip_d, strip_v, *ends)
    )


def solution(mesh):
    in_specs = (
        P(None, "gx", "gy", None),
        P(None, "gx", "gy", None),
        P(None, "gx", "gy", None),
        P("gx", "gy", None),
        P("gy", None),
        P("gy", None),
        P("gx", "gy"),
        P("gx", "gy"),
    )
    out_specs = (P(None, "gx", "gy", None), P(None, "gx", "gy", None), P("gx", "gy"), P("gx", "gy"))
    body = functools.partial(on_device, mesh.shape["gx"], mesh.shape["gy"])
    return jax.shard_map(body, mesh=mesh, in_specs=in_specs, out_specs=out_specs, check_vma=False)
```

```python
import functools

import jax
import jax.numpy as jnp
from jax import lax
from jax.experimental import pallas as pl
from jax.experimental.pallas import tpu as pltpu
from jax.sharding import PartitionSpec as P

TILE_X = 8
TILE_Y = 16
PTS = 128
SPLIT = 4

HORIZON = 3.5
DELTA_SQ = 0.25
PENALTY = 4.0
BEND = 0.5
STEP_DT = 0.2

F32 = jnp.float32
I32 = jnp.int32

STRIDE = 24
WIDE = 640
PAD = 16


def bond_offsets():
    limit = HORIZON * HORIZON - DELTA_SQ
    found = []
    for oy in range(-4, 5):
        for ox in range(-4, 5):
            near = max(abs(ox) - 0.4, 0.0) ** 2 + max(abs(oy) - 0.4, 0.0) ** 2
            if near < limit and (ox or oy):
                found.append((ox, oy))
    return found


OFFSETS = bond_offsets()
SIDEWAYS = sorted({oy for _, oy in OFFSETS})


def sign(value):
    return (value > 0) - (value < 0)


def lanes():
    return lax.broadcasted_iota(I32, (8, PTS), 1)


def subs():
    return lax.broadcasted_iota(I32, (8, PTS), 0)


def turn(values, shift):
    size = values.shape[1]
    return pltpu.roll(values, shift % size, 1) if shift % size else values


def slot(dx, dy):
    return 3 * (dx + 1) + dy + 1


def lane_masks():
    lane = lanes()
    row, col = lane // TILE_Y, lane % TILE_Y
    masks = {}
    for o in (1, 2, 3):
        masks["col_at", o] = col < o
        masks["col_at", -o] = col >= TILE_Y - o
        masks["col_from", o] = col >= TILE_Y - o
        masks["col_from", -o] = col < o
        masks["row_at", o] = row < o
        masks["row_at", -o] = row >= TILE_X - o
        masks["row_from", o] = row >= TILE_X - o
        masks["row_from", -o] = row < o
    bits = {}
    for ox in range(-3, 4):
        bits[ox] = jnp.left_shift(jnp.int32(1), 4 * row + ((row + ox) & 7) // 2)
    return masks, bits


def moved(get, oy, masks):
    out = {}
    for dx in (-1, 0, 1):
        held = get(dx, 0)
        if oy:
            held = turn(jnp.where(masks["col_at", oy], get(dx, sign(oy)), held), -oy)
        out[dx] = held
    return out


def across(cells, ox, masks):
    if not ox:
        return cells[0]
    return turn(jnp.where(masks["row_at", ox], cells[sign(ox)], cells[0]), -TILE_Y * ox)


def first_forces(get_jx, get_jy, get_dx, get_dy, get_words, keep=None, both=True):
    masks, bits = lane_masks()
    jx0, jy0, dx0, dy0 = get_jx(0, 0), get_jy(0, 0), get_dx(0, 0), get_dy(0, 0)
    fx = jnp.zeros((8, PTS), F32)
    fy = jnp.zeros((8, PTS), F32)
    for oy in SIDEWAYS:
        jxs, jys = moved(get_jx, oy, masks), moved(get_jy, oy, masks)
        dxs, dys = moved(get_dx, oy, masks), moved(get_dy, oy, masks)
        words = {}
        for dx in (-1, 0, 1):
            words[dx] = get_words(dx, 0)
            if oy:
                words[dx] = jnp.where(masks["col_from", oy], get_words(dx, sign(oy)), words[dx])
        for number, (ox, other) in enumerate(OFFSETS):
            if other != oy:
                continue
            word = words[0]
            if ox:
                word = jnp.where(masks["row_from", ox], words[sign(ox)], word)
            intact = (word & bits[ox]) != 0
            rest_x = across(jxs, ox, masks) - (jx0 - float(ox))
            rest_y = across(jys, ox, masks) - (jy0 - float(oy))
            now_x = across(dxs, ox, masks) - (dx0 - float(ox))
            now_y = across(dys, ox, masks) - (dy0 - float(oy))
            rest_sq = rest_x * rest_x + rest_y * rest_y + DELTA_SQ
            now_sq = now_x * now_x + now_y * now_y + DELTA_SQ
            rest_inv = lax.rsqrt(rest_sq)
            reach = jnp.maximum(1.0 - rest_sq * rest_inv * (1.0 / HORIZON), 0.0)
            weight = jnp.where(intact, reach * reach, 0.0)
            level = weight * rest_inv
            if keep is not None:
                keep(number, weight, level)
            factor = level - weight * lax.rsqrt(now_sq)
            fx = fx + factor * now_x
            if both:
                fy = fy + factor * now_y
    return fx, fy


def pick_lanes(block, index):
    return jnp.take_along_axis(block, index, axis=1, mode="promise_in_bounds")


def flips(blocks):
    lane, sub = lanes(), subs()
    for level in (2, 1, 0):
        step = 1 << level
        stay = ((lane >> (level + 4)) ^ (sub >> level)) & 1 == 0
        if step == 4:
            others = [turn(pltpu.roll(block, 4, 0), 64) for block in blocks]
        else:
            low = (sub >> level) & 1 == 0
            index = lane ^ (TILE_Y * step)
            others = [jnp.where(low, pltpu.roll(block, 8 - step, 0), pltpu.roll(block, step, 0)) for block in blocks]
            others = [pick_lanes(block, index) for block in others]
        blocks = [jnp.where(stay, block, other) for block, other in zip(blocks, others)]
    return blocks


def flip(block):
    return flips([block])[0]


def side_columns(row):
    return pick_lanes(jnp.broadcast_to(row, (8, PTS)), TILE_Y * subs() + (lanes() & (TILE_Y - 1)))


def word_row(packed, s):
    word = jnp.where(subs() == lanes() // TILE_Y, jnp.broadcast_to(packed[:, s : s + 1], (8, PTS)), 0)
    for step in (4, 2, 1):
        word = word | pltpu.roll(word, step, 0)
    return word


def sideways(cells, beside, oy):
    if not oy:
        return cells
    lane = lanes()
    mask = lane < oy if oy > 0 else lane >= PTS + oy
    return turn(jnp.where(mask, beside, cells), -oy)


FROM = 5


def group_masks():
    lane, sub = lanes(), subs()
    row = (sub + FROM) & (TILE_X - 1)
    col = lane & (TILE_Y - 1)
    masks, bits = {}, {}
    for o in (1, 2, 3):
        masks["col", o] = col >= TILE_Y - o
        masks["col", -o] = col < o
        masks["row", o] = row >= TILE_X - o
        masks["row", -o] = row < o
    for ox in range(-3, 4):
        bits[ox] = jnp.left_shift(jnp.int32(1), 4 * row + ((row + ox) & 7) // 2)
    return masks, bits


def group_first(cell, word, keep):
    masks, bits = group_masks()
    zero = [cell(f, 0, 0) for f in range(4)]
    fx = jnp.zeros((8, PTS), F32)
    fy = jnp.zeros((8, PTS), F32)
    plain = [word(slot(dx, 0)) for dx in (-1, 0, 1)]
    for oy in SIDEWAYS:
        words = plain
        if oy:
            words = [jnp.where(masks["col", oy], word(slot(dx, sign(oy))), plain[dx + 1]) for dx in (-1, 0, 1)]
        base_y, base_v = zero[1] - float(oy), zero[3] - float(oy)
        for number, (ox, other) in enumerate(OFFSETS):
            if other != oy:
                continue
            picked = words[1]
            if ox:
                picked = jnp.where(masks["row", ox], words[sign(ox) + 1], picked)
            intact = (picked & bits[ox]) != 0
            rest_x = cell(0, oy, ox) - (zero[0] - float(ox))
            rest_y = cell(1, oy, ox) - base_y
            now_x = cell(2, oy, ox) - (zero[2] - float(ox))
            now_y = cell(3, oy, ox) - base_v
            rest_sq = rest_x * rest_x + rest_y * rest_y + DELTA_SQ
            now_sq = now_x * now_x + now_y * now_y + DELTA_SQ
            rest_inv = lax.rsqrt(rest_sq)
            reach = jnp.maximum(1.0 - rest_sq * rest_inv * (1.0 / HORIZON), 0.0)
            weight = jnp.where(intact, reach * reach, 0.0)
            level = weight * rest_inv
            keep(number, weight, level)
            factor = level - weight * lax.rsqrt(now_sq)
            fx = fx + factor * now_x
            fy = fy + factor * now_y
    return fx, fy


def group_second(cell, kept):
    zero = [cell(f, 0, 0) for f in range(2)]
    fx = jnp.zeros((8, PTS), F32)
    fy = jnp.zeros((8, PTS), F32)
    for number, (ox, oy) in enumerate(OFFSETS):
        now_x = cell(0, oy, ox) - (zero[0] - float(ox))
        now_y = cell(1, oy, ox) - (zero[1] - float(oy))
        now_sq = now_x * now_x + now_y * now_y + DELTA_SQ
        weight, level = kept(number)
        factor = level - weight * lax.rsqrt(now_sq)
        fx = fx + factor * now_x
        fy = fy + factor * now_y
    return fx, fy


def joined(low_part, high_part):
    return jnp.left_shift(high_part.astype(I32), 16) | low_part.astype(I32)


def widen(row_of, count):
    lane, sub = lanes(), subs()
    index = sub * TILE_Y + (lane % 64) // SPLIT
    out = []
    for j in range(count):
        left, right = (
            pick_lanes(jnp.broadcast_to(row_of(b), (8, PTS)), index) for b in (2 * j, 2 * j + 1)
        )
        out.append(jnp.where(lane < 64, left, right))
    return out


def narrow(block_of, tiles):
    lane, sub = lanes(), subs()
    out = []
    for b in tiles:
        held = block_of(b // 2)
        held = held + turn(held, -1)
        held = held + turn(held, -2)
        picked = pick_lanes(held, 64 * (b % 2) + SPLIT * (lane % TILE_Y))
        out.append(jnp.sum(jnp.where(sub == lane // TILE_Y, picked, 0.0), axis=0, keepdims=True))
    return out


def lay_out(ref, at, j, block):
    for row in range(TILE_X):
        ref[at + (row, slice(None), slice(j * PTS, (j + 1) * PTS))] = jnp.broadcast_to(block[row : row + 1], (8, PTS))


class Place:
    def __init__(self, nx, ny, shell_rows, shell_cols):
        self.nx, self.ny = nx, ny
        self.gx, self.gy = lax.axis_index("gx"), lax.axis_index("gy")
        self.shell_rows, self.shell_cols = shell_rows, shell_cols
        self.width = shell_cols * ny
        self.band = shell_rows * nx // TILE_X
        self.bands = shell_rows // self.band
        self.front = self.gx == nx - 1

    def sides(self, first, second):
        even = self.gy % 2 == 0
        right = jnp.where(even, first, second)
        left = jnp.where(even, second, first)
        right = jnp.where(self.gy < self.ny - 1, right, 0.0)
        left = jnp.where(self.gy > 0, left, 0.0)
        return right, left

    def nodes(self, row, columns):
        shape = (8, columns)
        col = lax.broadcasted_iota(I32, shape, 1)
        if columns > self.shell_cols:
            col = jnp.where(col >= self.shell_cols + 64, col - columns, col)
        first = (self.gx * self.shell_rows + row) * self.width + self.gy * self.shell_cols
        return (first + lax.broadcasted_iota(I32, shape, 0) * self.width + col).astype(F32)

    def band_of(self, row):
        return jnp.clip((self.gx * self.shell_rows + row + self.band) // self.band - 1, 0, TILE_X - 1)


Y_ROWS = 88


def fetch(pairs, sems):
    copies = [pltpu.make_async_copy(source, target, sems.at[n]) for n, (source, target) in enumerate(pairs)]
    for copy in copies:
        copy.start()
    for copy in copies:
        copy.wait()


def pack_sides(place_args, *refs):
    sources, (first, second), held, (wide_ref, sems) = refs[:8], refs[8:10], refs[10:18], refs[18:]
    place = Place(*place_args)
    fetch(list(zip(sources, held)), sems)
    disp, vel, jit, words, node, inter, shell, speed = held
    tiles = disp.shape[2]
    even = place.gy % 2 == 0
    blocks = place.shell_cols // PTS
    numbers = node[...].astype(F32)
    edge_blocks = (0, blocks - 1)
    for j in edge_blocks:
        lay_out(wide_ref, (), j, widen(lambda b: numbers[b : b + 1], blocks)[j])
    held = {}
    for j in edge_blocks:
        total = jnp.zeros((8, PTS), F32)
        for part in range(place.bands):
            summed = jnp.zeros((8, PTS), F32)
            for row in range(part * place.band, (part + 1) * place.band, 8):
                wanted = wide_ref[place.band_of(row), :, j * PTS : (j + 1) * PTS]
                ids = place.nodes(row, PTS) + float(j * PTS)
                summed = summed + jnp.where(wanted == ids, shell[row : row + 8, j * PTS : (j + 1) * PTS], 0.0)
            summed = jnp.sum(summed, axis=0, keepdims=True)
            total = total + jnp.where(subs() == place.band_of(part * place.band), summed, 0.0)
        held[j] = total
    met = narrow(lambda j: held[j], (0, tiles - 1))

    def send(ref, to_right):
        edge = jnp.where(to_right, tiles - 1, 0)
        for f, source in enumerate((disp, disp, vel, vel, jit, jit)):
            ref[8 * f : 8 * f + 8, :] = jnp.where(
                to_right, source[f % 2, :, tiles - 1, :], source[f % 2, :, 0, :]
            )
        ref[48:Y_ROWS, :] = jnp.zeros((Y_ROWS - 48, PTS), F32)
        edge_words = jnp.where(to_right, words[:, tiles - 1, :], words[:, 0, :])
        ref[48:56, 0:9] = (edge_words & 65535).astype(F32)
        ref[56:64, 0:9] = jnp.right_shift(edge_words, 16).astype(F32)
        ref[64:65, :] = jnp.where(to_right, numbers[tiles - 1 : tiles], numbers[0:1])
        ref[65:66, :] = jnp.where(to_right, inter[tiles - 1 : tiles, :], inter[0:1, :])
        ref[66:67, :] = jnp.where(to_right, met[1], met[0])
        for f, source in enumerate((shell, speed)):
            last = jnp.transpose(source[:, place.shell_cols - PTS :])[PTS - 8 :]
            head = jnp.transpose(source[:, 0:PTS])[:8]
            ref[72 + 8 * f : 80 + 8 * f, :] = jnp.where(to_right, last, head)

    send(first, even)
    send(second, jnp.logical_not(even))


HALO_ROWS = 120
CONTACT_ROWS = 24


def shell_strip(right, left, at):
    middle = jnp.zeros((PTS - 16, PTS), F32)
    return jnp.transpose(jnp.concatenate([right[at : at + 8], middle, left[at : at + 8]], axis=0))


def laplace_pass(source, target, blocks):
    for k in blocks:
        row = 8 * k
        here = source[row : row + 8, :]
        around = source[row - 1 : row + 7, :] + source[row + 1 : row + 9, :] + turn(here, 1) + turn(here, -1)
        target[row : row + 8, :] = around - 4.0 * here


def laplace_of(source, k):
    row = 8 * k
    here = source[row : row + 8, :]
    around = source[row - 1 : row + 7, :] + source[row + 1 : row + 9, :] + turn(here, 1) + turn(here, -1)
    return around - 4.0 * here


def pack_ends(
    place_args, shifts, disp, vel, jit, words, node, inter, shell, speed, first, second, *refs
):
    place = Place(*place_args)
    outs = refs[: len(shifts)]
    own, strip_d, strip_v, grid, tall, tall_v, bent, wide_ref = refs[len(shifts) :]
    rows_a, tiles = disp.shape[1], disp.shape[2]
    rows, cols = place.shell_rows, place.shell_cols
    right, left = place.sides(first[...], second[...])

    grid[...] = jnp.zeros_like(grid)
    for f, (source, at) in enumerate(((jit, 32), (jit, 40), (disp, 0), (disp, 8))):
        for level, a in enumerate((rows_a - 2, rows_a - 1)):
            base = (level + 1) * STRIDE
            values, from_right, from_left = source[f % 2, a], right[at + a : at + a + 1], left[at + a : at + a + 1]
            if f >= 2:
                far = 32 + 8 * (f % 2) + a
                values = values + jit[f % 2, a]
                from_right = from_right + right[far : far + 1]
                from_left = from_left + left[far : far + 1]
            grid[f, base + 8 : base + 16, :] = values
            grid[f, base + 16 : base + 17, :] = from_right
            grid[f, base + 7 : base + 8, :] = from_left

    def tile_getter(f):
        held = {}

        def get(dx, dy):
            if (dx, dy) not in held:
                base = (2 + dx) * STRIDE + 8 + dy
                held[dx, dy] = turn(grid[f, base : base + 8, :], TILE_Y * dy)
            return held[dx, dy]

        return get

    def words_getter():
        held = {}
        sub = subs()

        def get(dx, dy):
            if (dx, dy) not in held:
                s = slot(dx, dy)
                word = jnp.broadcast_to(words[rows_a - 1, :, s : s + 1], (8, PTS))
                if dx > 0:
                    word = jnp.zeros_like(word)
                if dy < 0:
                    word = jnp.where((sub == 0) & (place.gy == 0), 0, word)
                if dy > 0:
                    word = jnp.where((sub == tiles - 1) & (place.gy == place.ny - 1), 0, word)
                held[dx, dy] = word
            return held[dx, dy]

        return get

    force, _ = first_forces(
        tile_getter(0), tile_getter(1), tile_getter(2), tile_getter(3), words_getter(), both=False
    )
    gap = disp[0, rows_a - 1] + inter[...]
    last = rows_a - 1
    own[0:8, :] = gap + STEP_DT * (vel[0, last] + STEP_DT * force)
    own[8:16, :] = gap
    own[16:24, :] = jnp.zeros((8, PTS), F32)
    own[16:17, :] = right[last : last + 1] + right[65:66]
    own[17:18, :] = left[last : last + 1] + left[65:66]

    halo_d = shell_strip(right, left, 72)
    halo_v = shell_strip(right, left, 80)
    strip_d[...] = halo_d
    strip_v[...] = halo_v
    tall[...] = jnp.zeros_like(tall)
    tall_v[...] = jnp.zeros_like(tall_v)
    tall[PAD : PAD + rows, 0:cols] = shell[...]
    tall[PAD : PAD + rows, cols:WIDE] = halo_d
    tall_v[PAD : PAD + rows, 0:cols] = speed[...]
    bent[...] = jnp.zeros_like(bent)
    span = range(PAD // 8 - 1, (PAD + rows) // 8 + 1)
    laplace_pass(tall, bent, span)
    numbers = node[...].astype(F32)
    for j, block in enumerate(widen(lambda b: numbers[b : b + 1], cols // PTS)):
        lay_out(wide_ref, (), j, block)
    sub_wide = lax.broadcasted_iota(I32, (8, cols), 0)
    ahead = jnp.zeros((8, cols), F32)
    met = jnp.zeros((8, cols), F32)
    parts = [[-8]] + [list(range(p * place.band, (p + 1) * place.band, 8)) for p in range(place.bands)] + [[rows]]
    for part in parts:
        soon = jnp.zeros((8, cols), F32)
        now = jnp.zeros((8, cols), F32)
        band = place.band_of(part[0])
        for row in part:
            k = (PAD + row) // 8
            hit = wide_ref[band] == place.nodes(row, cols)
            bending = laplace_of(bent, k)[:, 0:cols]
            here = tall[PAD + row : PAD + row + 8, 0:cols]
            later = here + STEP_DT * (tall_v[PAD + row : PAD + row + 8, 0:cols] - (STEP_DT * BEND) * bending)
            soon = soon + jnp.where(hit, later, 0.0)
            if 0 <= row < rows:
                now = now + jnp.where(hit, here, 0.0)
        ahead = ahead + jnp.where(sub_wide == band, jnp.sum(soon, axis=0, keepdims=True), 0.0)
        if 0 <= part[0] < rows:
            met = met + jnp.where(sub_wide == band, jnp.sum(now, axis=0, keepdims=True), 0.0)
    base = CONTACT_ROWS
    own[base + 16 : base + 24, :] = jnp.zeros((8, PTS), F32)
    for b, row in enumerate(narrow(lambda j: ahead[:, j * PTS : (j + 1) * PTS], range(tiles))):
        own[base + b : base + b + 1, :] = row
    for b, row in enumerate(narrow(lambda j: met[:, j * PTS : (j + 1) * PTS], range(tiles))):
        own[base + 8 + b : base + 9 + b, :] = row
    own[base + 16 : base + 17, :] = right[66:67]
    own[base + 17 : base + 18, :] = left[66:67]

    mine = jnp.where(place.front, own[0:CONTACT_ROWS, :], own[base : base + CONTACT_ROWS, :])
    for shift, out in zip(shifts, outs):
        at = 0
        if shift & (shift + 1) == 0:
            at = HALO_ROWS
            down = (place.gx ^ shift) > place.gx
            edge = jnp.where(down, rows_a - 1, 0)
            for f, source in enumerate((disp, disp, vel, vel, jit, jit)):
                out[8 * f : 8 * f + 8, :] = source[f % 2, edge]
            out[48:80, :] = jnp.zeros((32, PTS), F32)
            edge_words = words[edge]
            out[48:56, 0:9] = (edge_words & 65535).astype(F32)
            out[56:64, 0:9] = jnp.right_shift(edge_words, 16).astype(F32)
            for f in range(8):
                for side, values in ((64, right), (72, left)):
                    low, high = values[8 * f : 8 * f + 1], values[8 * f + rows_a - 1 : 8 * f + rows_a]
                    out[side + f : side + f + 1, :] = jnp.where(down, high, low)
            for j in range(WIDE // PTS):
                cut = slice(j * PTS, (j + 1) * PTS)
                if j < cols // PTS:
                    d_low, d_high = shell[0:4, cut], shell[rows - 4 : rows, cut]
                    v_low, v_high = speed[0:2, cut], speed[rows - 2 : rows, cut]
                else:
                    d_low, d_high = halo_d[0:4], halo_d[rows - 4 : rows]
                    v_low, v_high = halo_v[0:2], halo_v[rows - 2 : rows]
                out[80 + 8 * j : 84 + 8 * j, :] = jnp.where(down, d_high, d_low)
                out[84 + 8 * j : 86 + 8 * j, :] = jnp.where(down, v_high, v_low)
                out[86 + 8 * j : 88 + 8 * j, :] = jnp.zeros((2, PTS), F32)
        out[at : at + CONTACT_ROWS, :] = mine


def inner_rows(place_args, disp, vel, jit, words, first, second, *refs):
    place = Place(*place_args)
    win, weights, levels, flat, lead, beside, tiles_f, ends_w, strips, kinds, groups_w = refs
    rows_a, tiles = disp.shape[1], disp.shape[2]
    right, left = place.sides(first[...], second[...])
    lane, sub = lanes(), subs()
    west, east = place.gy == 0, place.gy == place.ny - 1
    north, south = place.gx == 0, place.gx == place.nx - 1
    leftward = (lane & (TILE_Y - 1)) >= TILE_Y // 2
    side = [jnp.where(leftward, left[8 * f : 8 * f + 8], right[8 * f : 8 * f + 8]) for f in range(6)]

    strips[...] = jnp.zeros_like(strips)
    for f in range(4):
        rest = jit[f % 2]
        whole = rest if f < 2 else rest + disp[f % 2]
        cols = side[4 + f % 2] if f < 2 else side[4 + f % 2] + side[f % 2]
        strips[f, 0, 8:16, :] = cols
        strips[f, 1, 8:16, :] = whole[:, 0, :]
        strips[f, 2, 8:16, :] = whole[:, tiles - 1, :]
        turned = flips([whole[a] for a in range(rows_a)])
        nears = [side_columns(cols[a : a + 1]) for a in range(rows_a)]
        for a, cells, near in zip(range(rows_a), turned, nears):
            for n, oy in enumerate(SIDEWAYS):
                shifted = sideways(cells, near, oy)
                if a < rows_a - 1:
                    win[f, n, a, 0:8, :] = shifted
                if a > 0:
                    win[f, n, a - 1, 8:16, :] = shifted
    for f in range(2):
        for a, cells in enumerate(flips([jit[f, a] + disp[f, a] + STEP_DT * vel[f, a] for a in range(rows_a)])):
            lead[f, a] = cells

    before = [None] * 9
    for a in range(rows_a):
        packed = words[a]
        for dx in (-1, 0, 1):
            for dy in (-1, 0, 1):
                s = slot(dx, dy)
                word = word_row(packed, s)
                if dy < 0:
                    word = jnp.where((lane < TILE_Y) & west, 0, word)
                if dy > 0:
                    word = jnp.where((lane >= PTS - TILE_Y) & east, 0, word)
                if dx < 0 and a == 0:
                    word = jnp.where(north, 0, word)
                if dx > 0 and a == rows_a - 1:
                    word = jnp.where(south, 0, word)
                if a:
                    groups_w[s, a - 1] = jnp.where(sub < TILE_X - FROM, before[s], word)
                if a in (0, rows_a - 1):
                    ends_w[s, min(a, 1)] = word
                before[s] = word
    left_words = joined(left[48:56], left[56:64])
    right_words = joined(right[48:56], right[56:64])
    for s in range(9):
        kinds[s] = jnp.where(
            leftward,
            jnp.broadcast_to(left_words[:, s : s + 1], (8, PTS)),
            jnp.broadcast_to(right_words[:, s : s + 1], (8, PTS)),
        )

    flat[...] = jnp.zeros_like(flat)

    @pl.loop(0, rows_a - 1)
    def _(k):
        def cell(f, oy, ox):
            return win[f, SIDEWAYS.index(oy), k, FROM + ox : FROM + ox + 8, :]

        def keep(number, weight, level):
            weights[number, k] = weight
            levels[number, k] = level

        fx, fy = group_first(cell, lambda s: groups_w[s, k], keep)
        at = pl.multiple_of(8 * k + 16, 8)
        flat[0, pl.ds(at, 8), :] = fx
        flat[1, pl.ds(at, 8), :] = fy

    def getter(f):
        held = {}

        def get(dx, dy):
            if (dx, dy) not in held:
                held[dx, dy] = turn(strips[f, dy % 3, 8 + dx : 16 + dx, :], TILE_Y * dy)
            return held[dx, dy]

        return get

    forces = first_forces(getter(0), getter(1), getter(2), getter(3), lambda dx, dy: kinds[slot(dx, dy)])
    for f in range(2):
        moved_side = side[4 + f] + side[f] + STEP_DT * (side[2 + f] + STEP_DT * forces[f])
        for a in range(rows_a):
            beside[f, a] = side_columns(moved_side[a : a + 1])
        for a, cells in enumerate(flips([flat[f, 8 * a + 11 : 8 * a + 19, :] for a in range(1, rows_a - 1)])):
            tiles_f[f, a + 1] = cells
        tiles_f[f, 0] = jnp.zeros((8, PTS), F32)
        tiles_f[f, rows_a - 1] = jnp.zeros((8, PTS), F32)


def both_steps(place_args, shifts, *refs):
    place = Place(*place_args)
    disp, vel, jit, words, node, inter, shell, speed, first, second, own, strip_d, strip_v = refs[:13]
    win, weights, levels, flat_in, lead, beside, tiles_f, ends_w = refs[13:21]
    ends = refs[21 : 21 + len(shifts)]
    out_disp, out_vel, out_shell, out_speed = refs[21 + len(shifts) : 25 + len(shifts)]
    tall, tall_v, bent, pushed, gaps, halo, ewin, ewords, eweights, elevels, flat, flat2, corners, kinds, swin = refs[
        25 + len(shifts) :
    ]
    rows_a, tiles = disp.shape[1], disp.shape[2]
    rows, cols = place.shell_rows, place.shell_cols
    right, left = place.sides(first[...], second[...])

    halo[...] = jnp.zeros_like(halo)
    contact = jnp.where(place.front, own[0:CONTACT_ROWS, :], 0.0)
    owners = own[CONTACT_ROWS:, :]
    for shift, ref in zip(shifts, ends):
        partner = place.gx ^ shift
        at = 0
        if shift & (shift + 1) == 0:
            at = HALO_ROWS

            @pl.when(partner == place.gx - 1)
            def _():
                halo[0] = ref[0:HALO_ROWS, :]

            @pl.when(partner == place.gx + 1)
            def _():
                halo[1] = ref[0:HALO_ROWS, :]

        got = ref[at : at + CONTACT_ROWS, :]
        contact = jnp.where(partner == place.nx - 1, got, contact)
        owners = owners + got

    tall[...] = jnp.zeros_like(tall)
    tall_v[...] = jnp.zeros_like(tall_v)
    tall[PAD : PAD + rows, 0:cols] = shell[...]
    tall[PAD : PAD + rows, cols:WIDE] = strip_d[...]
    tall_v[PAD : PAD + rows, 0:cols] = speed[...]
    tall_v[PAD : PAD + rows, cols:WIDE] = strip_v[...]
    for j in range(WIDE // PTS):
        cut = slice(j * PTS, (j + 1) * PTS)
        tall[PAD - 4 : PAD, cut] = halo[0, 80 + 8 * j : 84 + 8 * j, :]
        tall_v[PAD - 2 : PAD, cut] = halo[0, 84 + 8 * j : 86 + 8 * j, :]
        tall[PAD + rows : PAD + rows + 4, cut] = halo[1, 80 + 8 * j : 84 + 8 * j, :]
        tall_v[PAD + rows : PAD + rows + 2, cut] = halo[1, 84 + 8 * j : 86 + 8 * j, :]
    numbers = node[...].astype(F32)
    node_rows = [numbers[b : b + 1] for b in range(tiles)] + [right[64:65], left[64:65]]
    gap_rows = [contact[8 + b : 9 + b] for b in range(tiles)] + [contact[16:17], contact[17:18]]
    soon_rows = [contact[b : b + 1] for b in range(tiles)]
    for j, (nodes, gap) in enumerate(zip(widen(node_rows.__getitem__, 5), widen(gap_rows.__getitem__, 5))):
        lay_out(gaps, (0,), j, nodes)
        lay_out(gaps, (1,), j, gap)
    for j, soon in enumerate(widen(soon_rows.__getitem__, 4)):
        lay_out(gaps, (2,), j, soon)
    bent[...] = jnp.zeros_like(bent)
    span = range(PAD // 8 - 1, (PAD + rows) // 8 + 1)
    laplace_pass(tall, bent, span)
    col = lax.broadcasted_iota(I32, (8, WIDE), 1)
    inside = jnp.where(col < cols, 1.0, 0.0)
    inside = jnp.where((col >= cols) & (col < cols + 64) & (place.gy < place.ny - 1), 1.0, inside)
    inside = jnp.where((col >= cols + 64) & (place.gy > 0), 1.0, inside)
    for k in span:
        row = 8 * k - PAD
        cut = slice(8 * k, 8 * k + 8)
        here = tall[cut, :]
        band = place.band_of(row)
        hit = gaps[0, band] == place.nodes(row, WIDE)
        push = jnp.where(hit, PENALTY * jnp.maximum(gaps[1, band] - here, 0.0), 0.0)
        fast = tall_v[cut, :] + STEP_DT * (push - BEND * laplace_of(bent, k))
        there = here + STEP_DT * fast
        keep = inside
        if row < 0:
            keep = inside * jnp.where(place.gx > 0, 1.0, 0.0)
        elif row >= rows:
            keep = inside * jnp.where(place.gx < place.nx - 1, 1.0, 0.0)
        tall[cut, :] = there * keep
        if 0 <= row < rows:
            tall_v[cut, :] = fast
            pushed[cut, :] = push
    laplace_pass(tall, bent, span)
    for k in range(PAD // 8, (PAD + rows) // 8):
        row = 8 * k - PAD
        cut = slice(8 * k, 8 * k + 8)
        here = tall[cut, 0:cols]
        band = place.band_of(row)
        hit = gaps[0, band, :, 0:cols] == place.nodes(row, cols)
        gap = gaps[2, band, :, 0:cols] - (STEP_DT * STEP_DT) * pushed[cut, 0:cols]
        push = jnp.where(hit, PENALTY * jnp.maximum(gap - here, 0.0), 0.0)
        fast = tall_v[cut, 0:cols] + STEP_DT * (push - BEND * laplace_of(bent, k)[:, 0:cols])
        out_speed[row : row + 8, :] = fast
        out_shell[row : row + 8, :] = here + STEP_DT * fast

    lane, sub = lanes(), subs()
    west, east = place.gy == 0, place.gy == place.ny - 1
    north, south = place.gx == 0, place.gx == place.nx - 1
    leftward = (lane & (TILE_Y - 1)) >= TILE_Y // 2
    topmost = lane >= PTS // 2
    last = rows_a - 1

    def side_row(end, part):
        return jnp.where(leftward[0:1], halo[end, 72 + part : 73 + part, :], halo[end, 64 + part : 65 + part, :])

    sides = {(end, part): side_row(end, part) for end in (0, 1) for part in range(6)}
    far_lead = {}
    for end in (0, 1):
        for f in range(2):
            rest = halo[end, 32 + 8 * f : 40 + 8 * f, :]
            whole = rest + halo[end, 8 * f : 8 * f + 8, :]
            far_lead[f, end] = flip(whole + STEP_DT * halo[end, 16 + 8 * f : 24 + 8 * f, :])
            for field, cells, row in (
                (f, rest, sides[end, 4 + f]),
                (2 + f, whole, sides[end, 4 + f] + sides[end, f]),
            ):
                cells = flip(cells)
                near = side_columns(row)
                for n, oy in enumerate(SIDEWAYS):
                    shifted = sideways(cells, near, oy)
                    if end == 0:
                        ewin[field, n, 0, 0:8, :] = shifted
                        ewin[field, n, 0, 8:16, :] = win[field, n, 0, 0:8, :]
                    else:
                        ewin[field, n, 1, 0:8, :] = win[field, n, rows_a - 2, 8:16, :]
                        ewin[field, n, 1, 8:16, :] = shifted
        packed = joined(halo[end, 48:56, :], halo[end, 56:64, :])
        for dx in (-1, 0, 1):
            for dy in (-1, 0, 1):
                s = slot(dx, dy)
                word = word_row(packed, s)
                if dy < 0:
                    word = jnp.where((lane < TILE_Y) & west, 0, word)
                if dy > 0:
                    word = jnp.where((lane >= PTS - TILE_Y) & east, 0, word)
                pair = (word, ends_w[s, 0]) if end == 0 else (ends_w[s, 1], word)
                ewords[s, end] = jnp.where(sub < TILE_X - FROM, *pair)

    flat[...] = flat_in[...]

    @pl.loop(0, 2)
    def _(e):
        def cell(f, oy, ox):
            return ewin[f, SIDEWAYS.index(oy), e, FROM + ox : FROM + ox + 8, :]

        def keep(number, weight, level):
            eweights[number, e] = weight
            elevels[number, e] = level

        fx, fy = group_first(cell, lambda s: ewords[s, e], keep)
        at = pl.multiple_of(8 + 8 * rows_a * e, 8)
        flat[0, pl.ds(at, 8), :] = fx
        flat[1, pl.ds(at, 8), :] = fy

    corners[...] = jnp.zeros_like(corners)
    for f in range(4):

        def strip(a, dy, f=f):
            if dy == 0:
                if 0 <= a < rows_a:
                    at = 32 + 8 * (f % 2) + a
                    row = jnp.where(leftward[0:1], left[at : at + 1], right[at : at + 1])
                    if f >= 2:
                        at = 8 * (f % 2) + a
                        row = row + jnp.where(leftward[0:1], left[at : at + 1], right[at : at + 1])
                    return row
                end = 0 if a < 0 else 1
                return sides[end, 4 + f % 2] + (sides[end, f % 2] if f >= 2 else 0.0)
            b = 0 if dy > 0 else tiles - 1
            if 0 <= a < rows_a:
                row = jit[f % 2, a, b : b + 1, :]
                return row + disp[f % 2, a, b : b + 1, :] if f >= 2 else row
            end = 0 if a < 0 else 1
            at = 32 + 8 * (f % 2) + b
            row = halo[end, at : at + 1, :]
            at = 8 * (f % 2) + b
            return row + halo[end, at : at + 1, :] if f >= 2 else row

        for dy in (-1, 0, 1):
            for dx in (-1, 0, 1):
                s = slot(dx, dy)
                corners[f, s, 0:1, :] = strip(dx, dy)
                corners[f, s, 1:2, :] = strip(last + dx, dy)
                if dx == 0:
                    corners[f, s, 2:3, :] = jnp.where(topmost[0:1], strip(-1, dy), strip(rows_a, dy))
                else:
                    corners[f, s, 2:3, :] = strip(0 if dx > 0 else last, dy)
    quarters = {}
    filler = jnp.zeros((5, PTS), F32)
    for end in (0, 1):
        for values, part in ((left, 72), (right, 64)):
            low = [values[48:49], values[48 + last : 49 + last], halo[end, part + 6 : part + 7, :], filler]
            high = [values[56:57], values[56 + last : 57 + last], halo[end, part + 7 : part + 8, :], filler]
            quarters[end, part] = joined(jnp.concatenate(low, axis=0), jnp.concatenate(high, axis=0))
    for dx in (-1, 0, 1):
        for dy in (-1, 0, 1):
            s = slot(dx, dy)
            upper, lower = (
                jnp.where(
                    leftward,
                    jnp.broadcast_to(quarters[end, 72][:, s : s + 1], (8, PTS)),
                    jnp.broadcast_to(quarters[end, 64][:, s : s + 1], (8, PTS)),
                )
                for end in (0, 1)
            )
            word = jnp.where(topmost, upper, lower)
            if dx < 0:
                word = jnp.where((sub == 0) & north, 0, word)
            if dx > 0:
                word = jnp.where((sub == 1) & south, 0, word)
            kinds[s] = word

    def getter(f):
        held = {}

        def get(dx, dy):
            if (dx, dy) not in held:
                held[dx, dy] = turn(corners[f, slot(dx, dy)], TILE_Y * dy)
            return held[dx, dy]

        return get

    side_f = first_forces(getter(0), getter(1), getter(2), getter(3), lambda dx, dy: kinds[slot(dx, dy)])

    here = jnp.where(place.front, 1.0, 0.0)
    push = PENALTY * here * jnp.maximum(contact[8:18] - owners[8:18], 0.0)
    side_push = jnp.where(leftward[0:1], push[9:10], push[8:9])
    push = push[0:8]

    for f in range(2):
        ends_beside = {}
        speeds = [jnp.where(leftward[0:1], left[16 + 8 * f + a : 17 + 8 * f + a], right[16 + 8 * f + a : 17 + 8 * f + a]) for a in (0, last)]
        speeds.append(jnp.where(topmost[0:1], sides[0, 2 + f], sides[1, 2 + f]))
        for n in range(3):
            force = side_f[f][n : n + 1]
            if n == 1 and f == 0:
                force = force - side_push
            row = corners[2 + f, slot(0, 0), n : n + 1, :] + STEP_DT * (speeds[n] + STEP_DT * force)
            ends_beside[n] = side_columns(row)
        for a in range(-1, rows_a + 1):
            if a in (-1, rows_a):
                cells, near = far_lead[f, 0 if a < 0 else 1], ends_beside[2]
            else:
                cells = lead[f, a]
                near = ends_beside[0] if a == 0 else ends_beside[1] if a == last else beside[f, a]
            cells = cells + (STEP_DT * STEP_DT) * flat[f, 8 * a + 11 : 8 * a + 19, :]
            if a == last and f == 0:
                cells = cells - (STEP_DT * STEP_DT) * flip(push)
            for n, oy in enumerate(SIDEWAYS):
                shifted = sideways(cells, near, oy)
                if a < rows_a:
                    swin[f, n, a + 1, 0:8, :] = shifted
                if a >= 0:
                    swin[f, n, a, 8:16, :] = shifted

    def second_group(k, kept):
        def cell(f, oy, ox):
            return swin[f, SIDEWAYS.index(oy), k, FROM + ox : FROM + ox + 8, :]

        fx, fy = group_second(cell, kept)
        at = pl.multiple_of(8 * k + 8, 8)
        flat2[0, pl.ds(at, 8), :] = fx
        flat2[1, pl.ds(at, 8), :] = fy

    @pl.loop(0, 2)
    def _(e):
        second_group(e * rows_a, lambda number: (eweights[number, e], elevels[number, e]))

    @pl.loop(0, rows_a - 1)
    def _(k):
        second_group(k + 1, lambda number: (weights[number, k], levels[number, k]))

    for f in range(2):
        thens = flips([flat2[f, 8 * a + 11 : 8 * a + 19, :] for a in range(rows_a)])
        end_was = flips([flat[f, 8 * a + 11 : 8 * a + 19, :] for a in (0, last)])
        for a in range(rows_a):
            was = end_was[min(a, 1)] if a in (0, last) else tiles_f[f, a]
            then = thens[a]
            if f == 0 and a == last:
                was = was - push
                gap = disp[0, last] + STEP_DT * (vel[0, last] + STEP_DT * was) + inter[...]
                reached = owners[0:8] + (STEP_DT * STEP_DT) * push
                then = then - PENALTY * here * jnp.maximum(gap - reached, 0.0)
            fast = vel[f, a] + STEP_DT * was
            faster = fast + STEP_DT * then
            out_vel[f, a] = faster
            out_disp[f, a] = disp[f, a] + STEP_DT * (fast + faster)


def on_device(nx, ny, disp, vel, jit, words, node, inter, shell, speed):
    rows_a = disp.shape[1]
    rows, cols = shell.shape
    place_args = (nx, ny, rows, cols)
    shifts = tuple(range(1, nx))
    base = (disp, vel, jit, words, node, inter, shell, speed)

    def call(body, out, scratch, *args, far=0):
        args = [pltpu.with_memory_space_constraint(x, pltpu.MemorySpace.HBM) for x in args[:far]] + list(args[far:])
        specs = [pl.BlockSpec(memory_space=pltpu.MemorySpace.HBM)] * far
        specs += [pl.BlockSpec(memory_space=pltpu.VMEM)] * (len(args) - far)
        return pl.pallas_call(
            body,
            out_shape=out,
            in_specs=specs,
            scratch_shapes=scratch,
            compiler_params=pltpu.CompilerParams(vmem_limit_bytes=20 * 1024 * 1024),
        )(*args)

    side = jax.ShapeDtypeStruct((Y_ROWS, PTS), F32)
    first, second, *base = call(
        functools.partial(pack_sides, place_args),
        [side, side] + [jax.ShapeDtypeStruct(x.shape, x.dtype) for x in base],
        [pltpu.VMEM((TILE_X, 8, cols), F32), pltpu.SemaphoreType.DMA((len(base),))],
        *base,
        far=len(base),
    )
    first = lax.ppermute(first, "gy", [(i, i ^ 1) for i in range(ny)])
    second = lax.ppermute(second, "gy", [(i, ((i - 1) ^ 1) + 1) for i in range(1, ny - 1)])

    tall = pltpu.VMEM((rows + 2 * PAD, WIDE), F32)
    outs = [
        jax.ShapeDtypeStruct((CONTACT_ROWS + (HALO_ROWS if s & (s + 1) == 0 else 0), PTS), F32) for s in shifts
    ]
    outs += [jax.ShapeDtypeStruct((2 * CONTACT_ROWS, PTS), F32)]
    outs += [jax.ShapeDtypeStruct((rows, PTS), F32)] * 2
    *ends, own, strip_d, strip_v = call(
        functools.partial(pack_ends, place_args, shifts),
        outs,
        [pltpu.VMEM((4, 4 * STRIDE, PTS), F32), tall, tall, tall, pltpu.VMEM((TILE_X, 8, cols), F32)],
        *base,
        first,
        second,
    )
    ends = [lax.ppermute(e, "gx", [(i, i ^ s) for i in range(nx)]) for s, e in zip(shifts, ends)]

    span, count = rows_a - 1, len(OFFSETS)

    def shaped(*shape, dtype=F32):
        return jax.ShapeDtypeStruct(shape + (PTS,), dtype)

    inner = call(
        functools.partial(inner_rows, place_args),
        [
            shaped(4, len(SIDEWAYS), span, 16),
            shaped(count, span, 8),
            shaped(count, span, 8),
            shaped(2, 8 * (rows_a + 3)),
            shaped(2, rows_a, 8),
            shaped(2, rows_a, 8),
            shaped(2, rows_a, 8),
            shaped(9, 2, 8, dtype=I32),
        ],
        [pltpu.VMEM((4, 3, 24, PTS), F32), pltpu.VMEM((9, 8, PTS), I32), pltpu.VMEM((9, span, 8, PTS), I32)],
        *base[:4],
        first,
        second,
    )

    scratch = [
        tall,
        tall,
        tall,
        tall,
        pltpu.VMEM((3, TILE_X, 8, WIDE), F32),
        pltpu.VMEM((2, HALO_ROWS, PTS), F32),
        pltpu.VMEM((4, len(SIDEWAYS), 2, 16, PTS), F32),
        pltpu.VMEM((9, 2, 8, PTS), I32),
        pltpu.VMEM((count, 2, 8, PTS), F32),
        pltpu.VMEM((count, 2, 8, PTS), F32),
        pltpu.VMEM((2, 8 * (rows_a + 3), PTS), F32),
        pltpu.VMEM((2, 8 * (rows_a + 3), PTS), F32),
        pltpu.VMEM((4, 9, 8, PTS), F32),
        pltpu.VMEM((9, 8, PTS), I32),
        pltpu.VMEM((2, len(SIDEWAYS), rows_a + 1, 16, PTS), F32),
    ]
    out = [jax.ShapeDtypeStruct(x.shape, F32) for x in (disp, vel, shell, speed)]
    return tuple(
        call(
            functools.partial(both_steps, place_args, shifts),
            out,
            scratch,
            *base,
            first,
            second,
            own,
            strip_d,
            strip_v,
            *inner,
            *ends,
        )
    )


def solution(mesh):
    in_specs = (
        P(None, "gx", "gy", None),
        P(None, "gx", "gy", None),
        P(None, "gx", "gy", None),
        P("gx", "gy", None),
        P("gy", None),
        P("gy", None),
        P("gx", "gy"),
        P("gx", "gy"),
    )
    out_specs = (P(None, "gx", "gy", None), P(None, "gx", "gy", None), P("gx", "gy"), P("gx", "gy"))
    body = functools.partial(on_device, mesh.shape["gx"], mesh.shape["gy"])
    return jax.shard_map(body, mesh=mesh, in_specs=in_specs, out_specs=out_specs, check_vma=False)
```

```python
import functools

import jax
import jax.numpy as jnp
from jax import lax
from jax.experimental import pallas as pl
from jax.experimental.pallas import tpu as pltpu
from jax.sharding import PartitionSpec as P

TILE_X = 8
TILE_Y = 16
PTS = 128
SPLIT = 4

HORIZON = 3.5
DELTA_SQ = 0.25
PENALTY = 4.0
BEND = 0.5
STEP_DT = 0.2

F32 = jnp.float32
I32 = jnp.int32

STRIDE = 24
WIDE = 640
PAD = 16


def bond_offsets():
    limit = HORIZON * HORIZON - DELTA_SQ
    found = []
    for oy in range(-4, 5):
        for ox in range(-4, 5):
            near = max(abs(ox) - 0.4, 0.0) ** 2 + max(abs(oy) - 0.4, 0.0) ** 2
            if near < limit and (ox or oy):
                found.append((ox, oy))
    return found


OFFSETS = bond_offsets()
SIDEWAYS = sorted({oy for _, oy in OFFSETS})


def sign(value):
    return (value > 0) - (value < 0)


def lanes():
    return lax.broadcasted_iota(I32, (8, PTS), 1)


def subs():
    return lax.broadcasted_iota(I32, (8, PTS), 0)


def turn(values, shift):
    size = values.shape[1]
    return pltpu.roll(values, shift % size, 1) if shift % size else values


def slot(dx, dy):
    return 3 * (dx + 1) + dy + 1


def lane_masks():
    lane = lanes()
    row, col = lane // TILE_Y, lane % TILE_Y
    masks = {}
    for o in (1, 2, 3):
        masks["col_at", o] = col < o
        masks["col_at", -o] = col >= TILE_Y - o
        masks["col_from", o] = col >= TILE_Y - o
        masks["col_from", -o] = col < o
        masks["row_at", o] = row < o
        masks["row_at", -o] = row >= TILE_X - o
        masks["row_from", o] = row >= TILE_X - o
        masks["row_from", -o] = row < o
    bits = {}
    for ox in range(-3, 4):
        bits[ox] = jnp.left_shift(jnp.int32(1), 4 * row + ((row + ox) & 7) // 2)
    return masks, bits


def moved(get, oy, masks):
    out = {}
    for dx in (-1, 0, 1):
        held = get(dx, 0)
        if oy:
            held = turn(jnp.where(masks["col_at", oy], get(dx, sign(oy)), held), -oy)
        out[dx] = held
    return out


def across(cells, ox, masks):
    if not ox:
        return cells[0]
    return turn(jnp.where(masks["row_at", ox], cells[sign(ox)], cells[0]), -TILE_Y * ox)


def first_forces(get_jx, get_jy, get_dx, get_dy, get_words, keep=None, both=True):
    masks, bits = lane_masks()
    jx0, jy0, dx0, dy0 = get_jx(0, 0), get_jy(0, 0), get_dx(0, 0), get_dy(0, 0)
    fx = jnp.zeros((8, PTS), F32)
    fy = jnp.zeros((8, PTS), F32)
    for oy in SIDEWAYS:
        jxs, jys = moved(get_jx, oy, masks), moved(get_jy, oy, masks)
        dxs, dys = moved(get_dx, oy, masks), moved(get_dy, oy, masks)
        words = {}
        for dx in (-1, 0, 1):
            words[dx] = get_words(dx, 0)
            if oy:
                words[dx] = jnp.where(masks["col_from", oy], get_words(dx, sign(oy)), words[dx])
        for number, (ox, other) in enumerate(OFFSETS):
            if other != oy:
                continue
            word = words[0]
            if ox:
                word = jnp.where(masks["row_from", ox], words[sign(ox)], word)
            intact = (word & bits[ox]) != 0
            rest_x = across(jxs, ox, masks) - (jx0 - float(ox))
            rest_y = across(jys, ox, masks) - (jy0 - float(oy))
            now_x = across(dxs, ox, masks) - (dx0 - float(ox))
            now_y = across(dys, ox, masks) - (dy0 - float(oy))
            rest_sq = rest_x * rest_x + rest_y * rest_y + DELTA_SQ
            now_sq = now_x * now_x + now_y * now_y + DELTA_SQ
            rest_inv = lax.rsqrt(rest_sq)
            reach = jnp.maximum(1.0 - rest_sq * rest_inv * (1.0 / HORIZON), 0.0)
            weight = jnp.where(intact, reach * reach, 0.0)
            level = weight * rest_inv
            if keep is not None:
                keep(number, weight, level)
            factor = level - weight * lax.rsqrt(now_sq)
            fx = fx + factor * now_x
            if both:
                fy = fy + factor * now_y
    return fx, fy


def pick_lanes(block, index):
    return jnp.take_along_axis(block, index, axis=1, mode="promise_in_bounds")


def flips(blocks):
    lane, sub = lanes(), subs()
    for level in (2, 1, 0):
        step = 1 << level
        stay = ((lane >> (level + 4)) ^ (sub >> level)) & 1 == 0
        if step == 4:
            others = [turn(pltpu.roll(block, 4, 0), 64) for block in blocks]
        else:
            low = (sub >> level) & 1 == 0
            index = lane ^ (TILE_Y * step)
            others = [jnp.where(low, pltpu.roll(block, 8 - step, 0), pltpu.roll(block, step, 0)) for block in blocks]
            others = [pick_lanes(block, index) for block in others]
        blocks = [jnp.where(stay, block, other) for block, other in zip(blocks, others)]
    return blocks


def flip(block):
    return flips([block])[0]


def side_columns(row):
    return pick_lanes(jnp.broadcast_to(row, (8, PTS)), TILE_Y * subs() + (lanes() & (TILE_Y - 1)))


def word_row(packed, s):
    word = jnp.where(subs() == lanes() // TILE_Y, jnp.broadcast_to(packed[:, s : s + 1], (8, PTS)), 0)
    for step in (4, 2, 1):
        word = word | pltpu.roll(word, step, 0)
    return word


def sideways(cells, beside, oy):
    if not oy:
        return cells
    lane = lanes()
    mask = lane < oy if oy > 0 else lane >= PTS + oy
    return turn(jnp.where(mask, beside, cells), -oy)


FROM = 5


def group_masks(start):
    lane, sub = lanes(), subs()
    row = (sub + start) & (TILE_X - 1)
    col = lane & (TILE_Y - 1)
    masks, bits = {}, {}
    for o in (1, 2, 3):
        masks["col", o] = col >= TILE_Y - o
        masks["col", -o] = col < o
        masks["row", o] = row >= TILE_X - o
        masks["row", -o] = row < o
    for ox in range(-3, 4):
        bits[ox] = jnp.left_shift(jnp.int32(1), 4 * row + ((row + ox) & 7) // 2)
    return masks, bits


def group_first(cell, word, keep, start=FROM):
    masks, bits = group_masks(start)
    zero = [cell(f, 0, 0) for f in range(4)]
    fx = jnp.zeros((8, PTS), F32)
    fy = jnp.zeros((8, PTS), F32)
    plain = [word(slot(dx, 0)) for dx in (-1, 0, 1)]
    for oy in SIDEWAYS:
        words = plain
        if oy:
            words = [jnp.where(masks["col", oy], word(slot(dx, sign(oy))), plain[dx + 1]) for dx in (-1, 0, 1)]
        base_y, base_v = zero[1] - float(oy), zero[3] - float(oy)
        for number, (ox, other) in enumerate(OFFSETS):
            if other != oy:
                continue
            picked = words[1]
            if ox:
                picked = jnp.where(masks["row", ox], words[sign(ox) + 1], picked)
            intact = (picked & bits[ox]) != 0
            rest_x = cell(0, oy, ox) - (zero[0] - float(ox))
            rest_y = cell(1, oy, ox) - base_y
            now_x = cell(2, oy, ox) - (zero[2] - float(ox))
            now_y = cell(3, oy, ox) - base_v
            rest_sq = rest_x * rest_x + rest_y * rest_y + DELTA_SQ
            now_sq = now_x * now_x + now_y * now_y + DELTA_SQ
            rest_inv = lax.rsqrt(rest_sq)
            reach = jnp.maximum(1.0 - rest_sq * rest_inv * (1.0 / HORIZON), 0.0)
            weight = jnp.where(intact, reach * reach, 0.0)
            level = weight * rest_inv
            keep(number, weight, level)
            factor = level - weight * lax.rsqrt(now_sq)
            fx = fx + factor * now_x
            fy = fy + factor * now_y
    return fx, fy


def group_second(cell, kept):
    zero = [cell(f, 0, 0) for f in range(2)]
    fx = jnp.zeros((8, PTS), F32)
    fy = jnp.zeros((8, PTS), F32)
    for number, (ox, oy) in enumerate(OFFSETS):
        now_x = cell(0, oy, ox) - (zero[0] - float(ox))
        now_y = cell(1, oy, ox) - (zero[1] - float(oy))
        now_sq = now_x * now_x + now_y * now_y + DELTA_SQ
        weight, level = kept(number)
        factor = level - weight * lax.rsqrt(now_sq)
        fx = fx + factor * now_x
        fy = fy + factor * now_y
    return fx, fy


def bending_of(row):
    here = row(0)
    one, two = row(-1) + row(1), row(-2) + row(2)
    beside = 2.0 * one - 8.0 * here
    out = two - 8.0 * one + 20.0 * here
    return out + turn(beside + turn(here, 1), 1) + turn(beside + turn(here, -1), -1)


def joined(low_part, high_part):
    return jnp.left_shift(high_part.astype(I32), 16) | low_part.astype(I32)


def widen(row_of, count):
    lane, sub = lanes(), subs()
    index = sub * TILE_Y + (lane % 64) // SPLIT
    out = []
    for j in range(count):
        left, right = (
            pick_lanes(jnp.broadcast_to(row_of(b), (8, PTS)), index) for b in (2 * j, 2 * j + 1)
        )
        out.append(jnp.where(lane < 64, left, right))
    return out


def narrow(block_of, tiles):
    lane, sub = lanes(), subs()
    out = []
    for b in tiles:
        held = block_of(b // 2)
        held = held + turn(held, -1)
        held = held + turn(held, -2)
        picked = pick_lanes(held, 64 * (b % 2) + SPLIT * (lane % TILE_Y))
        out.append(jnp.sum(jnp.where(sub == lane // TILE_Y, picked, 0.0), axis=0, keepdims=True))
    return out


def lay_out(ref, at, j, block):
    for row in range(TILE_X):
        ref[at + (row, slice(None), slice(j * PTS, (j + 1) * PTS))] = jnp.broadcast_to(block[row : row + 1], (8, PTS))


class Place:
    def __init__(self, nx, ny, shell_rows, shell_cols):
        self.nx, self.ny = nx, ny
        self.gx, self.gy = lax.axis_index("gx"), lax.axis_index("gy")
        self.shell_rows, self.shell_cols = shell_rows, shell_cols
        self.width = shell_cols * ny
        self.band = shell_rows * nx // TILE_X
        self.bands = shell_rows // self.band
        self.front = self.gx == nx - 1

    def sides(self, first, second):
        even = self.gy % 2 == 0
        right = jnp.where(even, first, second)
        left = jnp.where(even, second, first)
        right = jnp.where(self.gy < self.ny - 1, right, 0.0)
        left = jnp.where(self.gy > 0, left, 0.0)
        return right, left

    def nodes(self, row, columns):
        shape = (8, columns)
        col = lax.broadcasted_iota(I32, shape, 1)
        if columns > self.shell_cols:
            col = jnp.where(col >= self.shell_cols + 64, col - columns, col)
        first = (self.gx * self.shell_rows + row) * self.width + self.gy * self.shell_cols
        return (first + lax.broadcasted_iota(I32, shape, 0) * self.width + col).astype(F32)

    def parts(self):
        inner = [list(range(p * self.band, (p + 1) * self.band, 8)) for p in range(self.bands)]
        return [[-8]] + inner + [[self.shell_rows]]

    def band_of(self, row):
        return jnp.clip((self.gx * self.shell_rows + row + self.band) // self.band - 1, 0, TILE_X - 1)


Y_ROWS = 88


def fetch(pairs, sems):
    copies = [pltpu.make_async_copy(source, target, sems.at[n]) for n, (source, target) in enumerate(pairs)]
    for copy in copies:
        copy.start()
    for copy in copies:
        copy.wait()


def pack_sides(place_args, *refs):
    sources, (first, second), held = refs[:8], refs[8:10], refs[10:16]
    shell, speed, wide_ref, sems = refs[16:]
    place = Place(*place_args)
    pairs = list(zip(sources[:6], held))
    for source, target in zip(sources[6:], (shell, speed)):
        for n, at in enumerate((0, place.shell_cols - PTS)):
            pairs.append((source.at[:, pl.ds(at, PTS)], target.at[n]))
    fetch(pairs, sems)
    disp, vel, jit, words, node, inter = held
    tiles = disp.shape[2]
    even = place.gy % 2 == 0
    blocks = place.shell_cols // PTS
    numbers = node[...].astype(F32)
    edge_blocks = (0, blocks - 1)
    for j in edge_blocks:
        lay_out(wide_ref, (), j, widen(lambda b: numbers[b : b + 1], blocks)[j])
    held = {}
    for j in edge_blocks:
        total = jnp.zeros((8, PTS), F32)
        for part in range(place.bands):
            summed = jnp.zeros((8, PTS), F32)
            for row in range(part * place.band, (part + 1) * place.band, 8):
                wanted = wide_ref[place.band_of(row), :, j * PTS : (j + 1) * PTS]
                ids = place.nodes(row, PTS) + float(j * PTS)
                summed = summed + jnp.where(wanted == ids, shell[min(j, 1), row : row + 8, :], 0.0)
            summed = jnp.sum(summed, axis=0, keepdims=True)
            total = total + jnp.where(subs() == place.band_of(part * place.band), summed, 0.0)
        held[j] = total
    met = narrow(lambda j: held[j], (0, tiles - 1))

    ends = [(jnp.transpose(x[1])[PTS - 8 :], jnp.transpose(x[0])[:8]) for x in (shell, speed)]

    def send(ref, to_right):
        edge = jnp.where(to_right, tiles - 1, 0)
        for f, source in enumerate((disp, disp, vel, vel, jit, jit)):
            ref[8 * f : 8 * f + 8, :] = jnp.where(
                to_right, source[f % 2, :, tiles - 1, :], source[f % 2, :, 0, :]
            )
        ref[48:Y_ROWS, :] = jnp.zeros((Y_ROWS - 48, PTS), F32)
        edge_words = jnp.where(to_right, words[:, tiles - 1, :], words[:, 0, :])
        ref[48:56, 0:9] = (edge_words & 65535).astype(F32)
        ref[56:64, 0:9] = jnp.right_shift(edge_words, 16).astype(F32)
        ref[64:65, :] = jnp.where(to_right, numbers[tiles - 1 : tiles], numbers[0:1])
        ref[65:66, :] = jnp.where(to_right, inter[tiles - 1 : tiles, :], inter[0:1, :])
        ref[66:67, :] = jnp.where(to_right, met[1], met[0])
        for f, source in enumerate((shell, speed)):
            ref[72 + 8 * f : 80 + 8 * f, :] = jnp.where(to_right, *ends[f])

    send(first, even)
    send(second, jnp.logical_not(even))


def own_parts(place_args, far_shell, far_speed, disp, vel, jit, words, node, *refs):
    place = Place(*place_args)
    shell, speed, lattice, lead, groups_w, ends_w, shore, tall, tall_v, wide_ref, sems = refs
    rows_a, tiles = disp.shape[1], disp.shape[2]
    rows, cols = place.shell_rows, place.shell_cols
    lane, sub = lanes(), subs()
    west, east = place.gy == 0, place.gy == place.ny - 1
    north, south = place.gx == 0, place.gx == place.nx - 1
    span = pl.ds(PAD, rows)
    copies = [
        pltpu.make_async_copy(source, target, sems.at[n])
        for n, (source, target) in enumerate(
            (
                (far_shell, shell),
                (far_speed, speed),
                (far_shell, tall.at[span, pl.ds(0, cols)]),
                (far_speed, tall_v.at[span, pl.ds(0, cols)]),
            )
        )
    ]
    for copy in copies:
        copy.start()
    for ref in (tall, tall_v):
        ref[0:PAD, :] = jnp.zeros((PAD, WIDE), F32)
        ref[PAD + rows :, :] = jnp.zeros((PAD, WIDE), F32)
        ref[PAD : PAD + rows, cols:WIDE] = jnp.zeros((rows, PTS), F32)

    for f in range(2):
        rest = [jit[f, a] for a in range(rows_a)]
        whole = [jit[f, a] + disp[f, a] for a in range(rows_a)]
        soon = [x + STEP_DT * vel[f, a] for a, x in enumerate(whole)]
        for a, (x, y, z) in enumerate(zip(flips(rest), flips(whole), flips(soon))):
            lattice[f, a] = x
            lattice[2 + f, a] = y
            lead[f, a] = z

    before = [None] * 9
    for a in range(rows_a):
        packed = words[a]
        for dx in (-1, 0, 1):
            for dy in (-1, 0, 1):
                s = slot(dx, dy)
                word = word_row(packed, s)
                if dy < 0:
                    word = jnp.where((lane < TILE_Y) & west, 0, word)
                if dy > 0:
                    word = jnp.where((lane >= PTS - TILE_Y) & east, 0, word)
                if dx < 0 and a == 0:
                    word = jnp.where(north, 0, word)
                if dx > 0 and a == rows_a - 1:
                    word = jnp.where(south, 0, word)
                if a:
                    groups_w[s, a - 1] = jnp.where(sub < TILE_X - FROM, before[s], word)
                if a in (0, rows_a - 1):
                    ends_w[s, min(a, 1)] = word
                before[s] = word

    numbers = node[...].astype(F32)
    for j, block in enumerate(widen(lambda b: numbers[b : b + 1], cols // PTS)):
        lay_out(wide_ref, (), j, block)
    for copy in copies:
        copy.wait()
    sub_wide = lax.broadcasted_iota(I32, (8, cols), 0)
    ahead = jnp.zeros((8, cols), F32)
    met = jnp.zeros((8, cols), F32)
    for part in place.parts():
        soon = jnp.zeros((8, cols), F32)
        now = jnp.zeros((8, cols), F32)
        band = place.band_of(part[0])
        for row in part:
            at = PAD + row
            hit = wide_ref[band] == place.nodes(row, cols)
            bending = bending_of(lambda o: tall[at + o : at + o + 8, :])[:, 0:cols]
            here = tall[at : at + 8, 0:cols]
            later = here + STEP_DT * (tall_v[at : at + 8, 0:cols] - (STEP_DT * BEND) * bending)
            soon = soon + jnp.where(hit, later, 0.0)
            if 0 <= row < rows:
                now = now + jnp.where(hit, here, 0.0)
        ahead = ahead + jnp.where(sub_wide == band, jnp.sum(soon, axis=0, keepdims=True), 0.0)
        if 0 <= part[0] < rows:
            met = met + jnp.where(sub_wide == band, jnp.sum(now, axis=0, keepdims=True), 0.0)
    for base, values in ((0, ahead), (tiles, met)):
        for b, row in enumerate(narrow(lambda j: values[:, j * PTS : (j + 1) * PTS], range(tiles))):
            shore[base + b : base + b + 1, :] = row


HALO_ROWS = 120
CONTACT_ROWS = 24


def shell_strip(right, left, at):
    middle = jnp.zeros((PTS - 16, PTS), F32)
    return jnp.transpose(jnp.concatenate([right[at : at + 8], middle, left[at : at + 8]], axis=0))


def pack_ends(
    place_args, shifts, disp, vel, jit, words, node, inter, shell, speed, lattice, ends_w, shore, first, second, *refs
):
    place = Place(*place_args)
    outs = refs[: len(shifts)]
    own, strip_d, strip_v, grid, tall, wide_ref = refs[len(shifts) :]
    rows_a, tiles = disp.shape[1], disp.shape[2]
    rows, cols = place.shell_rows, place.shell_cols
    right, left = place.sides(first[...], second[...])
    lane, sub = lanes(), subs()
    leftward = (lane[0:1] & (TILE_Y - 1)) >= TILE_Y // 2
    last = rows_a - 1

    for f in range(4):
        for level, a in enumerate((last - 1, last)):
            at = 32 + 8 * (f % 2) + a
            row = jnp.where(leftward, left[at : at + 1], right[at : at + 1])
            if f >= 2:
                at = 8 * (f % 2) + a
                row = row + jnp.where(leftward, left[at : at + 1], right[at : at + 1])
            near = side_columns(row)
            for n, oy in enumerate(SIDEWAYS):
                grid[f, n, 8 * level : 8 * level + 8, :] = sideways(lattice[f, a], near, oy)
        for n in range(len(SIDEWAYS)):
            grid[f, n, 16:24, :] = jnp.zeros((8, PTS), F32)
    force, _ = group_first(
        lambda f, oy, ox: grid[f, SIDEWAYS.index(oy), 8 + ox : 16 + ox, :],
        lambda s: ends_w[s, 1] if s < 6 else jnp.zeros((8, PTS), I32),
        lambda number, weight, level: None,
        start=0,
    )
    gap = disp[0, last] + inter[...]
    own[0:8, :] = gap + STEP_DT * (vel[0, last] + STEP_DT * flip(force))
    own[8:16, :] = gap
    own[16:24, :] = jnp.zeros((8, PTS), F32)
    own[16:17, :] = right[last : last + 1] + right[65:66]
    own[17:18, :] = left[last : last + 1] + left[65:66]

    halo_d = shell_strip(right, left, 72)
    halo_v = shell_strip(right, left, 80)
    strip_d[...] = halo_d
    strip_v[...] = halo_v
    for at in (0, 8, PAD + rows, PAD + rows + 8):
        tall[at : at + 8, :] = jnp.zeros((8, PTS), F32)
    tall[PAD : PAD + rows, :] = halo_d
    numbers = node[...].astype(F32)
    blocks = widen(lambda b: numbers[b : b + 1], cols // PTS)
    low = lane < PTS // 2
    lay_out(wide_ref, (), 0, jnp.where(low, blocks[0], blocks[-1]))
    far = jnp.where(low, 0.0, float(cols - PTS))
    ahead = jnp.zeros((8, PTS), F32)
    for part in place.parts():
        soon = jnp.zeros((8, PTS), F32)
        band = place.band_of(part[0])
        for row in part:
            at = PAD + row
            here = tall[at : at + 8, :]
            column = 2.0 * (tall[at - 1 : at + 7, :] + tall[at + 1 : at + 9, :]) - 8.0 * here
            from_left = turn(jnp.where(low, 0.0, column), 1) + turn(jnp.where(low, 0.0, here), 2)
            from_right = turn(jnp.where(low, column, 0.0), -1) + turn(jnp.where(low, here, 0.0), -2)
            hit = wide_ref[band] == place.nodes(row, PTS) + far
            soon = soon + jnp.where(hit, jnp.where(low, from_left, from_right), 0.0)
        ahead = ahead + jnp.where(sub == band, jnp.sum(soon, axis=0, keepdims=True), 0.0)
    base = CONTACT_ROWS
    own[base + 16 : base + 24, :] = jnp.zeros((8, PTS), F32)
    own[base : base + 16, :] = shore[...]
    for b, row in zip((0, tiles - 1), narrow(lambda j: ahead, (0, tiles - 1))):
        own[base + b : base + b + 1, :] = shore[b : b + 1, :] - (STEP_DT * STEP_DT * BEND) * row
    own[base + 16 : base + 17, :] = right[66:67]
    own[base + 17 : base + 18, :] = left[66:67]

    mine = jnp.where(place.front, own[0:CONTACT_ROWS, :], own[base : base + CONTACT_ROWS, :])
    for shift, out in zip(shifts, outs):
        at = 0
        if shift & (shift + 1) == 0:
            at = HALO_ROWS
            down = (place.gx ^ shift) > place.gx
            edge = jnp.where(down, rows_a - 1, 0)
            for f, source in enumerate((disp, disp, vel, vel, jit, jit)):
                out[8 * f : 8 * f + 8, :] = source[f % 2, edge]
            out[48:80, :] = jnp.zeros((32, PTS), F32)
            edge_words = words[edge]
            out[48:56, 0:9] = (edge_words & 65535).astype(F32)
            out[56:64, 0:9] = jnp.right_shift(edge_words, 16).astype(F32)
            for f in range(8):
                for side, values in ((64, right), (72, left)):
                    low, high = values[8 * f : 8 * f + 1], values[8 * f + rows_a - 1 : 8 * f + rows_a]
                    out[side + f : side + f + 1, :] = jnp.where(down, high, low)
            for j in range(WIDE // PTS):
                cut = slice(j * PTS, (j + 1) * PTS)
                if j < cols // PTS:
                    d_low, d_high = shell[0:4, cut], shell[rows - 4 : rows, cut]
                    v_low, v_high = speed[0:2, cut], speed[rows - 2 : rows, cut]
                else:
                    d_low, d_high = halo_d[0:4], halo_d[rows - 4 : rows]
                    v_low, v_high = halo_v[0:2], halo_v[rows - 2 : rows]
                out[80 + 8 * j : 84 + 8 * j, :] = jnp.where(down, d_high, d_low)
                out[84 + 8 * j : 86 + 8 * j, :] = jnp.where(down, v_high, v_low)
                out[86 + 8 * j : 88 + 8 * j, :] = jnp.zeros((2, PTS), F32)
        out[at : at + CONTACT_ROWS, :] = mine


def inner_rows(place_args, disp, jit, shell, speed, lattice, groups_w, first, second, strip_d, strip_v, *refs):
    place = Place(*place_args)
    win, weights, levels, flat, beside, tiles_f, mid, strips, kinds, panes = refs
    cols = place.shell_cols
    rows_a, tiles = disp.shape[1], disp.shape[2]
    right, left = place.sides(first[...], second[...])
    lane = lanes()
    leftward = (lane & (TILE_Y - 1)) >= TILE_Y // 2
    side = [jnp.where(leftward, left[8 * f : 8 * f + 8], right[8 * f : 8 * f + 8]) for f in range(6)]

    strips[...] = jnp.zeros_like(strips)
    for f in range(4):
        rest = jit[f % 2]
        whole = rest if f < 2 else rest + disp[f % 2]
        beyond = side[4 + f % 2] if f < 2 else side[4 + f % 2] + side[f % 2]
        strips[f, 0, 8:16, :] = beyond
        strips[f, 1, 8:16, :] = whole[:, 0, :]
        strips[f, 2, 8:16, :] = whole[:, tiles - 1, :]
        nears = [side_columns(beyond[a : a + 1]) for a in range(rows_a)]
        for a, near in enumerate(nears):
            cells = lattice[f, a]
            for n, oy in enumerate(SIDEWAYS):
                shifted = sideways(cells, near, oy)
                if a < rows_a - 1:
                    win[f, n, a, 0:8, :] = shifted
                if a > 0:
                    win[f, n, a - 1, 8:16, :] = shifted
    left_words = joined(left[48:56], left[56:64])
    right_words = joined(right[48:56], right[56:64])
    for s in range(9):
        kinds[s] = jnp.where(
            leftward,
            jnp.broadcast_to(left_words[:, s : s + 1], (8, PTS)),
            jnp.broadcast_to(right_words[:, s : s + 1], (8, PTS)),
        )

    flat[...] = jnp.zeros_like(flat)

    blocks = mid.shape[0]
    for n in range(blocks):
        panes[n, :, 0:cols] = shell[8 * n : 8 * n + 24, :]
        panes[n, :, cols:WIDE] = strip_d[8 * n : 8 * n + 24, :]
    each = -(-blocks // (rows_a - 1))

    def bend_block(n):
        at = pl.multiple_of(8 * n + 8, 8)
        bending = bending_of(lambda o: panes[n, 8 + o : 16 + o, :])
        mid[n, :, 0:cols] = speed[pl.ds(at, 8), :] - (STEP_DT * BEND) * bending[:, 0:cols]
        mid[n, :, cols:WIDE] = strip_v[pl.ds(at, 8), :] - (STEP_DT * BEND) * bending[:, cols:WIDE]

    @pl.loop(0, rows_a - 1)
    def _(k):
        for part in range(each):
            bend_block(jnp.minimum(each * k + part, blocks - 1))

        def cell(f, oy, ox):
            return win[f, SIDEWAYS.index(oy), k, FROM + ox : FROM + ox + 8, :]

        def keep(number, weight, level):
            weights[number, k] = weight
            levels[number, k] = level

        fx, fy = group_first(cell, lambda s: groups_w[s, k], keep)
        at = pl.multiple_of(8 * k + 16, 8)
        flat[0, pl.ds(at, 8), :] = fx
        flat[1, pl.ds(at, 8), :] = fy

    def getter(f):
        held = {}

        def get(dx, dy):
            if (dx, dy) not in held:
                held[dx, dy] = turn(strips[f, dy % 3, 8 + dx : 16 + dx, :], TILE_Y * dy)
            return held[dx, dy]

        return get

    forces = first_forces(getter(0), getter(1), getter(2), getter(3), lambda dx, dy: kinds[slot(dx, dy)])
    for f in range(2):
        moved_side = side[4 + f] + side[f] + STEP_DT * (side[2 + f] + STEP_DT * forces[f])
        for a in range(rows_a):
            beside[f, a] = side_columns(moved_side[a : a + 1])
        for a, cells in enumerate(flips([flat[f, 8 * a + 11 : 8 * a + 19, :] for a in range(1, rows_a - 1)])):
            tiles_f[f, a + 1] = cells
        tiles_f[f, 0] = jnp.zeros((8, PTS), F32)
        tiles_f[f, rows_a - 1] = jnp.zeros((8, PTS), F32)


def both_steps(place_args, shifts, *refs):
    place = Place(*place_args)
    disp, vel, node, inter, shell, speed, first, second, own, strip_d, strip_v = refs[:11]
    lead, ends_w, win, weights, levels, flat_in, beside, tiles_f, mid = refs[11:20]
    ends = refs[20 : 20 + len(shifts)]
    targets = refs[20 + len(shifts) : 24 + len(shifts)]
    scratch = refs[24 + len(shifts) :]
    out_disp, out_vel, out_shell, out_speed, gaps, halo, rim, rim_v, panes, fasts, pushed, ewin, ewords = scratch[:13]
    eweights, elevels, flat, flat2, seams, kinds, swin, sems = scratch[13:]
    outs = (out_disp, out_vel, out_shell, out_speed)
    copies = [pltpu.make_async_copy(x, y, sems.at[n]) for n, (x, y) in enumerate(zip(outs, targets))]
    rows_a, tiles = disp.shape[1], disp.shape[2]
    rows, cols = place.shell_rows, place.shell_cols
    blocks = rows // 8
    right, left = place.sides(first[...], second[...])

    halo[...] = jnp.zeros_like(halo)
    contact = jnp.where(place.front, own[0:CONTACT_ROWS, :], 0.0)
    owners = own[CONTACT_ROWS:, :]
    for shift, ref in zip(shifts, ends):
        partner = place.gx ^ shift
        at = 0
        if shift & (shift + 1) == 0:
            at = HALO_ROWS

            @pl.when(partner == place.gx - 1)
            def _():
                halo[0] = ref[0:HALO_ROWS, :]

            @pl.when(partner == place.gx + 1)
            def _():
                halo[1] = ref[0:HALO_ROWS, :]

        got = ref[at : at + CONTACT_ROWS, :]
        contact = jnp.where(partner == place.nx - 1, got, contact)
        owners = owners + got

    def wide(source, strip, row, count):
        return jnp.concatenate([source[row : row + count, :], strip[row : row + count, :]], axis=1)

    zeros = jnp.zeros((8, WIDE), F32)
    rim[0, 16:32, :] = wide(shell, strip_d, 0, 16)
    rim[1, 0:16, :] = wide(shell, strip_d, rows - 16, 16)
    rim_v[0, 8:16, :] = wide(speed, strip_v, 0, 8)
    rim_v[1, 0:8, :] = wide(speed, strip_v, rows - 8, 8)
    for ref, at in ((rim, (0, 0)), (rim, (0, 8)), (rim, (1, 16)), (rim, (1, 24)), (rim_v, (0, 0)), (rim_v, (1, 8))):
        ref[at[0], at[1] : at[1] + 8, :] = zeros
    for j in range(WIDE // PTS):
        cut = slice(j * PTS, (j + 1) * PTS)
        rim[0, 12:16, cut] = halo[0, 80 + 8 * j : 84 + 8 * j, :]
        rim_v[0, 6:8, cut] = halo[0, 84 + 8 * j : 86 + 8 * j, :]
        rim[1, 16:20, cut] = halo[1, 80 + 8 * j : 84 + 8 * j, :]
        rim_v[1, 8:10, cut] = halo[1, 84 + 8 * j : 86 + 8 * j, :]
    numbers = node[...].astype(F32)
    node_rows = [numbers[b : b + 1] for b in range(tiles)] + [right[64:65], left[64:65]]
    gap_rows = [contact[8 + b : 9 + b] for b in range(tiles)] + [contact[16:17], contact[17:18]]
    soon_rows = [contact[b : b + 1] for b in range(tiles)]
    for j, (nodes, gap) in enumerate(zip(widen(node_rows.__getitem__, 5), widen(gap_rows.__getitem__, 5))):
        lay_out(gaps, (0,), j, nodes)
        lay_out(gaps, (1,), j, gap)
    for j, soon in enumerate(widen(soon_rows.__getitem__, 4)):
        lay_out(gaps, (2,), j, soon)
    col = lax.broadcasted_iota(I32, (8, WIDE), 1)
    inside = jnp.where(col < cols, 1.0, 0.0)
    inside = jnp.where((col >= cols) & (col < cols + 64) & (place.gy < place.ny - 1), 1.0, inside)
    inside = jnp.where((col >= cols + 64) & (place.gy > 0), 1.0, inside)
    for n in range(-1, blocks + 1):
        row = 8 * n
        if 0 < n < blocks - 1:
            here, steady = wide(shell, strip_d, row, 8), mid[n - 1]
        else:
            end = 0 if n < 1 else 1
            at = row + 16 if end == 0 else row - rows + 16
            here = rim[end, at : at + 8, :]
            bending = bending_of(lambda o: rim[end, at + o : at + o + 8, :])
            steady = rim_v[end, at - 8 : at, :] - (STEP_DT * BEND) * bending
        band = place.band_of(row)
        hit = gaps[0, band] == place.nodes(row, WIDE)
        push = jnp.where(hit, PENALTY * jnp.maximum(gaps[1, band] - here, 0.0), 0.0)
        fast = steady + STEP_DT * push
        keep = inside
        if n < 0:
            keep = inside * jnp.where(place.gx > 0, 1.0, 0.0)
        elif n == blocks:
            keep = inside * jnp.where(place.gx < place.nx - 1, 1.0, 0.0)
        there = (here + STEP_DT * fast) * keep
        for part in (-1, 0, 1):
            if 0 <= n - part < blocks:
                panes[n - part, 8 + 8 * part : 16 + 8 * part, :] = there
        if 0 <= n < blocks:
            fasts[n] = fast[:, 0:cols]
            pushed[n] = push[:, 0:cols]

    lane, sub = lanes(), subs()
    west, east = place.gy == 0, place.gy == place.ny - 1
    north, south = place.gx == 0, place.gx == place.nx - 1
    leftward = (lane & (TILE_Y - 1)) >= TILE_Y // 2
    last = rows_a - 1
    high = lane >= PTS // 2
    segment = ((lane + 16) >> 5) & 3

    def side_row(end, part):
        return jnp.where(leftward[0:1], halo[end, 72 + part : 73 + part, :], halo[end, 64 + part : 65 + part, :])

    def near_row(a, part):
        at = 8 * part + a
        return jnp.where(leftward[0:1], left[at : at + 1], right[at : at + 1])

    border = (-1, 0, last, rows_a)
    sides = {}
    for part in range(6):
        for a in border:
            sides[a, part] = near_row(a, part) if 0 <= a <= last else side_row(0 if a < 0 else 1, part)
    lead_side, far_lead = {}, {}
    straight = SIDEWAYS.index(0)
    turned = flips(
        [
            piece
            for end in (0, 1)
            for f in range(2)
            for rest in (halo[end, 32 + 8 * f : 40 + 8 * f, :],)
            for whole in (rest + halo[end, 8 * f : 8 * f + 8, :],)
            for piece in (rest, whole, whole + STEP_DT * halo[end, 16 + 8 * f : 24 + 8 * f, :])
        ]
    )
    for f in range(2):
        for a in border:
            lead_side[f, a] = side_columns(sides[a, 4 + f] + sides[a, f] + STEP_DT * sides[a, 2 + f])
        for end in (0, 1):
            far_lead[f, end] = turned[6 * end + 3 * f + 2]
        for field in (f, 2 + f):
            cells, near = {}, {}
            for a in border:
                near[a] = side_columns(sides[a, 4 + f] + sides[a, f] if field >= 2 else sides[a, 4 + f])
            cells[-1], cells[rows_a] = (turned[6 * end + 3 * f + field // 2] for end in (0, 1))
            cells[0] = win[field, straight, 0, 0:8, :]
            cells[last] = win[field, straight, rows_a - 2, 8:16, :]
            for n, oy in enumerate(SIDEWAYS):
                ewin[field, n, 0, 0:8, :] = sideways(cells[-1], near[-1], oy)
                ewin[field, n, 0, 8:16, :] = win[field, n, 0, 0:8, :]
                ewin[field, n, 1, 0:8, :] = win[field, n, rows_a - 2, 8:16, :]
                ewin[field, n, 1, 8:16, :] = sideways(cells[rows_a], near[rows_a], oy)
            for half, (up, down) in enumerate(((-1, last), (0, rows_a))):
                pieces = [
                    jnp.where(high, near[up], cells[up]),
                    turn(jnp.where(high, cells[up], near[up]), 32),
                    turn(jnp.where(high, near[down], cells[down]), 64),
                    turn(jnp.where(high, cells[down], near[down]), 96),
                ]
                seam = pieces[3]
                for q in (2, 1, 0):
                    seam = jnp.where(segment == q, pieces[q], seam)
                for n, oy in enumerate(SIDEWAYS):
                    seams[field, n, 8 * half : 8 * half + 8, :] = turn(seam, -oy)
    for end in (0, 1):
        packed = joined(halo[end, 48:56, :], halo[end, 56:64, :])
        for dx in (-1, 0, 1):
            for dy in (-1, 0, 1):
                s = slot(dx, dy)
                word = word_row(packed, s)
                if dy < 0:
                    word = jnp.where((lane < TILE_Y) & west, 0, word)
                if dy > 0:
                    word = jnp.where((lane >= PTS - TILE_Y) & east, 0, word)
                pair = (word, ends_w[s, 0]) if end == 0 else (ends_w[s, 1], word)
                ewords[s, end] = jnp.where(sub < TILE_X - FROM, *pair)
    parts = []
    for at in (0, 1):
        rows_w = []
        for a in (-1, last, 0, rows_a):
            for values, part in ((left, 72), (right, 64)):
                if 0 <= a <= last:
                    rows_w.append(values[48 + 8 * at + a : 49 + 8 * at + a])
                else:
                    end = 0 if a < 0 else 1
                    rows_w.append(halo[end, part + 6 + at : part + 7 + at, :])
        parts.append(jnp.concatenate(rows_w, axis=0))
    packed = joined(*parts)
    for dx in (-1, 0, 1):
        for dy in (-1, 0, 1):
            s = slot(dx, dy)
            word = jnp.broadcast_to(packed[:, s : s + 1], (8, PTS))
            upper, lower = jnp.where(sub == segment, word, 0), jnp.where(sub == segment + 4, word, 0)
            for step in (4, 2, 1):
                upper, lower = upper | pltpu.roll(upper, step, 0), lower | pltpu.roll(lower, step, 0)
            if dx < 0:
                lower = jnp.where((segment < 2) & north, 0, lower)
            if dx > 0:
                upper = jnp.where((segment >= 2) & south, 0, upper)
            kinds[s] = jnp.where(sub < TILE_X - FROM, upper, lower)

    flat[...] = flat_in[...]
    for e in (0, 1):

        def keep_end(number, weight, level, e=e):
            eweights[number, e] = weight
            elevels[number, e] = level

        found = group_first(
            lambda f, oy, ox: ewin[f, SIDEWAYS.index(oy), e, FROM + ox : FROM + ox + 8, :],
            lambda s: ewords[s, e],
            keep_end,
        )
        for f in range(2):
            flat[f, 8 + 8 * rows_a * e : 16 + 8 * rows_a * e, :] = found[f]
    seam_f = group_first(
        lambda f, oy, ox: seams[f, SIDEWAYS.index(oy), FROM + ox : FROM + ox + 8, :],
        lambda s: kinds[s],
        lambda number, weight, level: None,
    )

    here = jnp.where(place.front, 1.0, 0.0)
    push = PENALTY * here * jnp.maximum(contact[8:18] - owners[8:18], 0.0)
    side_push = side_columns(jnp.where(leftward[0:1], push[9:10], push[8:9]))
    push = push[0:8]
    push_rows = flip(push)

    square = STEP_DT * STEP_DT
    for f in range(2):
        force = pltpu.roll(seam_f[f], FROM, 0)
        above = square * jnp.where(high, force, turn(force, -32))
        below = square * jnp.where(high, turn(force, -64), turn(force, -96))
        nears = {-1: lead_side[f, -1] + above, rows_a: lead_side[f, rows_a] + below}
        nears[0] = jnp.where(sub < FROM, lead_side[f, 0] + above, beside[f, 0])
        nears[last] = jnp.where(sub < FROM, beside[f, last], lead_side[f, last] + below)
        if f == 0:
            nears[last] = nears[last] - square * side_push
        for a in range(-1, rows_a + 1):
            cells = far_lead[f, 0 if a < 0 else 1] if a in (-1, rows_a) else lead[f, a]
            cells = cells + square * flat[f, 8 * a + 11 : 8 * a + 19, :]
            if a == last and f == 0:
                cells = cells - square * push_rows
            near = nears[a] if a in nears else beside[f, a]
            for n, oy in enumerate(SIDEWAYS):
                shifted = sideways(cells, near, oy)
                if a < rows_a:
                    swin[f, n, a + 1, 0:8, :] = shifted
                if a >= 0:
                    swin[f, n, a, 8:16, :] = shifted

    def second_group(k, kept):
        def cell(f, oy, ox):
            return swin[f, SIDEWAYS.index(oy), k, FROM + ox : FROM + ox + 8, :]

        fx, fy = group_second(cell, kept)
        at = pl.multiple_of(8 * k + 8, 8)
        flat2[0, pl.ds(at, 8), :] = fx
        flat2[1, pl.ds(at, 8), :] = fy

    def second_rows(n):
        row = pl.multiple_of(8 * n, 8)
        here = panes[n, 8:16, 0:cols]
        band = place.band_of(row)
        hit = gaps[0, band, :, 0:cols] == place.nodes(row, cols)
        gap = gaps[2, band, :, 0:cols] - square * pushed[n]
        push = jnp.where(hit, PENALTY * jnp.maximum(gap - here, 0.0), 0.0)
        bending = bending_of(lambda o: panes[n, 8 + o : 16 + o, :])[:, 0:cols]
        fast = fasts[n] + STEP_DT * (push - BEND * bending)
        out_speed[pl.ds(row, 8), :] = fast
        out_shell[pl.ds(row, 8), :] = here + STEP_DT * fast

    inner = rows_a - 1
    each = blocks // rows_a

    @pl.loop(0, inner)
    def _(k):
        second_group(k + 1, lambda number: (weights[number, k], levels[number, k]))
        for part in range(each):
            second_rows(each * k + part)

    tail = blocks - each * inner
    half = -(-tail // 2)

    @pl.loop(0, 2)
    def _(e):
        second_group(e * rows_a, lambda number: (eweights[number, e], elevels[number, e]))
        for part in range(half):
            second_rows(jnp.minimum(each * inner + half * e + part, blocks - 1))

    copies[2].start()
    copies[3].start()

    for f in range(2):
        thens = flips([flat2[f, 8 * a + 11 : 8 * a + 19, :] for a in range(rows_a)])
        end_was = flips([flat[f, 8 * a + 11 : 8 * a + 19, :] for a in (0, last)])
        for a in range(rows_a):
            was = end_was[min(a, 1)] if a in (0, last) else tiles_f[f, a]
            then = thens[a]
            if f == 0 and a == last:
                was = was - push
                gap = disp[0, last] + STEP_DT * (vel[0, last] + STEP_DT * was) + inter[...]
                reached = owners[0:8] + square * push
                then = then - PENALTY * here * jnp.maximum(gap - reached, 0.0)
            fast = vel[f, a] + STEP_DT * was
            faster = fast + STEP_DT * then
            out_vel[f, a] = faster
            out_disp[f, a] = disp[f, a] + STEP_DT * (fast + faster)
    copies[0].start()
    copies[1].start()
    for copy in copies:
        copy.wait()


def on_device(nx, ny, disp, vel, jit, words, node, inter, shell, speed):
    rows_a = disp.shape[1]
    rows, cols = shell.shape
    place_args = (nx, ny, rows, cols)
    shifts = tuple(range(1, nx))
    span, count, blocks = rows_a - 1, len(OFFSETS), rows // 8

    def call(body, out, scratch, *args, far=0, **more):
        args = [pltpu.with_memory_space_constraint(x, pltpu.MemorySpace.HBM) for x in args[:far]] + list(args[far:])
        specs = [pl.BlockSpec(memory_space=pltpu.MemorySpace.HBM)] * far
        specs += [pl.BlockSpec(memory_space=pltpu.VMEM)] * (len(args) - far)
        return pl.pallas_call(
            body,
            out_shape=out,
            in_specs=specs,
            scratch_shapes=scratch,
            **more,
            compiler_params=pltpu.CompilerParams(vmem_limit_bytes=20 * 1024 * 1024),
        )(*args)

    def shaped(*shape, dtype=F32):
        return jax.ShapeDtypeStruct(shape + (PTS,), dtype)

    def like(*arrays):
        return [jax.ShapeDtypeStruct(x.shape, x.dtype) for x in arrays]

    wide = pltpu.VMEM((TILE_X, 8, cols), F32)
    tall = pltpu.VMEM((rows + 2 * PAD, WIDE), F32)
    edges = pltpu.VMEM((2, rows, PTS), F32)
    far_shell, far_speed = shell, speed
    small = (disp, vel, jit, words, node, inter)
    first, second, *small = call(
        functools.partial(pack_sides, place_args),
        [shaped(Y_ROWS)] * 2 + like(*small),
        [edges, edges, wide, pltpu.SemaphoreType.DMA((10,))],
        *small,
        far_shell,
        far_speed,
        far=8,
    )
    disp, vel, jit, words, node, inter = small
    first = lax.ppermute(first, "gy", [(i, i ^ 1) for i in range(ny)])
    second = lax.ppermute(
        second,
        ("gx", "gy"),
        [
            (i * ny + j, i * ny + ((j - 1) ^ 1) + 1 if 0 < j < ny - 1 else (i ^ 1) * ny + j)
            for i in range(nx)
            for j in range(ny)
        ],
    )

    shell, speed, lattice, lead, groups_w, ends_w, shore = call(
        functools.partial(own_parts, place_args),
        like(far_shell, far_speed)
        + [
            shaped(4, rows_a, 8),
            shaped(2, rows_a, 8),
            shaped(9, span, 8, dtype=I32),
            shaped(9, 2, 8, dtype=I32),
            shaped(2 * disp.shape[2]),
        ],
        [tall, tall, wide, pltpu.SemaphoreType.DMA((4,))],
        far_shell,
        far_speed,
        disp,
        vel,
        jit,
        words,
        node,
        far=2,
    )

    outs = [shaped(CONTACT_ROWS + (HALO_ROWS if s & (s + 1) == 0 else 0)) for s in shifts]
    *ends, own, strip_d, strip_v = call(
        functools.partial(pack_ends, place_args, shifts),
        outs + [shaped(2 * CONTACT_ROWS), shaped(rows), shaped(rows)],
        [
            pltpu.VMEM((4, len(SIDEWAYS), 24, PTS), F32),
            pltpu.VMEM((rows + 2 * PAD, PTS), F32),
            pltpu.VMEM((TILE_X, 8, PTS), F32),
        ],
        *small,
        shell,
        speed,
        lattice,
        ends_w,
        shore,
        first,
        second,
    )
    ends = [lax.ppermute(e, "gx", [(i, i ^ s) for i in range(nx)]) for s, e in zip(shifts, ends)]

    inner = call(
        functools.partial(inner_rows, place_args),
        [
            shaped(4, len(SIDEWAYS), span, 16),
            shaped(count, span, 8),
            shaped(count, span, 8),
            shaped(2, 8 * (rows_a + 3)),
            shaped(2, rows_a, 8),
            shaped(2, rows_a, 8),
            jax.ShapeDtypeStruct((blocks - 2, 8, WIDE), F32),
        ],
        [
            pltpu.VMEM((4, 3, 24, PTS), F32),
            pltpu.VMEM((9, 8, PTS), I32),
            pltpu.VMEM((blocks - 2, 24, WIDE), F32),
        ],
        disp,
        jit,
        shell,
        speed,
        lattice,
        groups_w,
        first,
        second,
        strip_d,
        strip_v,
    )

    out = [jax.ShapeDtypeStruct(x.shape, F32) for x in (disp, vel, shell, speed)]
    scratch = [pltpu.VMEM(x.shape, F32) for x in out] + [
        pltpu.VMEM((3, TILE_X, 8, WIDE), F32),
        pltpu.VMEM((2, HALO_ROWS, PTS), F32),
        pltpu.VMEM((2, 32, WIDE), F32),
        pltpu.VMEM((2, 16, WIDE), F32),
        pltpu.VMEM((blocks, 24, WIDE), F32),
        pltpu.VMEM((blocks, 8, cols), F32),
        pltpu.VMEM((blocks, 8, cols), F32),
        pltpu.VMEM((4, len(SIDEWAYS), 2, 16, PTS), F32),
        pltpu.VMEM((9, 2, 8, PTS), I32),
        pltpu.VMEM((count, 2, 8, PTS), F32),
        pltpu.VMEM((count, 2, 8, PTS), F32),
        pltpu.VMEM((2, 8 * (rows_a + 3), PTS), F32),
        pltpu.VMEM((2, 8 * (rows_a + 3), PTS), F32),
        pltpu.VMEM((4, len(SIDEWAYS), 16, PTS), F32),
        pltpu.VMEM((9, 8, PTS), I32),
        pltpu.VMEM((2, len(SIDEWAYS), rows_a + 1, 16, PTS), F32),
        pltpu.SemaphoreType.DMA((4,)),
    ]
    return tuple(
        call(
            functools.partial(both_steps, place_args, shifts),
            out,
            scratch,
            disp,
            vel,
            node,
            inter,
            shell,
            speed,
            first,
            second,
            own,
            strip_d,
            strip_v,
            lead,
            ends_w,
            *inner,
            *ends,
            out_specs=[pl.BlockSpec(memory_space=pltpu.MemorySpace.HBM)] * 4,
        )
    )


def solution(mesh):
    in_specs = (
        P(None, "gx", "gy", None),
        P(None, "gx", "gy", None),
        P(None, "gx", "gy", None),
        P("gx", "gy", None),
        P("gy", None),
        P("gy", None),
        P("gx", "gy"),
        P("gx", "gy"),
    )
    out_specs = (P(None, "gx", "gy", None), P(None, "gx", "gy", None), P("gx", "gy"), P("gx", "gy"))
    body = functools.partial(on_device, mesh.shape["gx"], mesh.shape["gy"])
    return jax.shard_map(body, mesh=mesh, in_specs=in_specs, out_specs=out_specs, check_vma=False)
```

```python
import functools

import jax
import jax.numpy as jnp
from jax import lax
from jax.experimental import pallas as pl
from jax.experimental.pallas import tpu as pltpu
from jax.sharding import PartitionSpec as P

TILE_X = 8
TILE_Y = 16
PTS = 128
SPLIT = 4

HORIZON = 3.5
DELTA_SQ = 0.25
PENALTY = 4.0
BEND = 0.5
STEP_DT = 0.2

F32 = jnp.float32
I32 = jnp.int32

STRIDE = 24
WIDE = 640
PAD = 16


def bond_offsets():
    limit = HORIZON * HORIZON - DELTA_SQ
    found = []
    for oy in range(-4, 5):
        for ox in range(-4, 5):
            near = max(abs(ox) - 0.4, 0.0) ** 2 + max(abs(oy) - 0.4, 0.0) ** 2
            if near < limit and (ox or oy):
                found.append((ox, oy))
    return found


OFFSETS = bond_offsets()
SIDEWAYS = sorted({oy for _, oy in OFFSETS})


def sign(value):
    return (value > 0) - (value < 0)


def lanes():
    return lax.broadcasted_iota(I32, (8, PTS), 1)


def subs():
    return lax.broadcasted_iota(I32, (8, PTS), 0)


def turn(values, shift):
    size = values.shape[1]
    return pltpu.roll(values, shift % size, 1) if shift % size else values


def slot(dx, dy):
    return 3 * (dx + 1) + dy + 1


def lane_masks():
    lane = lanes()
    row, col = lane // TILE_Y, lane % TILE_Y
    masks = {}
    for o in (1, 2, 3):
        masks["col_at", o] = col < o
        masks["col_at", -o] = col >= TILE_Y - o
        masks["col_from", o] = col >= TILE_Y - o
        masks["col_from", -o] = col < o
        masks["row_at", o] = row < o
        masks["row_at", -o] = row >= TILE_X - o
        masks["row_from", o] = row >= TILE_X - o
        masks["row_from", -o] = row < o
    bits = {}
    for ox in range(-3, 4):
        bits[ox] = jnp.left_shift(jnp.int32(1), 4 * row + ((row + ox) & 7) // 2)
    return masks, bits


def moved(get, oy, masks):
    out = {}
    for dx in (-1, 0, 1):
        held = get(dx, 0)
        if oy:
            held = turn(jnp.where(masks["col_at", oy], get(dx, sign(oy)), held), -oy)
        out[dx] = held
    return out


def across(cells, ox, masks):
    if not ox:
        return cells[0]
    return turn(jnp.where(masks["row_at", ox], cells[sign(ox)], cells[0]), -TILE_Y * ox)


def first_forces(get_jx, get_jy, get_dx, get_dy, get_words, keep=None, both=True):
    masks, bits = lane_masks()
    jx0, jy0, dx0, dy0 = get_jx(0, 0), get_jy(0, 0), get_dx(0, 0), get_dy(0, 0)
    fx = jnp.zeros((8, PTS), F32)
    fy = jnp.zeros((8, PTS), F32)
    for oy in SIDEWAYS:
        jxs, jys = moved(get_jx, oy, masks), moved(get_jy, oy, masks)
        dxs, dys = moved(get_dx, oy, masks), moved(get_dy, oy, masks)
        words = {}
        for dx in (-1, 0, 1):
            words[dx] = get_words(dx, 0)
            if oy:
                words[dx] = jnp.where(masks["col_from", oy], get_words(dx, sign(oy)), words[dx])
        for number, (ox, other) in enumerate(OFFSETS):
            if other != oy:
                continue
            word = words[0]
            if ox:
                word = jnp.where(masks["row_from", ox], words[sign(ox)], word)
            intact = (word & bits[ox]) != 0
            rest_x = across(jxs, ox, masks) - (jx0 - float(ox))
            rest_y = across(jys, ox, masks) - (jy0 - float(oy))
            now_x = across(dxs, ox, masks) - (dx0 - float(ox))
            now_y = across(dys, ox, masks) - (dy0 - float(oy))
            rest_sq = rest_x * rest_x + rest_y * rest_y + DELTA_SQ
            now_sq = now_x * now_x + now_y * now_y + DELTA_SQ
            rest_inv = lax.rsqrt(rest_sq)
            reach = jnp.maximum(1.0 - rest_sq * rest_inv * (1.0 / HORIZON), 0.0)
            weight = jnp.where(intact, reach * reach, 0.0)
            level = weight * rest_inv
            if keep is not None:
                keep(number, weight, level)
            factor = level - weight * lax.rsqrt(now_sq)
            fx = fx + factor * now_x
            if both:
                fy = fy + factor * now_y
    return fx, fy


def pick_lanes(block, index):
    return jnp.take_along_axis(block, index, axis=1, mode="promise_in_bounds")


def flips(blocks):
    lane, sub = lanes(), subs()
    for level in (2, 1, 0):
        step = 1 << level
        stay = ((lane >> (level + 4)) ^ (sub >> level)) & 1 == 0
        if step == 4:
            others = [turn(pltpu.roll(block, 4, 0), 64) for block in blocks]
        else:
            low = (sub >> level) & 1 == 0
            index = lane ^ (TILE_Y * step)
            others = [jnp.where(low, pltpu.roll(block, 8 - step, 0), pltpu.roll(block, step, 0)) for block in blocks]
            others = [pick_lanes(block, index) for block in others]
        blocks = [jnp.where(stay, block, other) for block, other in zip(blocks, others)]
    return blocks


def flip(block):
    return flips([block])[0]


def side_columns(row):
    return pick_lanes(jnp.broadcast_to(row, (8, PTS)), TILE_Y * subs() + (lanes() & (TILE_Y - 1)))


def word_row(packed, s):
    word = jnp.where(subs() == lanes() // TILE_Y, jnp.broadcast_to(packed[:, s : s + 1], (8, PTS)), 0)
    for step in (4, 2, 1):
        word = word | pltpu.roll(word, step, 0)
    return word


def sideways(cells, beside, oy):
    if not oy:
        return cells
    lane = lanes()
    mask = lane < oy if oy > 0 else lane >= PTS + oy
    return turn(jnp.where(mask, beside, cells), -oy)


FROM = 5


def group_masks(start):
    lane, sub = lanes(), subs()
    row = (sub + start) & (TILE_X - 1)
    col = lane & (TILE_Y - 1)
    masks, bits = {}, {}
    for o in (1, 2, 3):
        masks["col", o] = col >= TILE_Y - o
        masks["col", -o] = col < o
        masks["row", o] = row >= TILE_X - o
        masks["row", -o] = row < o
    for ox in range(-3, 4):
        bits[ox] = jnp.left_shift(jnp.int32(1), 4 * row + ((row + ox) & 7) // 2)
    return masks, bits


def group_first(cell, word, keep, start=FROM):
    masks, bits = group_masks(start)
    zero = [cell(f, 0, 0) for f in range(4)]
    fx = jnp.zeros((8, PTS), F32)
    fy = jnp.zeros((8, PTS), F32)
    plain = [word(slot(dx, 0)) for dx in (-1, 0, 1)]
    for oy in SIDEWAYS:
        words = plain
        if oy:
            words = [jnp.where(masks["col", oy], word(slot(dx, sign(oy))), plain[dx + 1]) for dx in (-1, 0, 1)]
        base_y, base_v = zero[1] - float(oy), zero[3] - float(oy)
        for number, (ox, other) in enumerate(OFFSETS):
            if other != oy:
                continue
            picked = words[1]
            if ox:
                picked = jnp.where(masks["row", ox], words[sign(ox) + 1], picked)
            intact = (picked & bits[ox]) != 0
            rest_x = cell(0, oy, ox) - (zero[0] - float(ox))
            rest_y = cell(1, oy, ox) - base_y
            now_x = cell(2, oy, ox) - (zero[2] - float(ox))
            now_y = cell(3, oy, ox) - base_v
            rest_sq = rest_x * rest_x + rest_y * rest_y + DELTA_SQ
            now_sq = now_x * now_x + now_y * now_y + DELTA_SQ
            rest_inv = lax.rsqrt(rest_sq)
            reach = jnp.maximum(1.0 - rest_sq * rest_inv * (1.0 / HORIZON), 0.0)
            weight = jnp.where(intact, reach * reach, 0.0)
            level = weight * rest_inv
            keep(number, weight, level)
            factor = level - weight * lax.rsqrt(now_sq)
            fx = fx + factor * now_x
            fy = fy + factor * now_y
    return fx, fy


def group_second(cell, kept):
    zero = [cell(f, 0, 0) for f in range(2)]
    fx = jnp.zeros((8, PTS), F32)
    fy = jnp.zeros((8, PTS), F32)
    for number, (ox, oy) in enumerate(OFFSETS):
        now_x = cell(0, oy, ox) - (zero[0] - float(ox))
        now_y = cell(1, oy, ox) - (zero[1] - float(oy))
        now_sq = now_x * now_x + now_y * now_y + DELTA_SQ
        weight, level = kept(number)
        factor = level - weight * lax.rsqrt(now_sq)
        fx = fx + factor * now_x
        fy = fy + factor * now_y
    return fx, fy


def bending_of(row):
    here = row(0)
    one, two = row(-1) + row(1), row(-2) + row(2)
    beside = 2.0 * one - 8.0 * here
    out = two - 8.0 * one + 20.0 * here
    return out + turn(beside + turn(here, 1), 1) + turn(beside + turn(here, -1), -1)


def joined(low_part, high_part):
    return jnp.left_shift(high_part.astype(I32), 16) | low_part.astype(I32)


def widen(row_of, count):
    lane, sub = lanes(), subs()
    index = sub * TILE_Y + (lane % 64) // SPLIT
    out = []
    for j in range(count):
        left, right = (
            pick_lanes(jnp.broadcast_to(row_of(b), (8, PTS)), index) for b in (2 * j, 2 * j + 1)
        )
        out.append(jnp.where(lane < 64, left, right))
    return out


def narrow(block_of, tiles):
    lane, sub = lanes(), subs()
    out, sums = [], {}
    for b in tiles:
        if b // 2 not in sums:
            held = block_of(b // 2)
            held = held + turn(held, -1)
            sums[b // 2] = held + turn(held, -2)
        held = sums[b // 2]
        picked = pick_lanes(held, 64 * (b % 2) + SPLIT * (lane % TILE_Y))
        out.append(jnp.sum(jnp.where(sub == lane // TILE_Y, picked, 0.0), axis=0, keepdims=True))
    return out


def lay_out(ref, at, j, block):
    for row in range(TILE_X):
        ref[at + (row, slice(None), slice(j * PTS, (j + 1) * PTS))] = jnp.broadcast_to(block[row : row + 1], (8, PTS))


class Place:
    def __init__(self, nx, ny, shell_rows, shell_cols):
        self.nx, self.ny = nx, ny
        self.gx, self.gy = lax.axis_index("gx"), lax.axis_index("gy")
        self.shell_rows, self.shell_cols = shell_rows, shell_cols
        self.width = shell_cols * ny
        self.band = shell_rows * nx // TILE_X
        self.bands = shell_rows // self.band
        self.front = self.gx == nx - 1

    def sides(self, first, second):
        even = self.gy % 2 == 0
        right = jnp.where(even, first, second)
        left = jnp.where(even, second, first)
        right = jnp.where(self.gy < self.ny - 1, right, 0.0)
        left = jnp.where(self.gy > 0, left, 0.0)
        return right, left

    def nodes(self, row, columns):
        shape = (8, columns)
        col = lax.broadcasted_iota(I32, shape, 1)
        if columns > self.shell_cols:
            col = jnp.where(col >= self.shell_cols + 64, col - columns, col)
        first = (self.gx * self.shell_rows + row) * self.width + self.gy * self.shell_cols
        return (first + lax.broadcasted_iota(I32, shape, 0) * self.width + col).astype(F32)

    def parts(self):
        inner = [list(range(p * self.band, (p + 1) * self.band, 8)) for p in range(self.bands)]
        return [[-8]] + inner + [[self.shell_rows]]

    def band_of(self, row):
        return jnp.clip((self.gx * self.shell_rows + row + self.band) // self.band - 1, 0, TILE_X - 1)


Y_ROWS = 88


def fetch(pairs, sems):
    copies = [pltpu.make_async_copy(source, target, sems.at[n]) for n, (source, target) in enumerate(pairs)]
    for copy in copies:
        copy.start()
    for copy in copies:
        copy.wait()


def pack_sides(place_args, *refs):
    sources, (first, second), held = refs[:8], refs[8:10], refs[10:16]
    shell, speed, wide_ref, sems = refs[16:]
    place = Place(*place_args)
    pairs = list(zip(sources[:6], held))
    for source, target in zip(sources[6:], (shell, speed)):
        for n, at in enumerate((0, place.shell_cols - PTS)):
            pairs.append((source.at[:, pl.ds(at, PTS)], target.at[n]))
    fetch(pairs, sems)
    disp, vel, jit, words, node, inter = held
    tiles = disp.shape[2]
    even = place.gy % 2 == 0
    blocks = place.shell_cols // PTS
    numbers = node[...].astype(F32)
    edge_blocks = (0, blocks - 1)
    for j in edge_blocks:
        lay_out(wide_ref, (), j, widen(lambda b: numbers[b : b + 1], blocks)[j])
    held = {}
    for j in edge_blocks:
        total = jnp.zeros((8, PTS), F32)
        for part in range(place.bands):
            summed = jnp.zeros((8, PTS), F32)
            for row in range(part * place.band, (part + 1) * place.band, 8):
                wanted = wide_ref[place.band_of(row), :, j * PTS : (j + 1) * PTS]
                ids = place.nodes(row, PTS) + float(j * PTS)
                summed = summed + jnp.where(wanted == ids, shell[min(j, 1), row : row + 8, :], 0.0)
            summed = jnp.sum(summed, axis=0, keepdims=True)
            total = total + jnp.where(subs() == place.band_of(part * place.band), summed, 0.0)
        held[j] = total
    met = narrow(lambda j: held[j], (0, tiles - 1))

    ends = [(jnp.transpose(x[1])[PTS - 8 :], jnp.transpose(x[0])[:8]) for x in (shell, speed)]

    def send(ref, to_right):
        edge = jnp.where(to_right, tiles - 1, 0)
        for f, source in enumerate((disp, disp, vel, vel, jit, jit)):
            ref[8 * f : 8 * f + 8, :] = jnp.where(
                to_right, source[f % 2, :, tiles - 1, :], source[f % 2, :, 0, :]
            )
        ref[48:Y_ROWS, :] = jnp.zeros((Y_ROWS - 48, PTS), F32)
        edge_words = jnp.where(to_right, words[:, tiles - 1, :], words[:, 0, :])
        ref[48:56, 0:9] = (edge_words & 65535).astype(F32)
        ref[56:64, 0:9] = jnp.right_shift(edge_words, 16).astype(F32)
        ref[64:65, :] = jnp.where(to_right, numbers[tiles - 1 : tiles], numbers[0:1])
        ref[65:66, :] = jnp.where(to_right, inter[tiles - 1 : tiles, :], inter[0:1, :])
        ref[66:67, :] = jnp.where(to_right, met[1], met[0])
        for f, source in enumerate((shell, speed)):
            ref[72 + 8 * f : 80 + 8 * f, :] = jnp.where(to_right, *ends[f])

    send(first, even)
    send(second, jnp.logical_not(even))


def own_parts(place_args, far_shell, far_speed, disp, vel, jit, words, node, *refs):
    place = Place(*place_args)
    shell, speed, lattice, lead, groups_w, ends_w, shore, tall, tall_v, wide_ref, sems = refs
    rows_a, tiles = disp.shape[1], disp.shape[2]
    rows, cols = place.shell_rows, place.shell_cols
    lane, sub = lanes(), subs()
    west, east = place.gy == 0, place.gy == place.ny - 1
    north, south = place.gx == 0, place.gx == place.nx - 1
    span = pl.ds(PAD, rows)
    copies = [
        pltpu.make_async_copy(source, target, sems.at[n])
        for n, (source, target) in enumerate(
            (
                (far_shell, shell),
                (far_speed, speed),
                (far_shell, tall.at[span]),
                (far_speed, tall_v.at[span]),
            )
        )
    ]
    for copy in copies:
        copy.start()
    for ref in (tall, tall_v):
        ref[0:PAD, :] = jnp.zeros((PAD, cols), F32)
        ref[PAD + rows :, :] = jnp.zeros((PAD, cols), F32)

    for f in range(2):
        rest = [jit[f, a] for a in range(rows_a)]
        whole = [jit[f, a] + disp[f, a] for a in range(rows_a)]
        soon = [x + STEP_DT * vel[f, a] for a, x in enumerate(whole)]
        for a, (x, y, z) in enumerate(zip(flips(rest), flips(whole), flips(soon))):
            lattice[f, a] = x
            lattice[2 + f, a] = y
            lead[f, a] = z

    before = [None] * 9
    for a in range(rows_a):
        packed = words[a]
        for dx in (-1, 0, 1):
            for dy in (-1, 0, 1):
                s = slot(dx, dy)
                word = word_row(packed, s)
                if dy < 0:
                    word = jnp.where((lane < TILE_Y) & west, 0, word)
                if dy > 0:
                    word = jnp.where((lane >= PTS - TILE_Y) & east, 0, word)
                if dx < 0 and a == 0:
                    word = jnp.where(north, 0, word)
                if dx > 0 and a == rows_a - 1:
                    word = jnp.where(south, 0, word)
                if a:
                    groups_w[s, a - 1] = jnp.where(sub < TILE_X - FROM, before[s], word)
                if a in (0, rows_a - 1):
                    ends_w[s, min(a, 1)] = word
                before[s] = word

    numbers = node[...].astype(F32)
    node_row = jnp.floor(numbers * (1.0 / place.width))
    node_col = numbers - node_row * place.width - (place.gy * cols).astype(F32)
    node_row = node_row - (place.gx * rows).astype(F32)
    at_row = widen(lambda b: node_row[b : b + 1], cols // PTS)
    at_col = jnp.concatenate(widen(lambda b: node_col[b : b + 1], cols // PTS), axis=1)
    col = lax.broadcasted_iota(I32, (8, cols), 1)
    split = col & (SPLIT - 1)
    near_row = jnp.concatenate(at_row, axis=1)
    near_row = jnp.where(split < SPLIT // 2, turn(near_row, SPLIT), turn(near_row, -SPLIT))
    for j, block in enumerate(at_row):
        lay_out(wide_ref, (0,), j, block)
        lay_out(wide_ref, (1,), j, near_row[:, j * PTS : (j + 1) * PTS])
    for copy in copies:
        copy.wait()
    sub_wide = lax.broadcasted_iota(I32, (8, cols), 0)
    row_wide = sub_wide.astype(F32)
    square = STEP_DT * STEP_DT * BEND
    sums = [jnp.zeros((8, cols), F32)] * 5
    for part in place.parts():
        found = [jnp.zeros((8, cols), F32)] * 5
        band = place.band_of(part[0])
        for row in part:
            at = PAD + row
            here = tall[at : at + 8, :]
            one = tall[at - 1 : at + 7, :] + tall[at + 1 : at + 9, :]
            two = tall[at - 2 : at + 6, :] + tall[at + 2 : at + 10, :]
            beside = 2.0 * one - 8.0 * here
            later = here + STEP_DT * tall_v[at : at + 8, :] - square * (two - 8.0 * one + 20.0 * here)
            hit = wide_ref[0, band] == row_wide + float(row)
            near = wide_ref[1, band] == row_wide + float(row)
            picks = ((hit, later), (hit, beside), (hit, here), (near, beside), (near, here))
            found = [x + jnp.where(mask, value, 0.0) for x, (mask, value) in zip(found, picks)]
        sums = [
            x + jnp.where(sub_wide == band, jnp.sum(y, axis=0, keepdims=True), 0.0) for x, y in zip(sums, found)
        ]
    later, beside, here, beside_near, here_near = sums
    spread = jnp.where(split < 3, turn(beside, -1), turn(beside_near, -1)) * (col < cols - 1).astype(F32)
    spread += jnp.where(split > 0, turn(beside, 1), turn(beside_near, 1)) * (col > 0).astype(F32)
    spread += jnp.where(split < 2, turn(here, -2), turn(here_near, -2)) * (col < cols - 2).astype(F32)
    spread += jnp.where(split > 1, turn(here, 2), turn(here_near, 2)) * (col > 1).astype(F32)
    hit = at_col == col.astype(F32)
    ahead = jnp.where(hit, later - square * spread, 0.0)
    met = jnp.where(hit, here, 0.0)
    for base, values in ((0, ahead), (tiles, met)):
        for b, row in enumerate(narrow(lambda j: values[:, j * PTS : (j + 1) * PTS], range(tiles))):
            shore[base + b : base + b + 1, :] = row


HALO_ROWS = 120
CONTACT_ROWS = 24


def shell_strip(right, left, at):
    middle = jnp.zeros((PTS - 16, PTS), F32)
    return jnp.transpose(jnp.concatenate([right[at : at + 8], middle, left[at : at + 8]], axis=0))


def pack_ends(
    place_args, shifts, disp, vel, jit, words, node, inter, shell, speed, lattice, ends_w, shore, first, second, *refs
):
    place = Place(*place_args)
    outs = refs[: len(shifts)]
    own, strip_d, strip_v, grid, tall, wide_ref = refs[len(shifts) :]
    rows_a, tiles = disp.shape[1], disp.shape[2]
    rows, cols = place.shell_rows, place.shell_cols
    right, left = place.sides(first[...], second[...])
    lane, sub = lanes(), subs()
    leftward = (lane[0:1] & (TILE_Y - 1)) >= TILE_Y // 2
    last = rows_a - 1

    for f in range(4):
        for level, a in enumerate((last - 1, last)):
            at = 32 + 8 * (f % 2) + a
            row = jnp.where(leftward, left[at : at + 1], right[at : at + 1])
            if f >= 2:
                at = 8 * (f % 2) + a
                row = row + jnp.where(leftward, left[at : at + 1], right[at : at + 1])
            near = side_columns(row)
            for n, oy in enumerate(SIDEWAYS):
                grid[f, n, 8 * level : 8 * level + 8, :] = sideways(lattice[f, a], near, oy)
        for n in range(len(SIDEWAYS)):
            grid[f, n, 16:24, :] = jnp.zeros((8, PTS), F32)
    force, _ = group_first(
        lambda f, oy, ox: grid[f, SIDEWAYS.index(oy), 8 + ox : 16 + ox, :],
        lambda s: ends_w[s, 1] if s < 6 else jnp.zeros((8, PTS), I32),
        lambda number, weight, level: None,
        start=0,
    )
    gap = disp[0, last] + inter[...]
    own[0:8, :] = gap + STEP_DT * (vel[0, last] + STEP_DT * flip(force))
    own[8:16, :] = gap
    own[16:24, :] = jnp.zeros((8, PTS), F32)
    own[16:17, :] = right[last : last + 1] + right[65:66]
    own[17:18, :] = left[last : last + 1] + left[65:66]

    halo_d = shell_strip(right, left, 72)
    halo_v = shell_strip(right, left, 80)
    strip_d[...] = halo_d
    strip_v[...] = halo_v
    for at in (0, 8, PAD + rows, PAD + rows + 8):
        tall[at : at + 8, :] = jnp.zeros((8, PTS), F32)
    tall[PAD : PAD + rows, :] = halo_d
    numbers = node[...].astype(F32)
    blocks = widen(lambda b: numbers[b : b + 1], cols // PTS)
    low = lane < PTS // 2
    lay_out(wide_ref, (), 0, jnp.where(low, blocks[0], blocks[-1]))
    far = jnp.where(low, 0.0, float(cols - PTS))
    ahead = jnp.zeros((8, PTS), F32)
    for part in place.parts():
        soon = jnp.zeros((8, PTS), F32)
        band = place.band_of(part[0])
        for row in part:
            at = PAD + row
            here = tall[at : at + 8, :]
            column = 2.0 * (tall[at - 1 : at + 7, :] + tall[at + 1 : at + 9, :]) - 8.0 * here
            from_left = turn(jnp.where(low, 0.0, column), 1) + turn(jnp.where(low, 0.0, here), 2)
            from_right = turn(jnp.where(low, column, 0.0), -1) + turn(jnp.where(low, here, 0.0), -2)
            hit = wide_ref[band] == place.nodes(row, PTS) + far
            soon = soon + jnp.where(hit, jnp.where(low, from_left, from_right), 0.0)
        ahead = ahead + jnp.where(sub == band, jnp.sum(soon, axis=0, keepdims=True), 0.0)
    base = CONTACT_ROWS
    own[base + 16 : base + 24, :] = jnp.zeros((8, PTS), F32)
    own[base : base + 16, :] = shore[...]
    for b, row in zip((0, tiles - 1), narrow(lambda j: ahead, (0, tiles - 1))):
        own[base + b : base + b + 1, :] = shore[b : b + 1, :] - (STEP_DT * STEP_DT * BEND) * row
    own[base + 16 : base + 17, :] = right[66:67]
    own[base + 17 : base + 18, :] = left[66:67]

    mine = jnp.where(place.front, own[0:CONTACT_ROWS, :], own[base : base + CONTACT_ROWS, :])
    for shift, out in zip(shifts, outs):
        at = 0
        if shift & (shift + 1) == 0:
            at = HALO_ROWS
            down = (place.gx ^ shift) > place.gx
            edge = jnp.where(down, rows_a - 1, 0)
            for f, source in enumerate((disp, disp, vel, vel, jit, jit)):
                out[8 * f : 8 * f + 8, :] = source[f % 2, edge]
            out[48:80, :] = jnp.zeros((32, PTS), F32)
            edge_words = words[edge]
            out[48:56, 0:9] = (edge_words & 65535).astype(F32)
            out[56:64, 0:9] = jnp.right_shift(edge_words, 16).astype(F32)
            for f in range(8):
                for side, values in ((64, right), (72, left)):
                    low, high = values[8 * f : 8 * f + 1], values[8 * f + rows_a - 1 : 8 * f + rows_a]
                    out[side + f : side + f + 1, :] = jnp.where(down, high, low)
            for j in range(WIDE // PTS):
                cut = slice(j * PTS, (j + 1) * PTS)
                if j < cols // PTS:
                    d_low, d_high = shell[0:4, cut], shell[rows - 4 : rows, cut]
                    v_low, v_high = speed[0:2, cut], speed[rows - 2 : rows, cut]
                else:
                    d_low, d_high = halo_d[0:4], halo_d[rows - 4 : rows]
                    v_low, v_high = halo_v[0:2], halo_v[rows - 2 : rows]
                out[80 + 8 * j : 84 + 8 * j, :] = jnp.where(down, d_high, d_low)
                out[84 + 8 * j : 86 + 8 * j, :] = jnp.where(down, v_high, v_low)
                out[86 + 8 * j : 88 + 8 * j, :] = jnp.zeros((2, PTS), F32)
        out[at : at + CONTACT_ROWS, :] = mine


def inner_rows(place_args, disp, jit, shell, speed, lattice, groups_w, first, second, strip_d, strip_v, *refs):
    place = Place(*place_args)
    win, weights, levels, flat, beside, tiles_f, mid, strips, kinds, panes = refs
    cols = place.shell_cols
    rows_a, tiles = disp.shape[1], disp.shape[2]
    right, left = place.sides(first[...], second[...])
    lane = lanes()
    leftward = (lane & (TILE_Y - 1)) >= TILE_Y // 2
    side = [jnp.where(leftward, left[8 * f : 8 * f + 8], right[8 * f : 8 * f + 8]) for f in range(6)]

    strips[...] = jnp.zeros_like(strips)
    for f in range(4):
        rest = jit[f % 2]
        whole = rest if f < 2 else rest + disp[f % 2]
        beyond = side[4 + f % 2] if f < 2 else side[4 + f % 2] + side[f % 2]
        strips[f, 0, 8:16, :] = beyond
        strips[f, 1, 8:16, :] = whole[:, 0, :]
        strips[f, 2, 8:16, :] = whole[:, tiles - 1, :]
        nears = [side_columns(beyond[a : a + 1]) for a in range(rows_a)]
        for a, near in enumerate(nears):
            cells = lattice[f, a]
            for n, oy in enumerate(SIDEWAYS):
                shifted = sideways(cells, near, oy)
                if a < rows_a - 1:
                    win[f, n, a, 0:8, :] = shifted
                if a > 0:
                    win[f, n, a - 1, 8:16, :] = shifted
    left_words = joined(left[48:56], left[56:64])
    right_words = joined(right[48:56], right[56:64])
    for s in range(9):
        kinds[s] = jnp.where(
            leftward,
            jnp.broadcast_to(left_words[:, s : s + 1], (8, PTS)),
            jnp.broadcast_to(right_words[:, s : s + 1], (8, PTS)),
        )

    flat[...] = jnp.zeros_like(flat)

    blocks = mid.shape[0]
    for n in range(blocks):
        panes[n, :, 0:cols] = shell[8 * n : 8 * n + 24, :]
        panes[n, :, cols:WIDE] = strip_d[8 * n : 8 * n + 24, :]
    each = -(-blocks // (rows_a - 1))

    def bend_block(n):
        at = pl.multiple_of(8 * n + 8, 8)
        bending = bending_of(lambda o: panes[n, 8 + o : 16 + o, :])
        mid[n, :, 0:cols] = speed[pl.ds(at, 8), :] - (STEP_DT * BEND) * bending[:, 0:cols]
        mid[n, :, cols:WIDE] = strip_v[pl.ds(at, 8), :] - (STEP_DT * BEND) * bending[:, cols:WIDE]

    @pl.loop(0, rows_a - 1)
    def _(k):
        for part in range(each):
            bend_block(jnp.minimum(each * k + part, blocks - 1))

        def cell(f, oy, ox):
            return win[f, SIDEWAYS.index(oy), k, FROM + ox : FROM + ox + 8, :]

        def keep(number, weight, level):
            weights[number, k] = weight
            levels[number, k] = level

        fx, fy = group_first(cell, lambda s: groups_w[s, k], keep)
        at = pl.multiple_of(8 * k + 16, 8)
        flat[0, pl.ds(at, 8), :] = fx
        flat[1, pl.ds(at, 8), :] = fy

    def getter(f):
        held = {}

        def get(dx, dy):
            if (dx, dy) not in held:
                held[dx, dy] = turn(strips[f, dy % 3, 8 + dx : 16 + dx, :], TILE_Y * dy)
            return held[dx, dy]

        return get

    forces = first_forces(getter(0), getter(1), getter(2), getter(3), lambda dx, dy: kinds[slot(dx, dy)])
    for f in range(2):
        moved_side = side[4 + f] + side[f] + STEP_DT * (side[2 + f] + STEP_DT * forces[f])
        for a in range(rows_a):
            beside[f, a] = side_columns(moved_side[a : a + 1])
        for a, cells in enumerate(flips([flat[f, 8 * a + 11 : 8 * a + 19, :] for a in range(1, rows_a - 1)])):
            tiles_f[f, a + 1] = cells
        tiles_f[f, 0] = jnp.zeros((8, PTS), F32)
        tiles_f[f, rows_a - 1] = jnp.zeros((8, PTS), F32)


def both_steps(place_args, shifts, *refs):
    place = Place(*place_args)
    disp, vel, node, inter, shell, speed, first, second, own, strip_d, strip_v = refs[:11]
    lead, ends_w, win, weights, levels, flat_in, beside, tiles_f, mid = refs[11:20]
    ends = refs[20 : 20 + len(shifts)]
    targets = refs[20 + len(shifts) : 24 + len(shifts)]
    scratch = refs[24 + len(shifts) :]
    out_disp, out_vel, out_shell, out_speed, gaps, halo, rim, rim_v, panes, fasts, hits, goals, ewin, ewords = scratch[:14]
    eweights, elevels, flat, flat2, seams, kinds, swin, sems = scratch[14:]
    outs = (out_disp, out_vel, out_shell, out_speed)
    copies = [pltpu.make_async_copy(x, y, sems.at[n]) for n, (x, y) in enumerate(zip(outs, targets))]
    rows_a, tiles = disp.shape[1], disp.shape[2]
    rows, cols = place.shell_rows, place.shell_cols
    blocks = rows // 8
    right, left = place.sides(first[...], second[...])

    halo[...] = jnp.zeros_like(halo)
    contact = jnp.where(place.front, own[0:CONTACT_ROWS, :], 0.0)
    owners = own[CONTACT_ROWS:, :]
    for shift, ref in zip(shifts, ends):
        partner = place.gx ^ shift
        at = 0
        if shift & (shift + 1) == 0:
            at = HALO_ROWS

            @pl.when(partner == place.gx - 1)
            def _():
                halo[0] = ref[0:HALO_ROWS, :]

            @pl.when(partner == place.gx + 1)
            def _():
                halo[1] = ref[0:HALO_ROWS, :]

        got = ref[at : at + CONTACT_ROWS, :]
        contact = jnp.where(partner == place.nx - 1, got, contact)
        owners = owners + got

    def wide(source, strip, row, count):
        return jnp.concatenate([source[row : row + count, :], strip[row : row + count, :]], axis=1)

    zeros = jnp.zeros((8, WIDE), F32)
    rim[0, 16:32, :] = wide(shell, strip_d, 0, 16)
    rim[1, 0:16, :] = wide(shell, strip_d, rows - 16, 16)
    rim_v[0, 8:16, :] = wide(speed, strip_v, 0, 8)
    rim_v[1, 0:8, :] = wide(speed, strip_v, rows - 8, 8)
    for ref, at in ((rim, (0, 0)), (rim, (0, 8)), (rim, (1, 16)), (rim, (1, 24)), (rim_v, (0, 0)), (rim_v, (1, 8))):
        ref[at[0], at[1] : at[1] + 8, :] = zeros
    for j in range(WIDE // PTS):
        cut = slice(j * PTS, (j + 1) * PTS)
        rim[0, 12:16, cut] = halo[0, 80 + 8 * j : 84 + 8 * j, :]
        rim_v[0, 6:8, cut] = halo[0, 84 + 8 * j : 86 + 8 * j, :]
        rim[1, 16:20, cut] = halo[1, 80 + 8 * j : 84 + 8 * j, :]
        rim_v[1, 8:10, cut] = halo[1, 84 + 8 * j : 86 + 8 * j, :]
    numbers = node[...].astype(F32)
    node_rows = [numbers[b : b + 1] for b in range(tiles)] + [right[64:65], left[64:65]]
    gap_rows = [contact[8 + b : 9 + b] for b in range(tiles)] + [contact[16:17], contact[17:18]]
    soon_rows = [contact[b : b + 1] for b in range(tiles)]
    for j, (nodes, gap) in enumerate(zip(widen(node_rows.__getitem__, 5), widen(gap_rows.__getitem__, 5))):
        lay_out(gaps, (0,), j, nodes)
        lay_out(gaps, (1,), j, gap)
    for j, soon in enumerate(widen(soon_rows.__getitem__, 4)):
        lay_out(gaps, (2,), j, soon)
    col = lax.broadcasted_iota(I32, (8, WIDE), 1)
    inside = jnp.where(col < cols, 1.0, 0.0)
    inside = jnp.where((col >= cols) & (col < cols + 64) & (place.gy < place.ny - 1), 1.0, inside)
    inside = jnp.where((col >= cols + 64) & (place.gy > 0), 1.0, inside)
    for n in range(-1, blocks + 1):
        row = 8 * n
        if 0 < n < blocks - 1:
            here, steady = wide(shell, strip_d, row, 8), mid[n - 1]
        else:
            end = 0 if n < 1 else 1
            at = row + 16 if end == 0 else row - rows + 16
            here = rim[end, at : at + 8, :]
            bending = bending_of(lambda o: rim[end, at + o : at + o + 8, :])
            steady = rim_v[end, at - 8 : at, :] - (STEP_DT * BEND) * bending
        band = place.band_of(row)
        hit = jnp.where(gaps[0, band] == place.nodes(row, WIDE), STEP_DT * PENALTY, 0.0)
        push = hit * jnp.maximum(gaps[1, band] - here, 0.0)
        fast = steady + push
        keep = inside
        if n < 0:
            keep = inside * jnp.where(place.gx > 0, 1.0, 0.0)
        elif n == blocks:
            keep = inside * jnp.where(place.gx < place.nx - 1, 1.0, 0.0)
        there = (here + STEP_DT * fast) * keep
        for part in (-1, 0, 1):
            if 0 <= n - part < blocks:
                panes[n - part, 8 + 8 * part : 16 + 8 * part, :] = there
        if 0 <= n < blocks:
            fasts[n] = fast[:, 0:cols]
            hits[n] = hit[:, 0:cols]
            goals[n] = gaps[2, band, :, 0:cols] - STEP_DT * push[:, 0:cols]

    lane, sub = lanes(), subs()
    west, east = place.gy == 0, place.gy == place.ny - 1
    north, south = place.gx == 0, place.gx == place.nx - 1
    leftward = (lane & (TILE_Y - 1)) >= TILE_Y // 2
    last = rows_a - 1
    high = lane >= PTS // 2
    segment = ((lane + 16) >> 5) & 3

    def side_row(end, part):
        return jnp.where(leftward[0:1], halo[end, 72 + part : 73 + part, :], halo[end, 64 + part : 65 + part, :])

    def near_row(a, part):
        at = 8 * part + a
        return jnp.where(leftward[0:1], left[at : at + 1], right[at : at + 1])

    border = (-1, 0, last, rows_a)
    sides = {}
    for part in range(6):
        for a in border:
            sides[a, part] = near_row(a, part) if 0 <= a <= last else side_row(0 if a < 0 else 1, part)
    lead_side, far_lead = {}, {}
    straight = SIDEWAYS.index(0)
    turned = flips(
        [
            piece
            for end in (0, 1)
            for f in range(2)
            for rest in (halo[end, 32 + 8 * f : 40 + 8 * f, :],)
            for whole in (rest + halo[end, 8 * f : 8 * f + 8, :],)
            for piece in (rest, whole, whole + STEP_DT * halo[end, 16 + 8 * f : 24 + 8 * f, :])
        ]
    )
    for f in range(2):
        for a in border:
            lead_side[f, a] = side_columns(sides[a, 4 + f] + sides[a, f] + STEP_DT * sides[a, 2 + f])
        for end in (0, 1):
            far_lead[f, end] = turned[6 * end + 3 * f + 2]
        for field in (f, 2 + f):
            cells, near = {}, {}
            for a in border:
                near[a] = side_columns(sides[a, 4 + f] + sides[a, f] if field >= 2 else sides[a, 4 + f])
            cells[-1], cells[rows_a] = (turned[6 * end + 3 * f + field // 2] for end in (0, 1))
            cells[0] = win[field, straight, 0, 0:8, :]
            cells[last] = win[field, straight, rows_a - 2, 8:16, :]
            for n, oy in enumerate(SIDEWAYS):
                ewin[field, n, 0, 0:8, :] = sideways(cells[-1], near[-1], oy)
                ewin[field, n, 0, 8:16, :] = win[field, n, 0, 0:8, :]
                ewin[field, n, 1, 0:8, :] = win[field, n, rows_a - 2, 8:16, :]
                ewin[field, n, 1, 8:16, :] = sideways(cells[rows_a], near[rows_a], oy)
            for half, (up, down) in enumerate(((-1, last), (0, rows_a))):
                pieces = [
                    jnp.where(high, near[up], cells[up]),
                    turn(jnp.where(high, cells[up], near[up]), 32),
                    turn(jnp.where(high, near[down], cells[down]), 64),
                    turn(jnp.where(high, cells[down], near[down]), 96),
                ]
                seam = pieces[3]
                for q in (2, 1, 0):
                    seam = jnp.where(segment == q, pieces[q], seam)
                for n, oy in enumerate(SIDEWAYS):
                    seams[field, n, 8 * half : 8 * half + 8, :] = turn(seam, -oy)
    for end in (0, 1):
        packed = joined(halo[end, 48:56, :], halo[end, 56:64, :])
        for dx in (-1, 0, 1):
            for dy in (-1, 0, 1):
                s = slot(dx, dy)
                word = word_row(packed, s)
                if dy < 0:
                    word = jnp.where((lane < TILE_Y) & west, 0, word)
                if dy > 0:
                    word = jnp.where((lane >= PTS - TILE_Y) & east, 0, word)
                pair = (word, ends_w[s, 0]) if end == 0 else (ends_w[s, 1], word)
                ewords[s, end] = jnp.where(sub < TILE_X - FROM, *pair)
    parts = []
    for at in (0, 1):
        rows_w = []
        for a in (-1, last, 0, rows_a):
            for values, part in ((left, 72), (right, 64)):
                if 0 <= a <= last:
                    rows_w.append(values[48 + 8 * at + a : 49 + 8 * at + a])
                else:
                    end = 0 if a < 0 else 1
                    rows_w.append(halo[end, part + 6 + at : part + 7 + at, :])
        parts.append(jnp.concatenate(rows_w, axis=0))
    packed = joined(*parts)
    for dx in (-1, 0, 1):
        for dy in (-1, 0, 1):
            s = slot(dx, dy)
            word = jnp.broadcast_to(packed[:, s : s + 1], (8, PTS))
            upper, lower = jnp.where(sub == segment, word, 0), jnp.where(sub == segment + 4, word, 0)
            for step in (4, 2, 1):
                upper, lower = upper | pltpu.roll(upper, step, 0), lower | pltpu.roll(lower, step, 0)
            if dx < 0:
                lower = jnp.where((segment < 2) & north, 0, lower)
            if dx > 0:
                upper = jnp.where((segment >= 2) & south, 0, upper)
            kinds[s] = jnp.where(sub < TILE_X - FROM, upper, lower)

    flat[...] = flat_in[...]
    for e in (0, 1):

        def keep_end(number, weight, level, e=e):
            eweights[number, e] = weight
            elevels[number, e] = level

        found = group_first(
            lambda f, oy, ox: ewin[f, SIDEWAYS.index(oy), e, FROM + ox : FROM + ox + 8, :],
            lambda s: ewords[s, e],
            keep_end,
        )
        for f in range(2):
            flat[f, 8 + 8 * rows_a * e : 16 + 8 * rows_a * e, :] = found[f]
    seam_f = group_first(
        lambda f, oy, ox: seams[f, SIDEWAYS.index(oy), FROM + ox : FROM + ox + 8, :],
        lambda s: kinds[s],
        lambda number, weight, level: None,
    )

    here = jnp.where(place.front, 1.0, 0.0)
    push = PENALTY * here * jnp.maximum(contact[8:18] - owners[8:18], 0.0)
    side_push = side_columns(jnp.where(leftward[0:1], push[9:10], push[8:9]))
    push = push[0:8]
    push_rows = flip(push)

    square = STEP_DT * STEP_DT
    for f in range(2):
        force = pltpu.roll(seam_f[f], FROM, 0)
        above = square * jnp.where(high, force, turn(force, -32))
        below = square * jnp.where(high, turn(force, -64), turn(force, -96))
        nears = {-1: lead_side[f, -1] + above, rows_a: lead_side[f, rows_a] + below}
        nears[0] = jnp.where(sub < FROM, lead_side[f, 0] + above, beside[f, 0])
        nears[last] = jnp.where(sub < FROM, beside[f, last], lead_side[f, last] + below)
        if f == 0:
            nears[last] = nears[last] - square * side_push
        for a in range(-1, rows_a + 1):
            cells = far_lead[f, 0 if a < 0 else 1] if a in (-1, rows_a) else lead[f, a]
            cells = cells + square * flat[f, 8 * a + 11 : 8 * a + 19, :]
            if a == last and f == 0:
                cells = cells - square * push_rows
            near = nears[a] if a in nears else beside[f, a]
            for n, oy in enumerate(SIDEWAYS):
                shifted = sideways(cells, near, oy)
                if a < rows_a:
                    swin[f, n, a + 1, 0:8, :] = shifted
                if a >= 0:
                    swin[f, n, a, 8:16, :] = shifted

    def second_group(k, kept):
        def cell(f, oy, ox):
            return swin[f, SIDEWAYS.index(oy), k, FROM + ox : FROM + ox + 8, :]

        fx, fy = group_second(cell, kept)
        at = pl.multiple_of(8 * k + 8, 8)
        flat2[0, pl.ds(at, 8), :] = fx
        flat2[1, pl.ds(at, 8), :] = fy

    def second_rows(n):
        row = pl.multiple_of(8 * n, 8)
        here = panes[n, 8:16, 0:cols]
        push = hits[n] * jnp.maximum(goals[n] - here, 0.0)
        bending = bending_of(lambda o: panes[n, 8 + o : 16 + o, :])[:, 0:cols]
        fast = fasts[n] + push - (STEP_DT * BEND) * bending
        out_speed[pl.ds(row, 8), :] = fast
        out_shell[pl.ds(row, 8), :] = here + STEP_DT * fast

    inner = rows_a - 1
    each = blocks // rows_a

    @pl.loop(0, inner)
    def _(k):
        second_group(k + 1, lambda number: (weights[number, k], levels[number, k]))
        for part in range(each):
            second_rows(each * k + part)

    tail = blocks - each * inner
    half = -(-tail // 2)

    @pl.loop(0, 2)
    def _(e):
        second_group(e * rows_a, lambda number: (eweights[number, e], elevels[number, e]))
        for part in range(half):
            second_rows(jnp.minimum(each * inner + half * e + part, blocks - 1))

    copies[2].start()
    copies[3].start()

    for f in range(2):
        thens = flips([flat2[f, 8 * a + 11 : 8 * a + 19, :] for a in range(rows_a)])
        end_was = flips([flat[f, 8 * a + 11 : 8 * a + 19, :] for a in (0, last)])
        for a in range(rows_a):
            was = end_was[min(a, 1)] if a in (0, last) else tiles_f[f, a]
            then = thens[a]
            if f == 0 and a == last:
                was = was - push
                gap = disp[0, last] + STEP_DT * (vel[0, last] + STEP_DT * was) + inter[...]
                reached = owners[0:8] + square * push
                then = then - PENALTY * here * jnp.maximum(gap - reached, 0.0)
            fast = vel[f, a] + STEP_DT * was
            faster = fast + STEP_DT * then
            out_vel[f, a] = faster
            out_disp[f, a] = disp[f, a] + STEP_DT * (fast + faster)
    copies[0].start()
    copies[1].start()
    for copy in copies:
        copy.wait()


def on_device(nx, ny, disp, vel, jit, words, node, inter, shell, speed):
    rows_a = disp.shape[1]
    rows, cols = shell.shape
    place_args = (nx, ny, rows, cols)
    shifts = tuple(range(1, nx))
    span, count, blocks = rows_a - 1, len(OFFSETS), rows // 8

    def call(body, out, scratch, *args, far=0, **more):
        args = [pltpu.with_memory_space_constraint(x, pltpu.MemorySpace.HBM) for x in args[:far]] + list(args[far:])
        specs = [pl.BlockSpec(memory_space=pltpu.MemorySpace.HBM)] * far
        specs += [pl.BlockSpec(memory_space=pltpu.VMEM)] * (len(args) - far)
        return pl.pallas_call(
            body,
            out_shape=out,
            in_specs=specs,
            scratch_shapes=scratch,
            **more,
            compiler_params=pltpu.CompilerParams(vmem_limit_bytes=20 * 1024 * 1024),
        )(*args)

    def shaped(*shape, dtype=F32):
        return jax.ShapeDtypeStruct(shape + (PTS,), dtype)

    def like(*arrays):
        return [jax.ShapeDtypeStruct(x.shape, x.dtype) for x in arrays]

    wide = pltpu.VMEM((TILE_X, 8, cols), F32)
    tall = pltpu.VMEM((rows + 2 * PAD, cols), F32)
    edges = pltpu.VMEM((2, rows, PTS), F32)
    far_shell, far_speed = shell, speed
    small = (disp, vel, jit, words, node, inter)
    first, second, *small = call(
        functools.partial(pack_sides, place_args),
        [shaped(Y_ROWS)] * 2 + like(*small),
        [edges, edges, wide, pltpu.SemaphoreType.DMA((10,))],
        *small,
        far_shell,
        far_speed,
        far=8,
    )
    disp, vel, jit, words, node, inter = small
    first = lax.ppermute(first, "gy", [(i, i ^ 1) for i in range(ny)])
    second = lax.ppermute(
        second,
        ("gx", "gy"),
        [
            (i * ny + j, i * ny + ((j - 1) ^ 1) + 1 if 0 < j < ny - 1 else (i ^ 1) * ny + j)
            for i in range(nx)
            for j in range(ny)
        ],
    )

    shell, speed, lattice, lead, groups_w, ends_w, shore = call(
        functools.partial(own_parts, place_args),
        like(far_shell, far_speed)
        + [
            shaped(4, rows_a, 8),
            shaped(2, rows_a, 8),
            shaped(9, span, 8, dtype=I32),
            shaped(9, 2, 8, dtype=I32),
            shaped(2 * disp.shape[2]),
        ],
        [tall, tall, pltpu.VMEM((2, TILE_X, 8, cols), F32), pltpu.SemaphoreType.DMA((4,))],
        far_shell,
        far_speed,
        disp,
        vel,
        jit,
        words,
        node,
        far=2,
    )

    outs = [shaped(CONTACT_ROWS + (HALO_ROWS if s & (s + 1) == 0 else 0)) for s in shifts]
    *ends, own, strip_d, strip_v = call(
        functools.partial(pack_ends, place_args, shifts),
        outs + [shaped(2 * CONTACT_ROWS), shaped(rows), shaped(rows)],
        [
            pltpu.VMEM((4, len(SIDEWAYS), 24, PTS), F32),
            pltpu.VMEM((rows + 2 * PAD, PTS), F32),
            pltpu.VMEM((TILE_X, 8, PTS), F32),
        ],
        *small,
        shell,
        speed,
        lattice,
        ends_w,
        shore,
        first,
        second,
    )
    ends = [lax.ppermute(e, "gx", [(i, i ^ s) for i in range(nx)]) for s, e in zip(shifts, ends)]

    inner = call(
        functools.partial(inner_rows, place_args),
        [
            shaped(4, len(SIDEWAYS), span, 16),
            shaped(count, span, 8),
            shaped(count, span, 8),
            shaped(2, 8 * (rows_a + 3)),
            shaped(2, rows_a, 8),
            shaped(2, rows_a, 8),
            jax.ShapeDtypeStruct((blocks - 2, 8, WIDE), F32),
        ],
        [
            pltpu.VMEM((4, 3, 24, PTS), F32),
            pltpu.VMEM((9, 8, PTS), I32),
            pltpu.VMEM((blocks - 2, 24, WIDE), F32),
        ],
        disp,
        jit,
        shell,
        speed,
        lattice,
        groups_w,
        first,
        second,
        strip_d,
        strip_v,
    )

    out = [jax.ShapeDtypeStruct(x.shape, F32) for x in (disp, vel, shell, speed)]
    scratch = [pltpu.VMEM(x.shape, F32) for x in out] + [
        pltpu.VMEM((3, TILE_X, 8, WIDE), F32),
        pltpu.VMEM((2, HALO_ROWS, PTS), F32),
        pltpu.VMEM((2, 32, WIDE), F32),
        pltpu.VMEM((2, 16, WIDE), F32),
        pltpu.VMEM((blocks, 24, WIDE), F32),
        pltpu.VMEM((blocks, 8, cols), F32),
        pltpu.VMEM((blocks, 8, cols), F32),
        pltpu.VMEM((blocks, 8, cols), F32),
        pltpu.VMEM((4, len(SIDEWAYS), 2, 16, PTS), F32),
        pltpu.VMEM((9, 2, 8, PTS), I32),
        pltpu.VMEM((count, 2, 8, PTS), F32),
        pltpu.VMEM((count, 2, 8, PTS), F32),
        pltpu.VMEM((2, 8 * (rows_a + 3), PTS), F32),
        pltpu.VMEM((2, 8 * (rows_a + 3), PTS), F32),
        pltpu.VMEM((4, len(SIDEWAYS), 16, PTS), F32),
        pltpu.VMEM((9, 8, PTS), I32),
        pltpu.VMEM((2, len(SIDEWAYS), rows_a + 1, 16, PTS), F32),
        pltpu.SemaphoreType.DMA((4,)),
    ]
    return tuple(
        call(
            functools.partial(both_steps, place_args, shifts),
            out,
            scratch,
            disp,
            vel,
            node,
            inter,
            shell,
            speed,
            first,
            second,
            own,
            strip_d,
            strip_v,
            lead,
            ends_w,
            *inner,
            *ends,
            out_specs=[pl.BlockSpec(memory_space=pltpu.MemorySpace.HBM)] * 4,
        )
    )


def solution(mesh):
    in_specs = (
        P(None, "gx", "gy", None),
        P(None, "gx", "gy", None),
        P(None, "gx", "gy", None),
        P("gx", "gy", None),
        P("gy", None),
        P("gy", None),
        P("gx", "gy"),
        P("gx", "gy"),
    )
    out_specs = (P(None, "gx", "gy", None), P(None, "gx", "gy", None), P("gx", "gy"), P("gx", "gy"))
    body = functools.partial(on_device, mesh.shape["gx"], mesh.shape["gy"])
    return jax.shard_map(body, mesh=mesh, in_specs=in_specs, out_specs=out_specs, check_vma=False)
```

```python
import functools

import jax
import jax.numpy as jnp
from jax import lax
from jax.experimental import pallas as pl
from jax.experimental.pallas import tpu as pltpu
from jax.sharding import PartitionSpec as P

TILE_X = 8
TILE_Y = 16
PTS = 128
SPLIT = 4

HORIZON = 3.5
DELTA_SQ = 0.25
PENALTY = 4.0
BEND = 0.5
STEP_DT = 0.2

F32 = jnp.float32
I32 = jnp.int32

STRIDE = 24
WIDE = 640
PAD = 16


def bond_offsets():
    limit = HORIZON * HORIZON - DELTA_SQ
    found = []
    for oy in range(-4, 5):
        for ox in range(-4, 5):
            near = max(abs(ox) - 0.4, 0.0) ** 2 + max(abs(oy) - 0.4, 0.0) ** 2
            if near < limit and (ox or oy):
                found.append((ox, oy))
    return found


OFFSETS = bond_offsets()
SIDEWAYS = sorted({oy for _, oy in OFFSETS})


def sign(value):
    return (value > 0) - (value < 0)


def lanes():
    return lax.broadcasted_iota(I32, (8, PTS), 1)


def subs():
    return lax.broadcasted_iota(I32, (8, PTS), 0)


def turn(values, shift):
    size = values.shape[1]
    return pltpu.roll(values, shift % size, 1) if shift % size else values


def slot(dx, dy):
    return 3 * (dx + 1) + dy + 1


def lane_masks():
    lane = lanes()
    row, col = lane // TILE_Y, lane % TILE_Y
    masks = {}
    for o in (1, 2, 3):
        masks["col_at", o] = col < o
        masks["col_at", -o] = col >= TILE_Y - o
        masks["col_from", o] = col >= TILE_Y - o
        masks["col_from", -o] = col < o
        masks["row_at", o] = row < o
        masks["row_at", -o] = row >= TILE_X - o
        masks["row_from", o] = row >= TILE_X - o
        masks["row_from", -o] = row < o
    bits = {}
    for ox in range(-3, 4):
        bits[ox] = jnp.left_shift(jnp.int32(1), 4 * row + ((row + ox) & 7) // 2)
    return masks, bits


def across(cells, ox, masks):
    if not ox:
        return cells[0]
    return turn(jnp.where(masks["row_at", ox], cells[sign(ox)], cells[0]), -TILE_Y * ox)


def pick_lanes(block, index):
    return jnp.take_along_axis(block, index, axis=1, mode="promise_in_bounds")


def flips(blocks):
    lane, sub = lanes(), subs()
    for level in (2, 1, 0):
        step = 1 << level
        stay = ((lane >> (level + 4)) ^ (sub >> level)) & 1 == 0
        if step == 4:
            others = [turn(pltpu.roll(block, 4, 0), 64) for block in blocks]
        else:
            low = (sub >> level) & 1 == 0
            index = lane ^ (TILE_Y * step)
            others = [jnp.where(low, pltpu.roll(block, 8 - step, 0), pltpu.roll(block, step, 0)) for block in blocks]
            others = [pick_lanes(block, index) for block in others]
        blocks = [jnp.where(stay, block, other) for block, other in zip(blocks, others)]
    return blocks


def flip(block):
    return flips([block])[0]


def side_columns(row):
    return pick_lanes(jnp.broadcast_to(row, (8, PTS)), TILE_Y * subs() + (lanes() & (TILE_Y - 1)))


def word_row(packed, s):
    word = jnp.where(subs() == lanes() // TILE_Y, jnp.broadcast_to(packed[:, s : s + 1], (8, PTS)), 0)
    for step in (4, 2, 1):
        word = word | pltpu.roll(word, step, 0)
    return word


def sideways(cells, beside, oy):
    if not oy:
        return cells
    lane = lanes()
    mask = lane < oy if oy > 0 else lane >= PTS + oy
    return turn(jnp.where(mask, beside, cells), -oy)


FROM = 5


def group_masks(start):
    lane, sub = lanes(), subs()
    row = (sub + start) & (TILE_X - 1)
    col = lane & (TILE_Y - 1)
    masks, bits = {}, {}
    for o in (1, 2, 3):
        masks["col", o] = col >= TILE_Y - o
        masks["col", -o] = col < o
        masks["row", o] = row >= TILE_X - o
        masks["row", -o] = row < o
    for ox in range(-3, 4):
        bits[ox] = jnp.left_shift(jnp.int32(1), 4 * row + ((row + ox) & 7) // 2)
    return masks, bits


def group_first(cell, word, keep, start=FROM):
    masks, bits = group_masks(start)
    zero = [cell(f, 0, 0) for f in range(4)]
    fx = jnp.zeros((8, PTS), F32)
    fy = jnp.zeros((8, PTS), F32)
    plain = [word(slot(dx, 0)) for dx in (-1, 0, 1)]
    for oy in SIDEWAYS:
        words = plain
        if oy:
            words = [jnp.where(masks["col", oy], word(slot(dx, sign(oy))), plain[dx + 1]) for dx in (-1, 0, 1)]
        base_y, base_v = zero[1] - float(oy), zero[3] - float(oy)
        for number, (ox, other) in enumerate(OFFSETS):
            if other != oy:
                continue
            picked = words[1]
            if ox:
                picked = jnp.where(masks["row", ox], words[sign(ox) + 1], picked)
            intact = (picked & bits[ox]) != 0
            rest_x = cell(0, oy, ox) - (zero[0] - float(ox))
            rest_y = cell(1, oy, ox) - base_y
            now_x = cell(2, oy, ox) - (zero[2] - float(ox))
            now_y = cell(3, oy, ox) - base_v
            rest_sq = rest_x * rest_x + rest_y * rest_y + DELTA_SQ
            now_sq = now_x * now_x + now_y * now_y + DELTA_SQ
            rest_inv = lax.rsqrt(rest_sq)
            reach = jnp.maximum(1.0 - rest_sq * rest_inv * (1.0 / HORIZON), 0.0)
            weight = jnp.where(intact, reach * reach, 0.0)
            level = weight * rest_inv
            keep(number, weight, level)
            factor = level - weight * lax.rsqrt(now_sq)
            fx = fx + factor * now_x
            fy = fy + factor * now_y
    return fx, fy


def group_second(cell, kept):
    zero = [cell(f, 0, 0) for f in range(2)]
    fx = jnp.zeros((8, PTS), F32)
    fy = jnp.zeros((8, PTS), F32)
    for number, (ox, oy) in enumerate(OFFSETS):
        now_x = cell(0, oy, ox) - (zero[0] - float(ox))
        now_y = cell(1, oy, ox) - (zero[1] - float(oy))
        now_sq = now_x * now_x + now_y * now_y + DELTA_SQ
        weight, level = kept(number)
        factor = level - weight * lax.rsqrt(now_sq)
        fx = fx + factor * now_x
        fy = fy + factor * now_y
    return fx, fy


def bending_of(row):
    here = row(0)
    one, two = row(-1) + row(1), row(-2) + row(2)
    beside = 2.0 * one - 8.0 * here
    out = two - 8.0 * one + 20.0 * here
    return out + turn(beside + turn(here, 1), 1) + turn(beside + turn(here, -1), -1)


def joined(low_part, high_part):
    return jnp.left_shift(high_part.astype(I32), 16) | low_part.astype(I32)


def widen(row_of, count):
    lane, sub = lanes(), subs()
    index = sub * TILE_Y + (lane % 64) // SPLIT
    out = []
    for j in range(count):
        left, right = (
            pick_lanes(jnp.broadcast_to(row_of(b), (8, PTS)), index) for b in (2 * j, 2 * j + 1)
        )
        out.append(jnp.where(lane < 64, left, right))
    return out


def narrow(block_of, tiles):
    lane, sub = lanes(), subs()
    out, sums = [], {}
    for b in tiles:
        if b // 2 not in sums:
            held = block_of(b // 2)
            held = held + turn(held, -1)
            sums[b // 2] = held + turn(held, -2)
        held = sums[b // 2]
        picked = pick_lanes(held, 64 * (b % 2) + SPLIT * (lane % TILE_Y))
        out.append(jnp.sum(jnp.where(sub == lane // TILE_Y, picked, 0.0), axis=0, keepdims=True))
    return out


def lay_out(ref, at, j, block):
    for row in range(TILE_X):
        ref[at + (row, slice(None), slice(j * PTS, (j + 1) * PTS))] = jnp.broadcast_to(block[row : row + 1], (8, PTS))


class Place:
    def __init__(self, nx, ny, shell_rows, shell_cols):
        self.nx, self.ny = nx, ny
        self.gx, self.gy = lax.axis_index("gx"), lax.axis_index("gy")
        self.shell_rows, self.shell_cols = shell_rows, shell_cols
        self.width = shell_cols * ny
        self.band = shell_rows * nx // TILE_X
        self.bands = shell_rows // self.band
        self.front = self.gx == nx - 1

    def sides(self, first, second):
        even = self.gy % 2 == 0
        right = jnp.where(even, first, second)
        left = jnp.where(even, second, first)
        right = jnp.where(self.gy < self.ny - 1, right, 0.0)
        left = jnp.where(self.gy > 0, left, 0.0)
        return right, left

    def nodes(self, row, columns):
        shape = (8, columns)
        col = lax.broadcasted_iota(I32, shape, 1)
        if columns > self.shell_cols:
            col = jnp.where(col >= self.shell_cols + 64, col - columns, col)
        first = (self.gx * self.shell_rows + row) * self.width + self.gy * self.shell_cols
        return (first + lax.broadcasted_iota(I32, shape, 0) * self.width + col).astype(F32)

    def parts(self):
        inner = [list(range(p * self.band, (p + 1) * self.band, 8)) for p in range(self.bands)]
        return [[-8]] + inner + [[self.shell_rows]]

    def band_of(self, row):
        return jnp.clip((self.gx * self.shell_rows + row + self.band) // self.band - 1, 0, TILE_X - 1)


Y_ROWS = 88


def fetch(pairs, sems):
    copies = [pltpu.make_async_copy(source, target, sems.at[n]) for n, (source, target) in enumerate(pairs)]
    for copy in copies:
        copy.start()
    for copy in copies:
        copy.wait()


def pack_sides(place_args, *refs):
    sources, (first, second), held = refs[:8], refs[8:10], refs[10:16]
    shell, speed, wide_ref, sems = refs[16:]
    place = Place(*place_args)
    pairs = list(zip(sources[:6], held))
    for source, target in zip(sources[6:], (shell, speed)):
        for n, at in enumerate((0, place.shell_cols - PTS)):
            pairs.append((source.at[:, pl.ds(at, PTS)], target.at[n]))
    fetch(pairs, sems)
    disp, vel, jit, words, node, inter = held
    tiles = disp.shape[2]
    even = place.gy % 2 == 0
    blocks = place.shell_cols // PTS
    numbers = node[...].astype(F32)
    edge_blocks = (0, blocks - 1)
    for j in edge_blocks:
        lay_out(wide_ref, (), j, widen(lambda b: numbers[b : b + 1], blocks)[j])
    held = {}
    for j in edge_blocks:
        total = jnp.zeros((8, PTS), F32)
        for part in range(place.bands):
            summed = jnp.zeros((8, PTS), F32)
            for row in range(part * place.band, (part + 1) * place.band, 8):
                wanted = wide_ref[place.band_of(row), :, j * PTS : (j + 1) * PTS]
                ids = place.nodes(row, PTS) + float(j * PTS)
                summed = summed + jnp.where(wanted == ids, shell[min(j, 1), row : row + 8, :], 0.0)
            summed = jnp.sum(summed, axis=0, keepdims=True)
            total = total + jnp.where(subs() == place.band_of(part * place.band), summed, 0.0)
        held[j] = total
    met = narrow(lambda j: held[j], (0, tiles - 1))

    ends = [(jnp.transpose(x[1])[PTS - 8 :], jnp.transpose(x[0])[:8]) for x in (shell, speed)]

    def send(ref, to_right):
        edge = jnp.where(to_right, tiles - 1, 0)
        for f, source in enumerate((disp, disp, vel, vel, jit, jit)):
            ref[8 * f : 8 * f + 8, :] = jnp.where(
                to_right, source[f % 2, :, tiles - 1, :], source[f % 2, :, 0, :]
            )
        ref[48:Y_ROWS, :] = jnp.zeros((Y_ROWS - 48, PTS), F32)
        edge_words = jnp.where(to_right, words[:, tiles - 1, :], words[:, 0, :])
        ref[48:56, 0:9] = (edge_words & 65535).astype(F32)
        ref[56:64, 0:9] = jnp.right_shift(edge_words, 16).astype(F32)
        ref[64:65, :] = jnp.where(to_right, numbers[tiles - 1 : tiles], numbers[0:1])
        ref[65:66, :] = jnp.where(to_right, inter[tiles - 1 : tiles, :], inter[0:1, :])
        ref[66:67, :] = jnp.where(to_right, met[1], met[0])
        for f, source in enumerate((shell, speed)):
            ref[72 + 8 * f : 80 + 8 * f, :] = jnp.where(to_right, *ends[f])

    send(first, even)
    send(second, jnp.logical_not(even))


def own_parts(place_args, far_shell, far_speed, disp, vel, jit, words, node, *refs):
    place = Place(*place_args)
    shell, speed, lattice, lead, rows_w, shore, tall, tall_v, wide_ref, sems = refs
    rows_a, tiles = disp.shape[1], disp.shape[2]
    rows, cols = place.shell_rows, place.shell_cols
    lane = lanes()
    west, east = place.gy == 0, place.gy == place.ny - 1
    north, south = place.gx == 0, place.gx == place.nx - 1
    span = pl.ds(PAD, rows)
    copies = [
        pltpu.make_async_copy(source, target, sems.at[n])
        for n, (source, target) in enumerate(
            (
                (far_shell, shell),
                (far_speed, speed),
                (far_shell, tall.at[span]),
                (far_speed, tall_v.at[span]),
            )
        )
    ]
    for copy in copies:
        copy.start()
    for ref in (tall, tall_v):
        ref[0:PAD, :] = jnp.zeros((PAD, cols), F32)
        ref[PAD + rows :, :] = jnp.zeros((PAD, cols), F32)

    @pl.loop(0, 2)
    def _(f):
        rest = [jit[f, a] for a in range(rows_a)]
        whole = [jit[f, a] + disp[f, a] for a in range(rows_a)]
        soon = [x + STEP_DT * vel[f, a] for a, x in enumerate(whole)]
        for a, (x, y, z) in enumerate(zip(flips(rest), flips(whole), flips(soon))):
            lattice[f, a] = x
            lattice[2 + f, a] = y
            lead[f, a] = z

    @pl.loop(0, rows_a)
    def _(a):
        packed = words[a]
        for dx in (-1, 0, 1):
            for dy in (-1, 0, 1):
                word = word_row(packed, slot(dx, dy))
                if dy < 0:
                    word = jnp.where((lane < TILE_Y) & west, 0, word)
                if dy > 0:
                    word = jnp.where((lane >= PTS - TILE_Y) & east, 0, word)
                if dx < 0:
                    word = jnp.where((a == 0) & north, 0, word)
                if dx > 0:
                    word = jnp.where((a == rows_a - 1) & south, 0, word)
                rows_w[slot(dx, dy), a] = word

    numbers = node[...].astype(F32)
    node_row = jnp.floor(numbers * (1.0 / place.width))
    node_col = numbers - node_row * place.width - (place.gy * cols).astype(F32)
    node_row = node_row - (place.gx * rows).astype(F32)
    at_row = widen(lambda b: node_row[b : b + 1], cols // PTS)
    at_col = jnp.concatenate(widen(lambda b: node_col[b : b + 1], cols // PTS), axis=1)
    col = lax.broadcasted_iota(I32, (8, cols), 1)
    split = col & (SPLIT - 1)
    near_row = jnp.concatenate(at_row, axis=1)
    near_row = jnp.where(split < SPLIT // 2, turn(near_row, SPLIT), turn(near_row, -SPLIT))
    for j, block in enumerate(at_row):
        lay_out(wide_ref, (0,), j, block)
        lay_out(wide_ref, (1,), j, near_row[:, j * PTS : (j + 1) * PTS])
    for copy in copies:
        copy.wait()
    sub_wide = lax.broadcasted_iota(I32, (8, cols), 0)
    row_wide = sub_wide.astype(F32)
    square = STEP_DT * STEP_DT * BEND
    sums = [jnp.zeros((8, cols), F32)] * 5
    for part in place.parts():
        found = [jnp.zeros((8, cols), F32)] * 5
        band = place.band_of(part[0])
        for row in part:
            at = PAD + row
            here = tall[at : at + 8, :]
            one = tall[at - 1 : at + 7, :] + tall[at + 1 : at + 9, :]
            two = tall[at - 2 : at + 6, :] + tall[at + 2 : at + 10, :]
            beside = 2.0 * one - 8.0 * here
            later = here + STEP_DT * tall_v[at : at + 8, :] - square * (two - 8.0 * one + 20.0 * here)
            hit = wide_ref[0, band] == row_wide + float(row)
            near = wide_ref[1, band] == row_wide + float(row)
            picks = ((hit, later), (hit, beside), (hit, here), (near, beside), (near, here))
            found = [x + jnp.where(mask, value, 0.0) for x, (mask, value) in zip(found, picks)]
        sums = [
            x + jnp.where(sub_wide == band, jnp.sum(y, axis=0, keepdims=True), 0.0) for x, y in zip(sums, found)
        ]
    later, beside, here, beside_near, here_near = sums
    spread = jnp.where(split < 3, turn(beside, -1), turn(beside_near, -1)) * (col < cols - 1).astype(F32)
    spread += jnp.where(split > 0, turn(beside, 1), turn(beside_near, 1)) * (col > 0).astype(F32)
    spread += jnp.where(split < 2, turn(here, -2), turn(here_near, -2)) * (col < cols - 2).astype(F32)
    spread += jnp.where(split > 1, turn(here, 2), turn(here_near, 2)) * (col > 1).astype(F32)
    hit = at_col == col.astype(F32)
    ahead = jnp.where(hit, later - square * spread, 0.0)
    met = jnp.where(hit, here, 0.0)
    for base, values in ((0, ahead), (tiles, met)):
        for b, row in enumerate(narrow(lambda j: values[:, j * PTS : (j + 1) * PTS], range(tiles))):
            shore[base + b : base + b + 1, :] = row


ROWS_AT, LEAD_AT, SIDE_AT, WORD_AT, SHELL_AT, HALO_ROWS = 2, 26, 32, 42, 50, 80
CONTACT_ROWS, OWN_ROWS = 18, 24


def shell_strip(right, left, at):
    middle = jnp.zeros((PTS - 16, PTS), F32)
    return jnp.transpose(jnp.concatenate([right[at : at + 8], middle, left[at : at + 8]], axis=0))


def pack_ends(
    place_args, shifts, disp, vel, jit, words, node, inter, shell, speed, lattice, lead, rows_w, shore, first, second, *refs
):
    place = Place(*place_args)
    outs = refs[: len(shifts)]
    own, strip_d, strip_v, grid, tall, wide_ref = refs[len(shifts) :]
    rows_a, tiles = disp.shape[1], disp.shape[2]
    rows, cols = place.shell_rows, place.shell_cols
    right, left = place.sides(first[...], second[...])
    lane, sub = lanes(), subs()
    leftward = (lane[0:1] & (TILE_Y - 1)) >= TILE_Y // 2
    last = rows_a - 1

    for f in range(4):
        for level, a in enumerate((last - 1, last)):
            at = 32 + 8 * (f % 2) + a
            row = jnp.where(leftward, left[at : at + 1], right[at : at + 1])
            if f >= 2:
                at = 8 * (f % 2) + a
                row = row + jnp.where(leftward, left[at : at + 1], right[at : at + 1])
            near = side_columns(row)
            for n, oy in enumerate(SIDEWAYS):
                grid[f, n, 8 * level : 8 * level + 8, :] = sideways(lattice[f, a], near, oy)
        for n in range(len(SIDEWAYS)):
            grid[f, n, 16:24, :] = jnp.zeros((8, PTS), F32)
    force, _ = group_first(
        lambda f, oy, ox: grid[f, SIDEWAYS.index(oy), 8 + ox : 16 + ox, :],
        lambda s: rows_w[s, last] if s < 6 else jnp.zeros((8, PTS), I32),
        lambda number, weight, level: None,
        start=0,
    )
    gap = disp[0, last] + inter[...]
    own[0:8, :] = gap + STEP_DT * (vel[0, last] + STEP_DT * flip(force))
    own[8:16, :] = gap
    own[16:17, :] = right[last : last + 1] + right[65:66]
    own[17:18, :] = left[last : last + 1] + left[65:66]

    halo_d = shell_strip(right, left, 72)
    halo_v = shell_strip(right, left, 80)
    strip_d[...] = halo_d
    strip_v[...] = halo_v
    for at in (0, 8, PAD + rows, PAD + rows + 8):
        tall[at : at + 8, :] = jnp.zeros((8, PTS), F32)
    tall[PAD : PAD + rows, :] = halo_d
    numbers = node[...].astype(F32)
    blocks = widen(lambda b: numbers[b : b + 1], cols // PTS)
    low = lane < PTS // 2
    lay_out(wide_ref, (), 0, jnp.where(low, blocks[0], blocks[-1]))
    far = jnp.where(low, 0.0, float(cols - PTS))
    ahead = jnp.zeros((8, PTS), F32)
    for part in place.parts():
        soon = jnp.zeros((8, PTS), F32)
        band = place.band_of(part[0])
        for row in part:
            at = PAD + row
            here = tall[at : at + 8, :]
            column = 2.0 * (tall[at - 1 : at + 7, :] + tall[at + 1 : at + 9, :]) - 8.0 * here
            from_left = turn(jnp.where(low, 0.0, column), 1) + turn(jnp.where(low, 0.0, here), 2)
            from_right = turn(jnp.where(low, column, 0.0), -1) + turn(jnp.where(low, here, 0.0), -2)
            hit = wide_ref[band] == place.nodes(row, PTS) + far
            soon = soon + jnp.where(hit, jnp.where(low, from_left, from_right), 0.0)
        ahead = ahead + jnp.where(sub == band, jnp.sum(soon, axis=0, keepdims=True), 0.0)
    base = OWN_ROWS
    own[base : base + 16, :] = shore[...]
    for b, row in zip((0, tiles - 1), narrow(lambda j: ahead, (0, tiles - 1))):
        own[base + b : base + b + 1, :] = shore[b : b + 1, :] - (STEP_DT * STEP_DT * BEND) * row
    own[base + 16 : base + 17, :] = right[66:67]
    own[base + 17 : base + 18, :] = left[66:67]

    mine = jnp.where(place.front, own[0:CONTACT_ROWS, :], own[base : base + CONTACT_ROWS, :])
    for shift, out in zip(shifts, outs):
        at = 0
        if shift & (shift + 1) == 0:
            at = HALO_ROWS
            down = (place.gx ^ shift) > place.gx
            out[0:ROWS_AT, :] = jnp.zeros((ROWS_AT, PTS), F32)
            for f in range(4):
                to = ROWS_AT + 6 * f
                out[to : to + 6, :] = jnp.where(down, lattice[f, last, 2:8, :], lattice[f, 0, 0:6, :])
            for f in range(2):
                to = LEAD_AT + 3 * f
                out[to : to + 3, :] = jnp.where(down, lead[f, last, 5:8, :], lead[f, 0, 0:3, :])

                def merged(part):
                    rows_of = [x[8 * part + a : 8 * part + a + 1] for a in (last, 0) for x in (left, right)]
                    return jnp.where(leftward, jnp.where(down, rows_of[0], rows_of[2]), jnp.where(down, rows_of[1], rows_of[3]))

                rest = merged(4 + f)
                whole = rest + merged(f)
                for n, values in enumerate((rest, whole, whole + STEP_DT * merged(2 + f))):
                    out[SIDE_AT + 2 * n + f : SIDE_AT + 2 * n + f + 1, :] = values
            for n, values in enumerate((left, right)):
                for part in range(2):
                    to, row = SIDE_AT + 6 + 2 * n + part, 48 + 8 * part
                    out[to : to + 1, :] = jnp.where(down, values[row + last : row + last + 1], values[row : row + 1])
            out[WORD_AT : WORD_AT + 8, :] = jnp.zeros((8, PTS), F32)
            edge_words = jnp.where(down, words[last], words[0])
            out[WORD_AT : WORD_AT + 8, 0:9] = (edge_words & 65535).astype(F32)
            out[WORD_AT : WORD_AT + 8, 16:25] = jnp.right_shift(edge_words, 16).astype(F32)
            for j in range(WIDE // PTS):
                cut = slice(j * PTS, (j + 1) * PTS)
                if j < cols // PTS:
                    d_low, d_high = shell[0:4, cut], shell[rows - 4 : rows, cut]
                    v_low, v_high = speed[0:2, cut], speed[rows - 2 : rows, cut]
                else:
                    d_low, d_high = halo_d[0:4], halo_d[rows - 4 : rows]
                    v_low, v_high = halo_v[0:2], halo_v[rows - 2 : rows]
                to = SHELL_AT + 6 * j
                out[to : to + 4, :] = jnp.where(down, d_high, d_low)
                out[to + 4 : to + 6, :] = jnp.where(down, v_high, v_low)
        out[at : at + CONTACT_ROWS, :] = mine


def inner_rows(place_args, disp, jit, shell, speed, lattice, rows_w, first, second, strip_d, strip_v, *refs):
    place = Place(*place_args)
    win, weights, levels, flat, beside, mid, strips, kinds, panes, hold, side = refs
    cols = place.shell_cols
    rows_a, tiles = disp.shape[1], disp.shape[2]
    right, left = place.sides(first[...], second[...])
    lane = lanes()
    leftward = (lane & (TILE_Y - 1)) >= TILE_Y // 2
    for f in range(6):
        side[f] = jnp.where(leftward, left[8 * f : 8 * f + 8], right[8 * f : 8 * f + 8])

    strips[...] = jnp.zeros_like(strips)

    @pl.loop(0, 2)
    def _(c):
        for part in range(2):
            f = c + 2 * part
            whole = jit[c] + disp[c] if part else jit[c]
            beyond = side[4 + c] + side[c] if part else side[4 + c]
            strips[f, 0, 8:16, :] = beyond
            strips[f, 1, 8:16, :] = turn(whole[:, 0, :], TILE_Y)
            strips[f, 2, 8:16, :] = turn(whole[:, tiles - 1, :], -TILE_Y)
            nears = [side_columns(beyond[a : a + 1]) for a in range(rows_a)]
            for a, near in enumerate(nears):
                cells = lattice[f, a]
                for n, oy in enumerate(SIDEWAYS):
                    shifted = sideways(cells, near, oy)
                    if a < rows_a - 1:
                        win[f, n, a, 0:8, :] = shifted
                    if a > 0:
                        win[f, n, a - 1, 8:16, :] = shifted

    left_words = joined(left[48:56], left[56:64])
    right_words = joined(right[48:56], right[56:64])
    for s in range(9):
        kinds[s] = jnp.where(
            leftward,
            jnp.broadcast_to(left_words[:, s : s + 1], (8, PTS)),
            jnp.broadcast_to(right_words[:, s : s + 1], (8, PTS)),
        )

    flat[...] = jnp.zeros_like(flat)

    blocks = mid.shape[0]

    for n in range(blocks):
        panes[n, :, 0:cols] = shell[8 * n : 8 * n + 24, :]
        panes[n, :, cols:WIDE] = strip_d[8 * n : 8 * n + 24, :]

    each = -(-blocks // (rows_a - 1))

    def bend_block(n):
        at = pl.multiple_of(8 * n + 8, 8)
        bending = bending_of(lambda o: panes[n, 8 + o : 16 + o, :])
        mid[n, :, 0:cols] = speed[pl.ds(at, 8), :] - (STEP_DT * BEND) * bending[:, 0:cols]
        mid[n, :, cols:WIDE] = strip_v[pl.ds(at, 8), :] - (STEP_DT * BEND) * bending[:, cols:WIDE]

    hold[...] = jnp.zeros_like(hold)
    reach_y = len(SIDEWAYS) // 2

    def side_bonds(k):
        masks, bits = lane_masks()
        oy = k - reach_y
        at = jnp.where(oy > 0, 1, jnp.where(oy < 0, 2, 0))
        towards = jnp.where(oy > 0, 1, jnp.where(oy < 0, -1, 0)) + 1
        col = lane & (TILE_Y - 1)
        crossed = (col < oy) | (col >= TILE_Y + oy)
        crossing = (col >= TILE_Y - oy) | (col < -oy)
        cells = [
            {
                dx: pltpu.roll(
                    jnp.where(crossed, strips[f, at, 8 + dx : 16 + dx, :], strips[f, 0, 8 + dx : 16 + dx, :]),
                    (PTS - oy) & (PTS - 1),
                    1,
                )
                for dx in (-1, 0, 1)
            }
            for f in range(4)
        ]
        words = [jnp.where(crossing, kinds[3 * dx + towards], kinds[3 * dx + 1]) for dx in range(3)]
        zero = [strips[f, 0, 8:16, :] for f in range(4)]
        step = oy.astype(F32)
        base_y, base_v = zero[1] - step, zero[3] - step
        fx, fy = hold[0], hold[1]
        for ox in range(-3, 4):
            word = words[1]
            if ox:
                word = jnp.where(masks["row_from", ox], words[sign(ox) + 1], word)
            rest_x = across(cells[0], ox, masks) - (zero[0] - float(ox))
            rest_y = across(cells[1], ox, masks) - base_y
            now_x = across(cells[2], ox, masks) - (zero[2] - float(ox))
            now_y = across(cells[3], ox, masks) - base_v
            rest_sq = rest_x * rest_x + rest_y * rest_y + DELTA_SQ
            now_sq = now_x * now_x + now_y * now_y + DELTA_SQ
            rest_inv = lax.rsqrt(rest_sq)
            reach = jnp.maximum(1.0 - rest_sq * rest_inv * (1.0 / HORIZON), 0.0)
            weight = jnp.where((word & bits[ox]) != 0, reach * reach, 0.0)
            factor = weight * (rest_inv - lax.rsqrt(now_sq))
            fx, fy = fx + factor * now_x, fy + factor * now_y
        hold[0], hold[1] = fx, fy

    if rows_a - 1 != len(SIDEWAYS):
        pl.loop(0, len(SIDEWAYS))(side_bonds)

    @pl.loop(0, rows_a - 1)
    def _(k):
        if rows_a - 1 == len(SIDEWAYS):
            side_bonds(k)
        for part in range(each):
            bend_block(jnp.minimum(each * k + part, blocks - 1))

        def cell(f, oy, ox):
            return win[f, SIDEWAYS.index(oy), k, FROM + ox : FROM + ox + 8, :]

        def keep(number, weight, level):
            weights[number, k] = weight
            levels[number, k] = level

        upper = subs() < TILE_X - FROM
        grouped = [jnp.where(upper, rows_w[s, k], rows_w[s, k + 1]) for s in range(9)]
        fx, fy = group_first(cell, grouped.__getitem__, keep)
        at = pl.multiple_of(8 * k + 16, 8)
        flat[0, pl.ds(at, 8), :] = fx
        flat[1, pl.ds(at, 8), :] = fy

    for f in range(2):
        moved_side = side[4 + f] + side[f] + STEP_DT * (side[2 + f] + STEP_DT * hold[f])
        for a in range(rows_a):
            beside[f, a] = side_columns(moved_side[a : a + 1])


def both_steps(place_args, shifts, *refs):
    place = Place(*place_args)
    disp, vel, node, inter, shell, speed, first, second, own, strip_d, strip_v = refs[:11]
    lead, rows_w, win, weights, levels, flat_in, beside, mid = refs[11:19]
    ends = refs[19 : 19 + len(shifts)]
    targets = refs[19 + len(shifts) : 23 + len(shifts)]
    scratch = refs[23 + len(shifts) :]
    out_disp, out_vel, out_shell, out_speed, gaps, halo, rim, rim_v, panes, fasts, hits, goals, ewin, ewords = scratch[:14]
    eweights, elevels, flat, flat2, seams, kinds, swin, sems = scratch[14:]
    outs = (out_disp, out_vel, out_shell, out_speed)
    copies = [pltpu.make_async_copy(x, y, sems.at[n]) for n, (x, y) in enumerate(zip(outs, targets))]
    rows_a, tiles = disp.shape[1], disp.shape[2]
    rows, cols = place.shell_rows, place.shell_cols
    blocks = rows // 8
    right, left = place.sides(first[...], second[...])

    halo[...] = jnp.zeros_like(halo)
    contact = jnp.where(place.front, own[0:CONTACT_ROWS, :], 0.0)
    owners = own[OWN_ROWS : OWN_ROWS + CONTACT_ROWS, :]
    for shift, ref in zip(shifts, ends):
        partner = place.gx ^ shift
        at = 0
        if shift & (shift + 1) == 0:
            at = HALO_ROWS

            @pl.when(partner == place.gx - 1)
            def _():
                halo[0] = ref[0:HALO_ROWS, :]

            @pl.when(partner == place.gx + 1)
            def _():
                halo[1] = ref[0:HALO_ROWS, :]

        got = ref[at : at + CONTACT_ROWS, :]
        contact = jnp.where(partner == place.nx - 1, got, contact)
        owners = owners + got

    def wide(source, strip, row, count):
        return jnp.concatenate([source[row : row + count, :], strip[row : row + count, :]], axis=1)

    zeros = jnp.zeros((8, WIDE), F32)
    rim[0, 16:32, :] = wide(shell, strip_d, 0, 16)
    rim[1, 0:16, :] = wide(shell, strip_d, rows - 16, 16)
    rim_v[0, 8:16, :] = wide(speed, strip_v, 0, 8)
    rim_v[1, 0:8, :] = wide(speed, strip_v, rows - 8, 8)
    for ref, at in ((rim, (0, 0)), (rim, (0, 8)), (rim, (1, 16)), (rim, (1, 24)), (rim_v, (0, 0)), (rim_v, (1, 8))):
        ref[at[0], at[1] : at[1] + 8, :] = zeros
    for j in range(WIDE // PTS):
        cut = slice(j * PTS, (j + 1) * PTS)
        at = SHELL_AT + 6 * j
        rim[0, 12:16, cut] = halo[0, at : at + 4, :]
        rim_v[0, 6:8, cut] = halo[0, at + 4 : at + 6, :]
        rim[1, 16:20, cut] = halo[1, at : at + 4, :]
        rim_v[1, 8:10, cut] = halo[1, at + 4 : at + 6, :]
    numbers = node[...].astype(F32)
    node_rows = [numbers[b : b + 1] for b in range(tiles)] + [right[64:65], left[64:65]]
    gap_rows = [contact[8 + b : 9 + b] for b in range(tiles)] + [contact[16:17], contact[17:18]]
    soon_rows = [contact[b : b + 1] for b in range(tiles)]
    for j, (nodes, gap) in enumerate(zip(widen(node_rows.__getitem__, 5), widen(gap_rows.__getitem__, 5))):
        lay_out(gaps, (0,), j, nodes)
        lay_out(gaps, (1,), j, gap)
    for j, soon in enumerate(widen(soon_rows.__getitem__, 4)):
        lay_out(gaps, (2,), j, soon)
    col = lax.broadcasted_iota(I32, (8, WIDE), 1)
    inside = jnp.where(col < cols, 1.0, 0.0)
    inside = jnp.where((col >= cols) & (col < cols + 64) & (place.gy < place.ny - 1), 1.0, inside)
    inside = jnp.where((col >= cols + 64) & (place.gy > 0), 1.0, inside)

    def first_rows(n, here, steady, keep=None):
        band = place.band_of(8 * n)
        hit = jnp.where(gaps[0, band] == place.nodes(8 * n, WIDE), STEP_DT * PENALTY, 0.0)
        push = hit * jnp.maximum(gaps[1, band] - here, 0.0)
        fast = steady + push
        there = (here + STEP_DT * fast) * (inside if keep is None else inside * keep)
        return there, fast[:, 0:cols], hit[:, 0:cols], gaps[2, band, :, 0:cols] - STEP_DT * push[:, 0:cols]

    for n in (-1, 0, blocks - 1, blocks):
        end = 0 if n < 1 else 1
        at = 8 * n + 16 if end == 0 else 8 * n - rows + 16
        bending = bending_of(lambda o: rim[end, at + o : at + o + 8, :])
        steady = rim_v[end, at - 8 : at, :] - (STEP_DT * BEND) * bending
        keep = None
        if n < 0:
            keep = jnp.where(place.gx > 0, 1.0, 0.0)
        elif n == blocks:
            keep = jnp.where(place.gx < place.nx - 1, 1.0, 0.0)
        there, *rest = first_rows(n, rim[end, at : at + 8, :], steady, keep)
        for part in (-1, 0, 1):
            if 0 <= n - part < blocks:
                panes[n - part, 8 + 8 * part : 16 + 8 * part, :] = there
        if 0 <= n < blocks:
            fasts[n], hits[n], goals[n] = rest

    def inner_block(n):
        at = pl.ds(pl.multiple_of(8 * n, 8), 8)
        there, *rest = first_rows(n, jnp.concatenate([shell[at, :], strip_d[at, :]], axis=1), mid[n - 1])
        for part in (-1, 0, 1):
            panes[n - part, 8 + 8 * part : 16 + 8 * part, :] = there
        fasts[n], hits[n], goals[n] = rest

    @pl.loop(0, (blocks - 2) // 2)
    def _(k):
        inner_block(2 * k + 1)
        inner_block(2 * k + 2)

    lane, sub = lanes(), subs()
    west, east = place.gy == 0, place.gy == place.ny - 1
    north, south = place.gx == 0, place.gx == place.nx - 1
    leftward = (lane & (TILE_Y - 1)) >= TILE_Y // 2
    last = rows_a - 1
    high = lane >= PTS // 2
    segment = ((lane + 16) >> 5) & 3

    def near_row(a, part):
        at = 8 * part + a
        return jnp.where(leftward[0:1], left[at : at + 1], right[at : at + 1])

    border = (-1, 0, last, rows_a)
    sides = {}
    for f in range(2):
        for a in (0, last):
            rest = near_row(a, 4 + f)
            whole = rest + near_row(a, f)
            sides[a, f] = (rest, whole, whole + STEP_DT * near_row(a, 2 + f))
        for a, end in ((-1, 0), (rows_a, 1)):
            sides[a, f] = [halo[end, SIDE_AT + 2 * n + f : SIDE_AT + 2 * n + f + 1, :] for n in range(3)]
    lead_side, far_lead = {}, {}
    straight = SIDEWAYS.index(0)
    for f in range(2):
        for a in border:
            lead_side[f, a] = side_columns(sides[a, f][2])
        at = LEAD_AT + 3 * f
        far_lead[f, 0], far_lead[f, 1] = halo[0, at - 5 : at + 3, :], halo[1, at : at + 8, :]
        for field in (f, 2 + f):
            cells, near = {}, {}
            for a in border:
                near[a] = side_columns(sides[a, f][field // 2])
            at = ROWS_AT + 6 * field
            cells[-1], cells[rows_a] = halo[0, at - 2 : at + 6, :], halo[1, at : at + 8, :]
            cells[0] = win[field, straight, 0, 0:8, :]
            cells[last] = win[field, straight, rows_a - 2, 8:16, :]
            for n, oy in enumerate(SIDEWAYS):
                ewin[field, n, 0, 0:8, :] = sideways(cells[-1], near[-1], oy)
                ewin[field, n, 0, 8:16, :] = win[field, n, 0, 0:8, :]
                ewin[field, n, 1, 0:8, :] = win[field, n, rows_a - 2, 8:16, :]
                ewin[field, n, 1, 8:16, :] = sideways(cells[rows_a], near[rows_a], oy)
            for half, (up, down) in enumerate(((-1, last), (0, rows_a))):
                pieces = [
                    jnp.where(high, near[up], cells[up]),
                    turn(jnp.where(high, cells[up], near[up]), 32),
                    turn(jnp.where(high, near[down], cells[down]), 64),
                    turn(jnp.where(high, cells[down], near[down]), 96),
                ]
                seam = pieces[3]
                for q in (2, 1, 0):
                    seam = jnp.where(segment == q, pieces[q], seam)
                for n, oy in enumerate(SIDEWAYS):
                    seams[field, n, 8 * half : 8 * half + 8, :] = turn(seam, -oy)
    for end in (0, 1):
        packed = halo[end, WORD_AT : WORD_AT + 8, :]
        packed = joined(packed, turn(packed, -16))
        for dx in (-1, 0, 1):
            for dy in (-1, 0, 1):
                s = slot(dx, dy)
                word = word_row(packed, s)
                if dy < 0:
                    word = jnp.where((lane < TILE_Y) & west, 0, word)
                if dy > 0:
                    word = jnp.where((lane >= PTS - TILE_Y) & east, 0, word)
                pair = (word, rows_w[s, 0]) if end == 0 else (rows_w[s, last], word)
                ewords[s, end] = jnp.where(sub < TILE_X - FROM, *pair)
    parts = []
    for at in (0, 1):
        rows_w = []
        for a in (-1, last, 0, rows_a):
            for n, values in enumerate((left, right)):
                if 0 <= a <= last:
                    rows_w.append(values[48 + 8 * at + a : 49 + 8 * at + a])
                else:
                    row = SIDE_AT + 6 + 2 * n + at
                    rows_w.append(halo[0 if a < 0 else 1, row : row + 1, :])
        parts.append(jnp.concatenate(rows_w, axis=0))
    packed = joined(*parts)
    for dx in (-1, 0, 1):
        for dy in (-1, 0, 1):
            s = slot(dx, dy)
            word = jnp.broadcast_to(packed[:, s : s + 1], (8, PTS))
            upper, lower = jnp.where(sub == segment, word, 0), jnp.where(sub == segment + 4, word, 0)
            for step in (4, 2, 1):
                upper, lower = upper | pltpu.roll(upper, step, 0), lower | pltpu.roll(lower, step, 0)
            if dx < 0:
                lower = jnp.where((segment < 2) & north, 0, lower)
            if dx > 0:
                upper = jnp.where((segment >= 2) & south, 0, upper)
            kinds[s] = jnp.where(sub < TILE_X - FROM, upper, lower)

    flat[...] = flat_in[...]
    for e in (0, 1):

        def keep_end(number, weight, level, e=e):
            eweights[number, e] = weight
            elevels[number, e] = level

        found = group_first(
            lambda f, oy, ox: ewin[f, SIDEWAYS.index(oy), e, FROM + ox : FROM + ox + 8, :],
            lambda s: ewords[s, e],
            keep_end,
        )
        for f in range(2):
            flat[f, 8 + 8 * rows_a * e : 16 + 8 * rows_a * e, :] = found[f]
    seam_f = group_first(
        lambda f, oy, ox: seams[f, SIDEWAYS.index(oy), FROM + ox : FROM + ox + 8, :],
        lambda s: kinds[s],
        lambda number, weight, level: None,
    )

    here = jnp.where(place.front, 1.0, 0.0)
    push = PENALTY * here * jnp.maximum(contact[8:18] - owners[8:18], 0.0)
    side_push = side_columns(jnp.where(leftward[0:1], push[9:10], push[8:9]))
    push = push[0:8]
    push_rows = flip(push)

    square = STEP_DT * STEP_DT
    for f in range(2):
        force = pltpu.roll(seam_f[f], FROM, 0)
        above = square * jnp.where(high, force, turn(force, -32))
        below = square * jnp.where(high, turn(force, -64), turn(force, -96))
        nears = {-1: lead_side[f, -1] + above, rows_a: lead_side[f, rows_a] + below}
        nears[0] = jnp.where(sub < FROM, lead_side[f, 0] + above, beside[f, 0])
        nears[last] = jnp.where(sub < FROM, beside[f, last], lead_side[f, last] + below)
        if f == 0:
            nears[last] = nears[last] - square * side_push
        for a in range(-1, rows_a + 1):
            cells = far_lead[f, 0 if a < 0 else 1] if a in (-1, rows_a) else lead[f, a]
            cells = cells + square * flat[f, 8 * a + 11 : 8 * a + 19, :]
            if a == last and f == 0:
                cells = cells - square * push_rows
            near = nears[a] if a in nears else beside[f, a]
            for n, oy in enumerate(SIDEWAYS):
                shifted = sideways(cells, near, oy)
                if a < rows_a:
                    swin[f, n, a + 1, 0:8, :] = shifted
                if a >= 0:
                    swin[f, n, a, 8:16, :] = shifted

    def second_group(k, kept):
        def cell(f, oy, ox):
            return swin[f, SIDEWAYS.index(oy), k, FROM + ox : FROM + ox + 8, :]

        fx, fy = group_second(cell, kept)
        at = pl.multiple_of(8 * k + 8, 8)
        flat2[0, pl.ds(at, 8), :] = fx
        flat2[1, pl.ds(at, 8), :] = fy

    def second_rows(n):
        row = pl.multiple_of(8 * n, 8)
        here = panes[n, 8:16, 0:cols]
        push = hits[n] * jnp.maximum(goals[n] - here, 0.0)
        bending = bending_of(lambda o: panes[n, 8 + o : 16 + o, :])[:, 0:cols]
        fast = fasts[n] + push - (STEP_DT * BEND) * bending
        out_speed[pl.ds(row, 8), :] = fast
        out_shell[pl.ds(row, 8), :] = here + STEP_DT * fast

    inner = rows_a - 1
    each = blocks // rows_a

    @pl.loop(0, inner // 2)
    def _(j):
        for h in range(2):
            k = 2 * j + h
            second_group(k + 1, lambda number: (weights[number, k], levels[number, k]))
            for part in range(each):
                second_rows(each * k + part)

    k = inner - 1
    second_group(k + 1, lambda number: (weights[number, k], levels[number, k]))
    for part in range(each):
        second_rows(each * k + part)

    tail = blocks - each * inner
    half = -(-tail // 2)

    @pl.loop(0, 2)
    def _(e):
        second_group(e * rows_a, lambda number: (eweights[number, e], elevels[number, e]))
        for part in range(half):
            second_rows(jnp.minimum(each * inner + half * e + part, blocks - 1))

    copies[2].start()
    copies[3].start()

    for f in range(2):
        thens = flips([flat2[f, 8 * a + 11 : 8 * a + 19, :] for a in range(rows_a)])
        wases = flips([flat[f, 8 * a + 11 : 8 * a + 19, :] for a in range(rows_a)])
        for a in range(rows_a):
            was = wases[a]
            then = thens[a]
            if f == 0 and a == last:
                was = was - push
                gap = disp[0, last] + STEP_DT * (vel[0, last] + STEP_DT * was) + inter[...]
                reached = owners[0:8] + square * push
                then = then - PENALTY * here * jnp.maximum(gap - reached, 0.0)
            fast = vel[f, a] + STEP_DT * was
            faster = fast + STEP_DT * then
            out_vel[f, a] = faster
            out_disp[f, a] = disp[f, a] + STEP_DT * (fast + faster)
    copies[0].start()
    copies[1].start()
    for copy in copies:
        copy.wait()


def on_device(nx, ny, disp, vel, jit, words, node, inter, shell, speed):
    rows_a = disp.shape[1]
    rows, cols = shell.shape
    place_args = (nx, ny, rows, cols)
    shifts = tuple(range(1, nx))
    span, count, blocks = rows_a - 1, len(OFFSETS), rows // 8

    def call(body, out, scratch, *args, far=0, **more):
        args = [pltpu.with_memory_space_constraint(x, pltpu.MemorySpace.HBM) for x in args[:far]] + list(args[far:])
        specs = [pl.BlockSpec(memory_space=pltpu.MemorySpace.HBM)] * far
        specs += [pl.BlockSpec(memory_space=pltpu.VMEM)] * (len(args) - far)
        return pl.pallas_call(
            body,
            out_shape=out,
            in_specs=specs,
            scratch_shapes=scratch,
            **more,
            compiler_params=pltpu.CompilerParams(vmem_limit_bytes=20 * 1024 * 1024),
        )(*args)

    def shaped(*shape, dtype=F32):
        return jax.ShapeDtypeStruct(shape + (PTS,), dtype)

    def like(*arrays):
        return [jax.ShapeDtypeStruct(x.shape, x.dtype) for x in arrays]

    wide = pltpu.VMEM((TILE_X, 8, cols), F32)
    tall = pltpu.VMEM((rows + 2 * PAD, cols), F32)
    edges = pltpu.VMEM((2, rows, PTS), F32)
    far_shell, far_speed = shell, speed
    small = (disp, vel, jit, words, node, inter)
    first, second, *small = call(
        functools.partial(pack_sides, place_args),
        [shaped(Y_ROWS)] * 2 + like(*small),
        [edges, edges, wide, pltpu.SemaphoreType.DMA((10,))],
        *small,
        far_shell,
        far_speed,
        far=8,
    )
    disp, vel, jit, words, node, inter = small
    first = lax.ppermute(first, "gy", [(i, i ^ 1) for i in range(ny)])
    second = lax.ppermute(
        second,
        ("gx", "gy"),
        [
            (i * ny + j, i * ny + ((j - 1) ^ 1) + 1 if 0 < j < ny - 1 else (i ^ 1) * ny + j)
            for i in range(nx)
            for j in range(ny)
        ],
    )

    shell, speed, lattice, lead, rows_w, shore = call(
        functools.partial(own_parts, place_args),
        like(far_shell, far_speed)
        + [
            shaped(4, rows_a, 8),
            shaped(2, rows_a, 8),
            shaped(9, rows_a, 8, dtype=I32),
            shaped(2 * disp.shape[2]),
        ],
        [tall, tall, pltpu.VMEM((2, TILE_X, 8, cols), F32), pltpu.SemaphoreType.DMA((4,))],
        far_shell,
        far_speed,
        disp,
        vel,
        jit,
        words,
        node,
        far=2,
    )

    outs = [shaped(CONTACT_ROWS + (HALO_ROWS if s & (s + 1) == 0 else 0)) for s in shifts]
    *ends, own, strip_d, strip_v = call(
        functools.partial(pack_ends, place_args, shifts),
        outs + [shaped(2 * OWN_ROWS), shaped(rows), shaped(rows)],
        [
            pltpu.VMEM((4, len(SIDEWAYS), 24, PTS), F32),
            pltpu.VMEM((rows + 2 * PAD, PTS), F32),
            pltpu.VMEM((TILE_X, 8, PTS), F32),
        ],
        *small,
        shell,
        speed,
        lattice,
        lead,
        rows_w,
        shore,
        first,
        second,
    )
    ends = [lax.ppermute(e, "gx", [(i, i ^ s) for i in range(nx)]) for s, e in zip(shifts, ends)]

    inner = call(
        functools.partial(inner_rows, place_args),
        [
            shaped(4, len(SIDEWAYS), span, 16),
            shaped(count, span, 8),
            shaped(count, span, 8),
            shaped(2, 8 * (rows_a + 3)),
            shaped(2, rows_a, 8),
            jax.ShapeDtypeStruct((blocks - 2, 8, WIDE), F32),
        ],
        [
            pltpu.VMEM((4, 3, 24, PTS), F32),
            pltpu.VMEM((9, 8, PTS), I32),
            pltpu.VMEM((blocks - 2, 24, WIDE), F32),
            pltpu.VMEM((2, 8, PTS), F32),
            pltpu.VMEM((6, 8, PTS), F32),
        ],
        disp,
        jit,
        shell,
        speed,
        lattice,
        rows_w,
        first,
        second,
        strip_d,
        strip_v,
    )

    out = [jax.ShapeDtypeStruct(x.shape, F32) for x in (disp, vel, shell, speed)]
    scratch = [pltpu.VMEM(x.shape, F32) for x in out] + [
        pltpu.VMEM((3, TILE_X, 8, WIDE), F32),
        pltpu.VMEM((2, HALO_ROWS, PTS), F32),
        pltpu.VMEM((2, 32, WIDE), F32),
        pltpu.VMEM((2, 16, WIDE), F32),
        pltpu.VMEM((blocks, 24, WIDE), F32),
        pltpu.VMEM((blocks, 8, cols), F32),
        pltpu.VMEM((blocks, 8, cols), F32),
        pltpu.VMEM((blocks, 8, cols), F32),
        pltpu.VMEM((4, len(SIDEWAYS), 2, 16, PTS), F32),
        pltpu.VMEM((9, 2, 8, PTS), I32),
        pltpu.VMEM((count, 2, 8, PTS), F32),
        pltpu.VMEM((count, 2, 8, PTS), F32),
        pltpu.VMEM((2, 8 * (rows_a + 3), PTS), F32),
        pltpu.VMEM((2, 8 * (rows_a + 3), PTS), F32),
        pltpu.VMEM((4, len(SIDEWAYS), 16, PTS), F32),
        pltpu.VMEM((9, 8, PTS), I32),
        pltpu.VMEM((2, len(SIDEWAYS), rows_a + 1, 16, PTS), F32),
        pltpu.SemaphoreType.DMA((4,)),
    ]
    return tuple(
        call(
            functools.partial(both_steps, place_args, shifts),
            out,
            scratch,
            disp,
            vel,
            node,
            inter,
            shell,
            speed,
            first,
            second,
            own,
            strip_d,
            strip_v,
            lead,
            rows_w,
            *inner,
            *ends,
            out_specs=[pl.BlockSpec(memory_space=pltpu.MemorySpace.HBM)] * 4,
        )
    )


def solution(mesh):
    in_specs = (
        P(None, "gx", "gy", None),
        P(None, "gx", "gy", None),
        P(None, "gx", "gy", None),
        P("gx", "gy", None),
        P("gy", None),
        P("gy", None),
        P("gx", "gy"),
        P("gx", "gy"),
    )
    out_specs = (P(None, "gx", "gy", None), P(None, "gx", "gy", None), P("gx", "gy"), P("gx", "gy"))
    body = functools.partial(on_device, mesh.shape["gx"], mesh.shape["gy"])
    return jax.shard_map(body, mesh=mesh, in_specs=in_specs, out_specs=out_specs, check_vma=False)
```

```python
import functools

import jax
import jax.numpy as jnp
from jax import lax
from jax.experimental import pallas as pl
from jax.experimental.pallas import tpu as pltpu
from jax.sharding import PartitionSpec as P

TILE_X = 8
TILE_Y = 16
PTS = 128
SPLIT = 4

HORIZON = 3.5
DELTA_SQ = 0.25
PENALTY = 4.0
BEND = 0.5
STEP_DT = 0.2

F32 = jnp.float32
I32 = jnp.int32

STRIDE = 24
WIDE = 640
PAD = 16


def bond_offsets():
    limit = HORIZON * HORIZON - DELTA_SQ
    found = []
    for oy in range(-4, 5):
        for ox in range(-4, 5):
            near = max(abs(ox) - 0.4, 0.0) ** 2 + max(abs(oy) - 0.4, 0.0) ** 2
            if near < limit and (ox or oy):
                found.append((ox, oy))
    return found


OFFSETS = bond_offsets()
SIDEWAYS = sorted({oy for _, oy in OFFSETS})


def sign(value):
    return (value > 0) - (value < 0)


def lanes():
    return lax.broadcasted_iota(I32, (8, PTS), 1)


def subs():
    return lax.broadcasted_iota(I32, (8, PTS), 0)


def turn(values, shift):
    size = values.shape[1]
    return pltpu.roll(values, shift % size, 1) if shift % size else values


def slot(dx, dy):
    return 3 * (dx + 1) + dy + 1


def lane_masks():
    lane = lanes()
    row, col = lane // TILE_Y, lane % TILE_Y
    masks = {}
    for o in (1, 2, 3):
        masks["col_at", o] = col < o
        masks["col_at", -o] = col >= TILE_Y - o
        masks["col_from", o] = col >= TILE_Y - o
        masks["col_from", -o] = col < o
        masks["row_at", o] = row < o
        masks["row_at", -o] = row >= TILE_X - o
        masks["row_from", o] = row >= TILE_X - o
        masks["row_from", -o] = row < o
    bits = {}
    for ox in range(-3, 4):
        bits[ox] = jnp.left_shift(jnp.int32(1), 4 * row + ((row + ox) & 7) // 2)
    return masks, bits


def across(cells, ox, masks):
    if not ox:
        return cells[0]
    return turn(jnp.where(masks["row_at", ox], cells[sign(ox)], cells[0]), -TILE_Y * ox)


def pick_lanes(block, index):
    return jnp.take_along_axis(block, index, axis=1, mode="promise_in_bounds")


def flips(blocks):
    lane, sub = lanes(), subs()
    for level in (2, 1, 0):
        step = 1 << level
        stay = ((lane >> (level + 4)) ^ (sub >> level)) & 1 == 0
        if step == 4:
            others = [turn(pltpu.roll(block, 4, 0), 64) for block in blocks]
        else:
            low = (sub >> level) & 1 == 0
            index = lane ^ (TILE_Y * step)
            others = [jnp.where(low, pltpu.roll(block, 8 - step, 0), pltpu.roll(block, step, 0)) for block in blocks]
            others = [pick_lanes(block, index) for block in others]
        blocks = [jnp.where(stay, block, other) for block, other in zip(blocks, others)]
    return blocks


def flip(block):
    return flips([block])[0]


def side_columns(row):
    return pick_lanes(jnp.broadcast_to(row, (8, PTS)), TILE_Y * subs() + (lanes() & (TILE_Y - 1)))


def word_row(packed, s):
    word = jnp.where(subs() == lanes() // TILE_Y, jnp.broadcast_to(packed[:, s : s + 1], (8, PTS)), 0)
    for step in (4, 2, 1):
        word = word | pltpu.roll(word, step, 0)
    return word


def sideways(cells, beside, oy):
    if not oy:
        return cells
    lane = lanes()
    mask = lane < oy if oy > 0 else lane >= PTS + oy
    return turn(jnp.where(mask, beside, cells), -oy)


FROM = 5


def group_masks(start):
    lane, sub = lanes(), subs()
    row = (sub + start) & (TILE_X - 1)
    col = lane & (TILE_Y - 1)
    masks, bits = {}, {}
    for o in (1, 2, 3):
        masks["col", o] = col >= TILE_Y - o
        masks["col", -o] = col < o
        masks["row", o] = row >= TILE_X - o
        masks["row", -o] = row < o
    for ox in range(-3, 4):
        bits[ox] = jnp.left_shift(jnp.int32(1), 4 * row + ((row + ox) & 7) // 2)
    return masks, bits


def group_first(cell, word, keep, start=FROM):
    masks, bits = group_masks(start)
    zero = [cell(f, 0, 0) for f in range(4)]
    fx = jnp.zeros((8, PTS), F32)
    fy = jnp.zeros((8, PTS), F32)
    plain = [word(slot(dx, 0)) for dx in (-1, 0, 1)]
    for oy in SIDEWAYS:
        words = plain
        if oy:
            words = [jnp.where(masks["col", oy], word(slot(dx, sign(oy))), plain[dx + 1]) for dx in (-1, 0, 1)]
        base_y, base_v = zero[1] - float(oy), zero[3] - float(oy)
        for number, (ox, other) in enumerate(OFFSETS):
            if other != oy:
                continue
            picked = words[1]
            if ox:
                picked = jnp.where(masks["row", ox], words[sign(ox) + 1], picked)
            intact = (picked & bits[ox]) != 0
            rest_x = cell(0, oy, ox) - (zero[0] - float(ox))
            rest_y = cell(1, oy, ox) - base_y
            now_x = cell(2, oy, ox) - (zero[2] - float(ox))
            now_y = cell(3, oy, ox) - base_v
            rest_sq = rest_x * rest_x + rest_y * rest_y + DELTA_SQ
            now_sq = now_x * now_x + now_y * now_y + DELTA_SQ
            rest_inv = lax.rsqrt(rest_sq)
            reach = jnp.maximum(1.0 - rest_sq * rest_inv * (1.0 / HORIZON), 0.0)
            weight = jnp.where(intact, reach * reach, 0.0)
            level = weight * rest_inv
            keep(number, weight, level)
            factor = level - weight * lax.rsqrt(now_sq)
            fx = fx + factor * now_x
            fy = fy + factor * now_y
    return fx, fy


def group_second(cell, kept):
    zero = [cell(f, 0, 0) for f in range(2)]
    fx = jnp.zeros((8, PTS), F32)
    fy = jnp.zeros((8, PTS), F32)
    for number, (ox, oy) in enumerate(OFFSETS):
        now_x = cell(0, oy, ox) - (zero[0] - float(ox))
        now_y = cell(1, oy, ox) - (zero[1] - float(oy))
        now_sq = now_x * now_x + now_y * now_y + DELTA_SQ
        weight, level = kept(number)
        factor = level - weight * lax.rsqrt(now_sq)
        fx = fx + factor * now_x
        fy = fy + factor * now_y
    return fx, fy


def bending_of(row):
    here = row(0)
    one, two = row(-1) + row(1), row(-2) + row(2)
    beside = 2.0 * one - 8.0 * here
    out = two - 8.0 * one + 20.0 * here
    return out + turn(beside + turn(here, 1), 1) + turn(beside + turn(here, -1), -1)


def joined(low_part, high_part):
    return jnp.left_shift(high_part.astype(I32), 16) | low_part.astype(I32)


def widen(row_of, count):
    lane, sub = lanes(), subs()
    index = sub * TILE_Y + (lane % 64) // SPLIT
    out = []
    for j in range(count):
        left, right = (
            pick_lanes(jnp.broadcast_to(row_of(b), (8, PTS)), index) for b in (2 * j, 2 * j + 1)
        )
        out.append(jnp.where(lane < 64, left, right))
    return out


def narrow(block_of, tiles):
    lane, sub = lanes(), subs()
    out, sums = [], {}
    for b in tiles:
        if b // 2 not in sums:
            held = block_of(b // 2)
            held = held + turn(held, -1)
            sums[b // 2] = held + turn(held, -2)
        held = sums[b // 2]
        picked = pick_lanes(held, 64 * (b % 2) + SPLIT * (lane % TILE_Y))
        out.append(jnp.sum(jnp.where(sub == lane // TILE_Y, picked, 0.0), axis=0, keepdims=True))
    return out


def lay_out(ref, at, j, block):
    for row in range(TILE_X):
        ref[at + (row, slice(None), slice(j * PTS, (j + 1) * PTS))] = jnp.broadcast_to(block[row : row + 1], (8, PTS))


class Place:
    def __init__(self, nx, ny, shell_rows, shell_cols):
        self.nx, self.ny = nx, ny
        self.gx, self.gy = lax.axis_index("gx"), lax.axis_index("gy")
        self.shell_rows, self.shell_cols = shell_rows, shell_cols
        self.width = shell_cols * ny
        self.band = shell_rows * nx // TILE_X
        self.bands = shell_rows // self.band
        self.front = self.gx == nx - 1

    def sides(self, first, second):
        even = self.gy % 2 == 0
        right = jnp.where(even, first, second)
        left = jnp.where(even, second, first)
        right = jnp.where(self.gy < self.ny - 1, right, 0.0)
        left = jnp.where(self.gy > 0, left, 0.0)
        return right, left

    def nodes(self, row, columns):
        shape = (8, columns)
        col = lax.broadcasted_iota(I32, shape, 1)
        if columns > self.shell_cols:
            col = jnp.where(col >= self.shell_cols + 64, col - columns, col)
        first = (self.gx * self.shell_rows + row) * self.width + self.gy * self.shell_cols
        return (first + lax.broadcasted_iota(I32, shape, 0) * self.width + col).astype(F32)

    def parts(self):
        inner = [list(range(p * self.band, (p + 1) * self.band, 8)) for p in range(self.bands)]
        return [[-8]] + inner + [[self.shell_rows]]

    def band_of(self, row):
        return jnp.clip((self.gx * self.shell_rows + row + self.band) // self.band - 1, 0, TILE_X - 1)


Y_ROWS = 88


def fetch(pairs, sems):
    copies = [pltpu.make_async_copy(source, target, sems.at[n]) for n, (source, target) in enumerate(pairs)]
    for copy in copies:
        copy.start()
    for copy in copies:
        copy.wait()


def pack_sides(place_args, *refs):
    sources, (first, second), held = refs[:8], refs[8:10], refs[10:16]
    shell, speed, wide_ref, sems = refs[16:]
    place = Place(*place_args)
    pairs = list(zip(sources[:6], held))
    for source, target in zip(sources[6:], (shell, speed)):
        for n, at in enumerate((0, place.shell_cols - PTS)):
            pairs.append((source.at[:, pl.ds(at, PTS)], target.at[n]))
    fetch(pairs, sems)
    disp, vel, jit, words, node, inter = held
    tiles = disp.shape[2]
    even = place.gy % 2 == 0
    blocks = place.shell_cols // PTS
    numbers = node[...].astype(F32)
    edge_blocks = (0, blocks - 1)
    for j in edge_blocks:
        lay_out(wide_ref, (), j, widen(lambda b: numbers[b : b + 1], blocks)[j])
    held = {}
    for j in edge_blocks:
        total = jnp.zeros((8, PTS), F32)
        for part in range(place.bands):
            summed = jnp.zeros((8, PTS), F32)
            for row in range(part * place.band, (part + 1) * place.band, 8):
                wanted = wide_ref[place.band_of(row), :, j * PTS : (j + 1) * PTS]
                ids = place.nodes(row, PTS) + float(j * PTS)
                summed = summed + jnp.where(wanted == ids, shell[min(j, 1), row : row + 8, :], 0.0)
            summed = jnp.sum(summed, axis=0, keepdims=True)
            total = total + jnp.where(subs() == place.band_of(part * place.band), summed, 0.0)
        held[j] = total
    met = narrow(lambda j: held[j], (0, tiles - 1))

    ends = [(jnp.transpose(x[1])[PTS - 8 :], jnp.transpose(x[0])[:8]) for x in (shell, speed)]

    def send(ref, to_right):
        edge = jnp.where(to_right, tiles - 1, 0)
        for f, source in enumerate((disp, disp, vel, vel, jit, jit)):
            ref[8 * f : 8 * f + 8, :] = jnp.where(
                to_right, source[f % 2, :, tiles - 1, :], source[f % 2, :, 0, :]
            )
        ref[48:Y_ROWS, :] = jnp.zeros((Y_ROWS - 48, PTS), F32)
        edge_words = jnp.where(to_right, words[:, tiles - 1, :], words[:, 0, :])
        ref[48:56, 0:9] = (edge_words & 65535).astype(F32)
        ref[56:64, 0:9] = jnp.right_shift(edge_words, 16).astype(F32)
        ref[64:65, :] = jnp.where(to_right, numbers[tiles - 1 : tiles], numbers[0:1])
        ref[65:66, :] = jnp.where(to_right, inter[tiles - 1 : tiles, :], inter[0:1, :])
        ref[66:67, :] = jnp.where(to_right, met[1], met[0])
        for f, source in enumerate((shell, speed)):
            ref[72 + 8 * f : 80 + 8 * f, :] = jnp.where(to_right, *ends[f])

    send(first, even)
    send(second, jnp.logical_not(even))


def own_parts(place_args, far_shell, far_speed, disp, vel, jit, words, node, *refs):
    place = Place(*place_args)
    shell, speed, lattice, lead, rows_w, shore, tall, tall_v, wide_ref, sems = refs
    rows_a, tiles = disp.shape[1], disp.shape[2]
    rows, cols = place.shell_rows, place.shell_cols
    lane = lanes()
    west, east = place.gy == 0, place.gy == place.ny - 1
    north, south = place.gx == 0, place.gx == place.nx - 1
    span = pl.ds(PAD, rows)
    copies = [
        pltpu.make_async_copy(source, target, sems.at[n])
        for n, (source, target) in enumerate(
            (
                (far_shell, shell),
                (far_speed, speed),
                (far_shell, tall.at[span]),
                (far_speed, tall_v.at[span]),
            )
        )
    ]
    for copy in copies:
        copy.start()
    for ref in (tall, tall_v):
        ref[0:PAD, :] = jnp.zeros((PAD, cols), F32)
        ref[PAD + rows :, :] = jnp.zeros((PAD, cols), F32)

    @pl.loop(0, 2)
    def _(f):
        rest = [jit[f, a] for a in range(rows_a)]
        whole = [jit[f, a] + disp[f, a] for a in range(rows_a)]
        soon = [x + STEP_DT * vel[f, a] for a, x in enumerate(whole)]
        for a, (x, y, z) in enumerate(zip(flips(rest), flips(whole), flips(soon))):
            lattice[f, a] = x
            lattice[2 + f, a] = y
            lead[f, a] = z

    @pl.loop(0, rows_a)
    def _(a):
        packed = words[a]
        for dx in (-1, 0, 1):
            for dy in (-1, 0, 1):
                word = word_row(packed, slot(dx, dy))
                if dy < 0:
                    word = jnp.where((lane < TILE_Y) & west, 0, word)
                if dy > 0:
                    word = jnp.where((lane >= PTS - TILE_Y) & east, 0, word)
                if dx < 0:
                    word = jnp.where((a == 0) & north, 0, word)
                if dx > 0:
                    word = jnp.where((a == rows_a - 1) & south, 0, word)
                rows_w[slot(dx, dy), a] = word

    numbers = node[...].astype(F32)
    node_row = jnp.floor(numbers * (1.0 / place.width))
    node_col = numbers - node_row * place.width - (place.gy * cols).astype(F32)
    node_row = node_row - (place.gx * rows).astype(F32)
    at_row = widen(lambda b: node_row[b : b + 1], cols // PTS)
    at_col = jnp.concatenate(widen(lambda b: node_col[b : b + 1], cols // PTS), axis=1)
    col = lax.broadcasted_iota(I32, (8, cols), 1)
    split = col & (SPLIT - 1)
    near_row = jnp.concatenate(at_row, axis=1)
    near_row = jnp.where(split < SPLIT // 2, turn(near_row, SPLIT), turn(near_row, -SPLIT))
    for j, block in enumerate(at_row):
        lay_out(wide_ref, (0,), j, block)
        lay_out(wide_ref, (1,), j, near_row[:, j * PTS : (j + 1) * PTS])
    for copy in copies:
        copy.wait()
    sub_wide = lax.broadcasted_iota(I32, (8, cols), 0)
    row_wide = sub_wide.astype(F32)
    square = STEP_DT * STEP_DT * BEND
    sums = [jnp.zeros((8, cols), F32)] * 5
    for part in place.parts():
        found = [jnp.zeros((8, cols), F32)] * 5
        band = place.band_of(part[0])
        for row in part:
            at = PAD + row
            here = tall[at : at + 8, :]
            one = tall[at - 1 : at + 7, :] + tall[at + 1 : at + 9, :]
            two = tall[at - 2 : at + 6, :] + tall[at + 2 : at + 10, :]
            beside = 2.0 * one - 8.0 * here
            later = here + STEP_DT * tall_v[at : at + 8, :] - square * (two - 8.0 * one + 20.0 * here)
            hit = wide_ref[0, band] == row_wide + float(row)
            near = wide_ref[1, band] == row_wide + float(row)
            picks = ((hit, later), (hit, beside), (hit, here), (near, beside), (near, here))
            found = [x + jnp.where(mask, value, 0.0) for x, (mask, value) in zip(found, picks)]
        sums = [
            x + jnp.where(sub_wide == band, jnp.sum(y, axis=0, keepdims=True), 0.0) for x, y in zip(sums, found)
        ]
    later, beside, here, beside_near, here_near = sums
    spread = jnp.where(split < 3, turn(beside, -1), turn(beside_near, -1)) * (col < cols - 1).astype(F32)
    spread += jnp.where(split > 0, turn(beside, 1), turn(beside_near, 1)) * (col > 0).astype(F32)
    spread += jnp.where(split < 2, turn(here, -2), turn(here_near, -2)) * (col < cols - 2).astype(F32)
    spread += jnp.where(split > 1, turn(here, 2), turn(here_near, 2)) * (col > 1).astype(F32)
    hit = at_col == col.astype(F32)
    ahead = jnp.where(hit, later - square * spread, 0.0)
    met = jnp.where(hit, here, 0.0)
    for base, values in ((0, ahead), (tiles, met)):
        for b, row in enumerate(narrow(lambda j: values[:, j * PTS : (j + 1) * PTS], range(tiles))):
            shore[base + b : base + b + 1, :] = row


ROWS_AT, LEAD_AT, SIDE_AT, WORD_AT, SHELL_AT, HALO_ROWS = 2, 26, 32, 42, 50, 80
CONTACT_ROWS, OWN_ROWS = 18, 24


def shell_strip(right, left, at):
    middle = jnp.zeros((PTS - 16, PTS), F32)
    return jnp.transpose(jnp.concatenate([right[at : at + 8], middle, left[at : at + 8]], axis=0))


def pack_ends(
    place_args, shifts, disp, vel, jit, words, node, inter, shell, speed, lattice, lead, rows_w, shore, first, second, *refs
):
    place = Place(*place_args)
    outs = refs[: len(shifts)]
    own, strip_d, strip_v, grid, tall, wide_ref = refs[len(shifts) :]
    rows_a, tiles = disp.shape[1], disp.shape[2]
    rows, cols = place.shell_rows, place.shell_cols
    right, left = place.sides(first[...], second[...])
    lane, sub = lanes(), subs()
    leftward = (lane[0:1] & (TILE_Y - 1)) >= TILE_Y // 2
    last = rows_a - 1

    for f in range(4):
        for level, a in enumerate((last - 1, last)):
            at = 32 + 8 * (f % 2) + a
            row = jnp.where(leftward, left[at : at + 1], right[at : at + 1])
            if f >= 2:
                at = 8 * (f % 2) + a
                row = row + jnp.where(leftward, left[at : at + 1], right[at : at + 1])
            near = side_columns(row)
            for n, oy in enumerate(SIDEWAYS):
                grid[f, n, 8 * level : 8 * level + 8, :] = sideways(lattice[f, a], near, oy)
        for n in range(len(SIDEWAYS)):
            grid[f, n, 16:24, :] = jnp.zeros((8, PTS), F32)
    force, _ = group_first(
        lambda f, oy, ox: grid[f, SIDEWAYS.index(oy), 8 + ox : 16 + ox, :],
        lambda s: rows_w[s, last] if s < 6 else jnp.zeros((8, PTS), I32),
        lambda number, weight, level: None,
        start=0,
    )
    gap = disp[0, last] + inter[...]
    own[0:8, :] = gap + STEP_DT * (vel[0, last] + STEP_DT * flip(force))
    own[8:16, :] = gap
    own[16:17, :] = right[last : last + 1] + right[65:66]
    own[17:18, :] = left[last : last + 1] + left[65:66]

    halo_d = shell_strip(right, left, 72)
    halo_v = shell_strip(right, left, 80)
    strip_d[...] = halo_d
    strip_v[...] = halo_v
    for at in (0, 8, PAD + rows, PAD + rows + 8):
        tall[at : at + 8, :] = jnp.zeros((8, PTS), F32)
    tall[PAD : PAD + rows, :] = halo_d
    numbers = node[...].astype(F32)
    blocks = widen(lambda b: numbers[b : b + 1], cols // PTS)
    low = lane < PTS // 2
    lay_out(wide_ref, (), 0, jnp.where(low, blocks[0], blocks[-1]))
    far = jnp.where(low, 0.0, float(cols - PTS))
    ahead = jnp.zeros((8, PTS), F32)
    for part in place.parts():
        soon = jnp.zeros((8, PTS), F32)
        band = place.band_of(part[0])
        for row in part:
            at = PAD + row
            here = tall[at : at + 8, :]
            column = 2.0 * (tall[at - 1 : at + 7, :] + tall[at + 1 : at + 9, :]) - 8.0 * here
            from_left = turn(jnp.where(low, 0.0, column), 1) + turn(jnp.where(low, 0.0, here), 2)
            from_right = turn(jnp.where(low, column, 0.0), -1) + turn(jnp.where(low, here, 0.0), -2)
            hit = wide_ref[band] == place.nodes(row, PTS) + far
            soon = soon + jnp.where(hit, jnp.where(low, from_left, from_right), 0.0)
        ahead = ahead + jnp.where(sub == band, jnp.sum(soon, axis=0, keepdims=True), 0.0)
    base = OWN_ROWS
    own[base : base + 16, :] = shore[...]
    for b, row in zip((0, tiles - 1), narrow(lambda j: ahead, (0, tiles - 1))):
        own[base + b : base + b + 1, :] = shore[b : b + 1, :] - (STEP_DT * STEP_DT * BEND) * row
    own[base + 16 : base + 17, :] = right[66:67]
    own[base + 17 : base + 18, :] = left[66:67]

    mine = jnp.where(place.front, own[0:CONTACT_ROWS, :], own[base : base + CONTACT_ROWS, :])
    for shift, out in zip(shifts, outs):
        at = 0
        if shift & (shift + 1) == 0:
            at = HALO_ROWS
            down = (place.gx ^ shift) > place.gx
            out[0:ROWS_AT, :] = jnp.zeros((ROWS_AT, PTS), F32)
            for f in range(4):
                to = ROWS_AT + 6 * f
                out[to : to + 6, :] = jnp.where(down, lattice[f, last, 2:8, :], lattice[f, 0, 0:6, :])
            for f in range(2):
                to = LEAD_AT + 3 * f
                out[to : to + 3, :] = jnp.where(down, lead[f, last, 5:8, :], lead[f, 0, 0:3, :])

                def merged(part):
                    rows_of = [x[8 * part + a : 8 * part + a + 1] for a in (last, 0) for x in (left, right)]
                    return jnp.where(leftward, jnp.where(down, rows_of[0], rows_of[2]), jnp.where(down, rows_of[1], rows_of[3]))

                rest = merged(4 + f)
                whole = rest + merged(f)
                for n, values in enumerate((rest, whole, whole + STEP_DT * merged(2 + f))):
                    out[SIDE_AT + 2 * n + f : SIDE_AT + 2 * n + f + 1, :] = values
            for n, values in enumerate((left, right)):
                for part in range(2):
                    to, row = SIDE_AT + 6 + 2 * n + part, 48 + 8 * part
                    out[to : to + 1, :] = jnp.where(down, values[row + last : row + last + 1], values[row : row + 1])
            out[WORD_AT : WORD_AT + 8, :] = jnp.zeros((8, PTS), F32)
            edge_words = jnp.where(down, words[last], words[0])
            out[WORD_AT : WORD_AT + 8, 0:9] = (edge_words & 65535).astype(F32)
            out[WORD_AT : WORD_AT + 8, 16:25] = jnp.right_shift(edge_words, 16).astype(F32)
            for j in range(WIDE // PTS):
                cut = slice(j * PTS, (j + 1) * PTS)
                if j < cols // PTS:
                    d_low, d_high = shell[0:4, cut], shell[rows - 4 : rows, cut]
                    v_low, v_high = speed[0:2, cut], speed[rows - 2 : rows, cut]
                else:
                    d_low, d_high = halo_d[0:4], halo_d[rows - 4 : rows]
                    v_low, v_high = halo_v[0:2], halo_v[rows - 2 : rows]
                to = SHELL_AT + 6 * j
                out[to : to + 4, :] = jnp.where(down, d_high, d_low)
                out[to + 4 : to + 6, :] = jnp.where(down, v_high, v_low)
        out[at : at + CONTACT_ROWS, :] = mine


def inner_rows(place_args, disp, jit, shell, speed, lattice, rows_w, first, second, strip_d, strip_v, *refs):
    place = Place(*place_args)
    win, weights, levels, flat, beside, mid, strips, kinds, panes, hold, side = refs
    cols = place.shell_cols
    rows_a, tiles = disp.shape[1], disp.shape[2]
    right, left = place.sides(first[...], second[...])
    lane = lanes()
    leftward = (lane & (TILE_Y - 1)) >= TILE_Y // 2
    for f in range(6):
        side[f] = jnp.where(leftward, left[8 * f : 8 * f + 8], right[8 * f : 8 * f + 8])

    strips[...] = jnp.zeros_like(strips)

    @pl.loop(0, 2)
    def _(c):
        for part in range(2):
            f = c + 2 * part
            whole = jit[c] + disp[c] if part else jit[c]
            beyond = side[4 + c] + side[c] if part else side[4 + c]
            strips[f, 0, 8:16, :] = beyond
            strips[f, 1, 8:16, :] = turn(whole[:, 0, :], TILE_Y)
            strips[f, 2, 8:16, :] = turn(whole[:, tiles - 1, :], -TILE_Y)
            nears = [side_columns(beyond[a : a + 1]) for a in range(rows_a)]
            for a, near in enumerate(nears):
                cells = lattice[f, a]
                for n, oy in enumerate(SIDEWAYS):
                    shifted = sideways(cells, near, oy)
                    if a < rows_a - 1:
                        win[f, n, a, 0:8, :] = shifted
                    if a > 0:
                        win[f, n, a - 1, 8:16, :] = shifted

    left_words = joined(left[48:56], left[56:64])
    right_words = joined(right[48:56], right[56:64])
    for s in range(9):
        kinds[s] = jnp.where(
            leftward,
            jnp.broadcast_to(left_words[:, s : s + 1], (8, PTS)),
            jnp.broadcast_to(right_words[:, s : s + 1], (8, PTS)),
        )

    flat[...] = jnp.zeros_like(flat)

    blocks = mid.shape[0]

    for n in range(blocks):
        panes[n, :, 0:cols] = shell[8 * n : 8 * n + 24, :]
        panes[n, :, cols:WIDE] = strip_d[8 * n : 8 * n + 24, :]

    each = -(-blocks // (rows_a - 1))

    def bend_block(n):
        at = pl.multiple_of(8 * n + 8, 8)
        bending = bending_of(lambda o: panes[n, 8 + o : 16 + o, :])
        mid[n, :, 0:cols] = speed[pl.ds(at, 8), :] - (STEP_DT * BEND) * bending[:, 0:cols]
        mid[n, :, cols:WIDE] = strip_v[pl.ds(at, 8), :] - (STEP_DT * BEND) * bending[:, cols:WIDE]

    hold[...] = jnp.zeros_like(hold)
    reach_y = len(SIDEWAYS) // 2

    def side_bonds(k):
        masks, bits = lane_masks()
        oy = k - reach_y
        at = jnp.where(oy > 0, 1, jnp.where(oy < 0, 2, 0))
        towards = jnp.where(oy > 0, 1, jnp.where(oy < 0, -1, 0)) + 1
        col = lane & (TILE_Y - 1)
        crossed = (col < oy) | (col >= TILE_Y + oy)
        crossing = (col >= TILE_Y - oy) | (col < -oy)
        cells = [
            {
                dx: pltpu.roll(
                    jnp.where(crossed, strips[f, at, 8 + dx : 16 + dx, :], strips[f, 0, 8 + dx : 16 + dx, :]),
                    (PTS - oy) & (PTS - 1),
                    1,
                )
                for dx in (-1, 0, 1)
            }
            for f in range(4)
        ]
        words = [jnp.where(crossing, kinds[3 * dx + towards], kinds[3 * dx + 1]) for dx in range(3)]
        zero = [strips[f, 0, 8:16, :] for f in range(4)]
        step = oy.astype(F32)
        base_y, base_v = zero[1] - step, zero[3] - step
        fx, fy = hold[0], hold[1]
        for ox in range(-3, 4):
            word = words[1]
            if ox:
                word = jnp.where(masks["row_from", ox], words[sign(ox) + 1], word)
            rest_x = across(cells[0], ox, masks) - (zero[0] - float(ox))
            rest_y = across(cells[1], ox, masks) - base_y
            now_x = across(cells[2], ox, masks) - (zero[2] - float(ox))
            now_y = across(cells[3], ox, masks) - base_v
            rest_sq = rest_x * rest_x + rest_y * rest_y + DELTA_SQ
            now_sq = now_x * now_x + now_y * now_y + DELTA_SQ
            rest_inv = lax.rsqrt(rest_sq)
            reach = jnp.maximum(1.0 - rest_sq * rest_inv * (1.0 / HORIZON), 0.0)
            weight = jnp.where((word & bits[ox]) != 0, reach * reach, 0.0)
            factor = weight * (rest_inv - lax.rsqrt(now_sq))
            fx, fy = fx + factor * now_x, fy + factor * now_y
        hold[0], hold[1] = fx, fy

    if rows_a - 1 != len(SIDEWAYS):
        pl.loop(0, len(SIDEWAYS))(side_bonds)

    @pl.loop(0, rows_a - 1)
    def _(k):
        if rows_a - 1 == len(SIDEWAYS):
            side_bonds(k)
        for part in range(each):
            bend_block(jnp.minimum(each * k + part, blocks - 1))

        def cell(f, oy, ox):
            return win[f, SIDEWAYS.index(oy), k, FROM + ox : FROM + ox + 8, :]

        def keep(number, weight, level):
            weights[number, k] = weight
            levels[number, k] = level

        upper = subs() < TILE_X - FROM
        grouped = [jnp.where(upper, rows_w[s, k], rows_w[s, k + 1]) for s in range(9)]
        fx, fy = group_first(cell, grouped.__getitem__, keep)
        at = pl.multiple_of(8 * k + 16, 8)
        flat[0, pl.ds(at, 8), :] = fx
        flat[1, pl.ds(at, 8), :] = fy

    for f in range(2):
        moved_side = side[4 + f] + side[f] + STEP_DT * (side[2 + f] + STEP_DT * hold[f])
        for a in range(rows_a):
            beside[f, a] = side_columns(moved_side[a : a + 1])


def both_steps(place_args, shifts, *refs):
    place = Place(*place_args)
    disp, vel, node, inter, shell, speed, first, second, own, strip_d, strip_v = refs[:11]
    lead, rows_w, win, weights, levels, flat_in, beside, mid = refs[11:19]
    ends = refs[19 : 19 + len(shifts)]
    targets = refs[19 + len(shifts) : 23 + len(shifts)]
    scratch = refs[23 + len(shifts) :]
    out_disp, out_vel, out_shell, out_speed, gaps, halo, rim, rim_v, panes, fasts, hits, goals, ewin, ewords = scratch[:14]
    eweights, elevels, flat, flat2, seams, kinds, swin, cast, sems = scratch[14:]
    outs = (out_disp, out_vel, out_shell, out_speed)
    pairs = [(x.at[f], y.at[f]) for x, y in zip(outs[:2], targets[:2]) for f in range(2)] + list(zip(outs[2:], targets[2:]))
    copies = [pltpu.make_async_copy(x, y, sems.at[n]) for n, (x, y) in enumerate(pairs)]
    rows_a, tiles = disp.shape[1], disp.shape[2]
    rows, cols = place.shell_rows, place.shell_cols
    blocks = rows // 8
    right, left = place.sides(first[...], second[...])

    halo[...] = jnp.zeros_like(halo)
    contact = jnp.where(place.front, own[0:CONTACT_ROWS, :], 0.0)
    owners = own[OWN_ROWS : OWN_ROWS + CONTACT_ROWS, :]
    for shift, ref in zip(shifts, ends):
        partner = place.gx ^ shift
        at = 0
        if shift & (shift + 1) == 0:
            at = HALO_ROWS

            @pl.when(partner == place.gx - 1)
            def _():
                halo[0] = ref[0:HALO_ROWS, :]

            @pl.when(partner == place.gx + 1)
            def _():
                halo[1] = ref[0:HALO_ROWS, :]

        got = ref[at : at + CONTACT_ROWS, :]
        contact = jnp.where(partner == place.nx - 1, got, contact)
        owners = owners + got

    def wide(source, strip, row, count):
        return jnp.concatenate([source[row : row + count, :], strip[row : row + count, :]], axis=1)

    zeros = jnp.zeros((8, WIDE), F32)
    rim[0, 16:32, :] = wide(shell, strip_d, 0, 16)
    rim[1, 0:16, :] = wide(shell, strip_d, rows - 16, 16)
    rim_v[0, 8:16, :] = wide(speed, strip_v, 0, 8)
    rim_v[1, 0:8, :] = wide(speed, strip_v, rows - 8, 8)
    for ref, at in ((rim, (0, 0)), (rim, (0, 8)), (rim, (1, 16)), (rim, (1, 24)), (rim_v, (0, 0)), (rim_v, (1, 8))):
        ref[at[0], at[1] : at[1] + 8, :] = zeros
    for j in range(WIDE // PTS):
        cut = slice(j * PTS, (j + 1) * PTS)
        at = SHELL_AT + 6 * j
        rim[0, 12:16, cut] = halo[0, at : at + 4, :]
        rim_v[0, 6:8, cut] = halo[0, at + 4 : at + 6, :]
        rim[1, 16:20, cut] = halo[1, at : at + 4, :]
        rim_v[1, 8:10, cut] = halo[1, at + 4 : at + 6, :]
    numbers = node[...].astype(F32)
    node_rows = [numbers[b : b + 1] for b in range(tiles)] + [right[64:65], left[64:65]]
    gap_rows = [contact[8 + b : 9 + b] for b in range(tiles)] + [contact[16:17], contact[17:18]]
    soon_rows = [contact[b : b + 1] for b in range(tiles)]
    for j, (nodes, gap) in enumerate(zip(widen(node_rows.__getitem__, 5), widen(gap_rows.__getitem__, 5))):
        lay_out(gaps, (0,), j, nodes)
        lay_out(gaps, (1,), j, gap)
    for j, soon in enumerate(widen(soon_rows.__getitem__, 4)):
        lay_out(gaps, (2,), j, soon)
    col = lax.broadcasted_iota(I32, (8, WIDE), 1)
    inside = jnp.where(col < cols, 1.0, 0.0)
    inside = jnp.where((col >= cols) & (col < cols + 64) & (place.gy < place.ny - 1), 1.0, inside)
    inside = jnp.where((col >= cols + 64) & (place.gy > 0), 1.0, inside)

    def first_rows(n, here, steady, keep=None):
        band = place.band_of(8 * n)
        hit = jnp.where(gaps[0, band] == place.nodes(8 * n, WIDE), STEP_DT * PENALTY, 0.0)
        push = hit * jnp.maximum(gaps[1, band] - here, 0.0)
        fast = steady + push
        there = (here + STEP_DT * fast) * (inside if keep is None else inside * keep)
        return there, fast[:, 0:cols], hit[:, 0:cols], gaps[2, band, :, 0:cols] - STEP_DT * push[:, 0:cols]

    for n in (-1, 0, blocks - 1, blocks):
        end = 0 if n < 1 else 1
        at = 8 * n + 16 if end == 0 else 8 * n - rows + 16
        bending = bending_of(lambda o: rim[end, at + o : at + o + 8, :])
        steady = rim_v[end, at - 8 : at, :] - (STEP_DT * BEND) * bending
        keep = None
        if n < 0:
            keep = jnp.where(place.gx > 0, 1.0, 0.0)
        elif n == blocks:
            keep = jnp.where(place.gx < place.nx - 1, 1.0, 0.0)
        there, *rest = first_rows(n, rim[end, at : at + 8, :], steady, keep)
        for part in (-1, 0, 1):
            if 0 <= n - part < blocks:
                panes[n - part, 8 + 8 * part : 16 + 8 * part, :] = there
        if 0 <= n < blocks:
            fasts[n], hits[n], goals[n] = rest

    def inner_block(n):
        at = pl.ds(pl.multiple_of(8 * n, 8), 8)
        there, *rest = first_rows(n, jnp.concatenate([shell[at, :], strip_d[at, :]], axis=1), mid[n - 1])
        for part in (-1, 0, 1):
            panes[n - part, 8 + 8 * part : 16 + 8 * part, :] = there
        fasts[n], hits[n], goals[n] = rest

    @pl.loop(0, (blocks - 2) // 2)
    def _(k):
        inner_block(2 * k + 1)
        inner_block(2 * k + 2)

    lane, sub = lanes(), subs()
    west, east = place.gy == 0, place.gy == place.ny - 1
    north, south = place.gx == 0, place.gx == place.nx - 1
    leftward = (lane & (TILE_Y - 1)) >= TILE_Y // 2
    last = rows_a - 1
    high = lane >= PTS // 2
    segment = ((lane + 16) >> 5) & 3

    def near_row(a, part):
        at = 8 * part + a
        return jnp.where(leftward[0:1], left[at : at + 1], right[at : at + 1])

    border = (-1, 0, last, rows_a)
    sides = {}
    for f in range(2):
        for a in (0, last):
            rest = near_row(a, 4 + f)
            whole = rest + near_row(a, f)
            sides[a, f] = (rest, whole, whole + STEP_DT * near_row(a, 2 + f))
        for a, end in ((-1, 0), (rows_a, 1)):
            sides[a, f] = [halo[end, SIDE_AT + 2 * n + f : SIDE_AT + 2 * n + f + 1, :] for n in range(3)]
    lead_side, far_lead = {}, {}
    straight = SIDEWAYS.index(0)
    for f in range(2):
        for a in border:
            lead_side[f, a] = side_columns(sides[a, f][2])
        at = LEAD_AT + 3 * f
        far_lead[f, 0], far_lead[f, 1] = halo[0, at - 5 : at + 3, :], halo[1, at : at + 8, :]
        for field in (f, 2 + f):
            cells, near = {}, {}
            for a in border:
                near[a] = side_columns(sides[a, f][field // 2])
            at = ROWS_AT + 6 * field
            cells[-1], cells[rows_a] = halo[0, at - 2 : at + 6, :], halo[1, at : at + 8, :]
            cells[0] = win[field, straight, 0, 0:8, :]
            cells[last] = win[field, straight, rows_a - 2, 8:16, :]
            for n, oy in enumerate(SIDEWAYS):
                ewin[field, n, 0, 0:8, :] = sideways(cells[-1], near[-1], oy)
                ewin[field, n, 0, 8:16, :] = win[field, n, 0, 0:8, :]
                ewin[field, n, 1, 0:8, :] = win[field, n, rows_a - 2, 8:16, :]
                ewin[field, n, 1, 8:16, :] = sideways(cells[rows_a], near[rows_a], oy)
            for half, (up, down) in enumerate(((-1, last), (0, rows_a))):
                pieces = [
                    jnp.where(high, near[up], cells[up]),
                    turn(jnp.where(high, cells[up], near[up]), 32),
                    turn(jnp.where(high, near[down], cells[down]), 64),
                    turn(jnp.where(high, cells[down], near[down]), 96),
                ]
                seam = pieces[3]
                for q in (2, 1, 0):
                    seam = jnp.where(segment == q, pieces[q], seam)
                for n, oy in enumerate(SIDEWAYS):
                    seams[field, n, 8 * half : 8 * half + 8, :] = turn(seam, -oy)
    for end in (0, 1):
        packed = halo[end, WORD_AT : WORD_AT + 8, :]
        packed = joined(packed, turn(packed, -16))
        for dx in (-1, 0, 1):
            for dy in (-1, 0, 1):
                s = slot(dx, dy)
                word = word_row(packed, s)
                if dy < 0:
                    word = jnp.where((lane < TILE_Y) & west, 0, word)
                if dy > 0:
                    word = jnp.where((lane >= PTS - TILE_Y) & east, 0, word)
                pair = (word, rows_w[s, 0]) if end == 0 else (rows_w[s, last], word)
                ewords[s, end] = jnp.where(sub < TILE_X - FROM, *pair)
    parts = []
    for at in (0, 1):
        rows_w = []
        for a in (-1, last, 0, rows_a):
            for n, values in enumerate((left, right)):
                if 0 <= a <= last:
                    rows_w.append(values[48 + 8 * at + a : 49 + 8 * at + a])
                else:
                    row = SIDE_AT + 6 + 2 * n + at
                    rows_w.append(halo[0 if a < 0 else 1, row : row + 1, :])
        parts.append(jnp.concatenate(rows_w, axis=0))
    packed = joined(*parts)
    for dx in (-1, 0, 1):
        for dy in (-1, 0, 1):
            s = slot(dx, dy)
            word = jnp.broadcast_to(packed[:, s : s + 1], (8, PTS))
            upper, lower = jnp.where(sub == segment, word, 0), jnp.where(sub == segment + 4, word, 0)
            for step in (4, 2, 1):
                upper, lower = upper | pltpu.roll(upper, step, 0), lower | pltpu.roll(lower, step, 0)
            if dx < 0:
                lower = jnp.where((segment < 2) & north, 0, lower)
            if dx > 0:
                upper = jnp.where((segment >= 2) & south, 0, upper)
            kinds[s] = jnp.where(sub < TILE_X - FROM, upper, lower)

    flat[...] = flat_in[...]
    for e in (0, 1):

        def keep_end(number, weight, level, e=e):
            eweights[number, e] = weight
            elevels[number, e] = level

        found = group_first(
            lambda f, oy, ox: ewin[f, SIDEWAYS.index(oy), e, FROM + ox : FROM + ox + 8, :],
            lambda s: ewords[s, e],
            keep_end,
        )
        for f in range(2):
            flat[f, 8 + 8 * rows_a * e : 16 + 8 * rows_a * e, :] = found[f]
    seam_f = group_first(
        lambda f, oy, ox: seams[f, SIDEWAYS.index(oy), FROM + ox : FROM + ox + 8, :],
        lambda s: kinds[s],
        lambda number, weight, level: None,
    )

    here = jnp.where(place.front, 1.0, 0.0)
    push = PENALTY * here * jnp.maximum(contact[8:18] - owners[8:18], 0.0)
    side_push = side_columns(jnp.where(leftward[0:1], push[9:10], push[8:9]))
    push = push[0:8]
    push_rows = flip(push)

    square = STEP_DT * STEP_DT
    for f in range(2):
        force = pltpu.roll(seam_f[f], FROM, 0)
        above = square * jnp.where(high, force, turn(force, -32))
        below = square * jnp.where(high, turn(force, -64), turn(force, -96))
        nears = {-1: lead_side[f, -1] + above, rows_a: lead_side[f, rows_a] + below}
        nears[0] = jnp.where(sub < FROM, lead_side[f, 0] + above, beside[f, 0])
        nears[last] = jnp.where(sub < FROM, beside[f, last], lead_side[f, last] + below)
        if f == 0:
            nears[last] = nears[last] - square * side_push
        for a in range(-1, rows_a + 1):
            cells = far_lead[f, 0 if a < 0 else 1] if a in (-1, rows_a) else lead[f, a]
            cells = cells + square * flat[f, 8 * a + 11 : 8 * a + 19, :]
            if a == last and f == 0:
                cells = cells - square * push_rows
            cast[f, 0, a + 1] = cells
            cast[f, 1, a + 1] = nears[a] if a in nears else beside[f, a]

    @pl.loop(0, 2)
    def _(f):
        for a in range(-1, rows_a + 1):
            cells, near = cast[f, 0, a + 1], cast[f, 1, a + 1]
            for n, oy in enumerate(SIDEWAYS):
                shifted = sideways(cells, near, oy)
                if a < rows_a:
                    swin[f, n, a + 1, 0:8, :] = shifted
                if a >= 0:
                    swin[f, n, a, 8:16, :] = shifted

    def second_group(k, kept):
        def cell(f, oy, ox):
            return swin[f, SIDEWAYS.index(oy), k, FROM + ox : FROM + ox + 8, :]

        fx, fy = group_second(cell, kept)
        at = pl.multiple_of(8 * k + 8, 8)
        flat2[0, pl.ds(at, 8), :] = fx
        flat2[1, pl.ds(at, 8), :] = fy

    def second_rows(n):
        row = pl.multiple_of(8 * n, 8)
        here = panes[n, 8:16, 0:cols]
        push = hits[n] * jnp.maximum(goals[n] - here, 0.0)
        bending = bending_of(lambda o: panes[n, 8 + o : 16 + o, :])[:, 0:cols]
        fast = fasts[n] + push - (STEP_DT * BEND) * bending
        out_speed[pl.ds(row, 8), :] = fast
        out_shell[pl.ds(row, 8), :] = here + STEP_DT * fast

    inner = rows_a - 1
    each = blocks // rows_a

    @pl.loop(0, inner // 2)
    def _(j):
        for h in range(2):
            k = 2 * j + h
            second_group(k + 1, lambda number: (weights[number, k], levels[number, k]))
            for part in range(each):
                second_rows(each * k + part)

    k = inner - 1
    second_group(k + 1, lambda number: (weights[number, k], levels[number, k]))
    for part in range(each):
        second_rows(each * k + part)

    tail = blocks - each * inner
    half = -(-tail // 2)

    @pl.loop(0, 2)
    def _(e):
        second_group(e * rows_a, lambda number: (eweights[number, e], elevels[number, e]))
        for part in range(half):
            second_rows(jnp.minimum(each * inner + half * e + part, blocks - 1))

    copies[4].start()
    copies[5].start()

    for f in range(2):
        thens = flips([flat2[f, 8 * a + 11 : 8 * a + 19, :] for a in range(rows_a)])
        wases = flips([flat[f, 8 * a + 11 : 8 * a + 19, :] for a in range(rows_a)])
        for a in range(rows_a):
            was = wases[a]
            then = thens[a]
            if f == 0 and a == last:
                was = was - push
                gap = disp[0, last] + STEP_DT * (vel[0, last] + STEP_DT * was) + inter[...]
                reached = owners[0:8] + square * push
                then = then - PENALTY * here * jnp.maximum(gap - reached, 0.0)
            fast = vel[f, a] + STEP_DT * was
            faster = fast + STEP_DT * then
            out_vel[f, a] = faster
            out_disp[f, a] = disp[f, a] + STEP_DT * (fast + faster)
        copies[f].start()
        copies[2 + f].start()
    for copy in copies:
        copy.wait()


def on_device(nx, ny, disp, vel, jit, words, node, inter, shell, speed):
    rows_a = disp.shape[1]
    rows, cols = shell.shape
    place_args = (nx, ny, rows, cols)
    shifts = tuple(range(1, nx))
    span, count, blocks = rows_a - 1, len(OFFSETS), rows // 8

    def call(body, out, scratch, *args, far=0, **more):
        args = [pltpu.with_memory_space_constraint(x, pltpu.MemorySpace.HBM) for x in args[:far]] + list(args[far:])
        specs = [pl.BlockSpec(memory_space=pltpu.MemorySpace.HBM)] * far
        specs += [pl.BlockSpec(memory_space=pltpu.VMEM)] * (len(args) - far)
        return pl.pallas_call(
            body,
            out_shape=out,
            in_specs=specs,
            scratch_shapes=scratch,
            **more,
            compiler_params=pltpu.CompilerParams(vmem_limit_bytes=20 * 1024 * 1024),
        )(*args)

    def shaped(*shape, dtype=F32):
        return jax.ShapeDtypeStruct(shape + (PTS,), dtype)

    def like(*arrays):
        return [jax.ShapeDtypeStruct(x.shape, x.dtype) for x in arrays]

    wide = pltpu.VMEM((TILE_X, 8, cols), F32)
    tall = pltpu.VMEM((rows + 2 * PAD, cols), F32)
    edges = pltpu.VMEM((2, rows, PTS), F32)
    far_shell, far_speed = shell, speed
    small = (disp, vel, jit, words, node, inter)
    first, second, *small = call(
        functools.partial(pack_sides, place_args),
        [shaped(Y_ROWS)] * 2 + like(*small),
        [edges, edges, wide, pltpu.SemaphoreType.DMA((10,))],
        *small,
        far_shell,
        far_speed,
        far=8,
    )
    disp, vel, jit, words, node, inter = small
    first = lax.ppermute(first, "gy", [(i, i ^ 1) for i in range(ny)])
    second = lax.ppermute(
        second,
        ("gx", "gy"),
        [
            (i * ny + j, i * ny + ((j - 1) ^ 1) + 1 if 0 < j < ny - 1 else (i ^ 1) * ny + j)
            for i in range(nx)
            for j in range(ny)
        ],
    )

    shell, speed, lattice, lead, rows_w, shore = call(
        functools.partial(own_parts, place_args),
        like(far_shell, far_speed)
        + [
            shaped(4, rows_a, 8),
            shaped(2, rows_a, 8),
            shaped(9, rows_a, 8, dtype=I32),
            shaped(2 * disp.shape[2]),
        ],
        [tall, tall, pltpu.VMEM((2, TILE_X, 8, cols), F32), pltpu.SemaphoreType.DMA((4,))],
        far_shell,
        far_speed,
        disp,
        vel,
        jit,
        words,
        node,
        far=2,
    )

    outs = [shaped(CONTACT_ROWS + (HALO_ROWS if s & (s + 1) == 0 else 0)) for s in shifts]
    *ends, own, strip_d, strip_v = call(
        functools.partial(pack_ends, place_args, shifts),
        outs + [shaped(2 * OWN_ROWS), shaped(rows), shaped(rows)],
        [
            pltpu.VMEM((4, len(SIDEWAYS), 24, PTS), F32),
            pltpu.VMEM((rows + 2 * PAD, PTS), F32),
            pltpu.VMEM((TILE_X, 8, PTS), F32),
        ],
        *small,
        shell,
        speed,
        lattice,
        lead,
        rows_w,
        shore,
        first,
        second,
    )
    ends = [
        lax.ppermute(
            e,
            ("gx", "gy"),
            [
                (i * ny + j, i * ny + (j ^ 1) if s & (s + 1) and nx - 1 not in (i, i ^ s) else (i ^ s) * ny + j)
                for i in range(nx)
                for j in range(ny)
            ],
        )
        for s, e in zip(shifts, ends)
    ]

    inner = call(
        functools.partial(inner_rows, place_args),
        [
            shaped(4, len(SIDEWAYS), span, 16),
            shaped(count, span, 8),
            shaped(count, span, 8),
            shaped(2, 8 * (rows_a + 3)),
            shaped(2, rows_a, 8),
            jax.ShapeDtypeStruct((blocks - 2, 8, WIDE), F32),
        ],
        [
            pltpu.VMEM((4, 3, 24, PTS), F32),
            pltpu.VMEM((9, 8, PTS), I32),
            pltpu.VMEM((blocks - 2, 24, WIDE), F32),
            pltpu.VMEM((2, 8, PTS), F32),
            pltpu.VMEM((6, 8, PTS), F32),
        ],
        disp,
        jit,
        shell,
        speed,
        lattice,
        rows_w,
        first,
        second,
        strip_d,
        strip_v,
    )

    out = [jax.ShapeDtypeStruct(x.shape, F32) for x in (disp, vel, shell, speed)]
    scratch = [pltpu.VMEM(x.shape, F32) for x in out] + [
        pltpu.VMEM((3, TILE_X, 8, WIDE), F32),
        pltpu.VMEM((2, HALO_ROWS, PTS), F32),
        pltpu.VMEM((2, 32, WIDE), F32),
        pltpu.VMEM((2, 16, WIDE), F32),
        pltpu.VMEM((blocks, 24, WIDE), F32),
        pltpu.VMEM((blocks, 8, cols), F32),
        pltpu.VMEM((blocks, 8, cols), F32),
        pltpu.VMEM((blocks, 8, cols), F32),
        pltpu.VMEM((4, len(SIDEWAYS), 2, 16, PTS), F32),
        pltpu.VMEM((9, 2, 8, PTS), I32),
        pltpu.VMEM((count, 2, 8, PTS), F32),
        pltpu.VMEM((count, 2, 8, PTS), F32),
        pltpu.VMEM((2, 8 * (rows_a + 3), PTS), F32),
        pltpu.VMEM((2, 8 * (rows_a + 3), PTS), F32),
        pltpu.VMEM((4, len(SIDEWAYS), 16, PTS), F32),
        pltpu.VMEM((9, 8, PTS), I32),
        pltpu.VMEM((2, len(SIDEWAYS), rows_a + 1, 16, PTS), F32),
        pltpu.VMEM((2, 2, rows_a + 2, 8, PTS), F32),
        pltpu.SemaphoreType.DMA((6,)),
    ]
    return tuple(
        call(
            functools.partial(both_steps, place_args, shifts),
            out,
            scratch,
            disp,
            vel,
            node,
            inter,
            shell,
            speed,
            first,
            second,
            own,
            strip_d,
            strip_v,
            lead,
            rows_w,
            *inner,
            *ends,
            out_specs=[pl.BlockSpec(memory_space=pltpu.MemorySpace.HBM)] * 4,
        )
    )


def solution(mesh):
    in_specs = (
        P(None, "gx", "gy", None),
        P(None, "gx", "gy", None),
        P(None, "gx", "gy", None),
        P("gx", "gy", None),
        P("gy", None),
        P("gy", None),
        P("gx", "gy"),
        P("gx", "gy"),
    )
    out_specs = (P(None, "gx", "gy", None), P(None, "gx", "gy", None), P("gx", "gy"), P("gx", "gy"))
    body = functools.partial(on_device, mesh.shape["gx"], mesh.shape["gy"])
    return jax.shard_map(body, mesh=mesh, in_specs=in_specs, out_specs=out_specs, check_vma=False)
```

```python
import functools

import jax
import jax.numpy as jnp
from jax import lax
from jax.experimental import pallas as pl
from jax.experimental.pallas import tpu as pltpu
from jax.sharding import PartitionSpec as P

TILE_X = 8
TILE_Y = 16
PTS = 128
SPLIT = 4

HORIZON = 3.5
DELTA_SQ = 0.25
PENALTY = 4.0
BEND = 0.5
STEP_DT = 0.2

F32 = jnp.float32
I32 = jnp.int32

STRIDE = 24
WIDE = 640
PAD = 16


def bond_offsets():
    limit = HORIZON * HORIZON - DELTA_SQ
    found = []
    for oy in range(-4, 5):
        for ox in range(-4, 5):
            near = max(abs(ox) - 0.4, 0.0) ** 2 + max(abs(oy) - 0.4, 0.0) ** 2
            if near < limit and (ox or oy):
                found.append((ox, oy))
    return found


OFFSETS = bond_offsets()
SIDEWAYS = sorted({oy for _, oy in OFFSETS})


def sign(value):
    return (value > 0) - (value < 0)


def lanes():
    return lax.broadcasted_iota(I32, (8, PTS), 1)


def subs():
    return lax.broadcasted_iota(I32, (8, PTS), 0)


def turn(values, shift):
    size = values.shape[1]
    return pltpu.roll(values, shift % size, 1) if shift % size else values


def slot(dx, dy):
    return 3 * (dx + 1) + dy + 1


def lane_masks():
    lane = lanes()
    row, col = lane // TILE_Y, lane % TILE_Y
    masks = {}
    for o in (1, 2, 3):
        masks["col_at", o] = col < o
        masks["col_at", -o] = col >= TILE_Y - o
        masks["col_from", o] = col >= TILE_Y - o
        masks["col_from", -o] = col < o
        masks["row_at", o] = row < o
        masks["row_at", -o] = row >= TILE_X - o
        masks["row_from", o] = row >= TILE_X - o
        masks["row_from", -o] = row < o
    bits = {}
    for ox in range(-3, 4):
        bits[ox] = jnp.left_shift(jnp.int32(1), 4 * row + ((row + ox) & 7) // 2)
    return masks, bits


def across(cells, ox, masks):
    if not ox:
        return cells[0]
    return turn(jnp.where(masks["row_at", ox], cells[sign(ox)], cells[0]), -TILE_Y * ox)


def pick_lanes(block, index):
    return jnp.take_along_axis(block, index, axis=1, mode="promise_in_bounds")


def flips(blocks):
    lane, sub = lanes(), subs()
    for level in (2, 1, 0):
        step = 1 << level
        stay = ((lane >> (level + 4)) ^ (sub >> level)) & 1 == 0
        if step == 4:
            others = [turn(pltpu.roll(block, 4, 0), 64) for block in blocks]
        else:
            low = (sub >> level) & 1 == 0
            index = lane ^ (TILE_Y * step)
            others = [jnp.where(low, pltpu.roll(block, 8 - step, 0), pltpu.roll(block, step, 0)) for block in blocks]
            others = [pick_lanes(block, index) for block in others]
        blocks = [jnp.where(stay, block, other) for block, other in zip(blocks, others)]
    return blocks


def flip(block):
    return flips([block])[0]


def side_columns(row):
    return pick_lanes(jnp.broadcast_to(row, (8, PTS)), TILE_Y * subs() + (lanes() & (TILE_Y - 1)))


def word_row(packed, s):
    word = jnp.where(subs() == lanes() // TILE_Y, jnp.broadcast_to(packed[:, s : s + 1], (8, PTS)), 0)
    for step in (4, 2, 1):
        word = word | pltpu.roll(word, step, 0)
    return word


def sideways(cells, beside, oy):
    if not oy:
        return cells
    lane = lanes()
    mask = lane < oy if oy > 0 else lane >= PTS + oy
    return turn(jnp.where(mask, beside, cells), -oy)


FROM = 5


def group_masks(start):
    lane, sub = lanes(), subs()
    row = (sub + start) & (TILE_X - 1)
    col = lane & (TILE_Y - 1)
    masks, bits = {}, {}
    for o in (1, 2, 3):
        masks["col", o] = col >= TILE_Y - o
        masks["col", -o] = col < o
        masks["row", o] = row >= TILE_X - o
        masks["row", -o] = row < o
    for ox in range(-3, 4):
        bits[ox] = jnp.left_shift(jnp.int32(1), 4 * row + ((row + ox) & 7) // 2)
    return masks, bits


def group_first(cell, word, keep, start=FROM):
    masks, bits = group_masks(start)
    zero = [cell(f, 0, 0) for f in range(4)]
    fx = jnp.zeros((8, PTS), F32)
    fy = jnp.zeros((8, PTS), F32)
    plain = [word(slot(dx, 0)) for dx in (-1, 0, 1)]
    for oy in SIDEWAYS:
        words = plain
        if oy:
            words = [jnp.where(masks["col", oy], word(slot(dx, sign(oy))), plain[dx + 1]) for dx in (-1, 0, 1)]
        base_y, base_v = zero[1] - float(oy), zero[3] - float(oy)
        for number, (ox, other) in enumerate(OFFSETS):
            if other != oy:
                continue
            picked = words[1]
            if ox:
                picked = jnp.where(masks["row", ox], words[sign(ox) + 1], picked)
            intact = (picked & bits[ox]) != 0
            rest_x = cell(0, oy, ox) - (zero[0] - float(ox))
            rest_y = cell(1, oy, ox) - base_y
            now_x = cell(2, oy, ox) - (zero[2] - float(ox))
            now_y = cell(3, oy, ox) - base_v
            rest_sq = rest_x * rest_x + rest_y * rest_y + DELTA_SQ
            now_sq = now_x * now_x + now_y * now_y + DELTA_SQ
            rest_inv = lax.rsqrt(rest_sq)
            reach = jnp.maximum(1.0 - rest_sq * rest_inv * (1.0 / HORIZON), 0.0)
            weight = jnp.where(intact, reach * reach, 0.0)
            level = weight * rest_inv
            keep(number, weight, level)
            factor = level - weight * lax.rsqrt(now_sq)
            fx = fx + factor * now_x
            fy = fy + factor * now_y
    return fx, fy


def group_second(cell, kept):
    zero = [cell(f, 0, 0) for f in range(2)]
    fx = jnp.zeros((8, PTS), F32)
    fy = jnp.zeros((8, PTS), F32)
    for number, (ox, oy) in enumerate(OFFSETS):
        now_x = cell(0, oy, ox) - (zero[0] - float(ox))
        now_y = cell(1, oy, ox) - (zero[1] - float(oy))
        now_sq = now_x * now_x + now_y * now_y + DELTA_SQ
        weight, level = kept(number)
        factor = level - weight * lax.rsqrt(now_sq)
        fx = fx + factor * now_x
        fy = fy + factor * now_y
    return fx, fy


def bending_of(row):
    here = row(0)
    one, two = row(-1) + row(1), row(-2) + row(2)
    beside = 2.0 * one - 8.0 * here
    out = two - 8.0 * one + 20.0 * here
    return out + turn(beside + turn(here, 1), 1) + turn(beside + turn(here, -1), -1)


def joined(low_part, high_part):
    return jnp.left_shift(high_part.astype(I32), 16) | low_part.astype(I32)


def widen(row_of, count):
    lane, sub = lanes(), subs()
    index = sub * TILE_Y + (lane % 64) // SPLIT
    out = []
    for j in range(count):
        left, right = (
            pick_lanes(jnp.broadcast_to(row_of(b), (8, PTS)), index) for b in (2 * j, 2 * j + 1)
        )
        out.append(jnp.where(lane < 64, left, right))
    return out


def narrow(block_of, tiles):
    lane, sub = lanes(), subs()
    out, sums = [], {}
    for b in tiles:
        if b // 2 not in sums:
            held = block_of(b // 2)
            held = held + turn(held, -1)
            sums[b // 2] = held + turn(held, -2)
        held = sums[b // 2]
        picked = pick_lanes(held, 64 * (b % 2) + SPLIT * (lane % TILE_Y))
        out.append(jnp.sum(jnp.where(sub == lane // TILE_Y, picked, 0.0), axis=0, keepdims=True))
    return out


def lay_out(ref, at, j, block, count=TILE_X):
    for row in range(count):
        ref[at + (row, slice(None), slice(j * PTS, (j + 1) * PTS))] = jnp.broadcast_to(block[row : row + 1], (8, PTS))


class Place:
    def __init__(self, nx, ny, shell_rows, shell_cols):
        self.nx, self.ny = nx, ny
        self.gx, self.gy = lax.axis_index("gx"), lax.axis_index("gy")
        self.shell_rows, self.shell_cols = shell_rows, shell_cols
        self.width = shell_cols * ny
        self.band = shell_rows * nx // TILE_X
        self.bands = shell_rows // self.band
        self.front = self.gx == nx - 1

    def sides(self, first, second):
        even = self.gy % 2 == 0
        right = jnp.where(even, first, second)
        left = jnp.where(even, second, first)
        right = jnp.where(self.gy < self.ny - 1, right, 0.0)
        left = jnp.where(self.gy > 0, left, 0.0)
        return right, left

    def nodes(self, row, columns):
        shape = (8, columns)
        col = lax.broadcasted_iota(I32, shape, 1)
        if columns > self.shell_cols:
            col = jnp.where(col >= self.shell_cols + 64, col - columns, col)
        first = (self.gx * self.shell_rows + row) * self.width + self.gy * self.shell_cols
        return (first + lax.broadcasted_iota(I32, shape, 0) * self.width + col).astype(F32)

    def parts(self):
        inner = [list(range(p * self.band, (p + 1) * self.band, 8)) for p in range(self.bands)]
        return [[-8]] + inner + [[self.shell_rows]]

    def met_bands(self, block):
        return pltpu.roll(block, (TILE_X + 1 - self.gx * self.bands) & (TILE_X - 1), 0)

    def met_band(self, row):
        return (row + self.band) // self.band

    def band_of(self, row):
        return jnp.clip((self.gx * self.shell_rows + row + self.band) // self.band - 1, 0, TILE_X - 1)


Y_ROWS = 88


def fetch(pairs, sems):
    copies = [pltpu.make_async_copy(source, target, sems.at[n]) for n, (source, target) in enumerate(pairs)]
    for copy in copies:
        copy.start()
    for copy in copies:
        copy.wait()


def pack_sides(place_args, *refs):
    sources, (first, second), held = refs[:8], refs[8:10], refs[10:16]
    shell, speed, wide_ref, sems = refs[16:]
    place = Place(*place_args)
    pairs = list(zip(sources[:6], held))
    for source, target in zip(sources[6:], (shell, speed)):
        for n, at in enumerate((0, place.shell_cols - PTS)):
            pairs.append((source.at[:, pl.ds(at, PTS)], target.at[n]))
    fetch(pairs, sems)
    disp, vel, jit, words, node, inter = held
    tiles = disp.shape[2]
    even = place.gy % 2 == 0
    blocks = place.shell_cols // PTS
    numbers = node[...].astype(F32)
    edge_blocks = (0, blocks - 1)
    for j in edge_blocks:
        lay_out(wide_ref, (), j, widen(lambda b: numbers[b : b + 1], blocks)[j])
    held = {}
    for j in edge_blocks:
        total = jnp.zeros((8, PTS), F32)
        for part in range(place.bands):
            summed = jnp.zeros((8, PTS), F32)
            for row in range(part * place.band, (part + 1) * place.band, 8):
                wanted = wide_ref[place.band_of(row), :, j * PTS : (j + 1) * PTS]
                ids = place.nodes(row, PTS) + float(j * PTS)
                summed = summed + jnp.where(wanted == ids, shell[min(j, 1), row : row + 8, :], 0.0)
            summed = jnp.sum(summed, axis=0, keepdims=True)
            total = total + jnp.where(subs() == place.band_of(part * place.band), summed, 0.0)
        held[j] = total
    met = narrow(lambda j: held[j], (0, tiles - 1))

    ends = [(jnp.transpose(x[1])[PTS - 8 :], jnp.transpose(x[0])[:8]) for x in (shell, speed)]

    def send(ref, to_right):
        edge = jnp.where(to_right, tiles - 1, 0)
        for f, source in enumerate((disp, disp, vel, vel, jit, jit)):
            ref[8 * f : 8 * f + 8, :] = jnp.where(
                to_right, source[f % 2, :, tiles - 1, :], source[f % 2, :, 0, :]
            )
        ref[48:Y_ROWS, :] = jnp.zeros((Y_ROWS - 48, PTS), F32)
        edge_words = jnp.where(to_right, words[:, tiles - 1, :], words[:, 0, :])
        ref[48:56, 0:9] = (edge_words & 65535).astype(F32)
        ref[56:64, 0:9] = jnp.right_shift(edge_words, 16).astype(F32)
        ref[64:65, :] = jnp.where(to_right, numbers[tiles - 1 : tiles], numbers[0:1])
        ref[65:66, :] = jnp.where(to_right, inter[tiles - 1 : tiles, :], inter[0:1, :])
        ref[66:67, :] = jnp.where(to_right, met[1], met[0])
        for f, source in enumerate((shell, speed)):
            ref[72 + 8 * f : 80 + 8 * f, :] = jnp.where(to_right, *ends[f])

    send(first, even)
    send(second, jnp.logical_not(even))


def own_parts(place_args, far_shell, far_speed, disp, vel, jit, words, node, *refs):
    place = Place(*place_args)
    shell, speed, lattice, lead, rows_w, shore, tall, tall_v, wide_ref, sems = refs
    rows_a, tiles = disp.shape[1], disp.shape[2]
    rows, cols = place.shell_rows, place.shell_cols
    lane = lanes()
    west, east = place.gy == 0, place.gy == place.ny - 1
    north, south = place.gx == 0, place.gx == place.nx - 1
    span = pl.ds(PAD, rows)
    copies = [
        pltpu.make_async_copy(source, target, sems.at[n])
        for n, (source, target) in enumerate(
            (
                (far_shell, shell),
                (far_speed, speed),
                (far_shell, tall.at[span]),
                (far_speed, tall_v.at[span]),
            )
        )
    ]
    for copy in copies:
        copy.start()
    for ref in (tall, tall_v):
        ref[0:PAD, :] = jnp.zeros((PAD, cols), F32)
        ref[PAD + rows :, :] = jnp.zeros((PAD, cols), F32)

    @pl.loop(0, 2)
    def _(f):
        rest = [jit[f, a] for a in range(rows_a)]
        whole = [jit[f, a] + disp[f, a] for a in range(rows_a)]
        soon = [x + STEP_DT * vel[f, a] for a, x in enumerate(whole)]
        for a, (x, y, z) in enumerate(zip(flips(rest), flips(whole), flips(soon))):
            lattice[f, a] = x
            lattice[2 + f, a] = y
            lead[f, a] = z

    @pl.loop(0, rows_a)
    def _(a):
        packed = words[a]
        for dx in (-1, 0, 1):
            for dy in (-1, 0, 1):
                word = word_row(packed, slot(dx, dy))
                if dy < 0:
                    word = jnp.where((lane < TILE_Y) & west, 0, word)
                if dy > 0:
                    word = jnp.where((lane >= PTS - TILE_Y) & east, 0, word)
                if dx < 0:
                    word = jnp.where((a == 0) & north, 0, word)
                if dx > 0:
                    word = jnp.where((a == rows_a - 1) & south, 0, word)
                rows_w[slot(dx, dy), a] = word

    numbers = node[...].astype(F32)
    node_row = jnp.floor(numbers * (1.0 / place.width))
    node_col = numbers - node_row * place.width - (place.gy * cols).astype(F32)
    node_row = node_row - (place.gx * rows).astype(F32)
    at_row = widen(lambda b: node_row[b : b + 1], cols // PTS)
    at_col = jnp.concatenate(widen(lambda b: node_col[b : b + 1], cols // PTS), axis=1)
    col = lax.broadcasted_iota(I32, (8, cols), 1)
    split = col & (SPLIT - 1)
    near_row = jnp.concatenate(at_row, axis=1)
    near_row = jnp.where(split < SPLIT // 2, turn(near_row, SPLIT), turn(near_row, -SPLIT))
    for j, block in enumerate(at_row):
        lay_out(wide_ref, (0,), j, place.met_bands(block), place.bands + 2)
        lay_out(wide_ref, (1,), j, place.met_bands(near_row[:, j * PTS : (j + 1) * PTS]), place.bands + 2)
    for copy in copies:
        copy.wait()
    sub_wide = lax.broadcasted_iota(I32, (8, cols), 0)
    row_wide = sub_wide.astype(F32)
    square = STEP_DT * STEP_DT * BEND
    sums = [jnp.zeros((8, cols), F32)] * 5
    for part in place.parts():
        found = [jnp.zeros((8, cols), F32)] * 5
        band = place.band_of(part[0])
        for row in part:
            at = PAD + row
            here = tall[at : at + 8, :]
            one = tall[at - 1 : at + 7, :] + tall[at + 1 : at + 9, :]
            two = tall[at - 2 : at + 6, :] + tall[at + 2 : at + 10, :]
            beside = 2.0 * one - 8.0 * here
            later = here + STEP_DT * tall_v[at : at + 8, :] - square * (two - 8.0 * one + 20.0 * here)
            hit = wide_ref[0, place.met_band(row)] == row_wide + float(row)
            near = wide_ref[1, place.met_band(row)] == row_wide + float(row)
            picks = ((hit, later), (hit, beside), (hit, here), (near, beside), (near, here))
            found = [x + jnp.where(mask, value, 0.0) for x, (mask, value) in zip(found, picks)]
        sums = [
            x + jnp.where(sub_wide == band, jnp.sum(y, axis=0, keepdims=True), 0.0) for x, y in zip(sums, found)
        ]
    later, beside, here, beside_near, here_near = sums
    spread = jnp.where(split < 3, turn(beside, -1), turn(beside_near, -1)) * (col < cols - 1).astype(F32)
    spread += jnp.where(split > 0, turn(beside, 1), turn(beside_near, 1)) * (col > 0).astype(F32)
    spread += jnp.where(split < 2, turn(here, -2), turn(here_near, -2)) * (col < cols - 2).astype(F32)
    spread += jnp.where(split > 1, turn(here, 2), turn(here_near, 2)) * (col > 1).astype(F32)
    hit = at_col == col.astype(F32)
    ahead = jnp.where(hit, later - square * spread, 0.0)
    met = jnp.where(hit, here, 0.0)
    for base, values in ((0, ahead), (tiles, met)):
        for b, row in enumerate(narrow(lambda j: values[:, j * PTS : (j + 1) * PTS], range(tiles))):
            shore[base + b : base + b + 1, :] = row


ROWS_AT, LEAD_AT, SIDE_AT, WORD_AT, SHELL_AT, HALO_ROWS = 2, 26, 32, 42, 50, 80
CONTACT_ROWS, OWN_ROWS = 18, 24


def shell_strip(right, left, at):
    middle = jnp.zeros((PTS - 16, PTS), F32)
    return jnp.transpose(jnp.concatenate([right[at : at + 8], middle, left[at : at + 8]], axis=0))


def pack_ends(
    place_args, shifts, disp, vel, jit, words, node, inter, shell, speed, lattice, lead, rows_w, shore, first, second, *refs
):
    place = Place(*place_args)
    outs = refs[: len(shifts)]
    own, strip_d, strip_v, grid, tall, wide_ref = refs[len(shifts) :]
    rows_a, tiles = disp.shape[1], disp.shape[2]
    rows, cols = place.shell_rows, place.shell_cols
    right, left = place.sides(first[...], second[...])
    lane, sub = lanes(), subs()
    leftward = (lane[0:1] & (TILE_Y - 1)) >= TILE_Y // 2
    last = rows_a - 1

    for f in range(4):
        for level, a in enumerate((last - 1, last)):
            at = 32 + 8 * (f % 2) + a
            row = jnp.where(leftward, left[at : at + 1], right[at : at + 1])
            if f >= 2:
                at = 8 * (f % 2) + a
                row = row + jnp.where(leftward, left[at : at + 1], right[at : at + 1])
            near = side_columns(row)
            for n, oy in enumerate(SIDEWAYS):
                grid[f, n, 8 * level : 8 * level + 8, :] = sideways(lattice[f, a], near, oy)
        for n in range(len(SIDEWAYS)):
            grid[f, n, 16:24, :] = jnp.zeros((8, PTS), F32)
    force, _ = group_first(
        lambda f, oy, ox: grid[f, SIDEWAYS.index(oy), 8 + ox : 16 + ox, :],
        lambda s: rows_w[s, last] if s < 6 else jnp.zeros((8, PTS), I32),
        lambda number, weight, level: None,
        start=0,
    )
    gap = disp[0, last] + inter[...]
    own[0:8, :] = gap + STEP_DT * (vel[0, last] + STEP_DT * flip(force))
    own[8:16, :] = gap
    own[16:17, :] = right[last : last + 1] + right[65:66]
    own[17:18, :] = left[last : last + 1] + left[65:66]

    halo_d = shell_strip(right, left, 72)
    halo_v = shell_strip(right, left, 80)
    strip_d[...] = halo_d
    strip_v[...] = halo_v
    for at in (0, 8, PAD + rows, PAD + rows + 8):
        tall[at : at + 8, :] = jnp.zeros((8, PTS), F32)
    tall[PAD : PAD + rows, :] = halo_d
    numbers = node[...].astype(F32)
    blocks = widen(lambda b: numbers[b : b + 1], cols // PTS)
    low = lane < PTS // 2
    lay_out(wide_ref, (), 0, jnp.where(low, blocks[0], blocks[-1]))
    far = jnp.where(low, 0.0, float(cols - PTS))
    ahead = jnp.zeros((8, PTS), F32)
    for part in place.parts():
        soon = jnp.zeros((8, PTS), F32)
        band = place.band_of(part[0])
        for row in part:
            at = PAD + row
            here = tall[at : at + 8, :]
            column = 2.0 * (tall[at - 1 : at + 7, :] + tall[at + 1 : at + 9, :]) - 8.0 * here
            from_left = turn(jnp.where(low, 0.0, column), 1) + turn(jnp.where(low, 0.0, here), 2)
            from_right = turn(jnp.where(low, column, 0.0), -1) + turn(jnp.where(low, here, 0.0), -2)
            hit = wide_ref[band] == place.nodes(row, PTS) + far
            soon = soon + jnp.where(hit, jnp.where(low, from_left, from_right), 0.0)
        ahead = ahead + jnp.where(sub == band, jnp.sum(soon, axis=0, keepdims=True), 0.0)
    base = OWN_ROWS
    own[base : base + 16, :] = shore[...]
    for b, row in zip((0, tiles - 1), narrow(lambda j: ahead, (0, tiles - 1))):
        own[base + b : base + b + 1, :] = shore[b : b + 1, :] - (STEP_DT * STEP_DT * BEND) * row
    own[base + 16 : base + 17, :] = right[66:67]
    own[base + 17 : base + 18, :] = left[66:67]

    mine = jnp.where(place.front, own[0:CONTACT_ROWS, :], own[base : base + CONTACT_ROWS, :])
    for shift, out in zip(shifts, outs):
        at = 0
        if shift & (shift + 1) == 0:
            at = HALO_ROWS
            down = (place.gx ^ shift) > place.gx
            out[0:ROWS_AT, :] = jnp.zeros((ROWS_AT, PTS), F32)
            for f in range(4):
                to = ROWS_AT + 6 * f
                out[to : to + 6, :] = jnp.where(down, lattice[f, last, 2:8, :], lattice[f, 0, 0:6, :])
            for f in range(2):
                to = LEAD_AT + 3 * f
                out[to : to + 3, :] = jnp.where(down, lead[f, last, 5:8, :], lead[f, 0, 0:3, :])

                def merged(part):
                    rows_of = [x[8 * part + a : 8 * part + a + 1] for a in (last, 0) for x in (left, right)]
                    return jnp.where(leftward, jnp.where(down, rows_of[0], rows_of[2]), jnp.where(down, rows_of[1], rows_of[3]))

                rest = merged(4 + f)
                whole = rest + merged(f)
                for n, values in enumerate((rest, whole, whole + STEP_DT * merged(2 + f))):
                    out[SIDE_AT + 2 * n + f : SIDE_AT + 2 * n + f + 1, :] = values
            for n, values in enumerate((left, right)):
                for part in range(2):
                    to, row = SIDE_AT + 6 + 2 * n + part, 48 + 8 * part
                    out[to : to + 1, :] = jnp.where(down, values[row + last : row + last + 1], values[row : row + 1])
            out[WORD_AT : WORD_AT + 8, :] = jnp.zeros((8, PTS), F32)
            edge_words = jnp.where(down, words[last], words[0])
            out[WORD_AT : WORD_AT + 8, 0:9] = (edge_words & 65535).astype(F32)
            out[WORD_AT : WORD_AT + 8, 16:25] = jnp.right_shift(edge_words, 16).astype(F32)
            for j in range(WIDE // PTS):
                cut = slice(j * PTS, (j + 1) * PTS)
                if j < cols // PTS:
                    d_low, d_high = shell[0:4, cut], shell[rows - 4 : rows, cut]
                    v_low, v_high = speed[0:2, cut], speed[rows - 2 : rows, cut]
                else:
                    d_low, d_high = halo_d[0:4], halo_d[rows - 4 : rows]
                    v_low, v_high = halo_v[0:2], halo_v[rows - 2 : rows]
                to = SHELL_AT + 6 * j
                out[to : to + 4, :] = jnp.where(down, d_high, d_low)
                out[to + 4 : to + 6, :] = jnp.where(down, v_high, v_low)
        out[at : at + CONTACT_ROWS, :] = mine


def inner_rows(place_args, disp, jit, shell, speed, lattice, rows_w, first, second, strip_d, strip_v, *refs):
    place = Place(*place_args)
    win, weights, levels, flat, beside, mid, strips, kinds, panes, hold, side = refs
    cols = place.shell_cols
    rows_a, tiles = disp.shape[1], disp.shape[2]
    right, left = place.sides(first[...], second[...])
    lane = lanes()
    leftward = (lane & (TILE_Y - 1)) >= TILE_Y // 2
    for f in range(6):
        side[f] = jnp.where(leftward, left[8 * f : 8 * f + 8], right[8 * f : 8 * f + 8])

    strips[...] = jnp.zeros_like(strips)

    @pl.loop(0, 2)
    def _(c):
        for part in range(2):
            f = c + 2 * part
            whole = jit[c] + disp[c] if part else jit[c]
            beyond = side[4 + c] + side[c] if part else side[4 + c]
            strips[f, 0, 8:16, :] = beyond
            strips[f, 1, 8:16, :] = turn(whole[:, 0, :], TILE_Y)
            strips[f, 2, 8:16, :] = turn(whole[:, tiles - 1, :], -TILE_Y)
            nears = [side_columns(beyond[a : a + 1]) for a in range(rows_a)]
            for a, near in enumerate(nears):
                cells = lattice[f, a]
                for n, oy in enumerate(SIDEWAYS):
                    shifted = sideways(cells, near, oy)
                    if a < rows_a - 1:
                        win[f, n, a, 0:8, :] = shifted
                    if a > 0:
                        win[f, n, a - 1, 8:16, :] = shifted

    left_words = joined(left[48:56], left[56:64])
    right_words = joined(right[48:56], right[56:64])
    for s in range(9):
        kinds[s] = jnp.where(
            leftward,
            jnp.broadcast_to(left_words[:, s : s + 1], (8, PTS)),
            jnp.broadcast_to(right_words[:, s : s + 1], (8, PTS)),
        )

    flat[...] = jnp.zeros_like(flat)

    blocks = mid.shape[0]

    for n in range(blocks):
        panes[n, :, 0:cols] = shell[8 * n : 8 * n + 24, :]
        panes[n, :, cols:WIDE] = strip_d[8 * n : 8 * n + 24, :]

    each = -(-blocks // (rows_a - 1))

    def bend_block(n):
        at = pl.multiple_of(8 * n + 8, 8)
        bending = bending_of(lambda o: panes[n, 8 + o : 16 + o, :])
        mid[n, :, 0:cols] = speed[pl.ds(at, 8), :] - (STEP_DT * BEND) * bending[:, 0:cols]
        mid[n, :, cols:WIDE] = strip_v[pl.ds(at, 8), :] - (STEP_DT * BEND) * bending[:, cols:WIDE]

    hold[...] = jnp.zeros_like(hold)
    reach_y = len(SIDEWAYS) // 2

    def side_bonds(k):
        masks, bits = lane_masks()
        oy = k - reach_y
        at = jnp.where(oy > 0, 1, jnp.where(oy < 0, 2, 0))
        towards = jnp.where(oy > 0, 1, jnp.where(oy < 0, -1, 0)) + 1
        col = lane & (TILE_Y - 1)
        crossed = (col < oy) | (col >= TILE_Y + oy)
        crossing = (col >= TILE_Y - oy) | (col < -oy)
        cells = [
            {
                dx: pltpu.roll(
                    jnp.where(crossed, strips[f, at, 8 + dx : 16 + dx, :], strips[f, 0, 8 + dx : 16 + dx, :]),
                    (PTS - oy) & (PTS - 1),
                    1,
                )
                for dx in (-1, 0, 1)
            }
            for f in range(4)
        ]
        words = [jnp.where(crossing, kinds[3 * dx + towards], kinds[3 * dx + 1]) for dx in range(3)]
        zero = [strips[f, 0, 8:16, :] for f in range(4)]
        step = oy.astype(F32)
        base_y, base_v = zero[1] - step, zero[3] - step
        fx, fy = hold[0], hold[1]
        for ox in range(-3, 4):
            word = words[1]
            if ox:
                word = jnp.where(masks["row_from", ox], words[sign(ox) + 1], word)
            rest_x = across(cells[0], ox, masks) - (zero[0] - float(ox))
            rest_y = across(cells[1], ox, masks) - base_y
            now_x = across(cells[2], ox, masks) - (zero[2] - float(ox))
            now_y = across(cells[3], ox, masks) - base_v
            rest_sq = rest_x * rest_x + rest_y * rest_y + DELTA_SQ
            now_sq = now_x * now_x + now_y * now_y + DELTA_SQ
            rest_inv = lax.rsqrt(rest_sq)
            reach = jnp.maximum(1.0 - rest_sq * rest_inv * (1.0 / HORIZON), 0.0)
            weight = jnp.where((word & bits[ox]) != 0, reach * reach, 0.0)
            factor = weight * (rest_inv - lax.rsqrt(now_sq))
            fx, fy = fx + factor * now_x, fy + factor * now_y
        hold[0], hold[1] = fx, fy

    if rows_a - 1 != len(SIDEWAYS):
        pl.loop(0, len(SIDEWAYS))(side_bonds)

    @pl.loop(0, rows_a - 1)
    def _(k):
        if rows_a - 1 == len(SIDEWAYS):
            side_bonds(k)
        for part in range(each):
            bend_block(jnp.minimum(each * k + part, blocks - 1))

        def cell(f, oy, ox):
            return win[f, SIDEWAYS.index(oy), k, FROM + ox : FROM + ox + 8, :]

        def keep(number, weight, level):
            weights[number, k] = weight
            levels[number, k] = level

        upper = subs() < TILE_X - FROM
        grouped = [jnp.where(upper, rows_w[s, k], rows_w[s, k + 1]) for s in range(9)]
        fx, fy = group_first(cell, grouped.__getitem__, keep)
        at = pl.multiple_of(8 * k + 16, 8)
        flat[0, pl.ds(at, 8), :] = fx
        flat[1, pl.ds(at, 8), :] = fy

    for f in range(2):
        moved_side = side[4 + f] + side[f] + STEP_DT * (side[2 + f] + STEP_DT * hold[f])
        for a in range(rows_a):
            beside[f, a] = side_columns(moved_side[a : a + 1])


def both_steps(place_args, shifts, *refs):
    place = Place(*place_args)
    disp, vel, node, inter, shell, speed, first, second, own, strip_d, strip_v = refs[:11]
    lead, rows_w, win, weights, levels, flat_in, beside, mid = refs[11:19]
    ends = refs[19 : 19 + len(shifts)]
    targets = refs[19 + len(shifts) : 23 + len(shifts)]
    scratch = refs[23 + len(shifts) :]
    out_disp, out_vel, out_shell, out_speed, gaps, halo, rim, rim_v, panes, fasts, hits, goals, ewin, ewords = scratch[:14]
    eweights, elevels, flat, flat2, seams, kinds, swin, cast, sems = scratch[14:]
    outs = (out_disp, out_vel, out_shell, out_speed)
    pairs = [(x.at[f], y.at[f]) for x, y in zip(outs[:2], targets[:2]) for f in range(2)] + list(zip(outs[2:], targets[2:]))
    copies = [pltpu.make_async_copy(x, y, sems.at[n]) for n, (x, y) in enumerate(pairs)]
    rows_a, tiles = disp.shape[1], disp.shape[2]
    rows, cols = place.shell_rows, place.shell_cols
    blocks = rows // 8
    right, left = place.sides(first[...], second[...])

    halo[...] = jnp.zeros_like(halo)
    contact = jnp.where(place.front, own[0:CONTACT_ROWS, :], 0.0)
    owners = own[OWN_ROWS : OWN_ROWS + CONTACT_ROWS, :]
    for shift, ref in zip(shifts, ends):
        partner = place.gx ^ shift
        at = 0
        if shift & (shift + 1) == 0:
            at = HALO_ROWS

            @pl.when(partner == place.gx - 1)
            def _():
                halo[0] = ref[0:HALO_ROWS, :]

            @pl.when(partner == place.gx + 1)
            def _():
                halo[1] = ref[0:HALO_ROWS, :]

        got = ref[at : at + CONTACT_ROWS, :]
        contact = jnp.where(partner == place.nx - 1, got, contact)
        owners = owners + got

    def wide(source, strip, row, count):
        return jnp.concatenate([source[row : row + count, :], strip[row : row + count, :]], axis=1)

    zeros = jnp.zeros((8, WIDE), F32)
    rim[0, 16:32, :] = wide(shell, strip_d, 0, 16)
    rim[1, 0:16, :] = wide(shell, strip_d, rows - 16, 16)
    rim_v[0, 8:16, :] = wide(speed, strip_v, 0, 8)
    rim_v[1, 0:8, :] = wide(speed, strip_v, rows - 8, 8)
    for ref, at in ((rim, (0, 0)), (rim, (0, 8)), (rim, (1, 16)), (rim, (1, 24)), (rim_v, (0, 0)), (rim_v, (1, 8))):
        ref[at[0], at[1] : at[1] + 8, :] = zeros
    for j in range(WIDE // PTS):
        cut = slice(j * PTS, (j + 1) * PTS)
        at = SHELL_AT + 6 * j
        rim[0, 12:16, cut] = halo[0, at : at + 4, :]
        rim_v[0, 6:8, cut] = halo[0, at + 4 : at + 6, :]
        rim[1, 16:20, cut] = halo[1, at : at + 4, :]
        rim_v[1, 8:10, cut] = halo[1, at + 4 : at + 6, :]
    numbers = node[...].astype(F32)
    node_rows = [numbers[b : b + 1] for b in range(tiles)] + [right[64:65], left[64:65]]
    gap_rows = [contact[8 + b : 9 + b] for b in range(tiles)] + [contact[16:17], contact[17:18]]
    soon_rows = [contact[b : b + 1] for b in range(tiles)]
    for j, (nodes, gap) in enumerate(zip(widen(node_rows.__getitem__, 5), widen(gap_rows.__getitem__, 5))):
        lay_out(gaps, (0,), j, place.met_bands(nodes), place.bands + 2)
        lay_out(gaps, (1,), j, place.met_bands(gap), place.bands + 2)
    for j, soon in enumerate(widen(soon_rows.__getitem__, 4)):
        lay_out(gaps, (2,), j, place.met_bands(soon), place.bands + 2)
    col = lax.broadcasted_iota(I32, (8, WIDE), 1)
    inside = jnp.where(col < cols, 1.0, 0.0)
    inside = jnp.where((col >= cols) & (col < cols + 64) & (place.gy < place.ny - 1), 1.0, inside)
    inside = jnp.where((col >= cols + 64) & (place.gy > 0), 1.0, inside)

    def first_rows(n, here, steady, keep=None):
        band = place.met_band(8 * n)
        hit = jnp.where(gaps[0, band] == place.nodes(8 * n, WIDE), STEP_DT * PENALTY, 0.0)
        push = hit * jnp.maximum(gaps[1, band] - here, 0.0)
        fast = steady + push
        there = (here + STEP_DT * fast) * (inside if keep is None else inside * keep)
        return there, fast[:, 0:cols], hit[:, 0:cols], gaps[2, band, :, 0:cols] - STEP_DT * push[:, 0:cols]

    for n in (-1, 0, blocks - 1, blocks):
        end = 0 if n < 1 else 1
        at = 8 * n + 16 if end == 0 else 8 * n - rows + 16
        bending = bending_of(lambda o: rim[end, at + o : at + o + 8, :])
        steady = rim_v[end, at - 8 : at, :] - (STEP_DT * BEND) * bending
        keep = None
        if n < 0:
            keep = jnp.where(place.gx > 0, 1.0, 0.0)
        elif n == blocks:
            keep = jnp.where(place.gx < place.nx - 1, 1.0, 0.0)
        there, *rest = first_rows(n, rim[end, at : at + 8, :], steady, keep)
        for part in (-1, 0, 1):
            if 0 <= n - part < blocks:
                panes[n - part, 8 + 8 * part : 16 + 8 * part, :] = there
        if 0 <= n < blocks:
            fasts[n], hits[n], goals[n] = rest

    def inner_block(n):
        at = pl.ds(pl.multiple_of(8 * n, 8), 8)
        there, *rest = first_rows(n, jnp.concatenate([shell[at, :], strip_d[at, :]], axis=1), mid[n - 1])
        for part in (-1, 0, 1):
            panes[n - part, 8 + 8 * part : 16 + 8 * part, :] = there
        fasts[n], hits[n], goals[n] = rest

    @pl.loop(0, (blocks - 2) // 2)
    def _(k):
        inner_block(2 * k + 1)
        inner_block(2 * k + 2)

    lane, sub = lanes(), subs()
    west, east = place.gy == 0, place.gy == place.ny - 1
    north, south = place.gx == 0, place.gx == place.nx - 1
    leftward = (lane & (TILE_Y - 1)) >= TILE_Y // 2
    last = rows_a - 1
    high = lane >= PTS // 2
    segment = ((lane + 16) >> 5) & 3

    def near_row(a, part):
        at = 8 * part + a
        return jnp.where(leftward[0:1], left[at : at + 1], right[at : at + 1])

    border = (-1, 0, last, rows_a)
    sides = {}
    for f in range(2):
        for a in (0, last):
            rest = near_row(a, 4 + f)
            whole = rest + near_row(a, f)
            sides[a, f] = (rest, whole, whole + STEP_DT * near_row(a, 2 + f))
        for a, end in ((-1, 0), (rows_a, 1)):
            sides[a, f] = [halo[end, SIDE_AT + 2 * n + f : SIDE_AT + 2 * n + f + 1, :] for n in range(3)]
    lead_side, far_lead = {}, {}
    straight = SIDEWAYS.index(0)
    for f in range(2):
        for a in border:
            lead_side[f, a] = side_columns(sides[a, f][2])
        at = LEAD_AT + 3 * f
        far_lead[f, 0], far_lead[f, 1] = halo[0, at - 5 : at + 3, :], halo[1, at : at + 8, :]
        for field in (f, 2 + f):
            cells, near = {}, {}
            for a in border:
                near[a] = side_columns(sides[a, f][field // 2])
            at = ROWS_AT + 6 * field
            cells[-1], cells[rows_a] = halo[0, at - 2 : at + 6, :], halo[1, at : at + 8, :]
            cells[0] = win[field, straight, 0, 0:8, :]
            cells[last] = win[field, straight, rows_a - 2, 8:16, :]
            for n, oy in enumerate(SIDEWAYS):
                ewin[field, n, 0, 0:8, :] = sideways(cells[-1], near[-1], oy)
                ewin[field, n, 0, 8:16, :] = win[field, n, 0, 0:8, :]
                ewin[field, n, 1, 0:8, :] = win[field, n, rows_a - 2, 8:16, :]
                ewin[field, n, 1, 8:16, :] = sideways(cells[rows_a], near[rows_a], oy)
            for half, (up, down) in enumerate(((-1, last), (0, rows_a))):
                pieces = [
                    jnp.where(high, near[up], cells[up]),
                    turn(jnp.where(high, cells[up], near[up]), 32),
                    turn(jnp.where(high, near[down], cells[down]), 64),
                    turn(jnp.where(high, cells[down], near[down]), 96),
                ]
                seam = pieces[3]
                for q in (2, 1, 0):
                    seam = jnp.where(segment == q, pieces[q], seam)
                for n, oy in enumerate(SIDEWAYS):
                    seams[field, n, 8 * half : 8 * half + 8, :] = turn(seam, -oy)
    for end in (0, 1):
        packed = halo[end, WORD_AT : WORD_AT + 8, :]
        packed = joined(packed, turn(packed, -16))
        for dx in (-1, 0, 1):
            for dy in (-1, 0, 1):
                s = slot(dx, dy)
                word = word_row(packed, s)
                if dy < 0:
                    word = jnp.where((lane < TILE_Y) & west, 0, word)
                if dy > 0:
                    word = jnp.where((lane >= PTS - TILE_Y) & east, 0, word)
                pair = (word, rows_w[s, 0]) if end == 0 else (rows_w[s, last], word)
                ewords[s, end] = jnp.where(sub < TILE_X - FROM, *pair)
    parts = []
    for at in (0, 1):
        rows_w = []
        for a in (-1, last, 0, rows_a):
            for n, values in enumerate((left, right)):
                if 0 <= a <= last:
                    rows_w.append(values[48 + 8 * at + a : 49 + 8 * at + a])
                else:
                    row = SIDE_AT + 6 + 2 * n + at
                    rows_w.append(halo[0 if a < 0 else 1, row : row + 1, :])
        parts.append(jnp.concatenate(rows_w, axis=0))
    packed = joined(*parts)
    for dx in (-1, 0, 1):
        for dy in (-1, 0, 1):
            s = slot(dx, dy)
            word = jnp.broadcast_to(packed[:, s : s + 1], (8, PTS))
            upper, lower = jnp.where(sub == segment, word, 0), jnp.where(sub == segment + 4, word, 0)
            for step in (4, 2, 1):
                upper, lower = upper | pltpu.roll(upper, step, 0), lower | pltpu.roll(lower, step, 0)
            if dx < 0:
                lower = jnp.where((segment < 2) & north, 0, lower)
            if dx > 0:
                upper = jnp.where((segment >= 2) & south, 0, upper)
            kinds[s] = jnp.where(sub < TILE_X - FROM, upper, lower)

    flat[...] = flat_in[...]
    for e in (0, 1):

        def keep_end(number, weight, level, e=e):
            eweights[number, e] = weight
            elevels[number, e] = level

        found = group_first(
            lambda f, oy, ox: ewin[f, SIDEWAYS.index(oy), e, FROM + ox : FROM + ox + 8, :],
            lambda s: ewords[s, e],
            keep_end,
        )
        for f in range(2):
            flat[f, 8 + 8 * rows_a * e : 16 + 8 * rows_a * e, :] = found[f]
    seam_f = group_first(
        lambda f, oy, ox: seams[f, SIDEWAYS.index(oy), FROM + ox : FROM + ox + 8, :],
        lambda s: kinds[s],
        lambda number, weight, level: None,
    )

    here = jnp.where(place.front, 1.0, 0.0)
    push = PENALTY * here * jnp.maximum(contact[8:18] - owners[8:18], 0.0)
    side_push = side_columns(jnp.where(leftward[0:1], push[9:10], push[8:9]))
    push = push[0:8]
    push_rows = flip(push)

    square = STEP_DT * STEP_DT
    for f in range(2):
        force = pltpu.roll(seam_f[f], FROM, 0)
        above = square * jnp.where(high, force, turn(force, -32))
        below = square * jnp.where(high, turn(force, -64), turn(force, -96))
        nears = {-1: lead_side[f, -1] + above, rows_a: lead_side[f, rows_a] + below}
        nears[0] = jnp.where(sub < FROM, lead_side[f, 0] + above, beside[f, 0])
        nears[last] = jnp.where(sub < FROM, beside[f, last], lead_side[f, last] + below)
        if f == 0:
            nears[last] = nears[last] - square * side_push
        for a in range(-1, rows_a + 1):
            cells = far_lead[f, 0 if a < 0 else 1] if a in (-1, rows_a) else lead[f, a]
            cells = cells + square * flat[f, 8 * a + 11 : 8 * a + 19, :]
            if a == last and f == 0:
                cells = cells - square * push_rows
            cast[f, 0, a + 1] = cells
            cast[f, 1, a + 1] = nears[a] if a in nears else beside[f, a]

    @pl.loop(0, 2)
    def _(f):
        for a in range(-1, rows_a + 1):
            cells, near = cast[f, 0, a + 1], cast[f, 1, a + 1]
            for n, oy in enumerate(SIDEWAYS):
                shifted = sideways(cells, near, oy)
                if a < rows_a:
                    swin[f, n, a + 1, 0:8, :] = shifted
                if a >= 0:
                    swin[f, n, a, 8:16, :] = shifted

    def second_group(k, kept):
        def cell(f, oy, ox):
            return swin[f, SIDEWAYS.index(oy), k, FROM + ox : FROM + ox + 8, :]

        fx, fy = group_second(cell, kept)
        at = pl.multiple_of(8 * k + 8, 8)
        flat2[0, pl.ds(at, 8), :] = fx
        flat2[1, pl.ds(at, 8), :] = fy

    def second_rows(n):
        row = pl.multiple_of(8 * n, 8)
        here = panes[n, 8:16, 0:cols]
        push = hits[n] * jnp.maximum(goals[n] - here, 0.0)
        bending = bending_of(lambda o: panes[n, 8 + o : 16 + o, :])[:, 0:cols]
        fast = fasts[n] + push - (STEP_DT * BEND) * bending
        out_speed[pl.ds(row, 8), :] = fast
        out_shell[pl.ds(row, 8), :] = here + STEP_DT * fast

    inner = rows_a - 1
    each = blocks // rows_a

    @pl.loop(0, inner // 2)
    def _(j):
        for h in range(2):
            k = 2 * j + h
            second_group(k + 1, lambda number: (weights[number, k], levels[number, k]))
            for part in range(each):
                second_rows(each * k + part)

    k = inner - 1
    second_group(k + 1, lambda number: (weights[number, k], levels[number, k]))
    for part in range(each):
        second_rows(each * k + part)

    tail = blocks - each * inner
    half = -(-tail // 2)

    @pl.loop(0, 2)
    def _(e):
        second_group(e * rows_a, lambda number: (eweights[number, e], elevels[number, e]))
        for part in range(half):
            second_rows(jnp.minimum(each * inner + half * e + part, blocks - 1))

    copies[4].start()
    copies[5].start()

    for f in range(2):
        thens = flips([flat2[f, 8 * a + 11 : 8 * a + 19, :] for a in range(rows_a)])
        wases = flips([flat[f, 8 * a + 11 : 8 * a + 19, :] for a in range(rows_a)])
        for a in range(rows_a):
            was = wases[a]
            then = thens[a]
            if f == 0 and a == last:
                was = was - push
                gap = disp[0, last] + STEP_DT * (vel[0, last] + STEP_DT * was) + inter[...]
                reached = owners[0:8] + square * push
                then = then - PENALTY * here * jnp.maximum(gap - reached, 0.0)
            fast = vel[f, a] + STEP_DT * was
            faster = fast + STEP_DT * then
            out_vel[f, a] = faster
            out_disp[f, a] = disp[f, a] + STEP_DT * (fast + faster)
        copies[f].start()
        copies[2 + f].start()
    for copy in copies:
        copy.wait()


def on_device(nx, ny, disp, vel, jit, words, node, inter, shell, speed):
    rows_a = disp.shape[1]
    rows, cols = shell.shape
    place_args = (nx, ny, rows, cols)
    shifts = tuple(range(1, nx))
    span, count, blocks = rows_a - 1, len(OFFSETS), rows // 8

    def call(body, out, scratch, *args, far=0, **more):
        args = [pltpu.with_memory_space_constraint(x, pltpu.MemorySpace.HBM) for x in args[:far]] + list(args[far:])
        specs = [pl.BlockSpec(memory_space=pltpu.MemorySpace.HBM)] * far
        specs += [pl.BlockSpec(memory_space=pltpu.VMEM)] * (len(args) - far)
        return pl.pallas_call(
            body,
            out_shape=out,
            in_specs=specs,
            scratch_shapes=scratch,
            **more,
            compiler_params=pltpu.CompilerParams(vmem_limit_bytes=20 * 1024 * 1024),
        )(*args)

    def shaped(*shape, dtype=F32):
        return jax.ShapeDtypeStruct(shape + (PTS,), dtype)

    def like(*arrays):
        return [jax.ShapeDtypeStruct(x.shape, x.dtype) for x in arrays]

    wide = pltpu.VMEM((TILE_X, 8, cols), F32)
    tall = pltpu.VMEM((rows + 2 * PAD, cols), F32)
    edges = pltpu.VMEM((2, rows, PTS), F32)
    far_shell, far_speed = shell, speed
    small = (disp, vel, jit, words, node, inter)
    first, second, *small = call(
        functools.partial(pack_sides, place_args),
        [shaped(Y_ROWS)] * 2 + like(*small),
        [edges, edges, wide, pltpu.SemaphoreType.DMA((10,))],
        *small,
        far_shell,
        far_speed,
        far=8,
    )
    disp, vel, jit, words, node, inter = small
    first = lax.ppermute(first, "gy", [(i, i ^ 1) for i in range(ny)])
    second = lax.ppermute(
        second,
        ("gx", "gy"),
        [
            (i * ny + j, i * ny + ((j - 1) ^ 1) + 1 if 0 < j < ny - 1 else (i ^ 1) * ny + j)
            for i in range(nx)
            for j in range(ny)
        ],
    )

    shell, speed, lattice, lead, rows_w, shore = call(
        functools.partial(own_parts, place_args),
        like(far_shell, far_speed)
        + [
            shaped(4, rows_a, 8),
            shaped(2, rows_a, 8),
            shaped(9, rows_a, 8, dtype=I32),
            shaped(2 * disp.shape[2]),
        ],
        [tall, tall, pltpu.VMEM((2, TILE_X, 8, cols), F32), pltpu.SemaphoreType.DMA((4,))],
        far_shell,
        far_speed,
        disp,
        vel,
        jit,
        words,
        node,
        far=2,
    )

    outs = [shaped(CONTACT_ROWS + (HALO_ROWS if s & (s + 1) == 0 else 0)) for s in shifts]
    *ends, own, strip_d, strip_v = call(
        functools.partial(pack_ends, place_args, shifts),
        outs + [shaped(2 * OWN_ROWS), shaped(rows), shaped(rows)],
        [
            pltpu.VMEM((4, len(SIDEWAYS), 24, PTS), F32),
            pltpu.VMEM((rows + 2 * PAD, PTS), F32),
            pltpu.VMEM((TILE_X, 8, PTS), F32),
        ],
        *small,
        shell,
        speed,
        lattice,
        lead,
        rows_w,
        shore,
        first,
        second,
    )
    ends = [
        lax.ppermute(
            e,
            ("gx", "gy"),
            [
                (i * ny + j, i * ny + (j ^ 1) if s & (s + 1) and nx - 1 not in (i, i ^ s) else (i ^ s) * ny + j)
                for i in range(nx)
                for j in range(ny)
            ],
        )
        for s, e in zip(shifts, ends)
    ]

    inner = call(
        functools.partial(inner_rows, place_args),
        [
            shaped(4, len(SIDEWAYS), span, 16),
            shaped(count, span, 8),
            shaped(count, span, 8),
            shaped(2, 8 * (rows_a + 3)),
            shaped(2, rows_a, 8),
            jax.ShapeDtypeStruct((blocks - 2, 8, WIDE), F32),
        ],
        [
            pltpu.VMEM((4, 3, 24, PTS), F32),
            pltpu.VMEM((9, 8, PTS), I32),
            pltpu.VMEM((blocks - 2, 24, WIDE), F32),
            pltpu.VMEM((2, 8, PTS), F32),
            pltpu.VMEM((6, 8, PTS), F32),
        ],
        disp,
        jit,
        shell,
        speed,
        lattice,
        rows_w,
        first,
        second,
        strip_d,
        strip_v,
    )

    out = [jax.ShapeDtypeStruct(x.shape, F32) for x in (disp, vel, shell, speed)]
    scratch = [pltpu.VMEM(x.shape, F32) for x in out] + [
        pltpu.VMEM((3, TILE_X, 8, WIDE), F32),
        pltpu.VMEM((2, HALO_ROWS, PTS), F32),
        pltpu.VMEM((2, 32, WIDE), F32),
        pltpu.VMEM((2, 16, WIDE), F32),
        pltpu.VMEM((blocks, 24, WIDE), F32),
        pltpu.VMEM((blocks, 8, cols), F32),
        pltpu.VMEM((blocks, 8, cols), F32),
        pltpu.VMEM((blocks, 8, cols), F32),
        pltpu.VMEM((4, len(SIDEWAYS), 2, 16, PTS), F32),
        pltpu.VMEM((9, 2, 8, PTS), I32),
        pltpu.VMEM((count, 2, 8, PTS), F32),
        pltpu.VMEM((count, 2, 8, PTS), F32),
        pltpu.VMEM((2, 8 * (rows_a + 3), PTS), F32),
        pltpu.VMEM((2, 8 * (rows_a + 3), PTS), F32),
        pltpu.VMEM((4, len(SIDEWAYS), 16, PTS), F32),
        pltpu.VMEM((9, 8, PTS), I32),
        pltpu.VMEM((2, len(SIDEWAYS), rows_a + 1, 16, PTS), F32),
        pltpu.VMEM((2, 2, rows_a + 2, 8, PTS), F32),
        pltpu.SemaphoreType.DMA((6,)),
    ]
    return tuple(
        call(
            functools.partial(both_steps, place_args, shifts),
            out,
            scratch,
            disp,
            vel,
            node,
            inter,
            shell,
            speed,
            first,
            second,
            own,
            strip_d,
            strip_v,
            lead,
            rows_w,
            *inner,
            *ends,
            out_specs=[pl.BlockSpec(memory_space=pltpu.MemorySpace.HBM)] * 4,
        )
    )


def solution(mesh):
    in_specs = (
        P(None, "gx", "gy", None),
        P(None, "gx", "gy", None),
        P(None, "gx", "gy", None),
        P("gx", "gy", None),
        P("gy", None),
        P("gy", None),
        P("gx", "gy"),
        P("gx", "gy"),
    )
    out_specs = (P(None, "gx", "gy", None), P(None, "gx", "gy", None), P("gx", "gy"), P("gx", "gy"))
    body = functools.partial(on_device, mesh.shape["gx"], mesh.shape["gy"])
    return jax.shard_map(body, mesh=mesh, in_specs=in_specs, out_specs=out_specs, check_vma=False)
```

```python
import functools

import jax
import jax.numpy as jnp
from jax import lax
from jax.experimental import pallas as pl
from jax.experimental.pallas import tpu as pltpu
from jax.sharding import PartitionSpec as P

TILE_X = 8
TILE_Y = 16
PTS = 128
SPLIT = 4

HORIZON = 3.5
DELTA_SQ = 0.25
PENALTY = 4.0
BEND = 0.5
STEP_DT = 0.2

F32 = jnp.float32
I32 = jnp.int32

STRIDE = 24
WIDE = 640
PAD = 16


def bond_offsets():
    limit = HORIZON * HORIZON - DELTA_SQ
    found = []
    for oy in range(-4, 5):
        for ox in range(-4, 5):
            near = max(abs(ox) - 0.4, 0.0) ** 2 + max(abs(oy) - 0.4, 0.0) ** 2
            if near < limit and (ox or oy):
                found.append((ox, oy))
    return found


OFFSETS = bond_offsets()
SIDEWAYS = sorted({oy for _, oy in OFFSETS})


def sign(value):
    return (value > 0) - (value < 0)


def lanes():
    return lax.broadcasted_iota(I32, (8, PTS), 1)


def subs():
    return lax.broadcasted_iota(I32, (8, PTS), 0)


def turn(values, shift):
    size = values.shape[1]
    return pltpu.roll(values, shift % size, 1) if shift % size else values


def slot(dx, dy):
    return 3 * (dx + 1) + dy + 1


def lane_masks():
    lane = lanes()
    row, col = lane // TILE_Y, lane % TILE_Y
    masks = {}
    for o in (1, 2, 3):
        masks["col_at", o] = col < o
        masks["col_at", -o] = col >= TILE_Y - o
        masks["col_from", o] = col >= TILE_Y - o
        masks["col_from", -o] = col < o
        masks["row_at", o] = row < o
        masks["row_at", -o] = row >= TILE_X - o
        masks["row_from", o] = row >= TILE_X - o
        masks["row_from", -o] = row < o
    bits = {}
    for ox in range(-3, 4):
        bits[ox] = jnp.left_shift(jnp.int32(1), 4 * row + ((row + ox) & 7) // 2)
    return masks, bits


def across(cells, ox, masks):
    if not ox:
        return cells[0]
    return turn(jnp.where(masks["row_at", ox], cells[sign(ox)], cells[0]), -TILE_Y * ox)


def pick_lanes(block, index):
    return jnp.take_along_axis(block, index, axis=1, mode="promise_in_bounds")


def flips(blocks):
    lane, sub = lanes(), subs()
    for level in (2, 1, 0):
        step = 1 << level
        stay = ((lane >> (level + 4)) ^ (sub >> level)) & 1 == 0
        if step == 4:
            others = [turn(pltpu.roll(block, 4, 0), 64) for block in blocks]
        else:
            low = (sub >> level) & 1 == 0
            index = lane ^ (TILE_Y * step)
            others = [jnp.where(low, pltpu.roll(block, 8 - step, 0), pltpu.roll(block, step, 0)) for block in blocks]
            others = [pick_lanes(block, index) for block in others]
        blocks = [jnp.where(stay, block, other) for block, other in zip(blocks, others)]
    return blocks


def flip(block):
    return flips([block])[0]


def side_columns(row):
    return pick_lanes(jnp.broadcast_to(row, (8, PTS)), TILE_Y * subs() + (lanes() & (TILE_Y - 1)))


def word_row(packed, s):
    word = jnp.where(subs() == lanes() // TILE_Y, jnp.broadcast_to(packed[:, s : s + 1], (8, PTS)), 0)
    for step in (4, 2, 1):
        word = word | pltpu.roll(word, step, 0)
    return word


def sideways(cells, beside, oy):
    if not oy:
        return cells
    lane = lanes()
    mask = lane < oy if oy > 0 else lane >= PTS + oy
    return turn(jnp.where(mask, beside, cells), -oy)


FROM = 5


def group_masks(start):
    lane, sub = lanes(), subs()
    row = (sub + start) & (TILE_X - 1)
    col = lane & (TILE_Y - 1)
    masks, bits = {}, {}
    for o in (1, 2, 3):
        masks["col", o] = col >= TILE_Y - o
        masks["col", -o] = col < o
        masks["row", o] = row >= TILE_X - o
        masks["row", -o] = row < o
    for ox in range(-3, 4):
        bits[ox] = jnp.left_shift(jnp.int32(1), 4 * row + ((row + ox) & 7) // 2)
    return masks, bits


def group_first(cell, word, keep, start=FROM):
    masks, bits = group_masks(start)
    zero = [cell(f, 0, 0) for f in range(4)]
    fx = jnp.zeros((8, PTS), F32)
    fy = jnp.zeros((8, PTS), F32)
    plain = [word(slot(dx, 0)) for dx in (-1, 0, 1)]
    for oy in SIDEWAYS:
        words = plain
        if oy:
            words = [jnp.where(masks["col", oy], word(slot(dx, sign(oy))), plain[dx + 1]) for dx in (-1, 0, 1)]
        base_y, base_v = zero[1] - float(oy), zero[3] - float(oy)
        for number, (ox, other) in enumerate(OFFSETS):
            if other != oy:
                continue
            picked = words[1]
            if ox:
                picked = jnp.where(masks["row", ox], words[sign(ox) + 1], picked)
            intact = (picked & bits[ox]) != 0
            rest_x = cell(0, oy, ox) - (zero[0] - float(ox))
            rest_y = cell(1, oy, ox) - base_y
            now_x = cell(2, oy, ox) - (zero[2] - float(ox))
            now_y = cell(3, oy, ox) - base_v
            rest_sq = rest_x * rest_x + rest_y * rest_y + DELTA_SQ
            now_sq = now_x * now_x + now_y * now_y + DELTA_SQ
            rest_inv = lax.rsqrt(rest_sq)
            reach = jnp.maximum(1.0 - rest_sq * rest_inv * (1.0 / HORIZON), 0.0)
            weight = jnp.where(intact, reach * reach, 0.0)
            level = weight * rest_inv
            keep(number, weight, level)
            factor = level - weight * lax.rsqrt(now_sq)
            fx = fx + factor * now_x
            fy = fy + factor * now_y
    return fx, fy


def group_second(cell, kept):
    zero = [cell(f, 0, 0) for f in range(2)]
    fx = jnp.zeros((8, PTS), F32)
    fy = jnp.zeros((8, PTS), F32)
    for number, (ox, oy) in enumerate(OFFSETS):
        now_x = cell(0, oy, ox) - (zero[0] - float(ox))
        now_y = cell(1, oy, ox) - (zero[1] - float(oy))
        now_sq = now_x * now_x + now_y * now_y + DELTA_SQ
        weight, level = kept(number)
        factor = level - weight * lax.rsqrt(now_sq)
        fx = fx + factor * now_x
        fy = fy + factor * now_y
    return fx, fy


def bending_of(row):
    here = row(0)
    one, two = row(-1) + row(1), row(-2) + row(2)
    beside = 2.0 * one - 8.0 * here
    out = two - 8.0 * one + 20.0 * here
    return out + turn(beside + turn(here, 1), 1) + turn(beside + turn(here, -1), -1)


def joined(low_part, high_part):
    return jnp.left_shift(high_part.astype(I32), 16) | low_part.astype(I32)


def widen(row_of, count):
    lane, sub = lanes(), subs()
    index = sub * TILE_Y + (lane % 64) // SPLIT
    out = []
    for j in range(count):
        left, right = (
            pick_lanes(jnp.broadcast_to(row_of(b), (8, PTS)), index) for b in (2 * j, 2 * j + 1)
        )
        out.append(jnp.where(lane < 64, left, right))
    return out


def narrow(block_of, tiles):
    lane, sub = lanes(), subs()
    out, sums = [], {}
    for b in tiles:
        if b // 2 not in sums:
            held = block_of(b // 2)
            held = held + turn(held, -1)
            sums[b // 2] = held + turn(held, -2)
        held = sums[b // 2]
        picked = pick_lanes(held, 64 * (b % 2) + SPLIT * (lane % TILE_Y))
        out.append(jnp.sum(jnp.where(sub == lane // TILE_Y, picked, 0.0), axis=0, keepdims=True))
    return out


def lay_out(ref, at, j, block, count=TILE_X):
    for row in range(count):
        ref[at + (row, slice(None), slice(j * PTS, (j + 1) * PTS))] = jnp.broadcast_to(block[row : row + 1], (8, PTS))


class Place:
    def __init__(self, nx, ny, shell_rows, shell_cols):
        self.nx, self.ny = nx, ny
        self.gx, self.gy = lax.axis_index("gx"), lax.axis_index("gy")
        self.shell_rows, self.shell_cols = shell_rows, shell_cols
        self.width = shell_cols * ny
        self.band = shell_rows * nx // TILE_X
        self.bands = shell_rows // self.band
        self.front = self.gx == nx - 1

    def sides(self, first, second):
        even = self.gy % 2 == 0
        right = jnp.where(even, first, second)
        left = jnp.where(even, second, first)
        right = jnp.where(self.gy < self.ny - 1, right, 0.0)
        left = jnp.where(self.gy > 0, left, 0.0)
        return right, left

    def nodes(self, row, columns):
        shape = (8, columns)
        col = lax.broadcasted_iota(I32, shape, 1)
        if columns > self.shell_cols:
            col = jnp.where(col >= self.shell_cols + 64, col - columns, col)
        first = (self.gx * self.shell_rows + row) * self.width + self.gy * self.shell_cols
        return (first + lax.broadcasted_iota(I32, shape, 0) * self.width + col).astype(F32)

    def parts(self):
        inner = [list(range(p * self.band, (p + 1) * self.band, 8)) for p in range(self.bands)]
        return [[-8]] + inner + [[self.shell_rows]]

    def met_bands(self, block):
        return pltpu.roll(block, (TILE_X + 1 - self.gx * self.bands) & (TILE_X - 1), 0)

    def met_band(self, row):
        return (row + self.band) // self.band

    def band_of(self, row):
        return jnp.clip((self.gx * self.shell_rows + row + self.band) // self.band - 1, 0, TILE_X - 1)


Y_ROWS = 88


def fetch(pairs, sems):
    copies = [pltpu.make_async_copy(source, target, sems.at[n]) for n, (source, target) in enumerate(pairs)]
    for copy in copies:
        copy.start()
    for copy in copies:
        copy.wait()


def pack_sides(place_args, *refs):
    sources, (first, second), held = refs[:8], refs[8:10], refs[10:16]
    shell, speed, wide_ref, sems = refs[16:]
    place = Place(*place_args)
    pairs = list(zip(sources[:6], held))
    for source, target in zip(sources[6:], (shell, speed)):
        for n, at in enumerate((0, place.shell_cols - PTS)):
            pairs.append((source.at[:, pl.ds(at, PTS)], target.at[n]))
    fetch(pairs, sems)
    disp, vel, jit, words, node, inter = held
    tiles = disp.shape[2]
    even = place.gy % 2 == 0
    blocks = place.shell_cols // PTS
    numbers = node[...].astype(F32)
    edge_blocks = (0, blocks - 1)
    for j in edge_blocks:
        lay_out(wide_ref, (), j, place.met_bands(widen(lambda b: numbers[b : b + 1], blocks)[j]), place.bands + 2)
    held = {}
    for j in edge_blocks:
        total = jnp.zeros((8, PTS), F32)
        for part in range(place.bands):
            summed = jnp.zeros((8, PTS), F32)
            for row in range(part * place.band, (part + 1) * place.band, 8):
                wanted = wide_ref[place.met_band(row), :, j * PTS : (j + 1) * PTS]
                ids = place.nodes(row, PTS) + float(j * PTS)
                summed = summed + jnp.where(wanted == ids, shell[min(j, 1), row : row + 8, :], 0.0)
            summed = jnp.sum(summed, axis=0, keepdims=True)
            total = total + jnp.where(subs() == place.band_of(part * place.band), summed, 0.0)
        held[j] = total
    met = narrow(lambda j: held[j], (0, tiles - 1))

    ends = [(jnp.transpose(x[1])[PTS - 8 :], jnp.transpose(x[0])[:8]) for x in (shell, speed)]

    def send(ref, to_right):
        edge = jnp.where(to_right, tiles - 1, 0)
        for f, source in enumerate((disp, disp, vel, vel, jit, jit)):
            ref[8 * f : 8 * f + 8, :] = jnp.where(
                to_right, source[f % 2, :, tiles - 1, :], source[f % 2, :, 0, :]
            )
        ref[48:Y_ROWS, :] = jnp.zeros((Y_ROWS - 48, PTS), F32)
        edge_words = jnp.where(to_right, words[:, tiles - 1, :], words[:, 0, :])
        ref[48:56, 0:9] = (edge_words & 65535).astype(F32)
        ref[56:64, 0:9] = jnp.right_shift(edge_words, 16).astype(F32)
        ref[64:65, :] = jnp.where(to_right, numbers[tiles - 1 : tiles], numbers[0:1])
        ref[65:66, :] = jnp.where(to_right, inter[tiles - 1 : tiles, :], inter[0:1, :])
        ref[66:67, :] = jnp.where(to_right, met[1], met[0])
        for f, source in enumerate((shell, speed)):
            ref[72 + 8 * f : 80 + 8 * f, :] = jnp.where(to_right, *ends[f])

    send(first, even)
    send(second, jnp.logical_not(even))


def own_parts(place_args, far_shell, far_speed, disp, vel, jit, words, node, *refs):
    place = Place(*place_args)
    shell, speed, lattice, lead, rows_w, shore, tall, tall_v, wide_ref, sems = refs
    rows_a, tiles = disp.shape[1], disp.shape[2]
    rows, cols = place.shell_rows, place.shell_cols
    lane = lanes()
    west, east = place.gy == 0, place.gy == place.ny - 1
    north, south = place.gx == 0, place.gx == place.nx - 1
    span = pl.ds(PAD, rows)
    copies = [
        pltpu.make_async_copy(source, target, sems.at[n])
        for n, (source, target) in enumerate(
            (
                (far_shell, shell),
                (far_speed, speed),
                (far_shell, tall.at[span]),
                (far_speed, tall_v.at[span]),
            )
        )
    ]
    for copy in copies:
        copy.start()
    for ref in (tall, tall_v):
        ref[0:PAD, :] = jnp.zeros((PAD, cols), F32)
        ref[PAD + rows :, :] = jnp.zeros((PAD, cols), F32)

    @pl.loop(0, 2)
    def _(f):
        rest = [jit[f, a] for a in range(rows_a)]
        whole = [jit[f, a] + disp[f, a] for a in range(rows_a)]
        soon = [x + STEP_DT * vel[f, a] for a, x in enumerate(whole)]
        for a, (x, y, z) in enumerate(zip(flips(rest), flips(whole), flips(soon))):
            lattice[f, a] = x
            lattice[2 + f, a] = y
            lead[f, a] = z

    @pl.loop(0, rows_a)
    def _(a):
        packed = words[a]
        for dx in (-1, 0, 1):
            for dy in (-1, 0, 1):
                word = word_row(packed, slot(dx, dy))
                if dy < 0:
                    word = jnp.where((lane < TILE_Y) & west, 0, word)
                if dy > 0:
                    word = jnp.where((lane >= PTS - TILE_Y) & east, 0, word)
                if dx < 0:
                    word = jnp.where((a == 0) & north, 0, word)
                if dx > 0:
                    word = jnp.where((a == rows_a - 1) & south, 0, word)
                rows_w[slot(dx, dy), a] = word

    numbers = node[...].astype(F32)
    node_row = jnp.floor(numbers * (1.0 / place.width))
    node_col = numbers - node_row * place.width - (place.gy * cols).astype(F32)
    node_row = node_row - (place.gx * rows).astype(F32)
    at_row = widen(lambda b: node_row[b : b + 1], cols // PTS)
    at_col = jnp.concatenate(widen(lambda b: node_col[b : b + 1], cols // PTS), axis=1)
    col = lax.broadcasted_iota(I32, (8, cols), 1)
    split = col & (SPLIT - 1)
    near_row = jnp.concatenate(at_row, axis=1)
    near_row = jnp.where(split < SPLIT // 2, turn(near_row, SPLIT), turn(near_row, -SPLIT))
    for j, block in enumerate(at_row):
        lay_out(wide_ref, (0,), j, place.met_bands(block), place.bands + 2)
        lay_out(wide_ref, (1,), j, place.met_bands(near_row[:, j * PTS : (j + 1) * PTS]), place.bands + 2)
    for copy in copies:
        copy.wait()
    sub_wide = lax.broadcasted_iota(I32, (8, cols), 0)
    row_wide = sub_wide.astype(F32)
    square = STEP_DT * STEP_DT * BEND
    sums = [jnp.zeros((8, cols), F32)] * 5
    for part in place.parts():
        found = [jnp.zeros((8, cols), F32)] * 5
        band = place.band_of(part[0])
        for row in part:
            at = PAD + row
            here = tall[at : at + 8, :]
            one = tall[at - 1 : at + 7, :] + tall[at + 1 : at + 9, :]
            two = tall[at - 2 : at + 6, :] + tall[at + 2 : at + 10, :]
            beside = 2.0 * one - 8.0 * here
            later = here + STEP_DT * tall_v[at : at + 8, :] - square * (two - 8.0 * one + 20.0 * here)
            hit = wide_ref[0, place.met_band(row)] == row_wide + float(row)
            near = wide_ref[1, place.met_band(row)] == row_wide + float(row)
            picks = ((hit, later), (hit, beside), (hit, here), (near, beside), (near, here))
            found = [x + jnp.where(mask, value, 0.0) for x, (mask, value) in zip(found, picks)]
        sums = [
            x + jnp.where(sub_wide == band, jnp.sum(y, axis=0, keepdims=True), 0.0) for x, y in zip(sums, found)
        ]
    later, beside, here, beside_near, here_near = sums
    spread = jnp.where(split < 3, turn(beside, -1), turn(beside_near, -1)) * (col < cols - 1).astype(F32)
    spread += jnp.where(split > 0, turn(beside, 1), turn(beside_near, 1)) * (col > 0).astype(F32)
    spread += jnp.where(split < 2, turn(here, -2), turn(here_near, -2)) * (col < cols - 2).astype(F32)
    spread += jnp.where(split > 1, turn(here, 2), turn(here_near, 2)) * (col > 1).astype(F32)
    hit = at_col == col.astype(F32)
    ahead = jnp.where(hit, later - square * spread, 0.0)
    met = jnp.where(hit, here, 0.0)
    for base, values in ((0, ahead), (tiles, met)):
        for b, row in enumerate(narrow(lambda j: values[:, j * PTS : (j + 1) * PTS], range(tiles))):
            shore[base + b : base + b + 1, :] = row


ROWS_AT, LEAD_AT, SIDE_AT, WORD_AT, SHELL_AT, HALO_ROWS = 2, 26, 32, 42, 50, 80
CONTACT_ROWS, OWN_ROWS = 18, 24


def shell_strip(right, left, at):
    middle = jnp.zeros((PTS - 16, PTS), F32)
    return jnp.transpose(jnp.concatenate([right[at : at + 8], middle, left[at : at + 8]], axis=0))


def pack_ends(
    place_args, shifts, disp, vel, jit, words, node, inter, shell, speed, lattice, lead, rows_w, shore, first, second, *refs
):
    place = Place(*place_args)
    outs = refs[: len(shifts)]
    own, strip_d, strip_v, grid, tall, wide_ref = refs[len(shifts) :]
    rows_a, tiles = disp.shape[1], disp.shape[2]
    rows, cols = place.shell_rows, place.shell_cols
    right, left = place.sides(first[...], second[...])
    lane, sub = lanes(), subs()
    leftward = (lane[0:1] & (TILE_Y - 1)) >= TILE_Y // 2
    last = rows_a - 1

    for f in range(4):
        for level, a in enumerate((last - 1, last)):
            at = 32 + 8 * (f % 2) + a
            row = jnp.where(leftward, left[at : at + 1], right[at : at + 1])
            if f >= 2:
                at = 8 * (f % 2) + a
                row = row + jnp.where(leftward, left[at : at + 1], right[at : at + 1])
            near = side_columns(row)
            for n, oy in enumerate(SIDEWAYS):
                grid[f, n, 8 * level : 8 * level + 8, :] = sideways(lattice[f, a], near, oy)
        for n in range(len(SIDEWAYS)):
            grid[f, n, 16:24, :] = jnp.zeros((8, PTS), F32)
    force, _ = group_first(
        lambda f, oy, ox: grid[f, SIDEWAYS.index(oy), 8 + ox : 16 + ox, :],
        lambda s: rows_w[s, last] if s < 6 else jnp.zeros((8, PTS), I32),
        lambda number, weight, level: None,
        start=0,
    )
    gap = disp[0, last] + inter[...]
    own[0:8, :] = gap + STEP_DT * (vel[0, last] + STEP_DT * flip(force))
    own[8:16, :] = gap
    own[16:17, :] = right[last : last + 1] + right[65:66]
    own[17:18, :] = left[last : last + 1] + left[65:66]

    halo_d = shell_strip(right, left, 72)
    halo_v = shell_strip(right, left, 80)
    strip_d[...] = halo_d
    strip_v[...] = halo_v
    for at in (0, 8, PAD + rows, PAD + rows + 8):
        tall[at : at + 8, :] = jnp.zeros((8, PTS), F32)
    tall[PAD : PAD + rows, :] = halo_d
    numbers = node[...].astype(F32)
    blocks = widen(lambda b: numbers[b : b + 1], cols // PTS)
    low = lane < PTS // 2
    lay_out(wide_ref, (), 0, place.met_bands(jnp.where(low, blocks[0], blocks[-1])), place.bands + 2)
    far = jnp.where(low, 0.0, float(cols - PTS))
    ahead = jnp.zeros((8, PTS), F32)
    for part in place.parts():
        soon = jnp.zeros((8, PTS), F32)
        band = place.band_of(part[0])
        for row in part:
            at = PAD + row
            here = tall[at : at + 8, :]
            column = 2.0 * (tall[at - 1 : at + 7, :] + tall[at + 1 : at + 9, :]) - 8.0 * here
            from_left = turn(jnp.where(low, 0.0, column), 1) + turn(jnp.where(low, 0.0, here), 2)
            from_right = turn(jnp.where(low, column, 0.0), -1) + turn(jnp.where(low, here, 0.0), -2)
            hit = wide_ref[place.met_band(row)] == place.nodes(row, PTS) + far
            soon = soon + jnp.where(hit, jnp.where(low, from_left, from_right), 0.0)
        ahead = ahead + jnp.where(sub == band, jnp.sum(soon, axis=0, keepdims=True), 0.0)
    base = OWN_ROWS
    own[base : base + 16, :] = shore[...]
    for b, row in zip((0, tiles - 1), narrow(lambda j: ahead, (0, tiles - 1))):
        own[base + b : base + b + 1, :] = shore[b : b + 1, :] - (STEP_DT * STEP_DT * BEND) * row
    own[base + 16 : base + 17, :] = right[66:67]
    own[base + 17 : base + 18, :] = left[66:67]

    mine = jnp.where(place.front, own[0:CONTACT_ROWS, :], own[base : base + CONTACT_ROWS, :])
    for shift, out in zip(shifts, outs):
        at = 0
        if shift & (shift + 1) == 0:
            at = HALO_ROWS
            down = (place.gx ^ shift) > place.gx
            out[0:ROWS_AT, :] = jnp.zeros((ROWS_AT, PTS), F32)
            for f in range(4):
                to = ROWS_AT + 6 * f
                out[to : to + 6, :] = jnp.where(down, lattice[f, last, 2:8, :], lattice[f, 0, 0:6, :])
            for f in range(2):
                to = LEAD_AT + 3 * f
                out[to : to + 3, :] = jnp.where(down, lead[f, last, 5:8, :], lead[f, 0, 0:3, :])

                def merged(part):
                    rows_of = [x[8 * part + a : 8 * part + a + 1] for a in (last, 0) for x in (left, right)]
                    return jnp.where(leftward, jnp.where(down, rows_of[0], rows_of[2]), jnp.where(down, rows_of[1], rows_of[3]))

                rest = merged(4 + f)
                whole = rest + merged(f)
                for n, values in enumerate((rest, whole, whole + STEP_DT * merged(2 + f))):
                    out[SIDE_AT + 2 * n + f : SIDE_AT + 2 * n + f + 1, :] = values
            for n, values in enumerate((left, right)):
                for part in range(2):
                    to, row = SIDE_AT + 6 + 2 * n + part, 48 + 8 * part
                    out[to : to + 1, :] = jnp.where(down, values[row + last : row + last + 1], values[row : row + 1])
            out[WORD_AT : WORD_AT + 8, :] = jnp.zeros((8, PTS), F32)
            edge_words = jnp.where(down, words[last], words[0])
            out[WORD_AT : WORD_AT + 8, 0:9] = (edge_words & 65535).astype(F32)
            out[WORD_AT : WORD_AT + 8, 16:25] = jnp.right_shift(edge_words, 16).astype(F32)
            for j in range(WIDE // PTS):
                cut = slice(j * PTS, (j + 1) * PTS)
                if j < cols // PTS:
                    d_low, d_high = shell[0:4, cut], shell[rows - 4 : rows, cut]
                    v_low, v_high = speed[0:2, cut], speed[rows - 2 : rows, cut]
                else:
                    d_low, d_high = halo_d[0:4], halo_d[rows - 4 : rows]
                    v_low, v_high = halo_v[0:2], halo_v[rows - 2 : rows]
                to = SHELL_AT + 6 * j
                out[to : to + 4, :] = jnp.where(down, d_high, d_low)
                out[to + 4 : to + 6, :] = jnp.where(down, v_high, v_low)
        out[at : at + CONTACT_ROWS, :] = mine


def inner_rows(place_args, disp, jit, shell, speed, lattice, rows_w, first, second, strip_d, strip_v, *refs):
    place = Place(*place_args)
    win, weights, levels, flat, beside, mid, strips, kinds, panes, hold, side = refs
    cols = place.shell_cols
    rows_a, tiles = disp.shape[1], disp.shape[2]
    right, left = place.sides(first[...], second[...])
    lane = lanes()
    leftward = (lane & (TILE_Y - 1)) >= TILE_Y // 2
    for f in range(6):
        side[f] = jnp.where(leftward, left[8 * f : 8 * f + 8], right[8 * f : 8 * f + 8])

    strips[...] = jnp.zeros_like(strips)

    @pl.loop(0, 2)
    def _(c):
        for part in range(2):
            f = c + 2 * part
            whole = jit[c] + disp[c] if part else jit[c]
            beyond = side[4 + c] + side[c] if part else side[4 + c]
            strips[f, 0, 8:16, :] = beyond
            strips[f, 1, 8:16, :] = turn(whole[:, 0, :], TILE_Y)
            strips[f, 2, 8:16, :] = turn(whole[:, tiles - 1, :], -TILE_Y)
            nears = [side_columns(beyond[a : a + 1]) for a in range(rows_a)]
            for a, near in enumerate(nears):
                cells = lattice[f, a]
                for n, oy in enumerate(SIDEWAYS):
                    shifted = sideways(cells, near, oy)
                    if a < rows_a - 1:
                        win[f, n, a, 0:8, :] = shifted
                    if a > 0:
                        win[f, n, a - 1, 8:16, :] = shifted

    left_words = joined(left[48:56], left[56:64])
    right_words = joined(right[48:56], right[56:64])
    for s in range(9):
        kinds[s] = jnp.where(
            leftward,
            jnp.broadcast_to(left_words[:, s : s + 1], (8, PTS)),
            jnp.broadcast_to(right_words[:, s : s + 1], (8, PTS)),
        )

    flat[...] = jnp.zeros_like(flat)

    blocks = mid.shape[0]

    for n in range(blocks):
        panes[n, :, 0:cols] = shell[8 * n : 8 * n + 24, :]
        panes[n, :, cols:WIDE] = strip_d[8 * n : 8 * n + 24, :]

    each = -(-blocks // (rows_a - 1))

    def bend_block(n):
        at = pl.multiple_of(8 * n + 8, 8)
        bending = bending_of(lambda o: panes[n, 8 + o : 16 + o, :])
        mid[n, :, 0:cols] = speed[pl.ds(at, 8), :] - (STEP_DT * BEND) * bending[:, 0:cols]
        mid[n, :, cols:WIDE] = strip_v[pl.ds(at, 8), :] - (STEP_DT * BEND) * bending[:, cols:WIDE]

    hold[...] = jnp.zeros_like(hold)
    reach_y = len(SIDEWAYS) // 2

    def side_bonds(k):
        masks, bits = lane_masks()
        oy = k - reach_y
        at = jnp.where(oy > 0, 1, jnp.where(oy < 0, 2, 0))
        towards = jnp.where(oy > 0, 1, jnp.where(oy < 0, -1, 0)) + 1
        col = lane & (TILE_Y - 1)
        crossed = (col < oy) | (col >= TILE_Y + oy)
        crossing = (col >= TILE_Y - oy) | (col < -oy)
        cells = [
            {
                dx: pltpu.roll(
                    jnp.where(crossed, strips[f, at, 8 + dx : 16 + dx, :], strips[f, 0, 8 + dx : 16 + dx, :]),
                    (PTS - oy) & (PTS - 1),
                    1,
                )
                for dx in (-1, 0, 1)
            }
            for f in range(4)
        ]
        words = [jnp.where(crossing, kinds[3 * dx + towards], kinds[3 * dx + 1]) for dx in range(3)]
        zero = [strips[f, 0, 8:16, :] for f in range(4)]
        step = oy.astype(F32)
        base_y, base_v = zero[1] - step, zero[3] - step
        fx, fy = hold[0], hold[1]
        for ox in range(-3, 4):
            word = words[1]
            if ox:
                word = jnp.where(masks["row_from", ox], words[sign(ox) + 1], word)
            rest_x = across(cells[0], ox, masks) - (zero[0] - float(ox))
            rest_y = across(cells[1], ox, masks) - base_y
            now_x = across(cells[2], ox, masks) - (zero[2] - float(ox))
            now_y = across(cells[3], ox, masks) - base_v
            rest_sq = rest_x * rest_x + rest_y * rest_y + DELTA_SQ
            now_sq = now_x * now_x + now_y * now_y + DELTA_SQ
            rest_inv = lax.rsqrt(rest_sq)
            reach = jnp.maximum(1.0 - rest_sq * rest_inv * (1.0 / HORIZON), 0.0)
            weight = jnp.where((word & bits[ox]) != 0, reach * reach, 0.0)
            factor = weight * (rest_inv - lax.rsqrt(now_sq))
            fx, fy = fx + factor * now_x, fy + factor * now_y
        hold[0], hold[1] = fx, fy

    if rows_a - 1 != len(SIDEWAYS):
        pl.loop(0, len(SIDEWAYS))(side_bonds)

    @pl.loop(0, rows_a - 1)
    def _(k):
        if rows_a - 1 == len(SIDEWAYS):
            side_bonds(k)
        for part in range(each):
            bend_block(jnp.minimum(each * k + part, blocks - 1))

        def cell(f, oy, ox):
            return win[f, SIDEWAYS.index(oy), k, FROM + ox : FROM + ox + 8, :]

        def keep(number, weight, level):
            weights[number, k] = weight
            levels[number, k] = level

        upper = subs() < TILE_X - FROM
        grouped = [jnp.where(upper, rows_w[s, k], rows_w[s, k + 1]) for s in range(9)]
        fx, fy = group_first(cell, grouped.__getitem__, keep)
        at = pl.multiple_of(8 * k + 16, 8)
        flat[0, pl.ds(at, 8), :] = fx
        flat[1, pl.ds(at, 8), :] = fy

    for f in range(2):
        moved_side = side[4 + f] + side[f] + STEP_DT * (side[2 + f] + STEP_DT * hold[f])
        for a in range(rows_a):
            beside[f, a] = side_columns(moved_side[a : a + 1])


def both_steps(place_args, shifts, *refs):
    place = Place(*place_args)
    disp, vel, node, inter, shell, speed, first, second, own, strip_d, strip_v = refs[:11]
    lead, rows_w, win, weights, levels, flat_in, beside, mid = refs[11:19]
    ends = refs[19 : 19 + len(shifts)]
    targets = refs[19 + len(shifts) : 23 + len(shifts)]
    scratch = refs[23 + len(shifts) :]
    out_disp, out_vel, out_shell, out_speed, gaps, halo, rim, rim_v, panes, fasts, hits, goals, ewin, ewords = scratch[:14]
    eweights, elevels, flat, flat2, seams, kinds, swin, cast, sems = scratch[14:]
    outs = (out_disp, out_vel, out_shell, out_speed)
    pairs = [(x.at[f], y.at[f]) for x, y in zip(outs[:2], targets[:2]) for f in range(2)] + list(zip(outs[2:], targets[2:]))
    copies = [pltpu.make_async_copy(x, y, sems.at[n]) for n, (x, y) in enumerate(pairs)]
    rows_a, tiles = disp.shape[1], disp.shape[2]
    rows, cols = place.shell_rows, place.shell_cols
    blocks = rows // 8
    right, left = place.sides(first[...], second[...])

    halo[...] = jnp.zeros_like(halo)
    contact = jnp.where(place.front, own[0:CONTACT_ROWS, :], 0.0)
    owners = own[OWN_ROWS : OWN_ROWS + CONTACT_ROWS, :]
    for shift, ref in zip(shifts, ends):
        partner = place.gx ^ shift
        at = 0
        if shift & (shift + 1) == 0:
            at = HALO_ROWS

            @pl.when(partner == place.gx - 1)
            def _():
                halo[0] = ref[0:HALO_ROWS, :]

            @pl.when(partner == place.gx + 1)
            def _():
                halo[1] = ref[0:HALO_ROWS, :]

        got = ref[at : at + CONTACT_ROWS, :]
        contact = jnp.where(partner == place.nx - 1, got, contact)
        owners = owners + got

    def wide(source, strip, row, count):
        return jnp.concatenate([source[row : row + count, :], strip[row : row + count, :]], axis=1)

    zeros = jnp.zeros((8, WIDE), F32)
    rim[0, 16:32, :] = wide(shell, strip_d, 0, 16)
    rim[1, 0:16, :] = wide(shell, strip_d, rows - 16, 16)
    rim_v[0, 8:16, :] = wide(speed, strip_v, 0, 8)
    rim_v[1, 0:8, :] = wide(speed, strip_v, rows - 8, 8)
    for ref, at in ((rim, (0, 0)), (rim, (0, 8)), (rim, (1, 16)), (rim, (1, 24)), (rim_v, (0, 0)), (rim_v, (1, 8))):
        ref[at[0], at[1] : at[1] + 8, :] = zeros
    for j in range(WIDE // PTS):
        cut = slice(j * PTS, (j + 1) * PTS)
        at = SHELL_AT + 6 * j
        rim[0, 12:16, cut] = halo[0, at : at + 4, :]
        rim_v[0, 6:8, cut] = halo[0, at + 4 : at + 6, :]
        rim[1, 16:20, cut] = halo[1, at : at + 4, :]
        rim_v[1, 8:10, cut] = halo[1, at + 4 : at + 6, :]
    numbers = node[...].astype(F32)
    node_rows = [numbers[b : b + 1] for b in range(tiles)] + [right[64:65], left[64:65]]
    gap_rows = [contact[8 + b : 9 + b] for b in range(tiles)] + [contact[16:17], contact[17:18]]
    soon_rows = [contact[b : b + 1] for b in range(tiles)]
    for j, (nodes, gap) in enumerate(zip(widen(node_rows.__getitem__, 5), widen(gap_rows.__getitem__, 5))):
        lay_out(gaps, (0,), j, place.met_bands(nodes), place.bands + 2)
        lay_out(gaps, (1,), j, place.met_bands(gap), place.bands + 2)
    for j, soon in enumerate(widen(soon_rows.__getitem__, 4)):
        lay_out(gaps, (2,), j, place.met_bands(soon), place.bands + 2)
    col = lax.broadcasted_iota(I32, (8, WIDE), 1)
    inside = jnp.where(col < cols, 1.0, 0.0)
    inside = jnp.where((col >= cols) & (col < cols + 64) & (place.gy < place.ny - 1), 1.0, inside)
    inside = jnp.where((col >= cols + 64) & (place.gy > 0), 1.0, inside)

    def first_rows(n, here, steady, keep=None):
        band = place.met_band(8 * n)
        hit = jnp.where(gaps[0, band] == place.nodes(8 * n, WIDE), STEP_DT * PENALTY, 0.0)
        push = hit * jnp.maximum(gaps[1, band] - here, 0.0)
        fast = steady + push
        there = (here + STEP_DT * fast) * (inside if keep is None else inside * keep)
        return there, fast[:, 0:cols], hit[:, 0:cols], gaps[2, band, :, 0:cols] - STEP_DT * push[:, 0:cols]

    for n in (-1, 0, blocks - 1, blocks):
        end = 0 if n < 1 else 1
        at = 8 * n + 16 if end == 0 else 8 * n - rows + 16
        bending = bending_of(lambda o: rim[end, at + o : at + o + 8, :])
        steady = rim_v[end, at - 8 : at, :] - (STEP_DT * BEND) * bending
        keep = None
        if n < 0:
            keep = jnp.where(place.gx > 0, 1.0, 0.0)
        elif n == blocks:
            keep = jnp.where(place.gx < place.nx - 1, 1.0, 0.0)
        there, *rest = first_rows(n, rim[end, at : at + 8, :], steady, keep)
        for part in (-1, 0, 1):
            if 0 <= n - part < blocks:
                panes[n - part, 8 + 8 * part : 16 + 8 * part, :] = there
        if 0 <= n < blocks:
            fasts[n], hits[n], goals[n] = rest

    def inner_block(n):
        at = pl.ds(pl.multiple_of(8 * n, 8), 8)
        there, *rest = first_rows(n, jnp.concatenate([shell[at, :], strip_d[at, :]], axis=1), mid[n - 1])
        for part in (-1, 0, 1):
            panes[n - part, 8 + 8 * part : 16 + 8 * part, :] = there
        fasts[n], hits[n], goals[n] = rest

    @pl.loop(0, (blocks - 2) // 2)
    def _(k):
        inner_block(2 * k + 1)
        inner_block(2 * k + 2)

    lane, sub = lanes(), subs()
    west, east = place.gy == 0, place.gy == place.ny - 1
    north, south = place.gx == 0, place.gx == place.nx - 1
    leftward = (lane & (TILE_Y - 1)) >= TILE_Y // 2
    last = rows_a - 1
    high = lane >= PTS // 2
    segment = ((lane + 16) >> 5) & 3

    def near_row(a, part):
        at = 8 * part + a
        return jnp.where(leftward[0:1], left[at : at + 1], right[at : at + 1])

    border = (-1, 0, last, rows_a)
    sides = {}
    for f in range(2):
        for a in (0, last):
            rest = near_row(a, 4 + f)
            whole = rest + near_row(a, f)
            sides[a, f] = (rest, whole, whole + STEP_DT * near_row(a, 2 + f))
        for a, end in ((-1, 0), (rows_a, 1)):
            sides[a, f] = [halo[end, SIDE_AT + 2 * n + f : SIDE_AT + 2 * n + f + 1, :] for n in range(3)]
    lead_side, far_lead = {}, {}
    straight = SIDEWAYS.index(0)
    for f in range(2):
        for a in border:
            lead_side[f, a] = side_columns(sides[a, f][2])
        at = LEAD_AT + 3 * f
        far_lead[f, 0], far_lead[f, 1] = halo[0, at - 5 : at + 3, :], halo[1, at : at + 8, :]
        for field in (f, 2 + f):
            cells, near = {}, {}
            for a in border:
                near[a] = side_columns(sides[a, f][field // 2])
            at = ROWS_AT + 6 * field
            cells[-1], cells[rows_a] = halo[0, at - 2 : at + 6, :], halo[1, at : at + 8, :]
            cells[0] = win[field, straight, 0, 0:8, :]
            cells[last] = win[field, straight, rows_a - 2, 8:16, :]
            for n, oy in enumerate(SIDEWAYS):
                ewin[field, n, 0, 0:8, :] = sideways(cells[-1], near[-1], oy)
                ewin[field, n, 0, 8:16, :] = win[field, n, 0, 0:8, :]
                ewin[field, n, 1, 0:8, :] = win[field, n, rows_a - 2, 8:16, :]
                ewin[field, n, 1, 8:16, :] = sideways(cells[rows_a], near[rows_a], oy)
            for half, (up, down) in enumerate(((-1, last), (0, rows_a))):
                pieces = [
                    jnp.where(high, near[up], cells[up]),
                    turn(jnp.where(high, cells[up], near[up]), 32),
                    turn(jnp.where(high, near[down], cells[down]), 64),
                    turn(jnp.where(high, cells[down], near[down]), 96),
                ]
                seam = pieces[3]
                for q in (2, 1, 0):
                    seam = jnp.where(segment == q, pieces[q], seam)
                for n, oy in enumerate(SIDEWAYS):
                    seams[field, n, 8 * half : 8 * half + 8, :] = turn(seam, -oy)
    for end in (0, 1):
        packed = halo[end, WORD_AT : WORD_AT + 8, :]
        packed = joined(packed, turn(packed, -16))
        for dx in (-1, 0, 1):
            for dy in (-1, 0, 1):
                s = slot(dx, dy)
                word = word_row(packed, s)
                if dy < 0:
                    word = jnp.where((lane < TILE_Y) & west, 0, word)
                if dy > 0:
                    word = jnp.where((lane >= PTS - TILE_Y) & east, 0, word)
                pair = (word, rows_w[s, 0]) if end == 0 else (rows_w[s, last], word)
                ewords[s, end] = jnp.where(sub < TILE_X - FROM, *pair)
    parts = []
    for at in (0, 1):
        rows_w = []
        for a in (-1, last, 0, rows_a):
            for n, values in enumerate((left, right)):
                if 0 <= a <= last:
                    rows_w.append(values[48 + 8 * at + a : 49 + 8 * at + a])
                else:
                    row = SIDE_AT + 6 + 2 * n + at
                    rows_w.append(halo[0 if a < 0 else 1, row : row + 1, :])
        parts.append(jnp.concatenate(rows_w, axis=0))
    packed = joined(*parts)
    for dx in (-1, 0, 1):
        for dy in (-1, 0, 1):
            s = slot(dx, dy)
            word = jnp.broadcast_to(packed[:, s : s + 1], (8, PTS))
            upper, lower = jnp.where(sub == segment, word, 0), jnp.where(sub == segment + 4, word, 0)
            for step in (4, 2, 1):
                upper, lower = upper | pltpu.roll(upper, step, 0), lower | pltpu.roll(lower, step, 0)
            if dx < 0:
                lower = jnp.where((segment < 2) & north, 0, lower)
            if dx > 0:
                upper = jnp.where((segment >= 2) & south, 0, upper)
            kinds[s] = jnp.where(sub < TILE_X - FROM, upper, lower)

    flat[...] = flat_in[...]
    for e in (0, 1):

        def keep_end(number, weight, level, e=e):
            eweights[number, e] = weight
            elevels[number, e] = level

        found = group_first(
            lambda f, oy, ox: ewin[f, SIDEWAYS.index(oy), e, FROM + ox : FROM + ox + 8, :],
            lambda s: ewords[s, e],
            keep_end,
        )
        for f in range(2):
            flat[f, 8 + 8 * rows_a * e : 16 + 8 * rows_a * e, :] = found[f]
    seam_f = group_first(
        lambda f, oy, ox: seams[f, SIDEWAYS.index(oy), FROM + ox : FROM + ox + 8, :],
        lambda s: kinds[s],
        lambda number, weight, level: None,
    )

    here = jnp.where(place.front, 1.0, 0.0)
    push = PENALTY * here * jnp.maximum(contact[8:18] - owners[8:18], 0.0)
    side_push = side_columns(jnp.where(leftward[0:1], push[9:10], push[8:9]))
    push = push[0:8]
    push_rows = flip(push)

    square = STEP_DT * STEP_DT
    for f in range(2):
        force = pltpu.roll(seam_f[f], FROM, 0)
        above = square * jnp.where(high, force, turn(force, -32))
        below = square * jnp.where(high, turn(force, -64), turn(force, -96))
        nears = {-1: lead_side[f, -1] + above, rows_a: lead_side[f, rows_a] + below}
        nears[0] = jnp.where(sub < FROM, lead_side[f, 0] + above, beside[f, 0])
        nears[last] = jnp.where(sub < FROM, beside[f, last], lead_side[f, last] + below)
        if f == 0:
            nears[last] = nears[last] - square * side_push
        for a in range(-1, rows_a + 1):
            cells = far_lead[f, 0 if a < 0 else 1] if a in (-1, rows_a) else lead[f, a]
            cells = cells + square * flat[f, 8 * a + 11 : 8 * a + 19, :]
            if a == last and f == 0:
                cells = cells - square * push_rows
            cast[f, 0, a + 1] = cells
            cast[f, 1, a + 1] = nears[a] if a in nears else beside[f, a]

    @pl.loop(0, 2)
    def _(f):
        for a in range(-1, rows_a + 1):
            cells, near = cast[f, 0, a + 1], cast[f, 1, a + 1]
            for n, oy in enumerate(SIDEWAYS):
                shifted = sideways(cells, near, oy)
                if a < rows_a:
                    swin[f, n, a + 1, 0:8, :] = shifted
                if a >= 0:
                    swin[f, n, a, 8:16, :] = shifted

    def second_group(k, kept):
        def cell(f, oy, ox):
            return swin[f, SIDEWAYS.index(oy), k, FROM + ox : FROM + ox + 8, :]

        fx, fy = group_second(cell, kept)
        at = pl.multiple_of(8 * k + 8, 8)
        flat2[0, pl.ds(at, 8), :] = fx
        flat2[1, pl.ds(at, 8), :] = fy

    def second_rows(n):
        row = pl.multiple_of(8 * n, 8)
        here = panes[n, 8:16, 0:cols]
        push = hits[n] * jnp.maximum(goals[n] - here, 0.0)
        bending = bending_of(lambda o: panes[n, 8 + o : 16 + o, :])[:, 0:cols]
        fast = fasts[n] + push - (STEP_DT * BEND) * bending
        out_speed[pl.ds(row, 8), :] = fast
        out_shell[pl.ds(row, 8), :] = here + STEP_DT * fast

    inner = rows_a - 1
    each = blocks // rows_a

    @pl.loop(0, inner // 2)
    def _(j):
        for h in range(2):
            k = 2 * j + h
            second_group(k + 1, lambda number: (weights[number, k], levels[number, k]))
            for part in range(each):
                second_rows(each * k + part)

    k = inner - 1
    second_group(k + 1, lambda number: (weights[number, k], levels[number, k]))
    for part in range(each):
        second_rows(each * k + part)

    tail = blocks - each * inner
    half = -(-tail // 2)

    @pl.loop(0, 2)
    def _(e):
        second_group(e * rows_a, lambda number: (eweights[number, e], elevels[number, e]))
        for part in range(half):
            second_rows(jnp.minimum(each * inner + half * e + part, blocks - 1))

    copies[4].start()
    copies[5].start()

    for f in range(2):
        thens = flips([flat2[f, 8 * a + 11 : 8 * a + 19, :] for a in range(rows_a)])
        wases = flips([flat[f, 8 * a + 11 : 8 * a + 19, :] for a in range(rows_a)])
        for a in range(rows_a):
            was = wases[a]
            then = thens[a]
            if f == 0 and a == last:
                was = was - push
                gap = disp[0, last] + STEP_DT * (vel[0, last] + STEP_DT * was) + inter[...]
                reached = owners[0:8] + square * push
                then = then - PENALTY * here * jnp.maximum(gap - reached, 0.0)
            fast = vel[f, a] + STEP_DT * was
            faster = fast + STEP_DT * then
            out_vel[f, a] = faster
            out_disp[f, a] = disp[f, a] + STEP_DT * (fast + faster)
        copies[f].start()
        copies[2 + f].start()
    for copy in copies:
        copy.wait()


def on_device(nx, ny, disp, vel, jit, words, node, inter, shell, speed):
    rows_a = disp.shape[1]
    rows, cols = shell.shape
    place_args = (nx, ny, rows, cols)
    shifts = tuple(range(1, nx))
    span, count, blocks = rows_a - 1, len(OFFSETS), rows // 8

    def call(body, out, scratch, *args, far=0, **more):
        args = [pltpu.with_memory_space_constraint(x, pltpu.MemorySpace.HBM) for x in args[:far]] + list(args[far:])
        specs = [pl.BlockSpec(memory_space=pltpu.MemorySpace.HBM)] * far
        specs += [pl.BlockSpec(memory_space=pltpu.VMEM)] * (len(args) - far)
        return pl.pallas_call(
            body,
            out_shape=out,
            in_specs=specs,
            scratch_shapes=scratch,
            **more,
            compiler_params=pltpu.CompilerParams(vmem_limit_bytes=20 * 1024 * 1024),
        )(*args)

    def shaped(*shape, dtype=F32):
        return jax.ShapeDtypeStruct(shape + (PTS,), dtype)

    def like(*arrays):
        return [jax.ShapeDtypeStruct(x.shape, x.dtype) for x in arrays]

    wide = pltpu.VMEM((TILE_X, 8, cols), F32)
    tall = pltpu.VMEM((rows + 2 * PAD, cols), F32)
    edges = pltpu.VMEM((2, rows, PTS), F32)
    far_shell, far_speed = shell, speed
    small = (disp, vel, jit, words, node, inter)
    first, second, *small = call(
        functools.partial(pack_sides, place_args),
        [shaped(Y_ROWS)] * 2 + like(*small),
        [edges, edges, wide, pltpu.SemaphoreType.DMA((10,))],
        *small,
        far_shell,
        far_speed,
        far=8,
    )
    disp, vel, jit, words, node, inter = small
    first = lax.ppermute(first, "gy", [(i, i ^ 1) for i in range(ny)])
    second = lax.ppermute(
        second,
        ("gx", "gy"),
        [
            (i * ny + j, i * ny + ((j - 1) ^ 1) + 1 if 0 < j < ny - 1 else (i ^ 1) * ny + j)
            for i in range(nx)
            for j in range(ny)
        ],
    )

    shell, speed, lattice, lead, rows_w, shore = call(
        functools.partial(own_parts, place_args),
        like(far_shell, far_speed)
        + [
            shaped(4, rows_a, 8),
            shaped(2, rows_a, 8),
            shaped(9, rows_a, 8, dtype=I32),
            shaped(2 * disp.shape[2]),
        ],
        [tall, tall, pltpu.VMEM((2, TILE_X, 8, cols), F32), pltpu.SemaphoreType.DMA((4,))],
        far_shell,
        far_speed,
        disp,
        vel,
        jit,
        words,
        node,
        far=2,
    )

    outs = [shaped(CONTACT_ROWS + (HALO_ROWS if s & (s + 1) == 0 else 0)) for s in shifts]
    *ends, own, strip_d, strip_v = call(
        functools.partial(pack_ends, place_args, shifts),
        outs + [shaped(2 * OWN_ROWS), shaped(rows), shaped(rows)],
        [
            pltpu.VMEM((4, len(SIDEWAYS), 24, PTS), F32),
            pltpu.VMEM((rows + 2 * PAD, PTS), F32),
            pltpu.VMEM((TILE_X, 8, PTS), F32),
        ],
        *small,
        shell,
        speed,
        lattice,
        lead,
        rows_w,
        shore,
        first,
        second,
    )
    ends = [
        lax.ppermute(
            e,
            ("gx", "gy"),
            [
                (i * ny + j, i * ny + (j ^ 1) if s & (s + 1) and nx - 1 not in (i, i ^ s) else (i ^ s) * ny + j)
                for i in range(nx)
                for j in range(ny)
            ],
        )
        for s, e in zip(shifts, ends)
    ]

    inner = call(
        functools.partial(inner_rows, place_args),
        [
            shaped(4, len(SIDEWAYS), span, 16),
            shaped(count, span, 8),
            shaped(count, span, 8),
            shaped(2, 8 * (rows_a + 3)),
            shaped(2, rows_a, 8),
            jax.ShapeDtypeStruct((blocks - 2, 8, WIDE), F32),
        ],
        [
            pltpu.VMEM((4, 3, 24, PTS), F32),
            pltpu.VMEM((9, 8, PTS), I32),
            pltpu.VMEM((blocks - 2, 24, WIDE), F32),
            pltpu.VMEM((2, 8, PTS), F32),
            pltpu.VMEM((6, 8, PTS), F32),
        ],
        disp,
        jit,
        shell,
        speed,
        lattice,
        rows_w,
        first,
        second,
        strip_d,
        strip_v,
    )

    out = [jax.ShapeDtypeStruct(x.shape, F32) for x in (disp, vel, shell, speed)]
    scratch = [pltpu.VMEM(x.shape, F32) for x in out] + [
        pltpu.VMEM((3, TILE_X, 8, WIDE), F32),
        pltpu.VMEM((2, HALO_ROWS, PTS), F32),
        pltpu.VMEM((2, 32, WIDE), F32),
        pltpu.VMEM((2, 16, WIDE), F32),
        pltpu.VMEM((blocks, 24, WIDE), F32),
        pltpu.VMEM((blocks, 8, cols), F32),
        pltpu.VMEM((blocks, 8, cols), F32),
        pltpu.VMEM((blocks, 8, cols), F32),
        pltpu.VMEM((4, len(SIDEWAYS), 2, 16, PTS), F32),
        pltpu.VMEM((9, 2, 8, PTS), I32),
        pltpu.VMEM((count, 2, 8, PTS), F32),
        pltpu.VMEM((count, 2, 8, PTS), F32),
        pltpu.VMEM((2, 8 * (rows_a + 3), PTS), F32),
        pltpu.VMEM((2, 8 * (rows_a + 3), PTS), F32),
        pltpu.VMEM((4, len(SIDEWAYS), 16, PTS), F32),
        pltpu.VMEM((9, 8, PTS), I32),
        pltpu.VMEM((2, len(SIDEWAYS), rows_a + 1, 16, PTS), F32),
        pltpu.VMEM((2, 2, rows_a + 2, 8, PTS), F32),
        pltpu.SemaphoreType.DMA((6,)),
    ]
    return tuple(
        call(
            functools.partial(both_steps, place_args, shifts),
            out,
            scratch,
            disp,
            vel,
            node,
            inter,
            shell,
            speed,
            first,
            second,
            own,
            strip_d,
            strip_v,
            lead,
            rows_w,
            *inner,
            *ends,
            out_specs=[pl.BlockSpec(memory_space=pltpu.MemorySpace.HBM)] * 4,
        )
    )


def solution(mesh):
    in_specs = (
        P(None, "gx", "gy", None),
        P(None, "gx", "gy", None),
        P(None, "gx", "gy", None),
        P("gx", "gy", None),
        P("gy", None),
        P("gy", None),
        P("gx", "gy"),
        P("gx", "gy"),
    )
    out_specs = (P(None, "gx", "gy", None), P(None, "gx", "gy", None), P("gx", "gy"), P("gx", "gy"))
    body = functools.partial(on_device, mesh.shape["gx"], mesh.shape["gy"])
    return jax.shard_map(body, mesh=mesh, in_specs=in_specs, out_specs=out_specs, check_vma=False)
```
